32 devices in a mesh: rows: 8 (over z, x), cols: 4 (over y, core).
Axes of the slice: x: 2, y: 2, z: 4, core: 2. Of those that a mesh axis runs over, the one named last changes fastest.
Arguments:
- states: bfloat16 [8, 96, 176, 768], P(None, 'rows', 'cols'), may hold values from -6 to 6
- heights: int32 [8], replicated, may hold values from 32 to 90, as said below
- widths: int32 [8], replicated, may hold values from 64 to 176, as said below
- first_gain: float32 [768], replicated, may hold values from 0.5 to 1.5
- first_shift: float32 [768], replicated, may hold values from -3 to 3
- filter_inner: bfloat16 [2, 8, 96, 96], P(None, 'cols'), may hold values from -0.4375 to 0.4375
- inner_bias: float32 [2, 8, 96], P(None, 'cols'), may hold values from -0.75 to 0.75
- filter_outer: bfloat16 [2, 8, 96, 96], P(None, 'cols'), may hold values from -0.4375 to 0.4375
- outer_bias: float32 [2, 8, 96], P(None, 'cols'), may hold values from -0.3125 to 0.3125
- later_gain: float32 [768], replicated, may hold values from 0.5 to 1.5
- later_shift: float32 [768], replicated, may hold values from -3 to 3
- expand_weight: bfloat16 [768, 3072], replicated, may hold values from -0.21875 to 0.21875
- expand_bias: float32 [3072], replicated, may hold values from -1.5 to 1.5
- reduce_weight: bfloat16 [3072, 768], replicated, may hold values from -0.109375 to 0.109375
- reduce_bias: float32 [768], replicated, may hold values from -1.5 to 1.5
- cotangent: bfloat16 [8, 96, 176, 768], P(None, 'rows', 'cols'), may hold values from -6 to 6
Outputs:
- result: bfloat16 [8, 96, 176, 768], P(None, 'rows', 'cols')
- states_grad: bfloat16 [8, 96, 176, 768], P(None, 'rows', 'cols')
- first_gain_grad: float32 [768], replicated
- first_shift_grad: float32 [768], replicated
- filter_inner_grad: float32 [2, 8, 96, 96], P(None, 'cols')
- inner_bias_grad: float32 [2, 8, 96], P(None, 'cols')
- filter_outer_grad: float32 [2, 8, 96, 96], P(None, 'cols')
- outer_bias_grad: float32 [2, 8, 96], P(None, 'cols')
- later_gain_grad: float32 [768], replicated
- later_shift_grad: float32 [768], replicated
- expand_weight_grad: float32 [768, 3072], replicated
- expand_bias_grad: float32 [3072], replicated
- reduce_weight_grad: float32 [3072, 768], replicated
- reduce_bias_grad: float32 [768], replicated
The draws below stay inside these ranges and needn't reach their ends.
Inputs may be any that keep to these rules, and one draw needn't show every extreme that they name: `heights`: some frame has exactly 90 rows. `widths`: some frame spans all 176 columns.
All inputs are finite; a program needn't handle non-finite values.
Results may differ from the reference program's by a relative error of at most 0.012.
The reference program's roundings to bfloat16 on the way count: a program that leaves them out, or rounds other values in their place, can miss the bound.
Values sent between devices are 32-bit elements; how exact they have to be, the bound alone decides.
A program may use at most 576 MiB of HBM per device.

```python
import jax
import jax.numpy as jnp
from jax import lax

C = 768
BLOCKS = 8
HID = 3072
BS = 96
H = 96
W = 176
BINS = 96
SUBS = 8


def draw_heights(key, part):
    key = jax.random.fold_in(key, 17)
    value_key, pick_key = jax.random.split(key)
    values = jax.random.randint(value_key, (SUBS,), H // 3, H - H // 16 + 1, dtype=jnp.int32)
    chosen = jax.random.randint(pick_key, (), 0, SUBS, dtype=jnp.int32)
    return jnp.where(jnp.arange(SUBS, dtype=jnp.int32) == chosen, H - H // 16, values).astype(jnp.int32)


def draw_widths(key, part):
    key = jax.random.fold_in(key, 29)
    value_key, pick_key = jax.random.split(key)
    values = jax.random.randint(value_key, (SUBS,), W * 4 // 11, W + 1, dtype=jnp.int32)
    chosen = jax.random.randint(pick_key, (), 0, SUBS, dtype=jnp.int32)
    return jnp.where(jnp.arange(SUBS, dtype=jnp.int32) == chosen, W, values).astype(jnp.int32)


def block_levels(rng, dims, cuts, low, high):
    level, own = 1.0, jax.random.fold_in(rng, 6)
    for axis_at, blocks in cuts:
        steps = jnp.exp(jax.random.uniform(jax.random.fold_in(own, axis_at), (blocks,), jnp.float32, low / len(cuts), high / len(cuts)))
        level = level * jnp.repeat(steps, dims[axis_at] // blocks).reshape([-1 if axis == axis_at else 1 for axis in range(len(dims))])
    return level


def noise(rng, shape, scale, limit, pieces=(), kind=jnp.bfloat16):
    array = scale * jax.random.normal(rng, shape, jnp.float32)
    if pieces:
        array = array * block_levels(rng, shape, pieces, -0.22, 0.18)
    return jnp.clip(array, -limit, limit).astype(kind)


def setup_inputs(seed: int = 0) -> dict:
    key_list = jax.random.split(jax.random.key(seed), 17)
    states = noise(key_list[0], (SUBS, H, W, C), 1.0, 6.0, ((1, 8), (2, 4)))
    heights = draw_heights(jax.random.fold_in(key_list[16], 71), 0)
    widths = draw_widths(jax.random.fold_in(key_list[16], 71), 0)
    first_gain = jnp.clip(1.0 + 0.1 * jax.random.normal(key_list[3], (C,), jnp.float32), 0.5, 1.5)
    first_shift = noise(key_list[4], (C,), 0.2, 3.0, (), jnp.float32)
    filter_inner = noise(key_list[5], (2, BLOCKS, BS, BS), (2 * BS) ** -0.5, 0.4375, ((1, 4),))
    inner_bias = noise(key_list[6], (2, BLOCKS, BS), 0.05, 0.75, ((1, 4),), jnp.float32)
    filter_outer = noise(key_list[7], (2, BLOCKS, BS, BS), (2 * BS) ** -0.5, 0.4375, ((1, 4),))
    outer_bias = noise(key_list[8], (2, BLOCKS, BS), 0.02, 0.3125, ((1, 4),), jnp.float32)
    later_gain = jnp.clip(1.0 + 0.1 * jax.random.normal(key_list[9], (C,), jnp.float32), 0.5, 1.5)
    later_shift = noise(key_list[10], (C,), 0.2, 3.0, (), jnp.float32)
    expand_weight = noise(key_list[11], (C, HID), C ** -0.5, 0.21875)
    expand_bias = noise(key_list[12], (HID,), 0.1, 1.5, (), jnp.float32)
    reduce_weight = noise(key_list[13], (HID, C), HID ** -0.5, 0.109375)
    reduce_bias = noise(key_list[14], (C,), 0.1, 1.5, (), jnp.float32)
    cotangent = noise(key_list[15], (SUBS, H, W, C), 1.0, 6.0, ((1, 8), (2, 4)))
    return dict(states=states, heights=heights, widths=widths, first_gain=first_gain, first_shift=first_shift, filter_inner=filter_inner, inner_bias=inner_bias, filter_outer=filter_outer, outer_bias=outer_bias, later_gain=later_gain, later_shift=later_shift, expand_weight=expand_weight, expand_bias=expand_bias, reduce_weight=reduce_weight, reduce_bias=reduce_bias, cotangent=cotangent)


@jax.custom_vjp
def low(v):
    return lax.optimization_barrier(v.astype(jnp.bfloat16)).astype(jnp.float32)

@jax.custom_vjp
def low_back(v):
    return v

def low_keep(v):
    return (low(v), None)

def low_pass(kept, grad):
    return (grad,)

def back_keep(v):
    return (v, None)

def back_low(kept, grad):
    return (low(grad),)
low.defvjp(low_keep, low_pass)
low_back.defvjp(back_keep, back_low)
norm_eps = 1e-06
shrink_width = 0.01
highest = lax.Precision.HIGHEST

def gelu_exact(v):
    return jax.nn.gelu(v, approximate=False)

def layer_norm(v, gain, shift):
    centre = lax.optimization_barrier(jnp.mean(v, axis=-1, keepdims=True))
    centred = v - centre
    spread = lax.optimization_barrier(jnp.mean(centred * centred, axis=-1, keepdims=True))
    return centred * lax.rsqrt(spread + norm_eps) * gain + shift

def complex_mix(real, imag, weight):
    first = jnp.einsum('hkbi,bio->hkbo', real, weight[0], precision=highest)
    second = jnp.einsum('hkbi,bio->hkbo', imag, weight[1], precision=highest)
    third = jnp.einsum('hkbi,bio->hkbo', imag, weight[0], precision=highest)
    fourth = jnp.einsum('hkbi,bio->hkbo', real, weight[1], precision=highest)
    return (low_back(first - second), low_back(third + fourth))

def frame_block(field, height, width, params):
    first_gain, first_shift, filter_inner, inner_bias, filter_outer, outer_bias, later_gain, later_shift, expand_weight, expand_bias, reduce_weight, reduce_bias = params
    row_ids = jnp.arange(H, dtype=jnp.int32)
    col_ids = jnp.arange(W, dtype=jnp.int32)
    mask = ((row_ids[:, None] < height) & (col_ids[None, :] < width)).astype(jnp.float32)[:, :, None]
    lower = mask * field
    filter_in = mask * layer_norm(lower, first_gain, first_shift)
    spectrum = jnp.fft.rfft2(filter_in, axes=(0, 1), norm='ortho')
    live = W // 2 + 1
    padding = ((0, 0), (0, BINS - live), (0, 0))
    real = jnp.pad(jnp.real(spectrum), padding).reshape(H, BINS, BLOCKS, BS)
    imag = jnp.pad(jnp.imag(spectrum), padding).reshape(H, BINS, BLOCKS, BS)
    inner_re, inner_im = complex_mix(low(real), low(imag), filter_inner)
    inner_re = gelu_exact(inner_re + inner_bias[0])
    inner_im = gelu_exact(inner_im + inner_bias[1])
    outer_re, outer_im = complex_mix(low(inner_re), low(inner_im), filter_outer)
    outer_re = outer_re + outer_bias[0]
    outer_im = outer_im + outer_bias[1]
    shrunk_re = outer_re - shrink_width * jnp.tanh(outer_re / shrink_width)
    shrunk_im = outer_im - shrink_width * jnp.tanh(outer_im / shrink_width)
    packed = lax.complex(shrunk_re, shrunk_im).reshape(H, BINS, C)[:, :live]
    spatial = jnp.fft.irfft2(packed, s=(H, W), axes=(0, 1), norm='ortho')
    mixed = lower + mask * (spatial + filter_in)
    flat = mixed.reshape(H * W, C)
    normed = layer_norm(flat, later_gain, later_shift)
    pre = low_back(jnp.dot(low(normed), expand_weight, precision=highest, preferred_element_type=jnp.float32)) + expand_bias
    hidden = gelu_exact(pre)
    branch = low_back(jnp.dot(low(hidden), reduce_weight, precision=highest, preferred_element_type=jnp.float32)) + reduce_bias
    return mask * (mixed + branch.reshape(H, W, C))

def reference(states, heights, widths, first_gain, first_shift, filter_inner, inner_bias, filter_outer, outer_bias, later_gain, later_shift, expand_weight, expand_bias, reduce_weight, reduce_bias, cotangent):
    params = tuple((p.astype(jnp.float32) for p in (first_gain, first_shift, filter_inner, inner_bias, filter_outer, outer_bias, later_gain, later_shift, expand_weight, expand_bias, reduce_weight, reduce_bias)))
    fields = states.astype(jnp.float32)

    def forward(fields, params):

        def one_frame(items):
            return frame_block(items[0], items[1], items[2], params)
        return lax.map(jax.checkpoint(one_frame), (fields, heights, widths))
    output, pullback = jax.vjp(forward, fields, params)
    field_grad, param_grads = pullback(cotangent.astype(jnp.float32))
    return (output.astype(jnp.bfloat16), field_grad.astype(jnp.bfloat16), param_grads[0], param_grads[1], param_grads[2], param_grads[3], param_grads[4], param_grads[5], param_grads[6], param_grads[7], param_grads[8], param_grads[9], param_grads[10], param_grads[11])
```

```python
import functools
import math

import jax
import jax.numpy as jnp
import numpy as np
from jax import lax
from jax.experimental import pallas as pl
from jax.experimental.pallas import tpu as pltpu
from jax.sharding import PartitionSpec as P

BS = 96
BINS = 96
PAIR = 2
GROUP = 8
norm_eps = 1e-06
shrink_width = 0.01
VMEM = 60 * 1024 * 1024
f32 = jnp.float32
bf16 = jnp.bfloat16


def phi_parts(v):
    cdf = 0.5 * (1.0 + lax.erf(v * math.sqrt(0.5)))
    slope = cdf + v * (jnp.exp(v * v * -0.5) * (1.0 / math.sqrt(2.0 * math.pi)))
    return cdf, slope


def dot(a, b):
    return lax.dot_general(a, b, (((1,), (0,)), ((), ())), preferred_element_type=f32)


def dot_tn(a, b):
    return lax.dot_general(a, b, (((0,), (0,)), ((), ())), preferred_element_type=f32)


def dot_nt(a, b):
    return lax.dot_general(a, b, (((1,), (1,)), ((), ())), preferred_element_type=f32)


def row_mask(meta, heights, widths, frame, row, cols_here):
    cols = meta[1] + lax.broadcasted_iota(jnp.int32, (cols_here, 1), 0)
    tall = (meta[0] + row < heights[frame]).astype(jnp.int32)
    return (cols < widths[frame] * tall).astype(f32)


def standardize(v):
    centre = jnp.mean(v, axis=-1, keepdims=True)
    centred = v - centre
    spread = jnp.mean(centred * centred, axis=-1, keepdims=True)
    scale = lax.rsqrt(spread + norm_eps)
    return centred * scale, scale


def standardize_back(grad, normal, scale):
    first = jnp.mean(grad, axis=-1, keepdims=True)
    second = jnp.mean(grad * normal, axis=-1, keepdims=True)
    return scale * (grad - first - normal * second)


def unpack_row(ref, i, cols_here, groups, width, pairs):
    half, j = divmod(i, pairs)
    parts = [
        ref[c, j * cols_here : (j + 1) * cols_here, half * width : (half + 1) * width]
        for c in range(groups)
    ]
    return jnp.concatenate(parts, axis=1) if groups > 1 else parts[0]


def first_kernel(meta, heights, widths, states, gain, shift, out):
    frame = pl.program_id(0)
    rows_here, cols_here, _ = states.shape[1:]
    groups, _, lanes = out.shape
    width = lanes // PAIR
    pairs = rows_here // PAIR
    for j in range(pairs):
        sides = []
        for half in range(PAIR):
            row = half * pairs + j
            mask = row_mask(meta, heights, widths, frame, row, cols_here)
            normal, _ = standardize(states[0, row].astype(f32) * mask)
            sides.append(mask * (normal * gain[...] + shift[...]))
        for c in range(groups):
            part = jnp.concatenate([s[:, c * width : (c + 1) * width] for s in sides], axis=1)
            out[c, j * cols_here : (j + 1) * cols_here, :] = part


def table_dot(table, x):
    rows = table.shape[0] // 2
    high = x.astype(bf16)
    both = dot(table[...], high)
    rest = dot(table[:rows, :], (x - high.astype(f32)).astype(bf16))
    return both[:rows] + both[rows:] + rest


def take_rows(step, block, table, wide, held, pairs, cols_here, fine):
    groups = block.shape[0]
    for j in range(pairs):
        for c in range(groups):
            wide[c * cols_here : (c + 1) * cols_here, :] = block[
                c, j * cols_here : (j + 1) * cols_here, :
            ]
        x = wide[...]
        held[step * pairs + j] = table_dot(table, x) if fine else dot(table[...], x.astype(bf16))


def give_rows(step, block, table, held, pairs, cols_here, factor):
    groups = block.shape[0]
    for j in range(pairs):
        plane = dot(table[...], held[step * pairs + j].astype(bf16)) * factor
        for c in range(groups):
            block[c, j * cols_here : (j + 1) * cols_here, :] = plane[
                c * cols_here : (c + 1) * cols_here, :
            ]


def bins_in(held, group, table, width, fine):
    kind = f32 if fine else bf16
    start = pl.multiple_of(group * GROUP, GROUP)
    real = jnp.swapaxes(held[:, pl.ds(start, GROUP), :], 0, 1).astype(kind)
    imag = jnp.swapaxes(held[:, pl.ds(BINS + start, GROUP), :], 0, 1).astype(kind)
    outs = []
    for k in range(GROUP):
        x = jnp.concatenate(
            [part[k][:, h * width : (h + 1) * width] for part in (real, imag) for h in range(PAIR)],
            axis=0,
        )
        outs.append(table_dot(table, x) if fine else dot(table[...], x))
    return outs


def bins_out(held, group, table, width, values):
    start = pl.multiple_of(group * GROUP, GROUP)
    short = held.shape[0]
    real, imag = [], []
    for value in values:
        z = dot(table[...], value)
        pieces = [z[i * short : (i + 1) * short, :] for i in range(2 * PAIR)]
        real.append(jnp.concatenate(pieces[:PAIR], axis=1))
        imag.append(jnp.concatenate(pieces[PAIR:], axis=1))
    held[:, pl.ds(start, GROUP), :] = jnp.swapaxes(jnp.stack(real, axis=0), 0, 1)
    held[:, pl.ds(BINS + start, GROUP), :] = jnp.swapaxes(jnp.stack(imag, axis=0), 0, 1)


def halves(v, count, tall):
    return [
        (v[k * 2 * tall : k * 2 * tall + tall], v[k * 2 * tall + tall : (k + 1) * 2 * tall])
        for k in range(count)
    ]


def complex_product(x, first, second, count, tall, conj):
    a = dot(x, first)
    b = dot(x, second)
    parts = []
    for (a_re, a_im), (b_re, b_im) in zip(halves(a, count, tall), halves(b, count, tall)):
        if conj:
            parts += [a_re + b_im, a_im - b_re]
        else:
            parts += [a_re - b_im, a_im + b_re]
    return parts


def spectral_forward_kernel(
    steps, pairs, cols_here, factor,
    block, table_in, table_down, table_up, table_out, inner, inner_bias, outer, outer_bias,
    out, entries, active, slope, damp,
    wide, held,
):
    i = pl.program_id(0)
    bin_steps = BINS // GROUP
    width = block.shape[2] // PAIR
    tall = held.shape[0] * PAIR

    @pl.when(i < steps)
    def _():
        take_rows(i, block, table_in, wide, held, pairs, cols_here, True)

    @pl.when((i >= steps) & (i < steps + bin_steps))
    def _():
        group = i - steps
        spec = bins_in(held, group, table_down, width, True)
        low = jnp.concatenate([(s * factor).astype(bf16) for s in spec], axis=0)
        entries[...] = low
        parts = complex_product(low, inner[0], inner[1], GROUP, tall, False)
        acts = []
        for n, part in enumerate(parts):
            v = part + inner_bias[n % 2 : n % 2 + 1, :]
            cdf, der = phi_parts(v)
            acts.append((v * cdf).astype(bf16))
            slope[n * tall : (n + 1) * tall, :] = der.astype(bf16)
        act = jnp.concatenate(acts, axis=0)
        active[...] = act
        parts = complex_product(act, outer[0], outer[1], GROUP, tall, False)
        shrunk = []
        for n, part in enumerate(parts):
            v = part + outer_bias[n % 2 : n % 2 + 1, :]
            t = jnp.tanh(v * (1.0 / shrink_width))
            shrunk.append((v - shrink_width * t).astype(bf16))
            damp[n * tall : (n + 1) * tall, :] = (t * t).astype(bf16)
        values = [jnp.concatenate(shrunk[2 * k : 2 * k + 2], axis=0) for k in range(GROUP)]
        bins_out(held, group, table_up, width, values)

    @pl.when(i >= steps + bin_steps)
    def _():
        give_rows(i - steps - bin_steps, out, table_out, held, pairs, cols_here, factor)


def spectral_backward_kernel(
    steps, pairs, cols_here, factor,
    block, table_in, table_down, table_up, table_out, inner_t, outer_t, entries, active, slope, damp,
    out, inner_grad, inner_bias_grad, outer_grad, outer_bias_grad,
    wide, held,
):
    i = pl.program_id(0)
    bin_steps = BINS // GROUP
    width = block.shape[2] // PAIR
    tall = held.shape[0] * PAIR

    @pl.when(i == 0)
    def _():
        for ref in (inner_grad, inner_bias_grad, outer_grad, outer_bias_grad):
            ref[...] = jnp.zeros_like(ref)

    @pl.when(i < steps)
    def _():
        take_rows(i, block, table_in, wide, held, pairs, cols_here, False)

    def weight_grads(ref, before, grads):
        plain = jnp.concatenate(grads, axis=0)
        turned = []
        for k in range(GROUP):
            turned += [grads[2 * k + 1], -grads[2 * k]]
        ref[0] += dot_tn(before, plain)
        ref[1] += dot_tn(before, jnp.concatenate(turned, axis=0))
        return plain

    @pl.when((i >= steps) & (i < steps + bin_steps))
    def _():
        group = i - steps
        spec = bins_in(held, group, table_down, width, False)
        grads = []
        sums = [0.0, 0.0]
        for k in range(GROUP):
            for side in range(2):
                at = (2 * k + side) * tall
                g = spec[k][side * tall : (side + 1) * tall] * factor
                g = g * damp[at : at + tall, :].astype(f32)
                sums[side] = sums[side] + jnp.sum(g, axis=0, keepdims=True)
                grads.append(g.astype(bf16))
        outer_bias_grad[...] += jnp.concatenate(sums, axis=0)
        low = weight_grads(outer_grad, active[...], grads)
        parts = complex_product(low, outer_t[0], outer_t[1], GROUP, tall, True)
        grads = []
        sums = [0.0, 0.0]
        for n, part in enumerate(parts):
            g = part * slope[n * tall : (n + 1) * tall, :].astype(f32)
            sums[n % 2] = sums[n % 2] + jnp.sum(g, axis=0, keepdims=True)
            grads.append(g.astype(bf16))
        inner_bias_grad[...] += jnp.concatenate(sums, axis=0)
        low = weight_grads(inner_grad, entries[...], grads)
        parts = complex_product(low, inner_t[0], inner_t[1], GROUP, tall, True)
        values = [
            jnp.concatenate([parts[2 * k], parts[2 * k + 1]], axis=0).astype(bf16)
            for k in range(GROUP)
        ]
        bins_out(held, group, table_up, width, values)

    @pl.when(i >= steps + bin_steps)
    def _():
        give_rows(i - steps - bin_steps, out, table_out, held, pairs, cols_here, factor)


def dense_kernel(
    meta, heights, widths,
    states, cot, spat, first_gain, first_shift, later_gain, later_shift,
    expand_bias, reduce_bias, expand_hbm, reduce_hbm,
    result, back, sums, expand_bias_grad, expand_grad_hbm, reduce_grad_hbm,
    expand, reduce, expand_grad, reduce_grad, mixed, normed, normal, low_out, branch, grad_n, copy_sem,
):
    frame = pl.program_id(0)
    hc = pl.program_id(1)
    last_hc = hc == pl.num_programs(1) - 1
    rows_here, cols_here, chans = states.shape[1:]
    groups, _, lanes = spat.shape
    width = lanes // PAIR
    pairs = rows_here // PAIR
    tokens = rows_here * cols_here
    chunk = tokens
    for size in (48, 32, 16):
        if tokens % size == 0:
            chunk = size
            break
    chunks = tokens // chunk
    slabs, _, slab = expand.shape

    @pl.when((frame == 0) & (hc == 0))
    def _():
        copies = [
            pltpu.make_async_copy(
                expand_hbm.at[:, pl.ds(s * slab, slab)], expand.at[s], copy_sem.at[s]
            )
            for s in range(slabs)
        ]
        copies.append(pltpu.make_async_copy(reduce_hbm, reduce, copy_sem.at[slabs]))
        for c in copies:
            c.start()
        expand_grad[...] = jnp.zeros_like(expand_grad)
        reduce_grad[...] = jnp.zeros_like(reduce_grad)
        sums[...] = jnp.zeros_like(sums)
        expand_bias_grad[...] = jnp.zeros_like(expand_bias_grad)
        for c in copies:
            c.wait()

    @pl.when(hc == 0)
    def _():
        for row in range(rows_here):
            mask = row_mask(meta, heights, widths, frame, row, cols_here)
            lower = mask * states[0, row].astype(f32)
            first, _ = standardize(lower)
            filter_in = first * first_gain[...] + first_shift[...]
            spatial = unpack_row(spat, row, cols_here, groups, width, pairs)
            at = slice(row * cols_here, (row + 1) * cols_here)
            mixed[at, :] = lower + mask * (spatial + filter_in)
            grad_n[at, :] = mask * cot[0, row].astype(f32)

        def token_chunk(n, carry):
            at = pl.ds(pl.multiple_of(n * chunk, chunk), chunk)
            later, _ = standardize(mixed[at, :])
            normal[at, :] = later
            normed[at, :] = (later * later_gain[...] + later_shift[...]).astype(bf16)
            go = grad_n[at, :]
            low_out[at, :] = go.astype(bf16)
            sums[0:1, :] += jnp.sum(go, axis=0, keepdims=True)
            return carry

        lax.fori_loop(0, chunks, token_chunk, 0)
        branch[...] = jnp.zeros_like(branch)
        grad_n[...] = jnp.zeros_like(grad_n)

    at = pl.ds(pl.multiple_of(hc * slab, slab), slab)
    weight_up = expand[hc]
    weight_down = reduce[at, :]
    x = normed[...]
    go = low_out[...]
    pre = dot(x, weight_up) + expand_bias[...]
    cdf, der = phi_parts(pre)
    hidden = (pre * cdf).astype(bf16)
    branch[...] += dot(hidden, weight_down)
    grad_pre = dot_nt(go, weight_down) * der
    expand_bias_grad[pl.ds(hc, 1), :] += jnp.sum(grad_pre, axis=0, keepdims=True)
    grad_low = grad_pre.astype(bf16)
    grad_n[...] += dot_nt(grad_low, weight_up)
    reduce_grad[at, :] += dot_tn(hidden, go)
    expand_grad[hc] += dot_tn(x, grad_low)

    @pl.when(last_hc)
    def _():
        def token_chunk(n, carry):
            at = pl.ds(pl.multiple_of(n * chunk, chunk), chunk)
            later, scale = standardize(mixed[at, :])
            g = grad_n[at, :]
            sums[1:2, :] += jnp.sum(g * later, axis=0, keepdims=True)
            sums[2:3, :] += jnp.sum(g, axis=0, keepdims=True)
            grad_n[at, :] = low_out[at, :].astype(f32) + standardize_back(
                g * later_gain[...], later, scale
            )
            return carry

        lax.fori_loop(0, chunks, token_chunk, 0)
        for j in range(pairs):
            sides = []
            for half in range(PAIR):
                row = half * pairs + j
                mask = row_mask(meta, heights, widths, frame, row, cols_here)
                at = slice(row * cols_here, (row + 1) * cols_here)
                out = mask * (mixed[at, :] + branch[at, :] + reduce_bias[...])
                result[0, row] = out.astype(bf16)
                sides.append(mask * grad_n[at, :])
            for c in range(groups):
                part = jnp.concatenate([s[:, c * width : (c + 1) * width] for s in sides], axis=1)
                back[c, j * cols_here : (j + 1) * cols_here, :] = part

    @pl.when(last_hc & (frame == pl.num_programs(0) - 1))
    def _():
        copies = [
            pltpu.make_async_copy(
                expand_grad.at[s], expand_grad_hbm.at[:, pl.ds(s * slab, slab)], copy_sem.at[s]
            )
            for s in range(slabs)
        ]
        copies.append(pltpu.make_async_copy(reduce_grad, reduce_grad_hbm, copy_sem.at[slabs]))
        for c in copies:
            c.start()
        for c in copies:
            c.wait()


def last_kernel(meta, heights, widths, states, back, spat, gain, out, sums):
    frame = pl.program_id(0)
    rows_here, cols_here, _ = states.shape[1:]
    groups, _, lanes = spat.shape
    width = lanes // PAIR
    pairs = rows_here // PAIR

    @pl.when(frame == 0)
    def _():
        sums[...] = jnp.zeros_like(sums)

    for row in range(rows_here):
        mask = row_mask(meta, heights, widths, frame, row, cols_here)
        normal, scale = standardize(mask * states[0, row].astype(f32))
        grad_mixed = unpack_row(back, row, cols_here, groups, width, pairs)
        spatial = unpack_row(spat, row, cols_here, groups, width, pairs)
        grad = mask * (grad_mixed + spatial)
        sums[0:1, :] += jnp.sum(grad * normal, axis=0, keepdims=True)
        sums[1:2, :] += jnp.sum(grad, axis=0, keepdims=True)
        grad = grad_mixed + standardize_back(grad * gain[...], normal, scale)
        out[0, row] = (mask * grad).astype(bf16)


def wide_tables(width):
    freq = np.arange(BINS)
    place = np.arange(width)
    angle = (freq[:, None] * place[None, :] % width) * (2.0 * math.pi / width)
    live = (2 * freq <= width).astype(np.float64)[:, None]
    edge = (freq == 0) | (2 * freq == width)
    weight = np.where(edge, 1.0, 2.0)[:, None] * live
    cosine, sine = np.cos(angle), np.sin(angle)
    plain = np.concatenate([live * cosine, -live * sine], axis=0)
    doubled = np.concatenate([weight * cosine, -weight * sine], axis=0)
    return plain, doubled


def tall_tables(height, rows_here):
    pairs = rows_here // PAIR
    order = np.array(
        [
            r * rows_here + h * pairs + j
            for h in range(PAIR)
            for r in range(height // rows_here)
            for j in range(pairs)
        ]
    )
    freq = np.arange(height)
    angle = (freq[:, None] * order[None, :] % height) * (2.0 * math.pi / height)
    cosine, sine = np.cos(angle), np.sin(angle)
    down = np.block([[cosine, sine], [-sine, cosine]])
    up = np.block([[cosine.T, -sine.T], [sine.T, cosine.T]])
    return down, up


def spread(weight):
    count = weight.shape[1]
    eye = jnp.eye(count, dtype=weight.dtype)
    full = jnp.einsum("rbio,bd->rbido", weight, eye)
    return full.reshape(2, count * BS, count * BS)


def gather_blocks(full):
    count = full.shape[1] // BS
    return jnp.stack(
        [full[:, b * BS : (b + 1) * BS, b * BS : (b + 1) * BS] for b in range(count)], axis=1
    )


def bias_rows(bias):
    return bias.reshape(2, -1)


def whole(shape):
    return pl.BlockSpec(shape, lambda *_: (0,) * len(shape))


def params(count):
    return pltpu.CompilerParams(
        dimension_semantics=("arbitrary",) * count, vmem_limit_bytes=VMEM
    )


def body(
    states,
    heights,
    widths,
    first_gain,
    first_shift,
    filter_inner,
    inner_bias,
    filter_outer,
    outer_bias,
    later_gain,
    later_shift,
    expand_weight,
    expand_bias,
    reduce_weight,
    reduce_bias,
    cotangent,
):
    frames, rows_here, cols_here, chans = states.shape
    ranks, groups = lax.axis_size("rows"), lax.axis_size("cols")
    assert frames == ranks and rows_here % PAIR == 0
    height, breadth = rows_here * ranks, cols_here * groups
    devices = ranks * groups
    pairs = rows_here // PAIR
    pixels = pairs * cols_here
    width = chans // groups
    lanes = width * PAIR
    tokens = rows_here * cols_here
    hidden = expand_weight.shape[1]
    factor = 1.0 / math.sqrt(height * breadth)

    meta = jnp.stack([lax.axis_index("rows") * rows_here, lax.axis_index("cols") * cols_here])
    meta = meta.astype(jnp.int32)
    row = lambda v: v.reshape(1, -1)

    tile = pl.BlockSpec((1, rows_here, cols_here, chans), lambda f, *_: (f, 0, 0, 0))
    packed = pl.BlockSpec((groups, pixels, lanes), lambda f, *_: (f, 0, 0))
    packed_shape = jax.ShapeDtypeStruct((devices, pixels, lanes), f32)
    chan_row = whole((1, chans))

    def exchange(v):
        return lax.all_to_all(v, ("rows", "cols"), 0, 0, tiled=True)

    sent = pl.pallas_call(
        first_kernel,
        grid_spec=pltpu.PrefetchScalarGridSpec(
            num_scalar_prefetch=3,
            grid=(frames,),
            in_specs=[tile, chan_row, chan_row],
            out_specs=packed,
        ),
        out_shape=packed_shape,
        compiler_params=params(1),
        name="first_norm",
    )(meta, heights, widths, states, row(first_gain), row(first_shift))

    plain, doubled = wide_tables(breadth)
    down, up = tall_tables(height, rows_here)
    as_table = lambda t: jnp.asarray(t, dtype=bf16)

    def fine_table(t):
        high = t.astype(jnp.bfloat16)
        return jnp.asarray(np.concatenate([high, (t - high.astype(np.float64)).astype(jnp.bfloat16)]))

    inner_full, outer_full = spread(filter_inner), spread(filter_outer)
    turn = lambda t: jnp.swapaxes(t, 1, 2)

    bin_steps = BINS // GROUP
    steps = ranks
    total = 2 * steps + bin_steps
    short = ranks * pairs
    group_rows = GROUP * 2 * height
    field_in = pl.BlockSpec((groups, pixels, lanes), lambda i: (jnp.minimum(i, steps - 1), 0, 0))
    field_out = pl.BlockSpec(
        (groups, pixels, lanes), lambda i: (jnp.maximum(i - steps - bin_steps, 0), 0, 0)
    )
    kept = pl.BlockSpec(
        (group_rows, width), lambda i: (jnp.clip(i - steps, 0, bin_steps - 1), 0)
    )
    kept_shape = jax.ShapeDtypeStruct((bin_steps * group_rows, width), bf16)
    def table_specs(parts):
        return [
            whole((parts * 2 * BINS, breadth)),
            whole((parts * 2 * height, 2 * height)),
            whole((2 * height, 2 * height)),
            whole((breadth, 2 * BINS)),
        ]

    mix_spec = whole((2, width, width))
    bias_spec = whole((2, width))
    scratch = [
        pltpu.VMEM((breadth, lanes), f32),
        pltpu.VMEM((short, 2 * BINS, lanes), f32),
    ]

    spatial, entries, active, slope, damp = pl.pallas_call(
        functools.partial(spectral_forward_kernel, steps, pairs, cols_here, factor),
        grid=(total,),
        in_specs=[field_in] + table_specs(2) + [mix_spec, bias_spec, mix_spec, bias_spec],
        out_specs=[field_out] + [kept] * 4,
        out_shape=[packed_shape] + [kept_shape] * 4,
        scratch_shapes=scratch,
        compiler_params=params(1),
        name="spectral_forward",
    )(
        exchange(sent),
        fine_table(plain),
        fine_table(down),
        as_table(up),
        as_table(doubled.T),
        inner_full,
        bias_rows(inner_bias),
        outer_full,
        bias_rows(outer_bias),
    )

    slabs = 6
    slab = hidden // slabs
    tile2 = pl.BlockSpec((1, rows_here, cols_here, chans), lambda f, h, *_: (f, 0, 0, 0))
    packed2 = pl.BlockSpec((groups, pixels, lanes), lambda f, h, *_: (f, 0, 0))
    anywhere = pl.BlockSpec(memory_space=pl.ANY)
    result, back, sums, expand_bias_grad, expand_grad, reduce_grad = pl.pallas_call(
        dense_kernel,
        grid_spec=pltpu.PrefetchScalarGridSpec(
            num_scalar_prefetch=3,
            grid=(frames, slabs),
            in_specs=[tile2, tile2, packed2]
            + [chan_row] * 4
            + [pl.BlockSpec((1, slab), lambda f, h, *_: (0, h)), chan_row, anywhere, anywhere],
            out_specs=[
                tile2,
                packed2,
                whole((8, chans)),
                whole((slabs, slab)),
                anywhere,
                anywhere,
            ],
            scratch_shapes=[
                pltpu.VMEM((slabs, chans, slab), bf16),
                pltpu.VMEM((hidden, chans), bf16),
                pltpu.VMEM((slabs, chans, slab), f32),
                pltpu.VMEM((hidden, chans), f32),
                pltpu.VMEM((tokens, chans), f32),
                pltpu.VMEM((tokens, chans), bf16),
                pltpu.VMEM((tokens, chans), f32),
                pltpu.VMEM((tokens, chans), bf16),
                pltpu.VMEM((tokens, chans), f32),
                pltpu.VMEM((tokens, chans), f32),
                pltpu.SemaphoreType.DMA((slabs + 1,)),
            ],
        ),
        out_shape=[
            jax.ShapeDtypeStruct(states.shape, bf16),
            packed_shape,
            jax.ShapeDtypeStruct((8, chans), f32),
            jax.ShapeDtypeStruct((slabs, slab), f32),
            jax.ShapeDtypeStruct((chans, hidden), f32),
            jax.ShapeDtypeStruct((hidden, chans), f32),
        ],
        compiler_params=params(2),
        name="dense_both_ways",
    )(
        meta,
        heights,
        widths,
        states,
        cotangent,
        exchange(spatial),
        row(first_gain),
        row(first_shift),
        row(later_gain),
        row(later_shift),
        row(expand_bias),
        row(reduce_bias),
        expand_weight,
        reduce_weight,
    )

    spatial_back, inner_grad, inner_bias_grad, outer_grad, outer_bias_grad = pl.pallas_call(
        functools.partial(spectral_backward_kernel, steps, pairs, cols_here, factor),
        grid=(total,),
        in_specs=[field_in] + table_specs(1) + [mix_spec, mix_spec] + [kept] * 4,
        out_specs=[field_out, mix_spec, bias_spec, mix_spec, bias_spec],
        out_shape=[
            packed_shape,
            jax.ShapeDtypeStruct((2, width, width), f32),
            jax.ShapeDtypeStruct((2, width), f32),
            jax.ShapeDtypeStruct((2, width, width), f32),
            jax.ShapeDtypeStruct((2, width), f32),
        ],
        scratch_shapes=scratch,
        compiler_params=params(1),
        name="spectral_backward",
    )(
        exchange(back),
        as_table(doubled),
        as_table(down),
        as_table(up),
        as_table(plain.T),
        turn(inner_full),
        turn(outer_full),
        entries,
        active,
        slope,
        damp,
    )

    states_grad, first_sums = pl.pallas_call(
        last_kernel,
        grid_spec=pltpu.PrefetchScalarGridSpec(
            num_scalar_prefetch=3,
            grid=(frames,),
            in_specs=[tile, packed, packed, chan_row],
            out_specs=[tile, whole((8, chans))],
        ),
        out_shape=[
            jax.ShapeDtypeStruct(states.shape, bf16),
            jax.ShapeDtypeStruct((8, chans), f32),
        ],
        compiler_params=params(1),
        name="first_norm_backward",
    )(meta, heights, widths, states, back, exchange(spatial_back), row(first_gain))

    inner_sum, inner_bias_sum, outer_sum, outer_bias_sum = lax.psum(
        (gather_blocks(inner_grad), inner_bias_grad, gather_blocks(outer_grad), outer_bias_grad),
        "rows",
    )
    expand_sum, reduce_sum = lax.psum((expand_grad, reduce_grad), ("rows", "cols"))
    small, first_small, expand_bias_sum = lax.psum(
        (sums, first_sums, expand_bias_grad), ("rows", "cols")
    )
    return (
        result,
        states_grad,
        first_small[0],
        first_small[1],
        inner_sum,
        inner_bias_sum.reshape(2, -1, BS),
        outer_sum,
        outer_bias_sum.reshape(2, -1, BS),
        small[1],
        small[2],
        expand_sum,
        expand_bias_sum.reshape(-1),
        reduce_sum,
        small[0],
    )


def solution(mesh):
    tile = P(None, "rows", "cols", None)
    mix = P(None, "cols", None, None)
    bias = P(None, "cols", None)
    in_specs = (
        tile, P(), P(), P(), P(), mix, bias, mix, bias, P(), P(), P(), P(), P(), P(), tile,
    )
    out_specs = (
        tile, tile, P(), P(), mix, bias, mix, bias, P(), P(), P(), P(), P(), P(),
    )
    return jax.shard_map(body, mesh=mesh, in_specs=in_specs, out_specs=out_specs, check_vma=False)
```

```python
import functools
import math

import jax
import jax.numpy as jnp
import numpy as np
from jax import lax
from jax.experimental import pallas as pl
from jax.experimental.pallas import tpu as pltpu
from jax.sharding import PartitionSpec as P

BS = 96
BINS = 96
PAIR = 2
GROUP = 8
PARTS = 3
norm_eps = 1e-06
shrink_width = 0.01
VMEM = 60 * 1024 * 1024
f32 = jnp.float32
bf16 = jnp.bfloat16


def phi_parts(v):
    cdf = 0.5 * (1.0 + lax.erf(v * math.sqrt(0.5)))
    slope = cdf + v * (jnp.exp(v * v * -0.5) * (1.0 / math.sqrt(2.0 * math.pi)))
    return cdf, slope


def dot(a, b):
    return lax.dot_general(a, b, (((1,), (0,)), ((), ())), preferred_element_type=f32)


def dot_tn(a, b):
    return lax.dot_general(a, b, (((0,), (0,)), ((), ())), preferred_element_type=f32)


def dot_nt(a, b):
    return lax.dot_general(a, b, (((1,), (1,)), ((), ())), preferred_element_type=f32)


def standardize(v):
    centre = jnp.mean(v, axis=-1, keepdims=True)
    centred = v - centre
    spread = jnp.mean(centred * centred, axis=-1, keepdims=True)
    scale = lax.rsqrt(spread + norm_eps)
    return centred * scale, scale


def standardize_back(grad, normal, scale):
    first = jnp.mean(grad, axis=-1, keepdims=True)
    second = jnp.mean(grad * normal, axis=-1, keepdims=True)
    return scale * (grad - first - normal * second)


def pack(sides, out, width):
    turned = [jnp.swapaxes(s, 0, 1) for s in sides]
    for c in range(out.shape[1]):
        out[:, c] = jnp.concatenate([t[:, :, c * width : (c + 1) * width] for t in turned], axis=2)


def unpack(ref, half, width):
    parts = [ref[:, c, :, half * width : (half + 1) * width] for c in range(ref.shape[1])]
    return jnp.swapaxes(jnp.concatenate(parts, axis=2) if len(parts) > 1 else parts[0], 0, 1)


def first_kernel(states, mask, gain, shift, out):
    width = out.shape[3] // PAIR
    sides = []
    for half in range(PAIR):
        inside = mask[half][..., :1]
        normal, _ = standardize(states[half].astype(f32) * inside)
        sides.append(inside * (normal * gain[...] + shift[...]))
    pack(sides, out, width)


def table_dot(table, x):
    rows = table.shape[0] // 2
    high = x.astype(bf16)
    both = dot(table[...], high)
    rest = dot(table[:rows, :], (x - high.astype(f32)).astype(bf16))
    return both[:rows] + both[rows:] + rest


def wide_in_kernel(cols_here, fine, block, table, held, wide):
    groups, rows = block.shape[1], block.shape[2] // cols_here
    for j in range(rows):
        for c in range(groups):
            wide[c * cols_here : (c + 1) * cols_here, :] = block[
                0, c, j * cols_here : (j + 1) * cols_here, :
            ]
        x = wide[...]
        y = table_dot(table, x) if fine else dot(table[...], x.astype(bf16))
        held[j, 0] = y[:BINS]
        held[j, 1] = y[BINS:]


def wide_out_kernel(cols_here, factor, held, table, block):
    groups, rows = block.shape[1], block.shape[2] // cols_here
    for j in range(rows):
        x = jnp.concatenate([held[j, 0], held[j, 1]], axis=0).astype(bf16)
        plane = dot(table[...], x) * factor
        for c in range(groups):
            block[0, c, j * cols_here : (j + 1) * cols_here, :] = plane[
                c * cols_here : (c + 1) * cols_here, :
            ]


def bins_in(held, table, width, fine):
    kind = f32 if fine else bf16
    turned = [
        [jnp.swapaxes(part[:, side], 0, 1).astype(kind) for part in held] for side in range(2)
    ]
    outs = []
    for k in range(GROUP):
        x = jnp.concatenate(
            [
                part[k][:, h * width : (h + 1) * width]
                for side in turned
                for h in range(PAIR)
                for part in side
            ],
            axis=0,
        )
        outs.append(table_dot(table, x) if fine else dot(table[...], x))
    return outs


def bins_out(held, table, width, values):
    short = held[0].shape[0]
    count = len(held)
    products = [dot(table[...], value) for value in values]
    for side in range(2):
        for q in range(count):
            rows = []
            for z in products:
                at = [((side * PAIR + h) * count + q) * short for h in range(PAIR)]
                rows.append(jnp.concatenate([z[a : a + short] for a in at], axis=1))
            held[q][:, side] = jnp.swapaxes(jnp.stack(rows, axis=0), 0, 1)


def halves(v, count, tall):
    return [
        (v[k * 2 * tall : k * 2 * tall + tall], v[k * 2 * tall + tall : (k + 1) * 2 * tall])
        for k in range(count)
    ]


def complex_product(x, first, second, count, tall, conj):
    a = dot(x, first)
    b = dot(x, second)
    parts = []
    for (a_re, a_im), (b_re, b_im) in zip(halves(a, count, tall), halves(b, count, tall)):
        if conj:
            parts += [a_re + b_im, a_im - b_re]
        else:
            parts += [a_re - b_im, a_im + b_re]
    return parts


def spectral_forward_kernel(factor, *refs):
    held, refs = refs[:PARTS], refs[PARTS:]
    table_down, table_up, inner, inner_bias, outer, outer_bias = refs[:6]
    given, (entries, active, slope, damp) = refs[6 : 6 + PARTS], refs[6 + PARTS :]
    width = inner.shape[2]
    tall = table_up.shape[0] // 2
    spec = bins_in(held, table_down, width, True)
    low = jnp.concatenate([(s * factor).astype(bf16) for s in spec], axis=0)
    entries[...] = low
    parts = complex_product(low, inner[0], inner[1], GROUP, tall, False)
    acts = []
    for n, part in enumerate(parts):
        v = part + inner_bias[n % 2 : n % 2 + 1, :]
        cdf, der = phi_parts(v)
        acts.append((v * cdf).astype(bf16))
        slope[n * tall : (n + 1) * tall, :] = der.astype(bf16)
    act = jnp.concatenate(acts, axis=0)
    active[...] = act
    parts = complex_product(act, outer[0], outer[1], GROUP, tall, False)
    shrunk = []
    for n, part in enumerate(parts):
        v = part + outer_bias[n % 2 : n % 2 + 1, :]
        t = jnp.tanh(v * (1.0 / shrink_width))
        shrunk.append((v - shrink_width * t).astype(bf16))
        damp[n * tall : (n + 1) * tall, :] = (t * t).astype(bf16)
    values = [jnp.concatenate(shrunk[2 * k : 2 * k + 2], axis=0) for k in range(GROUP)]
    bins_out(given, table_up, width, values)


def spectral_backward_kernel(factor, *refs):
    held, refs = refs[:PARTS], refs[PARTS:]
    table_down, table_up, inner_t, outer_t, entries, active, slope, damp = refs[:8]
    given, refs = refs[8 : 8 + PARTS], refs[8 + PARTS :]
    inner_grad, inner_bias_grad, outer_grad, outer_bias_grad = refs
    width = inner_t.shape[2]
    tall = table_up.shape[0] // 2

    @pl.when(pl.program_id(0) == 0)
    def _():
        for ref in (inner_grad, inner_bias_grad, outer_grad, outer_bias_grad):
            ref[...] = jnp.zeros_like(ref)

    def weight_grads(ref, before, grads):
        plain = jnp.concatenate(grads, axis=0)
        turned = []
        for k in range(GROUP):
            turned += [grads[2 * k + 1], -grads[2 * k]]
        ref[0] += dot_tn(before, plain)
        ref[1] += dot_tn(before, jnp.concatenate(turned, axis=0))
        return plain

    spec = bins_in(held, table_down, width, False)
    grads = []
    sums = [0.0, 0.0]
    for k in range(GROUP):
        for side in range(2):
            at = (2 * k + side) * tall
            g = spec[k][side * tall : (side + 1) * tall] * factor
            g = g * damp[at : at + tall, :].astype(f32)
            sums[side] = sums[side] + jnp.sum(g, axis=0, keepdims=True)
            grads.append(g.astype(bf16))
    outer_bias_grad[...] += jnp.concatenate(sums, axis=0)
    low = weight_grads(outer_grad, active[...], grads)
    parts = complex_product(low, outer_t[0], outer_t[1], GROUP, tall, True)
    grads = []
    sums = [0.0, 0.0]
    for n, part in enumerate(parts):
        g = part * slope[n * tall : (n + 1) * tall, :].astype(f32)
        sums[n % 2] = sums[n % 2] + jnp.sum(g, axis=0, keepdims=True)
        grads.append(g.astype(bf16))
    inner_bias_grad[...] += jnp.concatenate(sums, axis=0)
    low = weight_grads(inner_grad, entries[...], grads)
    parts = complex_product(low, inner_t[0], inner_t[1], GROUP, tall, True)
    values = [
        jnp.concatenate([parts[2 * k], parts[2 * k + 1]], axis=0).astype(bf16)
        for k in range(GROUP)
    ]
    bins_out(given, table_up, width, values)


def dense_kernel(steps, slabs, first_part, *refs):
    (
        states, cot, spat, mask, first_gain, first_shift, later_gain, later_shift,
        expand_bias, reduce_bias, expand_hbm, reduce_hbm,
    ) = refs[:12]
    refs = refs[12:]
    if not first_part:
        grads_before = refs[0]
        refs = refs[2:]
    result, back, sums, expand_bias_grad, grads_hbm = refs[:5]
    (
        expand, reduce, expand_grad, reduce_grad, mixed, normed, low_out, branch, grad_n,
        hidden_all, grad_all, copy_sem,
    ) = refs[5:]
    step = pl.program_id(0)
    chans = states.shape[3]
    width = spat.shape[3] // PAIR
    side_tokens = states.shape[1] * states.shape[2]
    slab = expand.shape[2]
    tokens = mixed.shape[0]
    square = states.shape[1:]

    def parts_of(grads):
        pairs = [(grads.at[pl.ds(s * chans, chans)], expand_grad.at[s]) for s in range(slabs)]
        return pairs + [(grads.at[pl.ds(slabs * chans, slabs * slab)], reduce_grad)]

    def fetches():
        copies = [
            pltpu.make_async_copy(
                expand_hbm.at[:, pl.ds(s * slab, slab)], expand.at[s], copy_sem.at[s]
            )
            for s in range(slabs)
        ]
        copies.append(pltpu.make_async_copy(reduce_hbm, reduce, copy_sem.at[slabs]))
        if not first_part:
            copies += [
                pltpu.make_async_copy(far, near, copy_sem.at[slabs + 1 + n])
                for n, (far, near) in enumerate(parts_of(grads_before))
            ]
        return copies

    @pl.when(step == 0)
    def _():
        for c in fetches():
            c.start()
        if first_part:
            expand_grad[...] = jnp.zeros_like(expand_grad)
            reduce_grad[...] = jnp.zeros_like(reduce_grad)
        sums[...] = jnp.zeros_like(sums)
        expand_bias_grad[...] = jnp.zeros_like(expand_bias_grad)

    @pl.when(step < steps)
    def _():
        start = pl.multiple_of(step * (PAIR * side_tokens), PAIR * side_tokens)
        for half in range(PAIR):
            at = pl.ds(start + half * side_tokens, side_tokens)
            inside = mask[half][..., :1]
            lower = inside * states[half].astype(f32)
            first, _ = standardize(lower)
            filter_in = first * first_gain[...] + first_shift[...]
            full = lower + inside * (unpack(spat, half, width) + filter_in)
            later, _ = standardize(full)
            full = full.reshape(side_tokens, chans)
            mixed[at, :] = full
            branch[at, :] = full + reduce_bias[...]
            normal = (later * later_gain[...] + later_shift[...]).reshape(side_tokens, chans)
            normed[at, :] = normal.astype(bf16)
            go = (inside * cot[half].astype(f32)).reshape(side_tokens, chans)
            low_out[at, :] = go.astype(bf16)
            grad_n[at, :] = jnp.zeros_like(full)
            sums[0:1, :] += jnp.sum(go, axis=0, keepdims=True)

    @pl.when(step == steps)
    def _():
        for c in fetches():
            c.wait()

    @pl.when((step >= steps) & (step < steps + slabs))
    def _():
        hc = step - steps
        at = pl.ds(pl.multiple_of(hc * slab, slab), slab)
        piece = tokens // 4 if tokens % 64 == 0 else tokens

        def some(n, carry):
            here = pl.ds(pl.multiple_of(n * piece, piece), piece)
            weight_up = expand[hc]
            weight_down = reduce[at, :]
            go = low_out[here, :]
            pre = dot(normed[here, :], weight_up) + expand_bias[...]
            cdf, der = phi_parts(pre)
            hidden = (pre * cdf).astype(bf16)
            hidden_all[here, :] = hidden
            branch[here, :] += dot(hidden, weight_down)
            grad_pre = dot_nt(go, weight_down) * der
            expand_bias_grad[pl.ds(hc, 1), :] += jnp.sum(grad_pre, axis=0, keepdims=True)
            grad_low = grad_pre.astype(bf16)
            grad_all[here, :] = grad_low
            grad_n[here, :] += dot_nt(grad_low, weight_up)
            return carry

        lax.fori_loop(0, tokens // piece, some, 0)
        reduce_grad[at, :] += dot_tn(hidden_all[...], low_out[...])
        expand_grad[hc] += dot_tn(normed[...], grad_all[...])

    @pl.when(step >= steps + slabs)
    def _():
        start = pl.multiple_of(
            (step - steps - slabs) * (PAIR * side_tokens), PAIR * side_tokens
        )
        sides = []
        for half in range(PAIR):
            at = pl.ds(start + half * side_tokens, side_tokens)
            inside = mask[half][..., :1]
            later, scale = standardize(mixed[at, :])
            g = grad_n[at, :]
            sums[1:2, :] += jnp.sum(g * later, axis=0, keepdims=True)
            sums[2:3, :] += jnp.sum(g, axis=0, keepdims=True)
            g = low_out[at, :].astype(f32) + standardize_back(g * later_gain[...], later, scale)
            sides.append(inside * g.reshape(square))
            result[half] = (inside * branch[at, :].reshape(square)).astype(bf16)
        pack(sides, back, width)

    @pl.when(step == pl.num_programs(0) - 1)
    def _():
        copies = [
            pltpu.make_async_copy(near, far, copy_sem.at[n])
            for n, (far, near) in enumerate(parts_of(grads_hbm))
        ]
        for c in copies:
            c.start()
        for c in copies:
            c.wait()


def last_kernel(states, back, spat, mask, gain, *refs):
    out, sums = refs[-2:]
    width = spat.shape[3] // PAIR
    chans = states.shape[3]

    @pl.when(pl.program_id(0) == 0)
    def _():
        sums[...] = jnp.zeros_like(sums)

    for half in range(PAIR):
        inside = mask[half][..., :1]
        normal, scale = standardize(inside * states[half].astype(f32))
        grad_mixed = unpack(back, half, width)
        grad = inside * (grad_mixed + unpack(spat, half, width))
        flat = (-1, chans)
        sums[0:1, :] += jnp.sum((grad * normal).reshape(flat), axis=0, keepdims=True)
        sums[1:2, :] += jnp.sum(grad.reshape(flat), axis=0, keepdims=True)
        grad = grad_mixed + standardize_back(grad * gain[...], normal, scale)
        out[half] = (inside * grad).astype(bf16)


def wide_tables(width):
    freq = np.arange(BINS)
    place = np.arange(width)
    angle = (freq[:, None] * place[None, :] % width) * (2.0 * math.pi / width)
    live = (2 * freq <= width).astype(np.float64)[:, None]
    edge = (freq == 0) | (2 * freq == width)
    weight = np.where(edge, 1.0, 2.0)[:, None] * live
    cosine, sine = np.cos(angle), np.sin(angle)
    plain = np.concatenate([live * cosine, -live * sine], axis=0)
    doubled = np.concatenate([weight * cosine, -weight * sine], axis=0)
    return plain, doubled


def tall_tables(height, rows_here):
    pairs = rows_here // PAIR
    rows = pairs // PARTS
    order = np.array(
        [
            r * rows_here + h * pairs + q * rows + j
            for h in range(PAIR)
            for q in range(PARTS)
            for r in range(height // rows_here)
            for j in range(rows)
        ]
    )
    freq = np.arange(height)
    angle = (freq[:, None] * order[None, :] % height) * (2.0 * math.pi / height)
    cosine, sine = np.cos(angle), np.sin(angle)
    down = np.block([[cosine, sine], [-sine, cosine]])
    up = np.block([[cosine.T, -sine.T], [sine.T, cosine.T]])
    return down, up


def spread(weight):
    count = weight.shape[1]
    eye = jnp.eye(count, dtype=weight.dtype)
    full = jnp.einsum("rbio,bd->rbido", weight, eye)
    return full.reshape(2, count * BS, count * BS)


def gather_blocks(full):
    count = full.shape[1] // BS
    return jnp.stack(
        [full[:, b * BS : (b + 1) * BS, b * BS : (b + 1) * BS] for b in range(count)], axis=1
    )


def bias_rows(bias):
    return bias.reshape(2, -1)


def whole(shape):
    return pl.BlockSpec(shape, lambda *_: (0,) * len(shape))


def call(kernel, grid, in_specs, out_specs, out_shape, name, flops=0, nbytes=0, scratch=(), **kw):
    return pl.pallas_call(
        kernel,
        grid=(grid,),
        in_specs=in_specs,
        out_specs=out_specs,
        out_shape=out_shape,
        scratch_shapes=scratch,
        compiler_params=pltpu.CompilerParams(
            dimension_semantics=("arbitrary",), vmem_limit_bytes=VMEM
        ),
        cost_estimate=pl.CostEstimate(flops=flops, bytes_accessed=nbytes, transcendentals=0),
        name=name,
        **kw,
    )


def body(
    states,
    heights,
    widths,
    first_gain,
    first_shift,
    filter_inner,
    inner_bias,
    filter_outer,
    outer_bias,
    later_gain,
    later_shift,
    expand_weight,
    expand_bias,
    reduce_weight,
    reduce_bias,
    cotangent,
):
    frames, rows_here, cols_here, chans = states.shape
    ranks, groups = lax.axis_size("rows"), lax.axis_size("cols")
    assert frames == ranks and rows_here % (PAIR * PARTS) == 0
    height, breadth = rows_here * ranks, cols_here * groups
    devices = ranks * groups
    pairs = rows_here // PAIR
    rows = pairs // PARTS
    pixels = rows * cols_here
    width = chans // groups
    lanes = width * PAIR
    hidden = expand_weight.shape[1]
    factor = 1.0 / math.sqrt(height * breadth)
    short = ranks * rows
    step_pixels = 8 if pixels % 8 == 0 else pixels
    steps = pixels // step_pixels
    tokens = PAIR * pixels * frames
    message = devices * pixels * lanes * 4
    row = lambda v: v.reshape(1, -1)
    shape = jax.ShapeDtypeStruct

    order = lambda v: jnp.transpose(v, (1, 2, 0, 3)).reshape(PAIR, pairs * cols_here, frames, chans)
    restore = lambda v: jnp.transpose(v.reshape(rows_here, cols_here, frames, chans), (2, 0, 1, 3))
    states_in, cot_in = order(states), order(cotangent)
    row_ids = lax.axis_index("rows") * rows_here + jnp.arange(rows_here, dtype=jnp.int32)
    col_ids = lax.axis_index("cols") * cols_here + jnp.arange(cols_here, dtype=jnp.int32)
    inside = (row_ids[:, None, None] < heights) & (col_ids[None, :, None] < widths)
    mask = jnp.broadcast_to(
        inside.astype(f32).reshape(PAIR, pairs * cols_here, frames, 1),
        (PAIR, pairs * cols_here, frames, 128),
    )

    buffers = {} if steps > 1 else {"pipeline_mode": pl.Buffered(1)}

    def token_spec(q, where, last=chans):
        return pl.BlockSpec(
            (PAIR, step_pixels, frames, last), lambda i: (0, q * steps + where(i), 0, 0), **buffers
        )

    def packed_spec(where):
        return pl.BlockSpec(
            (ranks, groups, step_pixels, lanes), lambda i: (0, 0, where(i), 0), **buffers
        )

    same = lambda i: i
    token_shape = shape((PAIR, pairs * cols_here, frames, chans), bf16)
    packed_shape = shape((ranks, groups, pixels, lanes), f32)
    chan_row = whole((1, chans))
    anywhere = pl.BlockSpec(memory_space=pl.ANY)

    def scatter(v, axis):
        return lax.psum_scatter(v, axis, scatter_dimension=0, tiled=True)

    def gather(v, axis):
        return lax.all_gather(v, axis, axis=0, tiled=True)

    def sum_small(v, *after):
        v = jnp.broadcast_to(behind(v, *after), (devices,) + v.shape)
        return jnp.sum(lax.all_to_all(v, ("rows", "cols"), 0, 0, tiled=True), axis=0)

    def behind(v, *after):
        return lax.optimization_barrier((v,) + after)[0] if after else v

    def exchange(v, *after):
        v = v.reshape(devices, pixels, lanes)
        v = behind(v, *after)
        v = lax.all_to_all(v, ("rows", "cols"), 0, 0, tiled=True)
        return v.reshape(ranks, groups, pixels, lanes)

    def first_norm(q):
        return call(
            first_kernel,
            steps,
            [token_spec(q, same), token_spec(q, same, 128), chan_row, chan_row],
            packed_spec(same),
            packed_shape,
            "first_norm",
            nbytes=2 * message,
        )(states_in, mask, row(first_gain), row(first_shift))

    plain, doubled = wide_tables(breadth)
    down, up = tall_tables(height, rows_here)
    as_table = lambda t: jnp.asarray(t, dtype=bf16)

    def fine_table(t):
        high = t.astype(jnp.bfloat16)
        return jnp.asarray(np.concatenate([high, (t - high.astype(np.float64)).astype(jnp.bfloat16)]))

    inner_full, outer_full = spread(filter_inner), spread(filter_outer)
    turn = lambda t: jnp.swapaxes(t, 1, 2)
    bin_steps = BINS // GROUP
    group_rows = GROUP * 2 * height
    held_shape = shape((short, 2, BINS, lanes), f32)
    held_row = pl.BlockSpec((rows, 2, BINS, lanes), lambda i: (i, 0, 0, 0))
    held_bins = pl.BlockSpec((short, 2, GROUP, lanes), lambda i: (0, 0, i, 0))
    field = pl.BlockSpec((1, groups, pixels, lanes), lambda i: (i, 0, 0, 0))
    kept = pl.BlockSpec((group_rows, width), lambda i: (i, 0))
    kept_shape = shape((bin_steps * group_rows, width), bf16)
    mix_spec = whole((2, width, width))
    bias_spec = whole((2, width))
    up_spec = whole((2 * height, 2 * height))

    def wide_in(v, table, fine):
        return call(
            functools.partial(wide_in_kernel, cols_here, fine),
            ranks,
            [field, whole(table.shape)],
            held_row,
            held_shape,
            "wide_in",
            nbytes=2 * message,
            scratch=[pltpu.VMEM((breadth, lanes), f32)],
        )(v, table)

    def wide_out(v, table):
        return call(
            functools.partial(wide_out_kernel, cols_here, factor),
            ranks,
            [held_row, whole(table.shape)],
            field,
            packed_shape,
            "wide_out",
            nbytes=2 * message,
        )(v, table)

    def spectral_forward(held):
        table = fine_table(down)
        outs = call(
            functools.partial(spectral_forward_kernel, factor),
            bin_steps,
            [held_bins] * PARTS
            + [whole(table.shape), up_spec, mix_spec, bias_spec, mix_spec, bias_spec],
            [held_bins] * PARTS + [kept] * 4,
            [held_shape] * PARTS + [kept_shape] * 4,
            "spectral_forward",
            flops=20 * 10**9,
            nbytes=8 * PARTS * message,
        )(
            *held,
            table,
            as_table(up),
            inner_full,
            bias_rows(inner_bias),
            outer_full,
            bias_rows(outer_bias),
        )
        return outs[:PARTS], outs[PARTS:]

    def spectral_backward(held, saved):
        outs = call(
            functools.partial(spectral_backward_kernel, factor),
            bin_steps,
            [held_bins] * PARTS + [up_spec, up_spec, mix_spec, mix_spec] + [kept] * 4,
            [held_bins] * PARTS + [mix_spec, bias_spec, mix_spec, bias_spec],
            [held_shape] * PARTS + [shape((2, width, width), f32), shape((2, width), f32)] * 2,
            "spectral_backward",
            flops=20 * 10**9,
            nbytes=8 * PARTS * message,
        )(*held, as_table(down), as_table(up), turn(inner_full), turn(outer_full), *saved)
        return outs[:PARTS], outs[PARTS:]

    slab = chans
    slabs = hidden // slab
    dense_steps = 2 * steps + slabs
    enter = lambda i: jnp.minimum(i, steps - 1)
    leave = lambda i: jnp.maximum(i - steps - slabs, 0)
    either = lambda i: jnp.where(i < steps + slabs, enter(i), leave(i))

    def dense(q, spatial, before):
        grads_before = () if q == 0 else before
        return call(
            functools.partial(dense_kernel, steps, slabs, q == 0),
            dense_steps,
            [token_spec(q, enter), token_spec(q, enter), packed_spec(enter)]
            + [token_spec(q, either, 128)]
            + [chan_row] * 4
            + [pl.BlockSpec((1, slab), lambda i: (0, jnp.clip(i - steps, 0, slabs - 1)))]
            + [chan_row]
            + [anywhere] * (2 + len(grads_before)),
            [
                token_spec(q, leave),
                packed_spec(leave),
                whole((8, chans)),
                whole((slabs, slab)),
                anywhere,
            ],
            [
                token_shape,
                packed_shape,
                shape((8, chans), f32),
                shape((slabs, slab), f32),
                shape((2 * hidden, chans), f32),
            ],
            "dense_both_ways",
            flops=12 * tokens * chans * hidden,
            nbytes=4 * message,
            scratch=[
                pltpu.VMEM((slabs, chans, slab), bf16),
                pltpu.VMEM((hidden, chans), bf16),
                pltpu.VMEM((slabs, chans, slab), f32),
                pltpu.VMEM((hidden, chans), f32),
                pltpu.VMEM((tokens, chans), f32),
                pltpu.VMEM((tokens, chans), bf16),
                pltpu.VMEM((tokens, chans), bf16),
                pltpu.VMEM((tokens, chans), f32),
                pltpu.VMEM((tokens, chans), f32),
                pltpu.VMEM((tokens, slab), bf16),
                pltpu.VMEM((tokens, slab), bf16),
                pltpu.SemaphoreType.DMA((2 * slabs + 2,)),
            ],
            input_output_aliases={} if q == 0 else {13: 0},
        )(
            states_in,
            cot_in,
            spatial,
            mask,
            row(first_gain),
            row(first_shift),
            row(later_gain),
            row(later_shift),
            row(expand_bias),
            row(reduce_bias),
            expand_weight,
            reduce_weight,
            *grads_before,
        )

    def last_norm(q, back, spatial, before):
        given = () if q == 0 else (before,)
        return call(
            last_kernel,
            steps,
            [token_spec(q, same), packed_spec(same), packed_spec(same), token_spec(q, same, 128)]
            + [chan_row]
            + [anywhere] * len(given),
            [token_spec(q, same), whole((8, chans))],
            [token_shape, shape((8, chans), f32)],
            "first_norm_backward",
            nbytes=4 * message,
            input_output_aliases={} if q == 0 else {5: 0},
        )(states_in, back, spatial, mask, row(first_gain), *given)

    def scatter(v, axis):
        return lax.psum_scatter(v, axis, scatter_dimension=0, tiled=True)

    def gather(v, axis):
        return lax.all_gather(v, axis, axis=0, tiled=True)

    def sum_small(v, *after):
        v = jnp.broadcast_to(behind(v, *after), (devices,) + v.shape)
        return jnp.sum(lax.all_to_all(v, ("rows", "cols"), 0, 0, tiled=True), axis=0)

    every = range(PARTS)
    got = []
    for q in every:
        got.append(exchange(first_norm(q), *got[-1:]))
    held = [wide_in(v, fine_table(plain), True) for v in got]
    given, saved = spectral_forward(held)

    made = [wide_out(v, as_table(doubled.T)) for v in given]
    spatial, backs, sums, expand_bias_grad, before = [], [], 0.0, 0.0, ()
    for q in range(PARTS + 1):
        if q < PARTS:
            spatial.append(exchange(made[q], *spatial[-1:], *backs[-1:]))
        if q > 0:
            result, back, part, bias_part, grads = dense(q - 1, spatial[q - 1], before)
            before = (grads, result)
            backs.append(back)
            sums, expand_bias_grad = sums + part, expand_bias_grad + bias_part
    got, held = spatial[-1:], []
    for q in every:
        got.append(exchange(backs[q], got[-1], backs[min(q + 1, PARTS - 1)], *held[-1:]))
        if q == 0:
            grads = scatter(behind(grads, got[-1]), "cols")
        else:
            held.append(wide_in(got[q], as_table(doubled), False))
    rows_of_sums = jnp.concatenate([sums[:3], expand_bias_grad.reshape(-1, chans)])
    rows_of_sums = jnp.pad(rows_of_sums, ((0, -rows_of_sums.shape[0] % 8), (0, 0)))
    dense_small = sum_small(rows_of_sums, got[-1], held[-1])
    held.append(wide_in(got[-1], as_table(doubled), False))
    grads = scatter(behind(grads, held[-1]), "rows")

    given, filter_grads = spectral_backward(held, saved)
    inner_grad, inner_bias_grad, outer_grad, outer_bias_grad = filter_grads
    filter_parts = (
        gather_blocks(inner_grad), inner_bias_grad, gather_blocks(outer_grad), outer_bias_grad
    )
    flat = jnp.concatenate([v.reshape(-1) for v in filter_parts])
    flat = lax.psum(jnp.pad(flat, (0, -flat.shape[0] % 1024)).reshape(-1, 128), "rows").reshape(-1)
    grads = gather(behind(grads, given[-1]), ("cols", "rows"))
    expand_sum = jnp.swapaxes(grads[:hidden].reshape(slabs, chans, slab), 0, 1)
    expand_sum = expand_sum.reshape(chans, hidden)
    reduce_sum = grads[hidden:]
    made = [wide_out(v, as_table(plain.T)) for v in given]
    got, first_sums, states_grad = [dense_small], [], None
    for q in range(PARTS + 1):
        if q < PARTS:
            got.append(exchange(made[q], got[-1], *first_sums[-1:]))
        if q > 0:
            states_grad, part = last_norm(q - 1, backs[q - 1], got[q], states_grad)
            first_sums.append(part)
    first_small = sum_small(sum(first_sums), got[-1])
    sizes = [v.size for v in filter_parts]
    ends = np.cumsum(sizes)
    filter_sums = [
        flat[e - n : e].reshape(v.shape) for e, n, v in zip(ends, sizes, filter_parts)
    ]
    inner_sum, inner_bias_sum, outer_sum, outer_bias_sum = filter_sums
    bias_rows_count = hidden // chans
    return (
        restore(result),
        restore(states_grad),
        first_small[0],
        first_small[1],
        inner_sum,
        inner_bias_sum.reshape(2, -1, BS),
        outer_sum,
        outer_bias_sum.reshape(2, -1, BS),
        dense_small[1],
        dense_small[2],
        expand_sum,
        dense_small[3 : 3 + bias_rows_count].reshape(-1),
        reduce_sum,
        dense_small[0],
    )


def solution(mesh):
    tile = P(None, "rows", "cols", None)
    mix = P(None, "cols", None, None)
    bias = P(None, "cols", None)
    in_specs = (
        tile, P(), P(), P(), P(), mix, bias, mix, bias, P(), P(), P(), P(), P(), P(), tile,
    )
    out_specs = (
        tile, tile, P(), P(), mix, bias, mix, bias, P(), P(), P(), P(), P(), P(),
    )
    return jax.shard_map(body, mesh=mesh, in_specs=in_specs, out_specs=out_specs, check_vma=False)
```

```python
import functools
import math

import jax
import jax.numpy as jnp
import numpy as np
from jax import lax
from jax.experimental import pallas as pl
from jax.experimental.pallas import tpu as pltpu
from jax.sharding import PartitionSpec as P

BS = 96
BINS = 96
PAIR = 2
GROUP = 8
PARTS = 3
norm_eps = 1e-06
shrink_width = 0.01
VMEM = 60 * 1024 * 1024
f32 = jnp.float32
bf16 = jnp.bfloat16


def phi_parts(v):
    cdf = 0.5 * (1.0 + lax.erf(v * math.sqrt(0.5)))
    slope = cdf + v * (jnp.exp(v * v * -0.5) * (1.0 / math.sqrt(2.0 * math.pi)))
    return cdf, slope


def dot(a, b):
    return lax.dot_general(a, b, (((1,), (0,)), ((), ())), preferred_element_type=f32)


def dot_tn(a, b):
    return lax.dot_general(a, b, (((0,), (0,)), ((), ())), preferred_element_type=f32)


def dot_nt(a, b):
    return lax.dot_general(a, b, (((1,), (1,)), ((), ())), preferred_element_type=f32)


def standardize(v):
    centre = jnp.mean(v, axis=-1, keepdims=True)
    centred = v - centre
    spread = jnp.mean(centred * centred, axis=-1, keepdims=True)
    scale = lax.rsqrt(spread + norm_eps)
    return centred * scale, scale


def standardize_back(grad, normal, scale):
    first = jnp.mean(grad, axis=-1, keepdims=True)
    second = jnp.mean(grad * normal, axis=-1, keepdims=True)
    return scale * (grad - first - normal * second)


def pack(sides, out, width):
    turned = [jnp.swapaxes(s, 0, 1) for s in sides]
    for c in range(out.shape[1]):
        out[:, c] = jnp.concatenate([t[:, :, c * width : (c + 1) * width] for t in turned], axis=2)


def unpack(ref, half, width):
    parts = [ref[:, c, :, half * width : (half + 1) * width] for c in range(ref.shape[1])]
    return jnp.swapaxes(jnp.concatenate(parts, axis=2) if len(parts) > 1 else parts[0], 0, 1)


def first_kernel(states, mask, gain, shift, out):
    width = out.shape[3] // PAIR
    sides = []
    for half in range(PAIR):
        inside = mask[half][..., :1]
        normal, _ = standardize(states[half].astype(f32) * inside)
        sides.append(inside * (normal * gain[...] + shift[...]))
    pack(sides, out, width)


def table_dot(table, x):
    rows = table.shape[0] // 2
    high = x.astype(bf16)
    both = dot(table[...], high)
    rest = dot(table[:rows, :], (x - high.astype(f32)).astype(bf16))
    return both[:rows] + both[rows:] + rest


def wide_in_kernel(cols_here, fine, block, table, held, wide):
    groups, rows = block.shape[1], block.shape[2] // cols_here
    for j in range(rows):
        for c in range(groups):
            wide[c * cols_here : (c + 1) * cols_here, :] = block[
                0, c, j * cols_here : (j + 1) * cols_here, :
            ]
        x = wide[...]
        y = table_dot(table, x) if fine else dot(table[...], x.astype(bf16))
        held[j, 0] = y[:BINS]
        held[j, 1] = y[BINS:]


def wide_out_kernel(cols_here, factor, held, table, block):
    groups, rows = block.shape[1], block.shape[2] // cols_here
    for j in range(rows):
        x = jnp.concatenate([held[j, 0], held[j, 1]], axis=0).astype(bf16)
        plane = dot(table[...], x) * factor
        for c in range(groups):
            block[0, c, j * cols_here : (j + 1) * cols_here, :] = plane[
                c * cols_here : (c + 1) * cols_here, :
            ]


def bins_in(held, table, width, fine):
    kind = f32 if fine else bf16
    turned = [
        [jnp.swapaxes(part[:, side], 0, 1).astype(kind) for part in held] for side in range(2)
    ]
    outs = []
    for k in range(GROUP):
        x = jnp.concatenate(
            [
                part[k][:, h * width : (h + 1) * width]
                for side in turned
                for h in range(PAIR)
                for part in side
            ],
            axis=0,
        )
        outs.append(table_dot(table, x) if fine else dot(table[...], x))
    return outs


def bins_out(held, table, width, values):
    short = held[0].shape[0]
    count = len(held)
    products = [dot(table[...], value) for value in values]
    for side in range(2):
        for q in range(count):
            rows = []
            for z in products:
                at = [((side * PAIR + h) * count + q) * short for h in range(PAIR)]
                rows.append(jnp.concatenate([z[a : a + short] for a in at], axis=1))
            held[q][:, side] = jnp.swapaxes(jnp.stack(rows, axis=0), 0, 1)


def halves(v, count, tall):
    return [
        (v[k * 2 * tall : k * 2 * tall + tall], v[k * 2 * tall + tall : (k + 1) * 2 * tall])
        for k in range(count)
    ]


def complex_product(x, first, second, count, tall, conj):
    a = dot(x, first)
    b = dot(x, second)
    parts = []
    for (a_re, a_im), (b_re, b_im) in zip(halves(a, count, tall), halves(b, count, tall)):
        if conj:
            parts += [a_re + b_im, a_im - b_re]
        else:
            parts += [a_re - b_im, a_im + b_re]
    return parts


def spectral_forward_kernel(factor, *refs):
    held, refs = refs[:PARTS], refs[PARTS:]
    table_down, table_up, inner, inner_bias, outer, outer_bias = refs[:6]
    given, (entries, active, slope, damp) = refs[6 : 6 + PARTS], refs[6 + PARTS :]
    width = inner.shape[2]
    tall = table_up.shape[0] // 2
    spec = bins_in(held, table_down, width, True)
    low = jnp.concatenate([(s * factor).astype(bf16) for s in spec], axis=0)
    entries[...] = low
    parts = complex_product(low, inner[0], inner[1], GROUP, tall, False)
    acts = []
    for n, part in enumerate(parts):
        v = part + inner_bias[n % 2 : n % 2 + 1, :]
        cdf, der = phi_parts(v)
        acts.append((v * cdf).astype(bf16))
        slope[n * tall : (n + 1) * tall, :] = der.astype(bf16)
    act = jnp.concatenate(acts, axis=0)
    active[...] = act
    parts = complex_product(act, outer[0], outer[1], GROUP, tall, False)
    shrunk = []
    for n, part in enumerate(parts):
        v = part + outer_bias[n % 2 : n % 2 + 1, :]
        t = jnp.tanh(v * (1.0 / shrink_width))
        shrunk.append((v - shrink_width * t).astype(bf16))
        damp[n * tall : (n + 1) * tall, :] = (t * t).astype(bf16)
    values = [jnp.concatenate(shrunk[2 * k : 2 * k + 2], axis=0) for k in range(GROUP)]
    bins_out(given, table_up, width, values)


def spectral_backward_kernel(factor, *refs):
    held, refs = refs[:PARTS], refs[PARTS:]
    table_down, table_up, inner_t, outer_t, entries, active, slope, damp = refs[:8]
    given, refs = refs[8 : 8 + PARTS], refs[8 + PARTS :]
    inner_grad, inner_bias_grad, outer_grad, outer_bias_grad = refs
    width = inner_t.shape[2]
    tall = table_up.shape[0] // 2

    @pl.when(pl.program_id(0) == 0)
    def _():
        for ref in (inner_grad, inner_bias_grad, outer_grad, outer_bias_grad):
            ref[...] = jnp.zeros_like(ref)

    def weight_grads(ref, before, grads):
        plain = jnp.concatenate(grads, axis=0)
        turned = []
        for k in range(GROUP):
            turned += [grads[2 * k + 1], -grads[2 * k]]
        ref[0] += dot_tn(before, plain)
        ref[1] += dot_tn(before, jnp.concatenate(turned, axis=0))
        return plain

    spec = bins_in(held, table_down, width, False)
    grads = []
    sums = [0.0, 0.0]
    for k in range(GROUP):
        for side in range(2):
            at = (2 * k + side) * tall
            g = spec[k][side * tall : (side + 1) * tall] * factor
            g = g * damp[at : at + tall, :].astype(f32)
            sums[side] = sums[side] + jnp.sum(g, axis=0, keepdims=True)
            grads.append(g.astype(bf16))
    outer_bias_grad[...] += jnp.concatenate(sums, axis=0)
    low = weight_grads(outer_grad, active[...], grads)
    parts = complex_product(low, outer_t[0], outer_t[1], GROUP, tall, True)
    grads = []
    sums = [0.0, 0.0]
    for n, part in enumerate(parts):
        g = part * slope[n * tall : (n + 1) * tall, :].astype(f32)
        sums[n % 2] = sums[n % 2] + jnp.sum(g, axis=0, keepdims=True)
        grads.append(g.astype(bf16))
    inner_bias_grad[...] += jnp.concatenate(sums, axis=0)
    low = weight_grads(inner_grad, entries[...], grads)
    parts = complex_product(low, inner_t[0], inner_t[1], GROUP, tall, True)
    values = [
        jnp.concatenate([parts[2 * k], parts[2 * k + 1]], axis=0).astype(bf16)
        for k in range(GROUP)
    ]
    bins_out(given, table_up, width, values)


def dense_kernel(steps, slabs, first_part, *refs):
    (
        states, cot, spat, mask, first_gain, first_shift, later_gain, later_shift,
        expand_bias, reduce_bias, expand_hbm, reduce_hbm,
    ) = refs[:12]
    refs = refs[12:]
    if not first_part:
        grads_before = refs[0]
        refs = refs[2:]
    result, back, later_grad, sums, expand_bias_grad, grads_hbm = refs[:6]
    (
        expand, reduce, expand_grad, reduce_grad, mixed, normed, low_out, branch, grad_n,
        hidden_all, grad_all, copy_sem,
    ) = refs[6:]
    step = pl.program_id(0)
    chans = states.shape[3]
    width = spat.shape[3] // PAIR
    side_tokens = states.shape[1] * states.shape[2]
    slab = expand.shape[2]
    tokens = mixed.shape[0]
    square = states.shape[1:]

    def parts_of(grads):
        pairs = [(grads.at[pl.ds(s * chans, chans)], expand_grad.at[s]) for s in range(slabs)]
        return pairs + [(grads.at[pl.ds(slabs * chans, slabs * slab)], reduce_grad)]

    def fetches():
        copies = [
            pltpu.make_async_copy(
                expand_hbm.at[:, pl.ds(s * slab, slab)], expand.at[s], copy_sem.at[s]
            )
            for s in range(slabs)
        ]
        copies.append(pltpu.make_async_copy(reduce_hbm, reduce, copy_sem.at[slabs]))
        if not first_part:
            copies += [
                pltpu.make_async_copy(far, near, copy_sem.at[slabs + 1 + n])
                for n, (far, near) in enumerate(parts_of(grads_before))
            ]
        return copies

    @pl.when(step == 0)
    def _():
        for c in fetches():
            c.start()
        if first_part:
            expand_grad[...] = jnp.zeros_like(expand_grad)
            reduce_grad[...] = jnp.zeros_like(reduce_grad)
        sums[...] = jnp.zeros_like(sums)
        expand_bias_grad[...] = jnp.zeros_like(expand_bias_grad)

    @pl.when(step < steps)
    def _():
        start = pl.multiple_of(step * (PAIR * side_tokens), PAIR * side_tokens)
        for half in range(PAIR):
            at = pl.ds(start + half * side_tokens, side_tokens)
            inside = mask[half][..., :1]
            lower = inside * states[half].astype(f32)
            first, _ = standardize(lower)
            filter_in = first * first_gain[...] + first_shift[...]
            full = lower + inside * (unpack(spat, half, width) + filter_in)
            later, _ = standardize(full)
            full = full.reshape(side_tokens, chans)
            mixed[at, :] = full
            branch[at, :] = full + reduce_bias[...]
            normal = (later * later_gain[...] + later_shift[...]).reshape(side_tokens, chans)
            normed[at, :] = normal.astype(bf16)
            go = (inside * cot[half].astype(f32)).reshape(side_tokens, chans)
            low_out[at, :] = go.astype(bf16)
            grad_n[at, :] = jnp.zeros_like(full)
            sums[0:1, :] += jnp.sum(go, axis=0, keepdims=True)

    @pl.when(step == steps)
    def _():
        for c in fetches():
            c.wait()

    @pl.when((step >= steps) & (step < steps + slabs))
    def _():
        hc = step - steps
        at = pl.ds(pl.multiple_of(hc * slab, slab), slab)
        piece = tokens // 4 if tokens % 64 == 0 else tokens

        def some(n, carry):
            here = pl.ds(pl.multiple_of(n * piece, piece), piece)
            weight_up = expand[hc]
            weight_down = reduce[at, :]
            go = low_out[here, :]
            pre = dot(normed[here, :], weight_up) + expand_bias[...]
            cdf, der = phi_parts(pre)
            hidden = (pre * cdf).astype(bf16)
            hidden_all[here, :] = hidden
            branch[here, :] += dot(hidden, weight_down)
            grad_pre = dot_nt(go, weight_down) * der
            expand_bias_grad[pl.ds(hc, 1), :] += jnp.sum(grad_pre, axis=0, keepdims=True)
            grad_low = grad_pre.astype(bf16)
            grad_all[here, :] = grad_low
            grad_n[here, :] += dot_nt(grad_low, weight_up)
            return carry

        lax.fori_loop(0, tokens // piece, some, 0)
        reduce_grad[at, :] += dot_tn(hidden_all[...], low_out[...])
        expand_grad[hc] += dot_tn(normed[...], grad_all[...])

    @pl.when(step >= steps + slabs)
    def _():
        start = pl.multiple_of(
            (step - steps - slabs) * (PAIR * side_tokens), PAIR * side_tokens
        )
        sides = []
        for half in range(PAIR):
            at = pl.ds(start + half * side_tokens, side_tokens)
            inside = mask[half][..., :1]
            later, scale = standardize(mixed[at, :])
            g = grad_n[at, :]
            sums[1:2, :] += jnp.sum(g * later, axis=0, keepdims=True)
            sums[2:3, :] += jnp.sum(g, axis=0, keepdims=True)
            g = low_out[at, :].astype(f32) + standardize_back(g * later_gain[...], later, scale)
            sides.append(inside * g.reshape(square))
            later_grad[half] = sides[-1]
            result[half] = (inside * branch[at, :].reshape(square)).astype(bf16)
        pack(sides, back, width)

    @pl.when(step == pl.num_programs(0) - 1)
    def _():
        copies = [
            pltpu.make_async_copy(near, far, copy_sem.at[n])
            for n, (far, near) in enumerate(parts_of(grads_hbm))
        ]
        for c in copies:
            c.start()
        for c in copies:
            c.wait()


def last_kernel(states, later_grad, spat, mask, gain, *refs):
    out, sums = refs[-2:]
    width = spat.shape[3] // PAIR
    chans = states.shape[3]

    @pl.when(pl.program_id(0) == 0)
    def _():
        sums[...] = jnp.zeros_like(sums)

    for half in range(PAIR):
        inside = mask[half][..., :1]
        normal, scale = standardize(inside * states[half].astype(f32))
        grad_mixed = later_grad[half]
        grad = inside * (grad_mixed + unpack(spat, half, width))
        flat = (-1, chans)
        sums[0:1, :] += jnp.sum((grad * normal).reshape(flat), axis=0, keepdims=True)
        sums[1:2, :] += jnp.sum(grad.reshape(flat), axis=0, keepdims=True)
        grad = grad_mixed + standardize_back(grad * gain[...], normal, scale)
        out[half] = (inside * grad).astype(bf16)


def sum_kernel(ranks, groups, own, out, got, send_sem, recv_sem):
    devices = ranks * groups
    me = lax.axis_index("rows") * groups + lax.axis_index("cols")

    def place(i):
        other = lax.rem(me + i, devices)
        return lax.div(other, groups), lax.rem(other, groups)

    def copy(i):
        return pltpu.make_async_remote_copy(
            src_ref=own,
            dst_ref=got.at[i],
            send_sem=send_sem.at[i],
            recv_sem=recv_sem.at[i],
            device_id=place(i),
            device_id_type=pl.DeviceIdType.MESH,
        )

    barrier = pltpu.get_barrier_semaphore()

    def greet(i, carry):
        pl.semaphore_signal(
            barrier, inc=1, device_id=place(i), device_id_type=pl.DeviceIdType.MESH
        )
        return carry

    def start(i, carry):
        copy(i).start()
        return carry

    def finish(i, carry):
        copy(i).wait()
        return carry

    lax.fori_loop(1, devices, greet, 0)
    pl.semaphore_wait(barrier, devices - 1)
    lax.fori_loop(1, devices, start, 0)
    lax.fori_loop(1, devices, finish, 0)
    out[...] = lax.fori_loop(1, devices, lambda i, total: total + got[i], own[...])


def split_kernel(slabs, grads, expand, reduce, copy_sem):
    chans = reduce.shape[1]
    copies = [
        pltpu.make_async_copy(
            grads.at[pl.ds(s * chans, chans)], expand.at[:, pl.ds(s * chans, chans)], copy_sem.at[s]
        )
        for s in range(slabs)
    ]
    copies.append(
        pltpu.make_async_copy(
            grads.at[pl.ds(slabs * chans, slabs * chans)], reduce, copy_sem.at[slabs]
        )
    )
    for c in copies:
        c.start()
    for c in copies:
        c.wait()


def wide_tables(width):
    freq = np.arange(BINS)
    place = np.arange(width)
    angle = (freq[:, None] * place[None, :] % width) * (2.0 * math.pi / width)
    live = (2 * freq <= width).astype(np.float64)[:, None]
    edge = (freq == 0) | (2 * freq == width)
    weight = np.where(edge, 1.0, 2.0)[:, None] * live
    cosine, sine = np.cos(angle), np.sin(angle)
    plain = np.concatenate([live * cosine, -live * sine], axis=0)
    doubled = np.concatenate([weight * cosine, -weight * sine], axis=0)
    return plain, doubled


def tall_tables(height, rows_here):
    pairs = rows_here // PAIR
    rows = pairs // PARTS
    order = np.array(
        [
            r * rows_here + h * pairs + q * rows + j
            for h in range(PAIR)
            for q in range(PARTS)
            for r in range(height // rows_here)
            for j in range(rows)
        ]
    )
    freq = np.arange(height)
    angle = (freq[:, None] * order[None, :] % height) * (2.0 * math.pi / height)
    cosine, sine = np.cos(angle), np.sin(angle)
    down = np.block([[cosine, sine], [-sine, cosine]])
    up = np.block([[cosine.T, -sine.T], [sine.T, cosine.T]])
    return down, up


def spread(weight):
    count = weight.shape[1]
    eye = jnp.eye(count, dtype=weight.dtype)
    full = jnp.einsum("rbio,bd->rbido", weight, eye)
    return full.reshape(2, count * BS, count * BS)


def gather_blocks(full):
    count = full.shape[1] // BS
    return jnp.stack(
        [full[:, b * BS : (b + 1) * BS, b * BS : (b + 1) * BS] for b in range(count)], axis=1
    )


def bias_rows(bias):
    return bias.reshape(2, -1)


def whole(shape):
    return pl.BlockSpec(shape, lambda *_: (0,) * len(shape))


def call(kernel, grid, in_specs, out_specs, out_shape, name, flops=0, nbytes=0, scratch=(), **kw):
    return pl.pallas_call(
        kernel,
        grid=(grid,),
        in_specs=in_specs,
        out_specs=out_specs,
        out_shape=out_shape,
        scratch_shapes=scratch,
        compiler_params=pltpu.CompilerParams(
            dimension_semantics=("arbitrary",), vmem_limit_bytes=VMEM
        ),
        cost_estimate=pl.CostEstimate(flops=flops, bytes_accessed=nbytes, transcendentals=0),
        name=name,
        **kw,
    )


def body(
    states,
    heights,
    widths,
    first_gain,
    first_shift,
    filter_inner,
    inner_bias,
    filter_outer,
    outer_bias,
    later_gain,
    later_shift,
    expand_weight,
    expand_bias,
    reduce_weight,
    reduce_bias,
    cotangent,
):
    frames, rows_here, cols_here, chans = states.shape
    ranks, groups = lax.axis_size("rows"), lax.axis_size("cols")
    assert frames == ranks and rows_here % (PAIR * PARTS) == 0
    height, breadth = rows_here * ranks, cols_here * groups
    devices = ranks * groups
    pairs = rows_here // PAIR
    rows = pairs // PARTS
    pixels = rows * cols_here
    width = chans // groups
    lanes = width * PAIR
    hidden = expand_weight.shape[1]
    factor = 1.0 / math.sqrt(height * breadth)
    short = ranks * rows
    step_pixels = 8 if pixels % 8 == 0 else pixels
    steps = pixels // step_pixels
    tokens = PAIR * pixels * frames
    message = devices * pixels * lanes * 4
    row = lambda v: v.reshape(1, -1)
    shape = jax.ShapeDtypeStruct

    order = lambda v: jnp.transpose(v, (1, 2, 0, 3)).reshape(PAIR, pairs * cols_here, frames, chans)
    restore = lambda v: jnp.transpose(v.reshape(rows_here, cols_here, frames, chans), (2, 0, 1, 3))
    states_in, cot_in = order(states), order(cotangent)
    row_ids = lax.axis_index("rows") * rows_here + jnp.arange(rows_here, dtype=jnp.int32)
    col_ids = lax.axis_index("cols") * cols_here + jnp.arange(cols_here, dtype=jnp.int32)
    inside = (row_ids[:, None, None] < heights) & (col_ids[None, :, None] < widths)
    mask = jnp.broadcast_to(
        inside.astype(f32).reshape(PAIR, pairs * cols_here, frames, 1),
        (PAIR, pairs * cols_here, frames, 128),
    )

    buffers = {} if steps > 1 else {"pipeline_mode": pl.Buffered(1)}

    def token_spec(q, where, last=chans):
        return pl.BlockSpec(
            (PAIR, step_pixels, frames, last), lambda i: (0, q * steps + where(i), 0, 0), **buffers
        )

    def packed_spec(where):
        return pl.BlockSpec(
            (ranks, groups, step_pixels, lanes), lambda i: (0, 0, where(i), 0), **buffers
        )

    same = lambda i: i
    token_shape = shape((PAIR, pairs * cols_here, frames, chans), bf16)
    packed_shape = shape((ranks, groups, pixels, lanes), f32)
    chan_row = whole((1, chans))
    anywhere = pl.BlockSpec(memory_space=pl.ANY)

    def scatter(v, axis):
        return lax.psum_scatter(v, axis, scatter_dimension=0, tiled=True)

    def gather(v, axis):
        return lax.all_gather(v, axis, axis=0, tiled=True)

    def sum_small(v):
        flat = v.reshape(-1, 128)
        flat = jnp.pad(flat, ((0, -flat.shape[0] % 8), (0, 0)))
        vmem = pl.BlockSpec(memory_space=pltpu.VMEM)
        return pl.pallas_call(
            functools.partial(sum_kernel, ranks, groups),
            in_specs=[vmem],
            out_specs=vmem,
            out_shape=shape(flat.shape, f32),
            scratch_shapes=[
                pltpu.VMEM((devices,) + flat.shape, f32),
                pltpu.SemaphoreType.DMA((devices,)),
                pltpu.SemaphoreType.DMA((devices,)),
            ],
            compiler_params=pltpu.CompilerParams(collective_id=0, has_side_effects=True),
            name="small_sums",
        )(flat).reshape(-1)[: v.size].reshape(v.shape)

    def split_grads(v):
        return pl.pallas_call(
            functools.partial(split_kernel, slabs),
            in_specs=[anywhere],
            out_specs=[anywhere, anywhere],
            out_shape=[shape((chans, hidden), f32), shape((hidden, chans), f32)],
            scratch_shapes=[pltpu.SemaphoreType.DMA((slabs + 1,))],
            name="split_gradients",
        )(v)

    def behind(v, *after):
        return lax.optimization_barrier((v,) + after)[0] if after else v

    def exchange(v, *after):
        v = v.reshape(devices, pixels, lanes)
        v = behind(v, *after)
        v = lax.all_to_all(v, ("rows", "cols"), 0, 0, tiled=True)
        return v.reshape(ranks, groups, pixels, lanes)

    def first_norm(q):
        return call(
            first_kernel,
            steps,
            [token_spec(q, same), token_spec(q, same, 128), chan_row, chan_row],
            packed_spec(same),
            packed_shape,
            "first_norm",
            nbytes=2 * message,
        )(states_in, mask, row(first_gain), row(first_shift))

    plain, doubled = wide_tables(breadth)
    down, up = tall_tables(height, rows_here)
    as_table = lambda t: jnp.asarray(t, dtype=bf16)

    def fine_table(t):
        high = t.astype(jnp.bfloat16)
        return jnp.asarray(np.concatenate([high, (t - high.astype(np.float64)).astype(jnp.bfloat16)]))

    inner_full, outer_full = spread(filter_inner), spread(filter_outer)
    turn = lambda t: jnp.swapaxes(t, 1, 2)
    bin_steps = BINS // GROUP
    group_rows = GROUP * 2 * height
    held_shape = shape((short, 2, BINS, lanes), f32)
    held_row = pl.BlockSpec((rows, 2, BINS, lanes), lambda i: (i, 0, 0, 0))
    held_bins = pl.BlockSpec((short, 2, GROUP, lanes), lambda i: (0, 0, i, 0))
    field = pl.BlockSpec((1, groups, pixels, lanes), lambda i: (i, 0, 0, 0))
    kept = pl.BlockSpec((group_rows, width), lambda i: (i, 0))
    kept_shape = shape((bin_steps * group_rows, width), bf16)
    mix_spec = whole((2, width, width))
    bias_spec = whole((2, width))
    up_spec = whole((2 * height, 2 * height))

    def wide_in(v, table, fine):
        return call(
            functools.partial(wide_in_kernel, cols_here, fine),
            ranks,
            [field, whole(table.shape)],
            held_row,
            held_shape,
            "wide_in",
            nbytes=2 * message,
            scratch=[pltpu.VMEM((breadth, lanes), f32)],
        )(v, table)

    def wide_out(v, table):
        return call(
            functools.partial(wide_out_kernel, cols_here, factor),
            ranks,
            [held_row, whole(table.shape)],
            field,
            packed_shape,
            "wide_out",
            nbytes=2 * message,
        )(v, table)

    def spectral_forward(held):
        table = fine_table(down)
        outs = call(
            functools.partial(spectral_forward_kernel, factor),
            bin_steps,
            [held_bins] * PARTS
            + [whole(table.shape), up_spec, mix_spec, bias_spec, mix_spec, bias_spec],
            [held_bins] * PARTS + [kept] * 4,
            [held_shape] * PARTS + [kept_shape] * 4,
            "spectral_forward",
            flops=20 * 10**9,
            nbytes=8 * PARTS * message,
        )(
            *held,
            table,
            as_table(up),
            inner_full,
            bias_rows(inner_bias),
            outer_full,
            bias_rows(outer_bias),
        )
        return outs[:PARTS], outs[PARTS:]

    def spectral_backward(held, saved):
        outs = call(
            functools.partial(spectral_backward_kernel, factor),
            bin_steps,
            [held_bins] * PARTS + [up_spec, up_spec, mix_spec, mix_spec] + [kept] * 4,
            [held_bins] * PARTS + [mix_spec, bias_spec, mix_spec, bias_spec],
            [held_shape] * PARTS + [shape((2, width, width), f32), shape((2, width), f32)] * 2,
            "spectral_backward",
            flops=20 * 10**9,
            nbytes=8 * PARTS * message,
        )(*held, as_table(down), as_table(up), turn(inner_full), turn(outer_full), *saved)
        return outs[:PARTS], outs[PARTS:]

    slab = chans
    slabs = hidden // slab
    dense_steps = 2 * steps + slabs
    enter = lambda i: jnp.minimum(i, steps - 1)
    leave = lambda i: jnp.maximum(i - steps - slabs, 0)
    either = lambda i: jnp.where(i < steps + slabs, enter(i), leave(i))

    def dense(q, spatial, before):
        grads_before = () if q == 0 else before
        return call(
            functools.partial(dense_kernel, steps, slabs, q == 0),
            dense_steps,
            [token_spec(q, enter), token_spec(q, enter), packed_spec(enter)]
            + [token_spec(q, either, 128)]
            + [chan_row] * 4
            + [pl.BlockSpec((1, slab), lambda i: (0, jnp.clip(i - steps, 0, slabs - 1)))]
            + [chan_row]
            + [anywhere] * (2 + len(grads_before)),
            [
                token_spec(q, leave),
                packed_spec(leave),
                token_spec(0, leave),
                whole((8, chans)),
                whole((slabs, slab)),
                anywhere,
            ],
            [
                token_shape,
                packed_shape,
                shape((PAIR, pixels, frames, chans), f32),
                shape((8, chans), f32),
                shape((slabs, slab), f32),
                shape((2 * hidden, chans), f32),
            ],
            "dense_both_ways",
            flops=12 * tokens * chans * hidden,
            nbytes=4 * message,
            scratch=[
                pltpu.VMEM((slabs, chans, slab), bf16),
                pltpu.VMEM((hidden, chans), bf16),
                pltpu.VMEM((slabs, chans, slab), f32),
                pltpu.VMEM((hidden, chans), f32),
                pltpu.VMEM((tokens, chans), f32),
                pltpu.VMEM((tokens, chans), bf16),
                pltpu.VMEM((tokens, chans), bf16),
                pltpu.VMEM((tokens, chans), f32),
                pltpu.VMEM((tokens, chans), f32),
                pltpu.VMEM((tokens, slab), bf16),
                pltpu.VMEM((tokens, slab), bf16),
                pltpu.SemaphoreType.DMA((2 * slabs + 2,)),
            ],
            input_output_aliases={} if q == 0 else {13: 0},
        )(
            states_in,
            cot_in,
            spatial,
            mask,
            row(first_gain),
            row(first_shift),
            row(later_gain),
            row(later_shift),
            row(expand_bias),
            row(reduce_bias),
            expand_weight,
            reduce_weight,
            *grads_before,
        )

    def last_norm(q, later_grad, spatial, before):
        given = () if q == 0 else (before,)
        return call(
            last_kernel,
            steps,
            [token_spec(q, same), token_spec(0, same), packed_spec(same), token_spec(q, same, 128)]
            + [chan_row]
            + [anywhere] * len(given),
            [token_spec(q, same), whole((8, chans))],
            [token_shape, shape((8, chans), f32)],
            "first_norm_backward",
            nbytes=4 * message,
            input_output_aliases={} if q == 0 else {5: 0},
        )(states_in, later_grad, spatial, mask, row(first_gain), *given)

    every = range(PARTS)
    got = []
    for q in every:
        got.append(exchange(first_norm(q), *got[-1:]))
    held = [wide_in(v, fine_table(plain), True) for v in got]
    given, saved = spectral_forward(held)

    made = [wide_out(v, as_table(doubled.T)) for v in given]
    spatial, backs, later_grads, sums, expand_bias_grad, before = [], [], [], 0.0, 0.0, ()
    for q in range(PARTS + 1):
        if q < PARTS:
            spatial.append(exchange(made[q], *spatial[-1:], *backs[-1:]))
        if q > 0:
            result, back, kept_grad, part, bias_part, grads = dense(q - 1, spatial[q - 1], before)
            before = (grads, result)
            backs.append(back)
            later_grads.append(kept_grad)
            sums, expand_bias_grad = sums + part, expand_bias_grad + bias_part
    got, held = spatial[-1:], []
    for q in every:
        got.append(exchange(backs[q], got[-1], backs[min(q + 1, PARTS - 1)], *held[-1:]))
        if q == 0:
            grads = scatter(behind(grads, got[-1]), "cols")
        else:
            held.append(wide_in(got[q], as_table(doubled), False))
    held.append(wide_in(behind(got[-1], held[-1]), as_table(doubled), False))
    grads = scatter(behind(grads, held[-1]), "rows")

    given, filter_grads = spectral_backward(held, saved)
    inner_grad, inner_bias_grad, outer_grad, outer_bias_grad = filter_grads
    filter_parts = (
        gather_blocks(inner_grad), inner_bias_grad, gather_blocks(outer_grad), outer_bias_grad
    )
    flat = jnp.concatenate([v.reshape(-1) for v in filter_parts])
    flat = lax.psum(jnp.pad(flat, (0, -flat.shape[0] % 1024)).reshape(-1, 128), "rows").reshape(-1)
    made = [wide_out(v, as_table(plain.T)) for v in given]
    got, first_sums, states_grad = [], [], None
    for q in range(PARTS + 1):
        if q < PARTS:
            got.append(exchange(made[q], *got[-1:], *first_sums[-1:]))
        if q == 0:
            grads = gather(behind(grads, got[0], flat, *made[1:2]), ("cols", "rows"))
            expand_sum, reduce_sum = split_grads(grads)
        else:
            if q == PARTS:
                states_grad = behind(states_grad, expand_sum)
            states_grad, part = last_norm(q - 1, later_grads[q - 1], got[q - 1], states_grad)
            first_sums.append(part)
    small = sum_small(
        jnp.concatenate([sum(first_sums)[:2], sums[:3], expand_bias_grad.reshape(-1, chans)])
    )
    sizes = [v.size for v in filter_parts]
    ends = np.cumsum(sizes)
    filter_sums = [
        flat[e - n : e].reshape(v.shape) for e, n, v in zip(ends, sizes, filter_parts)
    ]
    inner_sum, inner_bias_sum, outer_sum, outer_bias_sum = filter_sums
    return (
        restore(result),
        restore(states_grad),
        small[0],
        small[1],
        inner_sum,
        inner_bias_sum.reshape(2, -1, BS),
        outer_sum,
        outer_bias_sum.reshape(2, -1, BS),
        small[3],
        small[4],
        expand_sum,
        small[5:].reshape(-1),
        reduce_sum,
        small[2],
    )


def solution(mesh):
    tile = P(None, "rows", "cols", None)
    mix = P(None, "cols", None, None)
    bias = P(None, "cols", None)
    in_specs = (
        tile, P(), P(), P(), P(), mix, bias, mix, bias, P(), P(), P(), P(), P(), P(), tile,
    )
    out_specs = (
        tile, tile, P(), P(), mix, bias, mix, bias, P(), P(), P(), P(), P(), P(),
    )
    return jax.shard_map(body, mesh=mesh, in_specs=in_specs, out_specs=out_specs, check_vma=False)
```

```python
import functools
import math

import jax
import jax.numpy as jnp
import numpy as np
from jax import lax
from jax.experimental import pallas as pl
from jax.experimental.pallas import tpu as pltpu
from jax.sharding import PartitionSpec as P

BS = 96
BINS = 96
PAIR = 2
GROUP = 8
PARTS = 3
norm_eps = 1e-06
shrink_width = 0.01
VMEM = 60 * 1024 * 1024
f32 = jnp.float32
bf16 = jnp.bfloat16


def phi_parts(v):
    cdf = 0.5 * (1.0 + lax.erf(v * math.sqrt(0.5)))
    slope = cdf + v * (jnp.exp(v * v * -0.5) * (1.0 / math.sqrt(2.0 * math.pi)))
    return cdf, slope


def dot(a, b):
    return lax.dot_general(a, b, (((1,), (0,)), ((), ())), preferred_element_type=f32)


def dot_tn(a, b):
    return lax.dot_general(a, b, (((0,), (0,)), ((), ())), preferred_element_type=f32)


def dot_nt(a, b):
    return lax.dot_general(a, b, (((1,), (1,)), ((), ())), preferred_element_type=f32)


def standardize(v):
    centre = jnp.mean(v, axis=-1, keepdims=True)
    centred = v - centre
    spread = jnp.mean(centred * centred, axis=-1, keepdims=True)
    scale = lax.rsqrt(spread + norm_eps)
    return centred * scale, scale


def standardize_back(grad, normal, scale):
    first = jnp.mean(grad, axis=-1, keepdims=True)
    second = jnp.mean(grad * normal, axis=-1, keepdims=True)
    return scale * (grad - first - normal * second)


def pack(sides, out, width):
    turned = [jnp.swapaxes(s, 0, 1) for s in sides]
    for c in range(out.shape[1]):
        out[:, c] = jnp.concatenate([t[:, :, c * width : (c + 1) * width] for t in turned], axis=2)


def unpack(ref, half, width):
    parts = [ref[:, c, :, half * width : (half + 1) * width] for c in range(ref.shape[1])]
    return jnp.swapaxes(jnp.concatenate(parts, axis=2) if len(parts) > 1 else parts[0], 0, 1)


def first_kernel(states, mask, gain, shift, out):
    width = out.shape[3] // PAIR
    sides = []
    for half in range(PAIR):
        inside = mask[half][..., :1]
        normal, _ = standardize(states[half].astype(f32) * inside)
        sides.append(inside * (normal * gain[...] + shift[...]))
    pack(sides, out, width)


def table_dot(table, x):
    rows = table.shape[0] // 2
    high = x.astype(bf16)
    both = dot(table[...], high)
    rest = dot(table[:rows, :], (x - high.astype(f32)).astype(bf16))
    return both[:rows] + both[rows:] + rest


def wide_in_kernel(cols_here, fine, block, table, held, wide):
    groups, rows = block.shape[1], block.shape[2] // cols_here
    for n in range(block.shape[0] * rows):
        r, j = divmod(n, rows)
        for c in range(groups):
            wide[n, c * cols_here : (c + 1) * cols_here, :] = block[
                r, c, j * cols_here : (j + 1) * cols_here, :
            ]
        x = wide[n]
        y = table_dot(table, x) if fine else dot(table[...], x.astype(bf16))
        held[n, 0] = y[:BINS]
        held[n, 1] = y[BINS:]


def wide_out_kernel(cols_here, factor, held, table, block):
    groups, rows = block.shape[1], block.shape[2] // cols_here
    for n in range(block.shape[0] * rows):
        r, j = divmod(n, rows)
        x = jnp.concatenate([held[n, 0], held[n, 1]], axis=0).astype(bf16)
        plane = dot(table[...], x) * factor
        for c in range(groups):
            block[r, c, j * cols_here : (j + 1) * cols_here, :] = plane[
                c * cols_here : (c + 1) * cols_here, :
            ]


def bins_in(held, table, width, fine):
    kind = f32 if fine else bf16
    turned = [
        [jnp.swapaxes(part[:, side], 0, 1).astype(kind) for part in held] for side in range(2)
    ]
    outs = []
    for k in range(GROUP):
        x = jnp.concatenate(
            [
                part[k][:, h * width : (h + 1) * width]
                for side in turned
                for h in range(PAIR)
                for part in side
            ],
            axis=0,
        )
        outs.append(table_dot(table, x) if fine else dot(table[...], x))
    return outs


def bins_out(held, table, width, values):
    short = held[0].shape[0]
    count = len(held)
    products = [dot(table[...], value) for value in values]
    for side in range(2):
        for q in range(count):
            rows = []
            for z in products:
                at = [((side * PAIR + h) * count + q) * short for h in range(PAIR)]
                rows.append(jnp.concatenate([z[a : a + short] for a in at], axis=1))
            held[q][:, side] = jnp.swapaxes(jnp.stack(rows, axis=0), 0, 1)


def halves(v, count, tall):
    return [
        (v[k * 2 * tall : k * 2 * tall + tall], v[k * 2 * tall + tall : (k + 1) * 2 * tall])
        for k in range(count)
    ]


def complex_product(x, first, second, count, tall, conj):
    a = dot(x, first)
    b = dot(x, second)
    parts = []
    for (a_re, a_im), (b_re, b_im) in zip(halves(a, count, tall), halves(b, count, tall)):
        if conj:
            parts += [a_re + b_im, a_im - b_re]
        else:
            parts += [a_re - b_im, a_im + b_re]
    return parts


def activate(low, mix, bias, tall):
    parts = complex_product(low, mix[0], mix[1], low.shape[0] // (2 * tall), tall, False)
    return [part + bias[n % 2 : n % 2 + 1, :] for n, part in enumerate(parts)]


def gelu_low(v):
    return (v * (0.5 * (1.0 + lax.erf(v * math.sqrt(0.5))))).astype(bf16)


def spectral_forward_kernel(factor, *refs):
    held, refs = refs[:PARTS], refs[PARTS:]
    table_down, table_up, inner, inner_bias, outer, outer_bias = refs[:6]
    given, entries = refs[6 : 6 + PARTS], refs[6 + PARTS]
    width = inner.shape[2]
    tall = table_up.shape[0] // 2
    spec = bins_in(held, table_down, width, True)
    low = jnp.concatenate([(s * factor).astype(bf16) for s in spec], axis=0)
    entries[...] = low
    act = jnp.concatenate([gelu_low(v) for v in activate(low, inner, inner_bias, tall)], axis=0)
    shrunk = [
        (v - shrink_width * jnp.tanh(v * (1.0 / shrink_width))).astype(bf16)
        for v in activate(act, outer, outer_bias, tall)
    ]
    values = [jnp.concatenate(shrunk[2 * k : 2 * k + 2], axis=0) for k in range(GROUP)]
    bins_out(given, table_up, width, values)


def spectral_keep_kernel(tall, entries, inner, inner_bias, outer, outer_bias, active, slope, damp):
    acts = []
    for n, v in enumerate(activate(entries[...], inner, inner_bias, tall)):
        cdf, der = phi_parts(v)
        acts.append((v * cdf).astype(bf16))
        slope[n * tall : (n + 1) * tall, :] = der.astype(bf16)
    act = jnp.concatenate(acts, axis=0)
    active[...] = act
    for n, v in enumerate(activate(act, outer, outer_bias, tall)):
        t = jnp.tanh(v * (1.0 / shrink_width))
        damp[n * tall : (n + 1) * tall, :] = (t * t).astype(bf16)


def spectral_backward_kernel(factor, *refs):
    held, refs = refs[:PARTS], refs[PARTS:]
    table_down, table_up, inner_t, outer_t, slope, damp = refs[:6]
    given, refs = refs[6 : 6 + PARTS], refs[6 + PARTS :]
    inner_low, inner_bias_grad, outer_low, outer_bias_grad = refs
    width = inner_t.shape[2]
    tall = table_up.shape[0] // 2

    @pl.when(pl.program_id(0) == 0)
    def _():
        for ref in (inner_bias_grad, outer_bias_grad):
            ref[...] = jnp.zeros_like(ref)

    spec = bins_in(held, table_down, width, False)
    grads = []
    sums = [0.0, 0.0]
    for k in range(GROUP):
        for side in range(2):
            at = (2 * k + side) * tall
            g = spec[k][side * tall : (side + 1) * tall] * factor
            g = g * damp[at : at + tall, :].astype(f32)
            sums[side] = sums[side] + jnp.sum(g, axis=0, keepdims=True)
            grads.append(g.astype(bf16))
    outer_bias_grad[...] += jnp.concatenate(sums, axis=0)
    low = jnp.concatenate(grads, axis=0)
    outer_low[...] = low
    parts = complex_product(low, outer_t[0], outer_t[1], GROUP, tall, True)
    grads = []
    sums = [0.0, 0.0]
    for n, part in enumerate(parts):
        g = part * slope[n * tall : (n + 1) * tall, :].astype(f32)
        sums[n % 2] = sums[n % 2] + jnp.sum(g, axis=0, keepdims=True)
        grads.append(g.astype(bf16))
    inner_bias_grad[...] += jnp.concatenate(sums, axis=0)
    low = jnp.concatenate(grads, axis=0)
    inner_low[...] = low
    parts = complex_product(low, inner_t[0], inner_t[1], GROUP, tall, True)
    values = [
        jnp.concatenate([parts[2 * k], parts[2 * k + 1]], axis=0).astype(bf16)
        for k in range(GROUP)
    ]
    bins_out(given, table_up, width, values)


def filter_grad_kernel(tall, entries, inner_low, active, outer_low, inner_grad, outer_grad):
    @pl.when(pl.program_id(0) == 0)
    def _():
        inner_grad[...] = jnp.zeros_like(inner_grad)
        outer_grad[...] = jnp.zeros_like(outer_grad)

    for before, low, grad in ((entries, inner_low, inner_grad), (active, outer_low, outer_grad)):
        turned = []
        for k in range(GROUP):
            top, bottom = low[2 * k * tall : (2 * k + 1) * tall], low[(2 * k + 1) * tall : (2 * k + 2) * tall]
            turned += [bottom, -top]
        grad[0] += dot_tn(before[...], low[...])
        grad[1] += dot_tn(before[...], jnp.concatenate(turned, axis=0))


def dense_kernel(steps, slabs, first_part, *refs):
    (
        states, cot, spat, mask, first_gain, first_shift, later_gain, later_shift,
        expand_bias, reduce_bias, expand_hbm, reduce_hbm,
    ) = refs[:12]
    refs = refs[12:]
    if not first_part:
        grads_before = refs[0]
        refs = refs[2:]
    result, back, later_grad, sums, expand_bias_grad, grads_hbm = refs[:6]
    (
        expand, reduce, expand_grad, reduce_grad, mixed, normed, low_out, branch, grad_n,
        hidden_all, grad_all, copy_sem,
    ) = refs[6:]
    step = pl.program_id(0)
    chans = states.shape[3]
    width = spat.shape[3] // PAIR
    side_tokens = states.shape[1] * states.shape[2]
    slab = expand.shape[2]
    tokens = mixed.shape[0]
    square = states.shape[1:]

    def parts_of(grads):
        pairs = [(grads.at[pl.ds(s * chans, chans)], expand_grad.at[s]) for s in range(slabs)]
        return pairs + [(grads.at[pl.ds(slabs * chans, slabs * slab)], reduce_grad)]

    def fetches():
        copies = [
            pltpu.make_async_copy(
                expand_hbm.at[:, pl.ds(s * slab, slab)], expand.at[s], copy_sem.at[s]
            )
            for s in range(slabs)
        ]
        copies.append(pltpu.make_async_copy(reduce_hbm, reduce, copy_sem.at[slabs]))
        if not first_part:
            copies += [
                pltpu.make_async_copy(far, near, copy_sem.at[slabs + 1 + n])
                for n, (far, near) in enumerate(parts_of(grads_before))
            ]
        return copies

    @pl.when(step == 0)
    def _():
        for c in fetches():
            c.start()
        if first_part:
            expand_grad[...] = jnp.zeros_like(expand_grad)
            reduce_grad[...] = jnp.zeros_like(reduce_grad)
        sums[...] = jnp.zeros_like(sums)
        expand_bias_grad[...] = jnp.zeros_like(expand_bias_grad)

    @pl.when(step < steps)
    def _():
        start = pl.multiple_of(step * (PAIR * side_tokens), PAIR * side_tokens)
        for half in range(PAIR):
            at = pl.ds(start + half * side_tokens, side_tokens)
            inside = mask[half][..., :1]
            lower = inside * states[half].astype(f32)
            first, _ = standardize(lower)
            filter_in = first * first_gain[...] + first_shift[...]
            full = lower + inside * (unpack(spat, half, width) + filter_in)
            later, _ = standardize(full)
            full = full.reshape(side_tokens, chans)
            mixed[at, :] = full
            branch[at, :] = full + reduce_bias[...]
            normal = (later * later_gain[...] + later_shift[...]).reshape(side_tokens, chans)
            normed[at, :] = normal.astype(bf16)
            go = (inside * cot[half].astype(f32)).reshape(side_tokens, chans)
            low_out[at, :] = go.astype(bf16)
            grad_n[at, :] = jnp.zeros_like(full)
            sums[0:1, :] += jnp.sum(go, axis=0, keepdims=True)

    @pl.when(step == steps)
    def _():
        for c in fetches():
            c.wait()

    @pl.when((step >= steps) & (step < steps + slabs))
    def _():
        hc = step - steps
        at = pl.ds(pl.multiple_of(hc * slab, slab), slab)
        piece = tokens // 4 if tokens % 64 == 0 else tokens

        def some(n, carry):
            here = pl.ds(pl.multiple_of(n * piece, piece), piece)
            weight_up = expand[hc]
            weight_down = reduce[at, :]
            go = low_out[here, :]
            pre = dot(normed[here, :], weight_up) + expand_bias[...]
            cdf, der = phi_parts(pre)
            hidden = (pre * cdf).astype(bf16)
            hidden_all[here, :] = hidden
            branch[here, :] += dot(hidden, weight_down)
            grad_pre = dot_nt(go, weight_down) * der
            expand_bias_grad[pl.ds(hc, 1), :] += jnp.sum(grad_pre, axis=0, keepdims=True)
            grad_low = grad_pre.astype(bf16)
            grad_all[here, :] = grad_low
            grad_n[here, :] += dot_nt(grad_low, weight_up)
            return carry

        lax.fori_loop(0, tokens // piece, some, 0)
        reduce_grad[at, :] += dot_tn(hidden_all[...], low_out[...])
        expand_grad[hc] += dot_tn(normed[...], grad_all[...])

    @pl.when(step >= steps + slabs)
    def _():
        start = pl.multiple_of(
            (step - steps - slabs) * (PAIR * side_tokens), PAIR * side_tokens
        )
        sides = []
        for half in range(PAIR):
            at = pl.ds(start + half * side_tokens, side_tokens)
            inside = mask[half][..., :1]
            later, scale = standardize(mixed[at, :])
            g = grad_n[at, :]
            sums[1:2, :] += jnp.sum(g * later, axis=0, keepdims=True)
            sums[2:3, :] += jnp.sum(g, axis=0, keepdims=True)
            g = low_out[at, :].astype(f32) + standardize_back(g * later_gain[...], later, scale)
            sides.append(inside * g.reshape(square))
            later_grad[half] = sides[-1]
            result[half] = (inside * branch[at, :].reshape(square)).astype(bf16)
        pack(sides, back, width)

    @pl.when(step == pl.num_programs(0) - 1)
    def _():
        copies = [
            pltpu.make_async_copy(near, far, copy_sem.at[n])
            for n, (far, near) in enumerate(parts_of(grads_hbm))
        ]
        for c in copies:
            c.start()
        for c in copies:
            c.wait()


def last_kernel(states, later_grad, spat, mask, gain, *refs):
    out, sums = refs[-2:]
    width = spat.shape[3] // PAIR
    chans = states.shape[3]

    @pl.when(pl.program_id(0) == 0)
    def _():
        sums[...] = jnp.zeros_like(sums)

    for half in range(PAIR):
        inside = mask[half][..., :1]
        normal, scale = standardize(inside * states[half].astype(f32))
        grad_mixed = later_grad[half]
        grad = inside * (grad_mixed + unpack(spat, half, width))
        flat = (-1, chans)
        sums[0:1, :] += jnp.sum((grad * normal).reshape(flat), axis=0, keepdims=True)
        sums[1:2, :] += jnp.sum(grad.reshape(flat), axis=0, keepdims=True)
        grad = grad_mixed + standardize_back(grad * gain[...], normal, scale)
        out[half] = (inside * grad).astype(bf16)


def sum_kernel(ranks, groups, own, out, got, send_sem, recv_sem):
    devices = ranks * groups
    me = lax.axis_index("rows") * groups + lax.axis_index("cols")

    def place(i):
        other = lax.rem(me + i, devices)
        return lax.div(other, groups), lax.rem(other, groups)

    def copy(i):
        return pltpu.make_async_remote_copy(
            src_ref=own,
            dst_ref=got.at[i],
            send_sem=send_sem.at[i],
            recv_sem=recv_sem.at[i],
            device_id=place(i),
            device_id_type=pl.DeviceIdType.MESH,
        )

    barrier = pltpu.get_barrier_semaphore()

    def greet(i, carry):
        pl.semaphore_signal(
            barrier, inc=1, device_id=place(i), device_id_type=pl.DeviceIdType.MESH
        )
        return carry

    def start(i, carry):
        copy(i).start()
        return carry

    def finish(i, carry):
        copy(i).wait()
        return carry

    lax.fori_loop(1, devices, greet, 0)
    pl.semaphore_wait(barrier, devices - 1)
    lax.fori_loop(1, devices, start, 0)
    lax.fori_loop(1, devices, finish, 0)
    out[...] = lax.fori_loop(1, devices, lambda i, total: total + got[i], own[...])


def rows_sum_kernel(ranks, own, out, got, done, pick_send, pick_recv, give_send, give_recv):
    me = lax.axis_index("rows")
    piece = own.shape[0] // ranks

    def at(ref, r):
        return ref.at[pl.ds(pl.multiple_of(r * piece, piece), piece)]

    def copy(src, dst, i, send, recv):
        return pltpu.make_async_remote_copy(
            src_ref=src,
            dst_ref=dst,
            send_sem=send.at[i],
            recv_sem=recv.at[i],
            device_id={"rows": lax.rem(me + i, ranks)},
            device_id_type=pl.DeviceIdType.MESH,
        )

    barrier = pltpu.get_barrier_semaphore()
    for i in range(1, ranks):
        pl.semaphore_signal(
            barrier,
            inc=1,
            device_id={"rows": lax.rem(me + i, ranks)},
            device_id_type=pl.DeviceIdType.MESH,
        )
    pl.semaphore_wait(barrier, ranks - 1)
    picks = [
        copy(at(own, lax.rem(me + i, ranks)), got.at[i], i, pick_send, pick_recv)
        for i in range(1, ranks)
    ]
    for c in picks:
        c.start()
    for c in picks:
        c.wait()
    start = pl.ds(pl.multiple_of(me * piece, piece), piece)
    total = own[start, :]
    for i in range(1, ranks):
        total = total + got[i]
    done[0] = total
    gives = [copy(done.at[0], done.at[i], i, give_send, give_recv) for i in range(1, ranks)]
    for c in gives:
        c.start()
    for c in gives:
        c.wait()
    out[start, :] = total
    for i in range(1, ranks):
        source = lax.rem(me - i + ranks, ranks)
        out[pl.ds(pl.multiple_of(source * piece, piece), piece), :] = done[i]


def split_kernel(expand_in, reduce_in, expand_out, reduce_out):
    expand_out[...] = expand_in[...]
    reduce_out[...] = reduce_in[...]


def wide_tables(width):
    freq = np.arange(BINS)
    place = np.arange(width)
    angle = (freq[:, None] * place[None, :] % width) * (2.0 * math.pi / width)
    live = (2 * freq <= width).astype(np.float64)[:, None]
    edge = (freq == 0) | (2 * freq == width)
    weight = np.where(edge, 1.0, 2.0)[:, None] * live
    cosine, sine = np.cos(angle), np.sin(angle)
    plain = np.concatenate([live * cosine, -live * sine], axis=0)
    doubled = np.concatenate([weight * cosine, -weight * sine], axis=0)
    return plain, doubled


def tall_tables(height, rows_here):
    pairs = rows_here // PAIR
    rows = pairs // PARTS
    order = np.array(
        [
            r * rows_here + h * pairs + q * rows + j
            for h in range(PAIR)
            for q in range(PARTS)
            for r in range(height // rows_here)
            for j in range(rows)
        ]
    )
    freq = np.arange(height)
    angle = (freq[:, None] * order[None, :] % height) * (2.0 * math.pi / height)
    cosine, sine = np.cos(angle), np.sin(angle)
    down = np.block([[cosine, sine], [-sine, cosine]])
    up = np.block([[cosine.T, -sine.T], [sine.T, cosine.T]])
    return down, up


def spread(weight):
    count = weight.shape[1]
    eye = jnp.eye(count, dtype=weight.dtype)
    full = jnp.einsum("rbio,bd->rbido", weight, eye)
    return full.reshape(2, count * BS, count * BS)


def gather_blocks(full):
    count = full.shape[1] // BS
    return jnp.stack(
        [full[:, b * BS : (b + 1) * BS, b * BS : (b + 1) * BS] for b in range(count)], axis=1
    )


def bias_rows(bias):
    return bias.reshape(2, -1)


def whole(shape):
    return pl.BlockSpec(shape, lambda *_: (0,) * len(shape))


def call(kernel, grid, in_specs, out_specs, out_shape, name, flops=0, nbytes=0, scratch=(), **kw):
    return pl.pallas_call(
        kernel,
        grid=(grid,),
        in_specs=in_specs,
        out_specs=out_specs,
        out_shape=out_shape,
        scratch_shapes=scratch,
        compiler_params=pltpu.CompilerParams(
            dimension_semantics=("arbitrary",), vmem_limit_bytes=VMEM
        ),
        cost_estimate=pl.CostEstimate(flops=flops, bytes_accessed=nbytes, transcendentals=0),
        name=name,
        **kw,
    )


def body(
    states,
    heights,
    widths,
    first_gain,
    first_shift,
    filter_inner,
    inner_bias,
    filter_outer,
    outer_bias,
    later_gain,
    later_shift,
    expand_weight,
    expand_bias,
    reduce_weight,
    reduce_bias,
    cotangent,
):
    frames, rows_here, cols_here, chans = states.shape
    ranks, groups = lax.axis_size("rows"), lax.axis_size("cols")
    assert frames == ranks and rows_here % (PAIR * PARTS) == 0
    height, breadth = rows_here * ranks, cols_here * groups
    devices = ranks * groups
    pairs = rows_here // PAIR
    rows = pairs // PARTS
    pixels = rows * cols_here
    width = chans // groups
    lanes = width * PAIR
    hidden = expand_weight.shape[1]
    factor = 1.0 / math.sqrt(height * breadth)
    short = ranks * rows
    step_pixels = 8 if pixels % 8 == 0 else pixels
    steps = pixels // step_pixels
    tokens = PAIR * pixels * frames
    message = devices * pixels * lanes * 4
    row = lambda v: v.reshape(1, -1)
    shape = jax.ShapeDtypeStruct

    order = lambda v: jnp.transpose(v, (1, 2, 0, 3)).reshape(PAIR, pairs * cols_here, frames, chans)
    restore = lambda v: jnp.transpose(v.reshape(rows_here, cols_here, frames, chans), (2, 0, 1, 3))
    states_in, cot_in = order(states), order(cotangent)
    row_ids = lax.axis_index("rows") * rows_here + jnp.arange(rows_here, dtype=jnp.int32)
    col_ids = lax.axis_index("cols") * cols_here + jnp.arange(cols_here, dtype=jnp.int32)
    inside = (row_ids[:, None, None] < heights) & (col_ids[None, :, None] < widths)
    mask = jnp.broadcast_to(
        inside.astype(f32).reshape(PAIR, pairs * cols_here, frames, 1),
        (PAIR, pairs * cols_here, frames, 128),
    )

    buffers = {} if steps > 1 else {"pipeline_mode": pl.Buffered(1)}

    def token_spec(q, where, last=chans):
        return pl.BlockSpec(
            (PAIR, step_pixels, frames, last), lambda i: (0, q * steps + where(i), 0, 0), **buffers
        )

    def packed_spec(where):
        return pl.BlockSpec(
            (ranks, groups, step_pixels, lanes), lambda i: (0, 0, where(i), 0), **buffers
        )

    same = lambda i: i
    token_shape = shape((PAIR, pairs * cols_here, frames, chans), bf16)
    packed_shape = shape((ranks, groups, pixels, lanes), f32)
    chan_row = whole((1, chans))
    anywhere = pl.BlockSpec(memory_space=pl.ANY)

    def scatter(v, axis):
        return lax.psum_scatter(v, axis, scatter_dimension=0, tiled=True)

    def gather(v, axis):
        return lax.all_gather(v, axis, axis=0, tiled=True)

    def sum_small(v):
        flat = v.reshape(-1, 128)
        flat = jnp.pad(flat, ((0, -flat.shape[0] % 8), (0, 0)))
        vmem = pl.BlockSpec(memory_space=pltpu.VMEM)
        return pl.pallas_call(
            functools.partial(sum_kernel, ranks, groups),
            in_specs=[vmem],
            out_specs=vmem,
            out_shape=shape(flat.shape, f32),
            scratch_shapes=[
                pltpu.VMEM((devices,) + flat.shape, f32),
                pltpu.SemaphoreType.DMA((devices,)),
                pltpu.SemaphoreType.DMA((devices,)),
            ],
            compiler_params=pltpu.CompilerParams(collective_id=0, has_side_effects=True),
            name="small_sums",
        )(flat).reshape(-1)[: v.size].reshape(v.shape)

    def sum_rows(v):
        flat = v.reshape(-1)
        flat = jnp.pad(flat, (0, -flat.shape[0] % (ranks * 1024))).reshape(-1, 128)
        slots = (ranks, flat.shape[0] // ranks, 128)
        vmem = pl.BlockSpec(memory_space=pltpu.VMEM)
        return pl.pallas_call(
            functools.partial(rows_sum_kernel, ranks),
            in_specs=[vmem],
            out_specs=vmem,
            out_shape=shape(flat.shape, f32),
            scratch_shapes=[pltpu.VMEM(slots, f32)] * 2 + [pltpu.SemaphoreType.DMA((ranks,))] * 4,
            compiler_params=pltpu.CompilerParams(collective_id=1, has_side_effects=True),
            name="filter_sums",
        )(flat).reshape(-1)[: v.size]

    def split_grads(v):
        cuts = 4
        piece = (chans // cuts, chans)
        return call(
            split_kernel,
            slabs * cuts,
            [
                pl.BlockSpec(piece, lambda i: (i, 0)),
                pl.BlockSpec(piece, lambda i: (slabs * cuts + i, 0)),
            ],
            [
                pl.BlockSpec(piece, lambda i: (lax.rem(i, cuts), lax.div(i, cuts))),
                pl.BlockSpec(piece, lambda i: (i, 0)),
            ],
            [shape((chans, hidden), f32), shape((hidden, chans), f32)],
            "split_gradients",
            nbytes=16 * chans * hidden,
        )(v, v)

    def behind(v, *after):
        return lax.optimization_barrier((v,) + after)[0] if after else v

    def exchange(v, *after):
        v = v.reshape(devices, pixels, lanes)
        v = behind(v, *after)
        v = lax.all_to_all(v, ("rows", "cols"), 0, 0, tiled=True)
        return v.reshape(ranks, groups, pixels, lanes)

    def first_norm(q):
        return call(
            first_kernel,
            steps,
            [token_spec(q, same), token_spec(q, same, 128), chan_row, chan_row],
            packed_spec(same),
            packed_shape,
            "first_norm",
            nbytes=2 * message,
        )(states_in, mask, row(first_gain), row(first_shift))

    plain, doubled = wide_tables(breadth)
    down, up = tall_tables(height, rows_here)
    as_table = lambda t: jnp.asarray(t, dtype=bf16)

    def fine_table(t):
        high = t.astype(jnp.bfloat16)
        return jnp.asarray(np.concatenate([high, (t - high.astype(np.float64)).astype(jnp.bfloat16)]))

    inner_full, outer_full = spread(filter_inner), spread(filter_outer)
    turn = lambda t: jnp.swapaxes(t, 1, 2)
    bin_steps = BINS // GROUP
    group_rows = GROUP * 2 * height
    held_shape = shape((short, 2, BINS, lanes), f32)
    at_once = 2
    held_row = pl.BlockSpec((at_once * rows, 2, BINS, lanes), lambda i: (i, 0, 0, 0))
    held_bins = pl.BlockSpec((short, 2, GROUP, lanes), lambda i: (0, 0, i, 0))
    field = pl.BlockSpec((at_once, groups, pixels, lanes), lambda i: (i, 0, 0, 0))
    kept = pl.BlockSpec((group_rows, width), lambda i: (i, 0))
    kept_shape = shape((bin_steps * group_rows, width), bf16)
    mix_spec = whole((2, width, width))
    bias_spec = whole((2, width))
    up_spec = whole((2 * height, 2 * height))

    def wide_in(v, table, fine):
        return call(
            functools.partial(wide_in_kernel, cols_here, fine),
            ranks // at_once,
            [field, whole(table.shape)],
            held_row,
            held_shape,
            "wide_in",
            nbytes=2 * message,
            scratch=[pltpu.VMEM((at_once * rows, breadth, lanes), f32)],
        )(v, table)

    def wide_out(v, table):
        return call(
            functools.partial(wide_out_kernel, cols_here, factor),
            ranks // at_once,
            [held_row, whole(table.shape)],
            field,
            packed_shape,
            "wide_out",
            nbytes=2 * message,
        )(v, table)

    forward_mix = (inner_full, bias_rows(inner_bias), outer_full, bias_rows(outer_bias))
    forward_specs = [mix_spec, bias_spec, mix_spec, bias_spec]

    def spectral_forward(held):
        table = fine_table(down)
        outs = call(
            functools.partial(spectral_forward_kernel, factor),
            bin_steps,
            [held_bins] * PARTS + [whole(table.shape), up_spec] + forward_specs,
            [held_bins] * PARTS + [kept],
            [held_shape] * PARTS + [kept_shape],
            "spectral_forward",
            flops=20 * 10**9,
            nbytes=8 * PARTS * message,
        )(*held, table, as_table(up), *forward_mix)
        return outs[:PARTS], outs[PARTS]

    def spectral_keep(entries):
        return call(
            functools.partial(spectral_keep_kernel, height),
            bin_steps,
            [kept] + forward_specs,
            [kept] * 3,
            [kept_shape] * 3,
            "spectral_keep",
            flops=10 * 10**9,
            nbytes=2 * PARTS * message,
        )(entries, *forward_mix)

    def spectral_backward(held, slope, damp):
        outs = call(
            functools.partial(spectral_backward_kernel, factor),
            bin_steps,
            [held_bins] * PARTS + [up_spec, up_spec, mix_spec, mix_spec] + [kept] * 2,
            [held_bins] * PARTS + [kept, bias_spec] * 2,
            [held_shape] * PARTS + [kept_shape, shape((2, width), f32)] * 2,
            "spectral_backward",
            flops=20 * 10**9,
            nbytes=8 * PARTS * message,
        )(*held, as_table(down), as_table(up), turn(inner_full), turn(outer_full), slope, damp)
        return outs[:PARTS], outs[PARTS:]

    def filter_grad(*operands):
        return call(
            functools.partial(filter_grad_kernel, height),
            bin_steps,
            [kept] * 4,
            [mix_spec] * 2,
            [shape((2, width, width), f32)] * 2,
            "filter_grad",
            flops=10 * 10**9,
            nbytes=2 * PARTS * message,
        )(*operands)

    slab = chans
    slabs = hidden // slab
    dense_steps = 2 * steps + slabs
    enter = lambda i: jnp.minimum(i, steps - 1)
    leave = lambda i: jnp.maximum(i - steps - slabs, 0)
    either = lambda i: jnp.where(i < steps + slabs, enter(i), leave(i))

    def dense(q, spatial, before):
        grads_before = () if q == 0 else before
        return call(
            functools.partial(dense_kernel, steps, slabs, q == 0),
            dense_steps,
            [token_spec(q, enter), token_spec(q, enter), packed_spec(enter)]
            + [token_spec(q, either, 128)]
            + [chan_row] * 4
            + [pl.BlockSpec((1, slab), lambda i: (0, jnp.clip(i - steps, 0, slabs - 1)))]
            + [chan_row]
            + [anywhere] * (2 + len(grads_before)),
            [
                token_spec(q, leave),
                packed_spec(leave),
                token_spec(0, leave),
                whole((8, chans)),
                whole((slabs, slab)),
                anywhere,
            ],
            [
                token_shape,
                packed_shape,
                shape((PAIR, pixels, frames, chans), f32),
                shape((8, chans), f32),
                shape((slabs, slab), f32),
                shape((2 * hidden, chans), f32),
            ],
            "dense_both_ways",
            flops=12 * tokens * chans * hidden,
            nbytes=4 * message,
            scratch=[
                pltpu.VMEM((slabs, chans, slab), bf16),
                pltpu.VMEM((hidden, chans), bf16),
                pltpu.VMEM((slabs, chans, slab), f32),
                pltpu.VMEM((hidden, chans), f32),
                pltpu.VMEM((tokens, chans), f32),
                pltpu.VMEM((tokens, chans), bf16),
                pltpu.VMEM((tokens, chans), bf16),
                pltpu.VMEM((tokens, chans), f32),
                pltpu.VMEM((tokens, chans), f32),
                pltpu.VMEM((tokens, slab), bf16),
                pltpu.VMEM((tokens, slab), bf16),
                pltpu.SemaphoreType.DMA((2 * slabs + 2,)),
            ],
            input_output_aliases={} if q == 0 else {13: 0},
        )(
            states_in,
            cot_in,
            spatial,
            mask,
            row(first_gain),
            row(first_shift),
            row(later_gain),
            row(later_shift),
            row(expand_bias),
            row(reduce_bias),
            expand_weight,
            reduce_weight,
            *grads_before,
        )

    def last_norm(q, later_grad, spatial, before):
        given = () if q == 0 else (before,)
        return call(
            last_kernel,
            steps,
            [token_spec(q, same), token_spec(0, same), packed_spec(same), token_spec(q, same, 128)]
            + [chan_row]
            + [anywhere] * len(given),
            [token_spec(q, same), whole((8, chans))],
            [token_shape, shape((8, chans), f32)],
            "first_norm_backward",
            nbytes=4 * message,
            input_output_aliases={} if q == 0 else {5: 0},
        )(states_in, later_grad, spatial, mask, row(first_gain), *given)

    every = range(PARTS)
    got = []
    for q in every:
        got.append(exchange(first_norm(q), *got[-1:]))
    held = [wide_in(v, fine_table(plain), True) for v in got]
    given, entries = spectral_forward(held)

    made = [wide_out(v, as_table(doubled.T)) for v in given]
    spatial, backs, later_grads, sums, expand_bias_grad, before = [], [], [], 0.0, 0.0, ()
    active, slope, damp = spectral_keep(entries)
    for q in range(PARTS + 1):
        if q < PARTS:
            beside = (active, *made[1:2]) if q == 1 else ()
            spatial.append(exchange(made[q], *spatial[-1:], *backs[-1:], *beside))
        if q > 0:
            result, back, kept_grad, part, bias_part, grads = dense(q - 1, spatial[q - 1], before)
            before = (grads, result)
            backs.append(back)
            later_grads.append(kept_grad)
            sums, expand_bias_grad = sums + part, expand_bias_grad + bias_part
    got, held = spatial[-1:], []
    for q in every:
        got.append(exchange(backs[q], got[-1], backs[min(q + 1, PARTS - 1)], *held[-1:]))
        if q == 0:
            grads = scatter(behind(grads, got[-1]), "cols")
        else:
            held.append(wide_in(got[q], as_table(doubled), False))
    held.append(wide_in(behind(got[-1], held[-1]), as_table(doubled), False))
    grads = scatter(behind(grads, held[-1]), "rows")

    given, (inner_low, inner_bias_grad, outer_low, outer_bias_grad) = spectral_backward(
        held, slope, damp
    )
    inner_grad, outer_grad = filter_grad(entries, inner_low, active, outer_low)
    filter_parts = (
        gather_blocks(inner_grad), inner_bias_grad, gather_blocks(outer_grad), outer_bias_grad
    )
    flat = sum_rows(jnp.concatenate([v.reshape(-1) for v in filter_parts]))
    made = [wide_out(v, as_table(plain.T)) for v in given]
    got, first_sums, states_grad = [], [], None
    for q in range(PARTS + 1):
        if q < PARTS:
            got.append(exchange(made[q], *got[-1:], *first_sums[-1:]))
        if q == 0:
            grads = gather(behind(grads, got[0], flat, *made[1:2]), ("cols", "rows"))
            expand_sum, reduce_sum = split_grads(grads)
        else:
            if q == PARTS:
                states_grad = behind(states_grad, expand_sum)
            states_grad, part = last_norm(q - 1, later_grads[q - 1], got[q - 1], states_grad)
            first_sums.append(part)
    small = sum_small(
        jnp.concatenate([sum(first_sums)[:2], sums[:3], expand_bias_grad.reshape(-1, chans)])
    )
    sizes = [v.size for v in filter_parts]
    ends = np.cumsum(sizes)
    filter_sums = [
        flat[e - n : e].reshape(v.shape) for e, n, v in zip(ends, sizes, filter_parts)
    ]
    inner_sum, inner_bias_sum, outer_sum, outer_bias_sum = filter_sums
    return (
        restore(result),
        restore(states_grad),
        small[0],
        small[1],
        inner_sum,
        inner_bias_sum.reshape(2, -1, BS),
        outer_sum,
        outer_bias_sum.reshape(2, -1, BS),
        small[3],
        small[4],
        expand_sum,
        small[5:].reshape(-1),
        reduce_sum,
        small[2],
    )


def solution(mesh):
    tile = P(None, "rows", "cols", None)
    mix = P(None, "cols", None, None)
    bias = P(None, "cols", None)
    in_specs = (
        tile, P(), P(), P(), P(), mix, bias, mix, bias, P(), P(), P(), P(), P(), P(), tile,
    )
    out_specs = (
        tile, tile, P(), P(), mix, bias, mix, bias, P(), P(), P(), P(), P(), P(),
    )
    return jax.shard_map(body, mesh=mesh, in_specs=in_specs, out_specs=out_specs, check_vma=False)
```

```python
import functools
import math

import jax
import jax.numpy as jnp
import numpy as np
from jax import lax
from jax.experimental import pallas as pl
from jax.experimental.pallas import tpu as pltpu
from jax.sharding import PartitionSpec as P

BS = 96
BINS = 96
PAIR = 2
GROUP = 8
PARTS = 3
norm_eps = 1e-06
shrink_width = 0.01
VMEM = 60 * 1024 * 1024
f32 = jnp.float32
bf16 = jnp.bfloat16


def phi_parts(v):
    cdf = 0.5 * (1.0 + lax.erf(v * math.sqrt(0.5)))
    slope = cdf + v * (jnp.exp(v * v * -0.5) * (1.0 / math.sqrt(2.0 * math.pi)))
    return cdf, slope


def dot(a, b):
    return lax.dot_general(a, b, (((1,), (0,)), ((), ())), preferred_element_type=f32)


def dot_tn(a, b):
    return lax.dot_general(a, b, (((0,), (0,)), ((), ())), preferred_element_type=f32)


def dot_nt(a, b):
    return lax.dot_general(a, b, (((1,), (1,)), ((), ())), preferred_element_type=f32)


def standardize(v):
    centre = jnp.mean(v, axis=-1, keepdims=True)
    centred = v - centre
    spread = jnp.mean(centred * centred, axis=-1, keepdims=True)
    scale = lax.rsqrt(spread + norm_eps)
    return centred * scale, scale


def standardize_back(grad, normal, scale):
    first = jnp.mean(grad, axis=-1, keepdims=True)
    second = jnp.mean(grad * normal, axis=-1, keepdims=True)
    return scale * (grad - first - normal * second)


def pack(sides, out, width):
    turned = [jnp.swapaxes(s, 0, 1) for s in sides]
    for c in range(out.shape[1]):
        out[:, c] = jnp.concatenate([t[:, :, c * width : (c + 1) * width] for t in turned], axis=2)


def unpack(ref, half, width):
    parts = [ref[:, c, :, half * width : (half + 1) * width] for c in range(ref.shape[1])]
    return jnp.swapaxes(jnp.concatenate(parts, axis=2) if len(parts) > 1 else parts[0], 0, 1)


def first_kernel(states, mask, gain, shift, out):
    width = out.shape[3] // PAIR
    sides = []
    for half in range(PAIR):
        inside = mask[half][..., :1]
        normal, _ = standardize(states[half].astype(f32) * inside)
        sides.append(inside * (normal * gain[...] + shift[...]))
    pack(sides, out, width)


def table_dot(table, x):
    rows = table.shape[0] // 2
    high = x.astype(bf16)
    both = dot(table[...], high)
    rest = dot(table[:rows, :], (x - high.astype(f32)).astype(bf16))
    return both[:rows] + both[rows:] + rest


def wide_in_kernel(cols_here, fine, block, table, held, wide):
    groups, rows = block.shape[1], block.shape[2] // cols_here
    for n in range(block.shape[0] * rows):
        r, j = divmod(n, rows)
        for c in range(groups):
            wide[n, c * cols_here : (c + 1) * cols_here, :] = block[
                r, c, j * cols_here : (j + 1) * cols_here, :
            ]
        x = wide[n]
        y = table_dot(table, x) if fine else dot(table[...], x.astype(bf16))
        held[n, 0] = y[:BINS]
        held[n, 1] = y[BINS:]


def wide_out_kernel(cols_here, factor, held, table, block):
    groups, rows = block.shape[1], block.shape[2] // cols_here
    for n in range(block.shape[0] * rows):
        r, j = divmod(n, rows)
        x = jnp.concatenate([held[n, 0], held[n, 1]], axis=0).astype(bf16)
        plane = dot(table[...], x) * factor
        for c in range(groups):
            block[r, c, j * cols_here : (j + 1) * cols_here, :] = plane[
                c * cols_here : (c + 1) * cols_here, :
            ]


def bins_in(held, table, width, fine):
    kind = f32 if fine else bf16
    turned = [
        [jnp.swapaxes(part[:, side], 0, 1).astype(kind) for part in held] for side in range(2)
    ]
    outs = []
    for k in range(GROUP):
        x = jnp.concatenate(
            [
                part[k][:, h * width : (h + 1) * width]
                for side in turned
                for h in range(PAIR)
                for part in side
            ],
            axis=0,
        )
        outs.append(table_dot(table, x) if fine else dot(table[...], x))
    return outs


def bins_out(held, table, width, values):
    short = held[0].shape[0]
    count = len(held)
    products = [dot(table[...], value) for value in values]
    for side in range(2):
        for q in range(count):
            rows = []
            for z in products:
                at = [((side * PAIR + h) * count + q) * short for h in range(PAIR)]
                rows.append(jnp.concatenate([z[a : a + short] for a in at], axis=1))
            held[q][:, side] = jnp.swapaxes(jnp.stack(rows, axis=0), 0, 1)


def halves(v, count, tall):
    return [
        (v[k * 2 * tall : k * 2 * tall + tall], v[k * 2 * tall + tall : (k + 1) * 2 * tall])
        for k in range(count)
    ]


def complex_product(x, first, second, count, tall, conj):
    a = dot(x, first)
    b = dot(x, second)
    parts = []
    for (a_re, a_im), (b_re, b_im) in zip(halves(a, count, tall), halves(b, count, tall)):
        if conj:
            parts += [a_re + b_im, a_im - b_re]
        else:
            parts += [a_re - b_im, a_im + b_re]
    return parts


def activate(low, mix, bias, tall):
    parts = complex_product(low, mix[0], mix[1], low.shape[0] // (2 * tall), tall, False)
    return [part + bias[n % 2 : n % 2 + 1, :] for n, part in enumerate(parts)]


def gelu_low(v):
    return (v * (0.5 * (1.0 + lax.erf(v * math.sqrt(0.5))))).astype(bf16)


def spectral_forward_kernel(factor, *refs):
    held, refs = refs[:PARTS], refs[PARTS:]
    table_down, table_up, inner, inner_bias, outer, outer_bias = refs[:6]
    given, entries = refs[6 : 6 + PARTS], refs[6 + PARTS]
    width = inner.shape[2]
    tall = table_up.shape[0] // 2
    spec = bins_in(held, table_down, width, True)
    low = jnp.concatenate([(s * factor).astype(bf16) for s in spec], axis=0)
    entries[...] = low
    act = jnp.concatenate([gelu_low(v) for v in activate(low, inner, inner_bias, tall)], axis=0)
    shrunk = [
        (v - shrink_width * jnp.tanh(v * (1.0 / shrink_width))).astype(bf16)
        for v in activate(act, outer, outer_bias, tall)
    ]
    values = [jnp.concatenate(shrunk[2 * k : 2 * k + 2], axis=0) for k in range(GROUP)]
    bins_out(given, table_up, width, values)


def spectral_keep_kernel(tall, entries, inner, inner_bias, outer, outer_bias, active, slope, damp):
    acts = []
    for n, v in enumerate(activate(entries[...], inner, inner_bias, tall)):
        cdf, der = phi_parts(v)
        acts.append((v * cdf).astype(bf16))
        slope[n * tall : (n + 1) * tall, :] = der.astype(bf16)
    act = jnp.concatenate(acts, axis=0)
    active[...] = act
    for n, v in enumerate(activate(act, outer, outer_bias, tall)):
        t = jnp.tanh(v * (1.0 / shrink_width))
        damp[n * tall : (n + 1) * tall, :] = (t * t).astype(bf16)


def spectral_backward_kernel(factor, *refs):
    held, refs = refs[:PARTS], refs[PARTS:]
    table_down, table_up, inner_t, outer_t, slope, damp = refs[:6]
    given, refs = refs[6 : 6 + PARTS], refs[6 + PARTS :]
    inner_low, inner_bias_grad, outer_low, outer_bias_grad = refs
    width = inner_t.shape[2]
    tall = table_up.shape[0] // 2

    @pl.when(pl.program_id(0) == 0)
    def _():
        for ref in (inner_bias_grad, outer_bias_grad):
            ref[...] = jnp.zeros_like(ref)

    spec = bins_in(held, table_down, width, False)
    grads = []
    sums = [0.0, 0.0]
    for k in range(GROUP):
        for side in range(2):
            at = (2 * k + side) * tall
            g = spec[k][side * tall : (side + 1) * tall] * factor
            g = g * damp[at : at + tall, :].astype(f32)
            sums[side] = sums[side] + jnp.sum(g, axis=0, keepdims=True)
            grads.append(g.astype(bf16))
    outer_bias_grad[...] += jnp.concatenate(sums, axis=0)
    low = jnp.concatenate(grads, axis=0)
    outer_low[...] = low
    parts = complex_product(low, outer_t[0], outer_t[1], GROUP, tall, True)
    grads = []
    sums = [0.0, 0.0]
    for n, part in enumerate(parts):
        g = part * slope[n * tall : (n + 1) * tall, :].astype(f32)
        sums[n % 2] = sums[n % 2] + jnp.sum(g, axis=0, keepdims=True)
        grads.append(g.astype(bf16))
    inner_bias_grad[...] += jnp.concatenate(sums, axis=0)
    low = jnp.concatenate(grads, axis=0)
    inner_low[...] = low
    parts = complex_product(low, inner_t[0], inner_t[1], GROUP, tall, True)
    values = [
        jnp.concatenate([parts[2 * k], parts[2 * k + 1]], axis=0).astype(bf16)
        for k in range(GROUP)
    ]
    bins_out(given, table_up, width, values)


def filter_grad_kernel(tall, entries, inner_low, active, outer_low, inner_grad, outer_grad):
    @pl.when(pl.program_id(0) == 0)
    def _():
        inner_grad[...] = jnp.zeros_like(inner_grad)
        outer_grad[...] = jnp.zeros_like(outer_grad)

    for before, low, grad in ((entries, inner_low, inner_grad), (active, outer_low, outer_grad)):
        turned = []
        for k in range(GROUP):
            top, bottom = low[2 * k * tall : (2 * k + 1) * tall], low[(2 * k + 1) * tall : (2 * k + 2) * tall]
            turned += [bottom, -top]
        grad[0] += dot_tn(before[...], low[...])
        grad[1] += dot_tn(before[...], jnp.concatenate(turned, axis=0))


def dense_kernel(steps, slabs, first_part, *refs):
    (
        states, cot, spat, mask, first_gain, first_shift, later_gain, later_shift,
        expand_bias, reduce_bias, expand_hbm, reduce_hbm,
    ) = refs[:12]
    refs = refs[12:]
    if not first_part:
        grads_before = refs[0]
        refs = refs[2:]
    result, back, later_grad, sums, expand_bias_grad, grads_hbm = refs[:6]
    (
        expand, reduce, expand_grad, reduce_grad, mixed, normed, low_out, branch, grad_n,
        hidden_all, grad_all, copy_sem,
    ) = refs[6:]
    step = pl.program_id(0)
    chans = states.shape[3]
    width = spat.shape[3] // PAIR
    side_tokens = states.shape[1] * states.shape[2]
    slab = expand.shape[2]
    tokens = mixed.shape[0]
    square = states.shape[1:]

    def parts_of(grads):
        pairs = [(grads.at[pl.ds(s * chans, chans)], expand_grad.at[s]) for s in range(slabs)]
        return pairs + [(grads.at[pl.ds(slabs * chans, slabs * slab)], reduce_grad)]

    def fetches():
        copies = [
            pltpu.make_async_copy(
                expand_hbm.at[:, pl.ds(s * slab, slab)], expand.at[s], copy_sem.at[s]
            )
            for s in range(slabs)
        ]
        copies.append(pltpu.make_async_copy(reduce_hbm, reduce, copy_sem.at[slabs]))
        if not first_part:
            copies += [
                pltpu.make_async_copy(far, near, copy_sem.at[slabs + 1 + n])
                for n, (far, near) in enumerate(parts_of(grads_before))
            ]
        return copies

    @pl.when(step == 0)
    def _():
        for c in fetches():
            c.start()
        if first_part:
            expand_grad[...] = jnp.zeros_like(expand_grad)
            reduce_grad[...] = jnp.zeros_like(reduce_grad)
        sums[...] = jnp.zeros_like(sums)
        expand_bias_grad[...] = jnp.zeros_like(expand_bias_grad)

    @pl.when(step < steps)
    def _():
        start = pl.multiple_of(step * (PAIR * side_tokens), PAIR * side_tokens)
        for half in range(PAIR):
            at = pl.ds(start + half * side_tokens, side_tokens)
            inside = mask[half][..., :1]
            lower = inside * states[half].astype(f32)
            first, _ = standardize(lower)
            filter_in = first * first_gain[...] + first_shift[...]
            full = lower + inside * (unpack(spat, half, width) + filter_in)
            later, _ = standardize(full)
            full = full.reshape(side_tokens, chans)
            mixed[at, :] = full
            branch[at, :] = full + reduce_bias[...]
            normal = (later * later_gain[...] + later_shift[...]).reshape(side_tokens, chans)
            normed[at, :] = normal.astype(bf16)
            go = (inside * cot[half].astype(f32)).reshape(side_tokens, chans)
            low_out[at, :] = go.astype(bf16)
            grad_n[at, :] = jnp.zeros_like(full)
            sums[0:1, :] += jnp.sum(go, axis=0, keepdims=True)

    @pl.when(step == steps)
    def _():
        for c in fetches():
            c.wait()

    @pl.when((step >= steps) & (step < steps + slabs))
    def _():
        hc = step - steps
        at = pl.ds(pl.multiple_of(hc * slab, slab), slab)
        piece = tokens // 4 if tokens % 64 == 0 else tokens

        def some(n, carry):
            here = pl.ds(pl.multiple_of(n * piece, piece), piece)
            weight_up = expand[hc]
            weight_down = reduce[at, :]
            go = low_out[here, :]
            pre = dot(normed[here, :], weight_up) + expand_bias[...]
            cdf, der = phi_parts(pre)
            hidden = (pre * cdf).astype(bf16)
            hidden_all[here, :] = hidden
            branch[here, :] += dot(hidden, weight_down)
            grad_pre = dot_nt(go, weight_down) * der
            expand_bias_grad[pl.ds(hc, 1), :] += jnp.sum(grad_pre, axis=0, keepdims=True)
            grad_low = grad_pre.astype(bf16)
            grad_all[here, :] = grad_low
            grad_n[here, :] += dot_nt(grad_low, weight_up)
            return carry

        lax.fori_loop(0, tokens // piece, some, 0)
        reduce_grad[at, :] += dot_tn(hidden_all[...], low_out[...])
        expand_grad[hc] += dot_tn(normed[...], grad_all[...])

    @pl.when(step >= steps + slabs)
    def _():
        start = pl.multiple_of(
            (step - steps - slabs) * (PAIR * side_tokens), PAIR * side_tokens
        )
        sides = []
        for half in range(PAIR):
            at = pl.ds(start + half * side_tokens, side_tokens)
            inside = mask[half][..., :1]
            later, scale = standardize(mixed[at, :])
            g = grad_n[at, :]
            sums[1:2, :] += jnp.sum(g * later, axis=0, keepdims=True)
            sums[2:3, :] += jnp.sum(g, axis=0, keepdims=True)
            g = low_out[at, :].astype(f32) + standardize_back(g * later_gain[...], later, scale)
            sides.append(inside * g.reshape(square))
            later_grad[half] = sides[-1]
            result[half] = (inside * branch[at, :].reshape(square)).astype(bf16)
        pack(sides, back, width)

    @pl.when(step == pl.num_programs(0) - 1)
    def _():
        copies = [
            pltpu.make_async_copy(near, far, copy_sem.at[n])
            for n, (far, near) in enumerate(parts_of(grads_hbm))
        ]
        for c in copies:
            c.start()
        for c in copies:
            c.wait()


def last_kernel(states, later_grad, spat, mask, gain, *refs):
    out, sums = refs[-2:]
    width = spat.shape[3] // PAIR
    chans = states.shape[3]

    @pl.when(pl.program_id(0) == 0)
    def _():
        sums[...] = jnp.zeros_like(sums)

    for half in range(PAIR):
        inside = mask[half][..., :1]
        normal, scale = standardize(inside * states[half].astype(f32))
        grad_mixed = later_grad[half]
        grad = inside * (grad_mixed + unpack(spat, half, width))
        flat = (-1, chans)
        sums[0:1, :] += jnp.sum((grad * normal).reshape(flat), axis=0, keepdims=True)
        sums[1:2, :] += jnp.sum(grad.reshape(flat), axis=0, keepdims=True)
        grad = grad_mixed + standardize_back(grad * gain[...], normal, scale)
        out[half] = (inside * grad).astype(bf16)


def sum_kernel(ranks, groups, own, out, got, send_sem, recv_sem):
    devices = ranks * groups
    me = lax.axis_index("rows") * groups + lax.axis_index("cols")

    def place(i):
        other = lax.rem(me + i, devices)
        return lax.div(other, groups), lax.rem(other, groups)

    def copy(i):
        return pltpu.make_async_remote_copy(
            src_ref=own,
            dst_ref=got.at[i],
            send_sem=send_sem.at[i],
            recv_sem=recv_sem.at[i],
            device_id=place(i),
            device_id_type=pl.DeviceIdType.MESH,
        )

    barrier = pltpu.get_barrier_semaphore()

    def greet(i, carry):
        pl.semaphore_signal(
            barrier, inc=1, device_id=place(i), device_id_type=pl.DeviceIdType.MESH
        )
        return carry

    def start(i, carry):
        copy(i).start()
        return carry

    def finish(i, carry):
        copy(i).wait()
        return carry

    lax.fori_loop(1, devices, greet, 0)
    pl.semaphore_wait(barrier, devices - 1)
    lax.fori_loop(1, devices, start, 0)
    lax.fori_loop(1, devices, finish, 0)
    out[...] = lax.fori_loop(1, devices, lambda i, total: total + got[i], own[...])


def rows_sum_kernel(ranks, own, out, got, done, pick_send, pick_recv, give_send, give_recv):
    me = lax.axis_index("rows")
    piece = own.shape[0] // ranks

    def at(ref, r):
        return ref.at[pl.ds(pl.multiple_of(r * piece, piece), piece)]

    def copy(src, dst, i, send, recv):
        return pltpu.make_async_remote_copy(
            src_ref=src,
            dst_ref=dst,
            send_sem=send.at[i],
            recv_sem=recv.at[i],
            device_id={"rows": lax.rem(me + i, ranks)},
            device_id_type=pl.DeviceIdType.MESH,
        )

    barrier = pltpu.get_barrier_semaphore()
    for i in range(1, ranks):
        pl.semaphore_signal(
            barrier,
            inc=1,
            device_id={"rows": lax.rem(me + i, ranks)},
            device_id_type=pl.DeviceIdType.MESH,
        )
    pl.semaphore_wait(barrier, ranks - 1)
    picks = [
        copy(at(own, lax.rem(me + i, ranks)), got.at[i], i, pick_send, pick_recv)
        for i in range(1, ranks)
    ]
    for c in picks:
        c.start()
    for c in picks:
        c.wait()
    start = pl.ds(pl.multiple_of(me * piece, piece), piece)
    total = own[start, :]
    for i in range(1, ranks):
        total = total + got[i]
    done[0] = total
    gives = [copy(done.at[0], done.at[i], i, give_send, give_recv) for i in range(1, ranks)]
    for c in gives:
        c.start()
    for c in gives:
        c.wait()
    out[start, :] = total
    for i in range(1, ranks):
        source = lax.rem(me - i + ranks, ranks)
        out[pl.ds(pl.multiple_of(source * piece, piece), piece), :] = done[i]


def split_kernel(expand_in, reduce_in, expand_out, reduce_out):
    expand_out[...] = expand_in[...]
    reduce_out[...] = reduce_in[...]


def wide_tables(width):
    freq = np.arange(BINS)
    place = np.arange(width)
    angle = (freq[:, None] * place[None, :] % width) * (2.0 * math.pi / width)
    live = (2 * freq <= width).astype(np.float64)[:, None]
    edge = (freq == 0) | (2 * freq == width)
    weight = np.where(edge, 1.0, 2.0)[:, None] * live
    cosine, sine = np.cos(angle), np.sin(angle)
    plain = np.concatenate([live * cosine, -live * sine], axis=0)
    doubled = np.concatenate([weight * cosine, -weight * sine], axis=0)
    return plain, doubled


def tall_tables(height, rows_here):
    pairs = rows_here // PAIR
    rows = pairs // PARTS
    order = np.array(
        [
            r * rows_here + h * pairs + q * rows + j
            for h in range(PAIR)
            for q in range(PARTS)
            for r in range(height // rows_here)
            for j in range(rows)
        ]
    )
    freq = np.arange(height)
    angle = (freq[:, None] * order[None, :] % height) * (2.0 * math.pi / height)
    cosine, sine = np.cos(angle), np.sin(angle)
    down = np.block([[cosine, sine], [-sine, cosine]])
    up = np.block([[cosine.T, -sine.T], [sine.T, cosine.T]])
    return down, up


def spread(weight):
    count = weight.shape[1]
    eye = jnp.eye(count, dtype=weight.dtype)
    full = jnp.einsum("rbio,bd->rbido", weight, eye)
    return full.reshape(2, count * BS, count * BS)


def gather_blocks(full):
    count = full.shape[1] // BS
    return jnp.stack(
        [full[:, b * BS : (b + 1) * BS, b * BS : (b + 1) * BS] for b in range(count)], axis=1
    )


def bias_rows(bias):
    return bias.reshape(2, -1)


def whole(shape):
    return pl.BlockSpec(shape, lambda *_: (0,) * len(shape))


def call(kernel, grid, in_specs, out_specs, out_shape, name, flops=0, nbytes=0, scratch=(), **kw):
    return pl.pallas_call(
        kernel,
        grid=(grid,),
        in_specs=in_specs,
        out_specs=out_specs,
        out_shape=out_shape,
        scratch_shapes=scratch,
        compiler_params=pltpu.CompilerParams(
            dimension_semantics=("arbitrary",), vmem_limit_bytes=VMEM
        ),
        cost_estimate=pl.CostEstimate(flops=flops, bytes_accessed=nbytes, transcendentals=0),
        name=name,
        **kw,
    )


def body(
    states,
    heights,
    widths,
    first_gain,
    first_shift,
    filter_inner,
    inner_bias,
    filter_outer,
    outer_bias,
    later_gain,
    later_shift,
    expand_weight,
    expand_bias,
    reduce_weight,
    reduce_bias,
    cotangent,
):
    frames, rows_here, cols_here, chans = states.shape
    ranks, groups = lax.axis_size("rows"), lax.axis_size("cols")
    assert frames == ranks and rows_here % (PAIR * PARTS) == 0
    height, breadth = rows_here * ranks, cols_here * groups
    devices = ranks * groups
    pairs = rows_here // PAIR
    rows = pairs // PARTS
    pixels = rows * cols_here
    width = chans // groups
    lanes = width * PAIR
    hidden = expand_weight.shape[1]
    factor = 1.0 / math.sqrt(height * breadth)
    short = ranks * rows
    step_pixels = 8 if pixels % 8 == 0 else pixels
    steps = pixels // step_pixels
    tokens = PAIR * pixels * frames
    message = devices * pixels * lanes * 4
    row = lambda v: v.reshape(1, -1)
    shape = jax.ShapeDtypeStruct

    order = lambda v: jnp.transpose(v, (1, 2, 0, 3)).reshape(PAIR, pairs * cols_here, frames, chans)
    restore = lambda v: jnp.transpose(v.reshape(rows_here, cols_here, frames, chans), (2, 0, 1, 3))
    states_in, cot_in = order(states), order(cotangent)
    row_ids = lax.axis_index("rows") * rows_here + jnp.arange(rows_here, dtype=jnp.int32)
    col_ids = lax.axis_index("cols") * cols_here + jnp.arange(cols_here, dtype=jnp.int32)
    inside = (row_ids[:, None, None] < heights) & (col_ids[None, :, None] < widths)
    mask = jnp.broadcast_to(
        inside.astype(f32).reshape(PAIR, pairs * cols_here, frames, 1),
        (PAIR, pairs * cols_here, frames, 128),
    )

    buffers = {} if steps > 1 else {"pipeline_mode": pl.Buffered(1)}

    def token_spec(q, where, last=chans):
        return pl.BlockSpec(
            (PAIR, step_pixels, frames, last), lambda i: (0, q * steps + where(i), 0, 0), **buffers
        )

    def packed_spec(where):
        return pl.BlockSpec(
            (ranks, groups, step_pixels, lanes), lambda i: (0, 0, where(i), 0), **buffers
        )

    same = lambda i: i
    token_shape = shape((PAIR, pairs * cols_here, frames, chans), bf16)
    packed_shape = shape((ranks, groups, pixels, lanes), f32)
    chan_row = whole((1, chans))
    anywhere = pl.BlockSpec(memory_space=pl.ANY)

    def scatter(v, axis):
        return lax.psum_scatter(v, axis, scatter_dimension=0, tiled=True)

    def gather(v, axis):
        return lax.all_gather(v, axis, axis=0, tiled=True)

    def sum_small(v):
        flat = v.reshape(-1, 128)
        flat = jnp.pad(flat, ((0, -flat.shape[0] % 8), (0, 0)))
        vmem = pl.BlockSpec(memory_space=pltpu.VMEM)
        return pl.pallas_call(
            functools.partial(sum_kernel, ranks, groups),
            in_specs=[vmem],
            out_specs=vmem,
            out_shape=shape(flat.shape, f32),
            scratch_shapes=[
                pltpu.VMEM((devices,) + flat.shape, f32),
                pltpu.SemaphoreType.DMA((devices,)),
                pltpu.SemaphoreType.DMA((devices,)),
            ],
            compiler_params=pltpu.CompilerParams(collective_id=0, has_side_effects=True),
            name="small_sums",
        )(flat).reshape(-1)[: v.size].reshape(v.shape)

    def sum_rows(v):
        flat = v.reshape(-1)
        flat = jnp.pad(flat, (0, -flat.shape[0] % (ranks * 1024))).reshape(-1, 128)
        slots = (ranks, flat.shape[0] // ranks, 128)
        vmem = pl.BlockSpec(memory_space=pltpu.VMEM)
        return pl.pallas_call(
            functools.partial(rows_sum_kernel, ranks),
            in_specs=[vmem],
            out_specs=vmem,
            out_shape=shape(flat.shape, f32),
            scratch_shapes=[pltpu.VMEM(slots, f32)] * 2 + [pltpu.SemaphoreType.DMA((ranks,))] * 4,
            compiler_params=pltpu.CompilerParams(collective_id=1, has_side_effects=True),
            name="filter_sums",
        )(flat).reshape(-1)[: v.size]

    def split_grads(v):
        cuts = 4
        piece = (chans // cuts, chans)
        return call(
            split_kernel,
            slabs * cuts,
            [
                pl.BlockSpec(piece, lambda i: (i, 0)),
                pl.BlockSpec(piece, lambda i: (slabs * cuts + i, 0)),
            ],
            [
                pl.BlockSpec(piece, lambda i: (lax.rem(i, cuts), lax.div(i, cuts))),
                pl.BlockSpec(piece, lambda i: (i, 0)),
            ],
            [shape((chans, hidden), f32), shape((hidden, chans), f32)],
            "split_gradients",
            nbytes=16 * chans * hidden,
        )(v, v)

    def behind(v, *after):
        return lax.optimization_barrier((v,) + after)[0] if after else v

    def exchange(v, *after):
        v = v.reshape(devices, pixels, lanes)
        v = behind(v, *after)
        v = lax.all_to_all(v, ("rows", "cols"), 0, 0, tiled=True)
        return v.reshape(ranks, groups, pixels, lanes)

    def first_norm(q):
        return call(
            first_kernel,
            steps,
            [token_spec(q, same), token_spec(q, same, 128), chan_row, chan_row],
            packed_spec(same),
            packed_shape,
            "first_norm",
            nbytes=2 * message,
        )(states_in, mask, row(first_gain), row(first_shift))

    plain, doubled = wide_tables(breadth)
    down, up = tall_tables(height, rows_here)
    as_table = lambda t: jnp.asarray(t, dtype=bf16)

    def fine_table(t):
        high = t.astype(jnp.bfloat16)
        return jnp.asarray(np.concatenate([high, (t - high.astype(np.float64)).astype(jnp.bfloat16)]))

    inner_full, outer_full = spread(filter_inner), spread(filter_outer)
    turn = lambda t: jnp.swapaxes(t, 1, 2)
    bin_steps = BINS // GROUP
    group_rows = GROUP * 2 * height
    held_shape = shape((short, 2, BINS, lanes), f32)
    at_once = 2
    held_row = pl.BlockSpec((at_once * rows, 2, BINS, lanes), lambda i: (i, 0, 0, 0))
    held_bins = pl.BlockSpec((short, 2, GROUP, lanes), lambda i: (0, 0, i, 0))
    field = pl.BlockSpec((at_once, groups, pixels, lanes), lambda i: (i, 0, 0, 0))
    kept = pl.BlockSpec((group_rows, width), lambda i: (i, 0))
    kept_shape = shape((bin_steps * group_rows, width), bf16)
    mix_spec = whole((2, width, width))
    bias_spec = whole((2, width))
    up_spec = whole((2 * height, 2 * height))

    def wide_in(v, table, fine):
        return call(
            functools.partial(wide_in_kernel, cols_here, fine),
            ranks // at_once,
            [field, whole(table.shape)],
            held_row,
            held_shape,
            "wide_in",
            nbytes=2 * message,
            scratch=[pltpu.VMEM((at_once * rows, breadth, lanes), f32)],
        )(v, table)

    def wide_out(v, table):
        return call(
            functools.partial(wide_out_kernel, cols_here, factor),
            ranks // at_once,
            [held_row, whole(table.shape)],
            field,
            packed_shape,
            "wide_out",
            nbytes=2 * message,
        )(v, table)

    forward_mix = (inner_full, bias_rows(inner_bias), outer_full, bias_rows(outer_bias))
    forward_specs = [mix_spec, bias_spec, mix_spec, bias_spec]

    def spectral_forward(held):
        table = fine_table(down)
        outs = call(
            functools.partial(spectral_forward_kernel, factor),
            bin_steps,
            [held_bins] * PARTS + [whole(table.shape), up_spec] + forward_specs,
            [held_bins] * PARTS + [kept],
            [held_shape] * PARTS + [kept_shape],
            "spectral_forward",
            flops=20 * 10**9,
            nbytes=8 * PARTS * message,
        )(*held, table, as_table(up), *forward_mix)
        return outs[:PARTS], outs[PARTS]

    def spectral_keep(entries):
        return call(
            functools.partial(spectral_keep_kernel, height),
            bin_steps,
            [kept] + forward_specs,
            [kept] * 3,
            [kept_shape] * 3,
            "spectral_keep",
            flops=10 * 10**9,
            nbytes=2 * PARTS * message,
        )(entries, *forward_mix)

    def spectral_backward(held, slope, damp):
        outs = call(
            functools.partial(spectral_backward_kernel, factor),
            bin_steps,
            [held_bins] * PARTS + [up_spec, up_spec, mix_spec, mix_spec] + [kept] * 2,
            [held_bins] * PARTS + [kept, bias_spec] * 2,
            [held_shape] * PARTS + [kept_shape, shape((2, width), f32)] * 2,
            "spectral_backward",
            flops=20 * 10**9,
            nbytes=8 * PARTS * message,
        )(*held, as_table(down), as_table(up), turn(inner_full), turn(outer_full), slope, damp)
        return outs[:PARTS], outs[PARTS:]

    def filter_grad(*operands):
        return call(
            functools.partial(filter_grad_kernel, height),
            bin_steps,
            [kept] * 4,
            [mix_spec] * 2,
            [shape((2, width, width), f32)] * 2,
            "filter_grad",
            flops=10 * 10**9,
            nbytes=2 * PARTS * message,
        )(*operands)

    slab = chans
    slabs = hidden // slab
    dense_steps = 2 * steps + slabs
    enter = lambda i: jnp.minimum(i, steps - 1)
    leave = lambda i: jnp.maximum(i - steps - slabs, 0)
    either = lambda i: jnp.where(i < steps + slabs, enter(i), leave(i))

    def dense(q, spatial, before):
        grads_before = () if q == 0 else before
        return call(
            functools.partial(dense_kernel, steps, slabs, q == 0),
            dense_steps,
            [token_spec(q, enter), token_spec(q, enter), packed_spec(enter)]
            + [token_spec(q, either, 128)]
            + [chan_row] * 4
            + [pl.BlockSpec((1, slab), lambda i: (0, jnp.clip(i - steps, 0, slabs - 1)))]
            + [chan_row]
            + [anywhere] * (2 + len(grads_before)),
            [
                token_spec(q, leave),
                packed_spec(leave),
                token_spec(0, leave),
                whole((8, chans)),
                whole((slabs, slab)),
                anywhere,
            ],
            [
                token_shape,
                packed_shape,
                shape((PAIR, pixels, frames, chans), f32),
                shape((8, chans), f32),
                shape((slabs, slab), f32),
                shape((2 * hidden, chans), f32),
            ],
            "dense_both_ways",
            flops=12 * tokens * chans * hidden,
            nbytes=4 * message,
            scratch=[
                pltpu.VMEM((slabs, chans, slab), bf16),
                pltpu.VMEM((hidden, chans), bf16),
                pltpu.VMEM((slabs, chans, slab), f32),
                pltpu.VMEM((hidden, chans), f32),
                pltpu.VMEM((tokens, chans), f32),
                pltpu.VMEM((tokens, chans), bf16),
                pltpu.VMEM((tokens, chans), bf16),
                pltpu.VMEM((tokens, chans), f32),
                pltpu.VMEM((tokens, chans), f32),
                pltpu.VMEM((tokens, slab), bf16),
                pltpu.VMEM((tokens, slab), bf16),
                pltpu.SemaphoreType.DMA((2 * slabs + 2,)),
            ],
            input_output_aliases={} if q == 0 else {13: 0},
        )(
            states_in,
            cot_in,
            spatial,
            mask,
            row(first_gain),
            row(first_shift),
            row(later_gain),
            row(later_shift),
            row(expand_bias),
            row(reduce_bias),
            expand_weight,
            reduce_weight,
            *grads_before,
        )

    def last_norm(q, later_grad, spatial, before):
        given = () if q == 0 else (before,)
        return call(
            last_kernel,
            steps,
            [token_spec(q, same), token_spec(0, same), packed_spec(same), token_spec(q, same, 128)]
            + [chan_row]
            + [anywhere] * len(given),
            [token_spec(q, same), whole((8, chans))],
            [token_shape, shape((8, chans), f32)],
            "first_norm_backward",
            nbytes=4 * message,
            input_output_aliases={} if q == 0 else {5: 0},
        )(states_in, later_grad, spatial, mask, row(first_gain), *given)

    every = range(PARTS)
    got = []
    for q in every:
        got.append(exchange(first_norm(q), *got[-1:]))
    held = [wide_in(v, fine_table(plain), True) for v in got]
    given, entries = spectral_forward(held)

    made = [wide_out(v, as_table(doubled.T)) for v in given]
    spatial, backs, later_grads, sums, expand_bias_grad, before = [], [], [], 0.0, 0.0, ()
    active, slope, damp = spectral_keep(entries)
    for q in range(PARTS + 1):
        if q < PARTS:
            beside = (active, *made[1:2]) if q == 1 else ()
            spatial.append(exchange(made[q], *spatial[-1:], *backs[-1:], *beside))
        if q > 0:
            result, back, kept_grad, part, bias_part, grads = dense(q - 1, spatial[q - 1], before)
            before = (grads, result)
            backs.append(back)
            later_grads.append(kept_grad)
            sums, expand_bias_grad = sums + part, expand_bias_grad + bias_part
    got, held = spatial[-1:], []
    for q in every:
        got.append(exchange(backs[q], got[-1], backs[min(q + 1, PARTS - 1)], *held[-1:]))
        if q == 0:
            grads = scatter(behind(grads, got[-1]), "cols")
        else:
            held.append(wide_in(got[q], as_table(doubled), False))
    held.append(wide_in(behind(got[-1], held[-1]), as_table(doubled), False))
    grads = scatter(behind(grads, held[-1]), "rows")

    given, (inner_low, inner_bias_grad, outer_low, outer_bias_grad) = spectral_backward(
        held, slope, damp
    )
    inner_grad, outer_grad = filter_grad(entries, inner_low, active, outer_low)
    filter_parts = (
        gather_blocks(inner_grad), inner_bias_grad, gather_blocks(outer_grad), outer_bias_grad
    )
    flat = sum_rows(jnp.concatenate([v.reshape(-1) for v in filter_parts]))
    made = [wide_out(v, as_table(plain.T)) for v in given]
    got, first_sums, states_grad = [], [], None
    for q in range(PARTS + 1):
        if q < PARTS:
            beside = (flat,) if q == PARTS - 1 else ()
            got.append(exchange(made[q], *got[-1:], *first_sums[-1:], *beside))
        if q == 0:
            grads = gather(behind(grads, got[0], flat, *made[1:2]), ("cols", "rows"))
            expand_sum, reduce_sum = split_grads(grads)
        else:
            if q == PARTS:
                states_grad = behind(states_grad, expand_sum)
            states_grad, part = last_norm(q - 1, later_grads[q - 1], got[q - 1], states_grad)
            first_sums.append(part)
    small = sum_small(
        jnp.concatenate([sum(first_sums)[:2], sums[:3], expand_bias_grad.reshape(-1, chans)])
    )
    sizes = [v.size for v in filter_parts]
    ends = np.cumsum(sizes)
    filter_sums = [
        flat[e - n : e].reshape(v.shape) for e, n, v in zip(ends, sizes, filter_parts)
    ]
    inner_sum, inner_bias_sum, outer_sum, outer_bias_sum = filter_sums
    return (
        restore(result),
        restore(states_grad),
        small[0],
        small[1],
        inner_sum,
        inner_bias_sum.reshape(2, -1, BS),
        outer_sum,
        outer_bias_sum.reshape(2, -1, BS),
        small[3],
        small[4],
        expand_sum,
        small[5:].reshape(-1),
        reduce_sum,
        small[2],
    )


def solution(mesh):
    tile = P(None, "rows", "cols", None)
    mix = P(None, "cols", None, None)
    bias = P(None, "cols", None)
    in_specs = (
        tile, P(), P(), P(), P(), mix, bias, mix, bias, P(), P(), P(), P(), P(), P(), tile,
    )
    out_specs = (
        tile, tile, P(), P(), mix, bias, mix, bias, P(), P(), P(), P(), P(), P(),
    )
    return jax.shard_map(body, mesh=mesh, in_specs=in_specs, out_specs=out_specs, check_vma=False)
```

```python
import functools
import math

import jax
import jax.numpy as jnp
import numpy as np
from jax import lax
from jax.experimental import pallas as pl
from jax.experimental.pallas import tpu as pltpu
from jax.sharding import PartitionSpec as P

BS = 96
BINS = 96
PAIR = 2
GROUP = 8
PARTS = 3
norm_eps = 1e-06
shrink_width = 0.01
VMEM = 60 * 1024 * 1024
f32 = jnp.float32
bf16 = jnp.bfloat16


def phi_parts(v):
    cdf = 0.5 * (1.0 + lax.erf(v * math.sqrt(0.5)))
    slope = cdf + v * (jnp.exp(v * v * -0.5) * (1.0 / math.sqrt(2.0 * math.pi)))
    return cdf, slope


def dot(a, b):
    return lax.dot_general(a, b, (((1,), (0,)), ((), ())), preferred_element_type=f32)


def dot_tn(a, b):
    return lax.dot_general(a, b, (((0,), (0,)), ((), ())), preferred_element_type=f32)


def dot_nt(a, b):
    return lax.dot_general(a, b, (((1,), (1,)), ((), ())), preferred_element_type=f32)


def standardize(v):
    centre = jnp.mean(v, axis=-1, keepdims=True)
    centred = v - centre
    spread = jnp.mean(centred * centred, axis=-1, keepdims=True)
    scale = lax.rsqrt(spread + norm_eps)
    return centred * scale, scale


def standardize_back(grad, normal, scale):
    first = jnp.mean(grad, axis=-1, keepdims=True)
    second = jnp.mean(grad * normal, axis=-1, keepdims=True)
    return scale * (grad - first - normal * second)


def pack(sides, outs, width, step):
    turned = [jnp.swapaxes(s, 0, 1) for s in sides]
    cut = width // len(outs)

    def lanes_of(c, g):
        start = c * width + g * cut
        return jnp.concatenate([t[:, :, start : start + cut] for t in turned], axis=2)

    for g, out in enumerate(outs):
        values = [lanes_of(c, g) for c in range(out.shape[1])]
        if len(outs) == 1:
            for c, v in enumerate(values):
                out[:, c] = v
            continue

        @pl.when(lax.rem(step, 2) == 0)
        def _():
            for c, v in enumerate(values):
                out[:, c] = jnp.concatenate([v, v], axis=2)

        @pl.when(lax.rem(step, 2) == 1)
        def _():
            for c, v in enumerate(values):
                out[:, c] = jnp.concatenate([out[:, c, :, : PAIR * cut], v], axis=2)


def unpack(refs, half, width, step):
    cut = width // len(refs)
    parts = []
    for c in range(refs[0].shape[1]):
        for ref in refs:
            part = ref[:, c, :, half * cut : (half + 1) * cut]
            if len(refs) > 1:
                later = (PAIR + half) * cut
                part = jnp.where(lax.rem(step, 2) == 1, ref[:, c, :, later : later + cut], part)
            parts.append(part)
    return jnp.swapaxes(jnp.concatenate(parts, axis=2) if len(parts) > 1 else parts[0], 0, 1)


def first_kernel(width, states, mask, gain, shift, *outs):
    sides = []
    for half in range(PAIR):
        inside = mask[half][..., :1]
        normal, _ = standardize(states[half].astype(f32) * inside)
        sides.append(inside * (normal * gain[...] + shift[...]))
    pack(sides, outs, width, pl.program_id(0))


def table_dot(table, x):
    rows = table.shape[0] // 2
    high = x.astype(bf16)
    both = dot(table[...], high)
    rest = dot(table[:rows, :], (x - high.astype(f32)).astype(bf16))
    return both[:rows] + both[rows:] + rest


def wide_in_kernel(cols_here, fine, block, table, held, wide):
    groups, rows = block.shape[1], block.shape[2] // cols_here
    for n in range(block.shape[0] * rows):
        r, j = divmod(n, rows)
        for c in range(groups):
            wide[n, c * cols_here : (c + 1) * cols_here, :] = block[
                r, c, j * cols_here : (j + 1) * cols_here, :
            ]
        x = wide[n]
        y = table_dot(table, x) if fine else dot(table[...], x.astype(bf16))
        held[n, 0] = y[:BINS]
        held[n, 1] = y[BINS:]


def wide_out_kernel(cols_here, factor, *refs):
    held, (table, block) = refs[:-2], refs[-2:]
    groups, rows = block.shape[1], block.shape[2] // cols_here
    cut = held[0].shape[3] // PAIR
    for n in range(block.shape[0] * rows):
        r, j = divmod(n, rows)
        x = [jnp.concatenate([part[n, 0], part[n, 1]], axis=0) for part in held]
        if len(x) > 1:
            x = [part[:, h * cut : (h + 1) * cut] for h in range(PAIR) for part in x]
            x = jnp.concatenate(x, axis=1)
        else:
            x = x[0]
        plane = dot(table[...], x.astype(bf16)) * factor
        for c in range(groups):
            block[r, c, j * cols_here : (j + 1) * cols_here, :] = plane[
                c * cols_here : (c + 1) * cols_here, :
            ]


def wide_in_split_kernel(cols_here, fine, block, table, held, wide, natural):
    groups, half = block.shape[1], block.shape[3] // 2
    rows = natural.shape[2] // cols_here
    for r in range(block.shape[0]):
        for c in range(groups):
            for s in range(natural.shape[2] // 8):
                natural[r, c, s * 8 : s * 8 + 8, :] = block[
                    r, c, (s // 2) * 8 : (s // 2) * 8 + 8, (s % 2) * half : (s % 2 + 1) * half
                ]
        for j in range(rows):
            n = r * rows + j
            for c in range(groups):
                wide[n, c * cols_here : (c + 1) * cols_here, :] = natural[
                    r, c, j * cols_here : (j + 1) * cols_here, :
                ]
            x = wide[n]
            y = table_dot(table, x) if fine else dot(table[...], x.astype(bf16))
            held[n, 0] = y[:BINS]
            held[n, 1] = y[BINS:]


def wide_out_split_kernel(cols_here, factor, held, table, block, natural):
    groups = block.shape[1]
    rows = natural.shape[2] // cols_here
    last = natural.shape[2] // 8 - 1
    for r in range(block.shape[0]):
        for j in range(rows):
            n = r * rows + j
            x = jnp.concatenate([held[n, 0], held[n, 1]], axis=0).astype(bf16)
            plane = dot(table[...], x) * factor
            for c in range(groups):
                natural[r, c, j * cols_here : (j + 1) * cols_here, :] = plane[
                    c * cols_here : (c + 1) * cols_here, :
                ]
        for c in range(groups):
            for m in range(block.shape[2] // 8):
                sides = [natural[r, c, at * 8 : at * 8 + 8, :] for at in (2 * m, min(2 * m + 1, last))]
                block[r, c, m * 8 : m * 8 + 8, :] = jnp.concatenate(sides, axis=1)


def bins_in(held, table, width, group, fine):
    kind = f32 if fine else bf16

    def lane(part, h):
        whole_width = part.shape[-1] // PAIR
        return h * whole_width + (group * width if whole_width > width else 0)

    turned = [
        [jnp.swapaxes(part[:, side], 0, 1).astype(kind) for part in held] for side in range(2)
    ]
    outs = []
    for k in range(GROUP):
        x = jnp.concatenate(
            [
                part[k][:, lane(part, h) : lane(part, h) + width]
                for side in turned
                for h in range(PAIR)
                for part in side
            ],
            axis=0,
        )
        outs.append(table_dot(table, x) if fine else dot(table[...], x))
    return outs


def bins_out(held, table, width, values):
    short = held[0].shape[0]
    count = len(held)
    products = [dot(table[...], value) for value in values]
    for side in range(2):
        for q in range(count):
            rows = []
            for z in products:
                at = [((side * PAIR + h) * count + q) * short for h in range(PAIR)]
                rows.append(jnp.concatenate([z[a : a + short] for a in at], axis=1))
            held[q][:, side] = jnp.swapaxes(jnp.stack(rows, axis=0), 0, 1)


def halves(v, count, tall):
    return [
        (v[k * 2 * tall : k * 2 * tall + tall], v[k * 2 * tall + tall : (k + 1) * 2 * tall])
        for k in range(count)
    ]


def complex_product(x, first, second, count, tall, conj):
    a = dot(x, first)
    b = dot(x, second)
    parts = []
    for (a_re, a_im), (b_re, b_im) in zip(halves(a, count, tall), halves(b, count, tall)):
        if conj:
            parts += [a_re + b_im, a_im - b_re]
        else:
            parts += [a_re - b_im, a_im + b_re]
    return parts


def activate(low, mix, bias, tall):
    parts = complex_product(low, mix[0], mix[1], low.shape[0] // (2 * tall), tall, False)
    return [part + bias[n % 2 : n % 2 + 1, :] for n, part in enumerate(parts)]


def gelu_low(v):
    return (v * (0.5 * (1.0 + lax.erf(v * math.sqrt(0.5))))).astype(bf16)


def spectral_forward_kernel(factor, group, *refs):
    held, refs = refs[:PARTS], refs[PARTS:]
    table_down, table_up, inner, inner_bias, outer, outer_bias = refs[:6]
    given, entries = refs[6 : 6 + PARTS], refs[6 + PARTS]
    width = inner.shape[2]
    tall = table_up.shape[0] // 2
    spec = bins_in(held, table_down, width, group, True)
    low = jnp.concatenate([(s * factor).astype(bf16) for s in spec], axis=0)
    entries[...] = low
    act = jnp.concatenate([gelu_low(v) for v in activate(low, inner, inner_bias, tall)], axis=0)
    shrunk = [
        (v - shrink_width * jnp.tanh(v * (1.0 / shrink_width))).astype(bf16)
        for v in activate(act, outer, outer_bias, tall)
    ]
    values = [jnp.concatenate(shrunk[2 * k : 2 * k + 2], axis=0) for k in range(GROUP)]
    bins_out(given, table_up, width, values)


def spectral_keep_kernel(tall, entries, inner, inner_bias, outer, outer_bias, active, slope, damp):
    acts = []
    for n, v in enumerate(activate(entries[...], inner, inner_bias, tall)):
        cdf, der = phi_parts(v)
        acts.append((v * cdf).astype(bf16))
        slope[n * tall : (n + 1) * tall, :] = der.astype(bf16)
    act = jnp.concatenate(acts, axis=0)
    active[...] = act
    for n, v in enumerate(activate(act, outer, outer_bias, tall)):
        t = jnp.tanh(v * (1.0 / shrink_width))
        damp[n * tall : (n + 1) * tall, :] = (t * t).astype(bf16)


def spectral_backward_kernel(factor, group, *refs):
    held, refs = refs[:PARTS], refs[PARTS:]
    table_down, table_up, inner_t, outer_t, slope, damp = refs[:6]
    given, refs = refs[6 : 6 + PARTS], refs[6 + PARTS :]
    inner_low, inner_bias_grad, outer_low, outer_bias_grad = refs
    width = inner_t.shape[2]
    tall = table_up.shape[0] // 2

    @pl.when(pl.program_id(0) == 0)
    def _():
        for ref in (inner_bias_grad, outer_bias_grad):
            ref[...] = jnp.zeros_like(ref)

    spec = bins_in(held, table_down, width, group, False)
    grads = []
    sums = [0.0, 0.0]
    for k in range(GROUP):
        for side in range(2):
            at = (2 * k + side) * tall
            g = spec[k][side * tall : (side + 1) * tall] * factor
            g = g * damp[at : at + tall, :].astype(f32)
            sums[side] = sums[side] + jnp.sum(g, axis=0, keepdims=True)
            grads.append(g.astype(bf16))
    outer_bias_grad[...] += jnp.concatenate(sums, axis=0)
    low = jnp.concatenate(grads, axis=0)
    outer_low[...] = low
    parts = complex_product(low, outer_t[0], outer_t[1], GROUP, tall, True)
    grads = []
    sums = [0.0, 0.0]
    for n, part in enumerate(parts):
        g = part * slope[n * tall : (n + 1) * tall, :].astype(f32)
        sums[n % 2] = sums[n % 2] + jnp.sum(g, axis=0, keepdims=True)
        grads.append(g.astype(bf16))
    inner_bias_grad[...] += jnp.concatenate(sums, axis=0)
    low = jnp.concatenate(grads, axis=0)
    inner_low[...] = low
    parts = complex_product(low, inner_t[0], inner_t[1], GROUP, tall, True)
    values = [
        jnp.concatenate([parts[2 * k], parts[2 * k + 1]], axis=0).astype(bf16)
        for k in range(GROUP)
    ]
    bins_out(given, table_up, width, values)


def filter_grad_kernel(tall, entries, inner_low, active, outer_low, inner_grad, outer_grad):
    @pl.when(pl.program_id(0) == 0)
    def _():
        inner_grad[...] = jnp.zeros_like(inner_grad)
        outer_grad[...] = jnp.zeros_like(outer_grad)

    for before, low, grad in ((entries, inner_low, inner_grad), (active, outer_low, outer_grad)):
        turned = []
        for k in range(GROUP):
            top, bottom = low[2 * k * tall : (2 * k + 1) * tall], low[(2 * k + 1) * tall : (2 * k + 2) * tall]
            turned += [bottom, -top]
        grad[0] += dot_tn(before[...], low[...])
        grad[1] += dot_tn(before[...], jnp.concatenate(turned, axis=0))


def dense_kernel(steps, slabs, width, first_part, arrays, *refs):
    spat, refs = refs[:arrays], refs[arrays:]
    (
        states, cot, mask, first_gain, first_shift, later_gain, later_shift,
        expand_bias, reduce_bias, expand_hbm, reduce_hbm,
    ) = refs[:11]
    refs = refs[11:]
    if not first_part:
        grads_before = refs[0]
        refs = refs[2:]
    back, refs = refs[:arrays], refs[arrays:]
    result, later_grad, sums, expand_bias_grad, grads_hbm = refs[:5]
    (
        expand, reduce, expand_grad, reduce_grad, mixed, normed, low_out, branch, grad_n,
        hidden_all, grad_all, copy_sem,
    ) = refs[5:]
    step = pl.program_id(0)
    chans = states.shape[3]
    side_tokens = states.shape[1] * states.shape[2]
    slab = expand.shape[2]
    tokens = mixed.shape[0]
    square = states.shape[1:]

    def parts_of(grads):
        pairs = [(grads.at[pl.ds(s * chans, chans)], expand_grad.at[s]) for s in range(slabs)]
        return pairs + [(grads.at[pl.ds(slabs * chans, slabs * slab)], reduce_grad)]

    def fetches():
        copies = [
            pltpu.make_async_copy(
                expand_hbm.at[:, pl.ds(s * slab, slab)], expand.at[s], copy_sem.at[s]
            )
            for s in range(slabs)
        ]
        copies.append(pltpu.make_async_copy(reduce_hbm, reduce, copy_sem.at[slabs]))
        if not first_part:
            copies += [
                pltpu.make_async_copy(far, near, copy_sem.at[slabs + 1 + n])
                for n, (far, near) in enumerate(parts_of(grads_before))
            ]
        return copies

    @pl.when(step == 0)
    def _():
        for c in fetches():
            c.start()
        if first_part:
            expand_grad[...] = jnp.zeros_like(expand_grad)
            reduce_grad[...] = jnp.zeros_like(reduce_grad)
        sums[...] = jnp.zeros_like(sums)
        expand_bias_grad[...] = jnp.zeros_like(expand_bias_grad)

    @pl.when(step < steps)
    def _():
        start = pl.multiple_of(step * (PAIR * side_tokens), PAIR * side_tokens)
        for half in range(PAIR):
            at = pl.ds(start + half * side_tokens, side_tokens)
            inside = mask[half][..., :1]
            lower = inside * states[half].astype(f32)
            first, _ = standardize(lower)
            filter_in = first * first_gain[...] + first_shift[...]
            full = lower + inside * (unpack(spat, half, width, step) + filter_in)
            later, _ = standardize(full)
            full = full.reshape(side_tokens, chans)
            mixed[at, :] = full
            branch[at, :] = full + reduce_bias[...]
            normal = (later * later_gain[...] + later_shift[...]).reshape(side_tokens, chans)
            normed[at, :] = normal.astype(bf16)
            go = (inside * cot[half].astype(f32)).reshape(side_tokens, chans)
            low_out[at, :] = go.astype(bf16)
            grad_n[at, :] = jnp.zeros_like(full)
            sums[0:1, :] += jnp.sum(go, axis=0, keepdims=True)

    @pl.when(step == steps)
    def _():
        for c in fetches():
            c.wait()

    @pl.when((step >= steps) & (step < steps + slabs))
    def _():
        hc = step - steps
        at = pl.ds(pl.multiple_of(hc * slab, slab), slab)
        piece = tokens // 4 if tokens % 64 == 0 else tokens

        def some(n, carry):
            here = pl.ds(pl.multiple_of(n * piece, piece), piece)
            weight_up = expand[hc]
            weight_down = reduce[at, :]
            go = low_out[here, :]
            pre = dot(normed[here, :], weight_up) + expand_bias[...]
            cdf, der = phi_parts(pre)
            hidden = (pre * cdf).astype(bf16)
            hidden_all[here, :] = hidden
            branch[here, :] += dot(hidden, weight_down)
            grad_pre = dot_nt(go, weight_down) * der
            expand_bias_grad[pl.ds(hc, 1), :] += jnp.sum(grad_pre, axis=0, keepdims=True)
            grad_low = grad_pre.astype(bf16)
            grad_all[here, :] = grad_low
            grad_n[here, :] += dot_nt(grad_low, weight_up)
            return carry

        lax.fori_loop(0, tokens // piece, some, 0)
        reduce_grad[at, :] += dot_tn(hidden_all[...], low_out[...])
        expand_grad[hc] += dot_tn(normed[...], grad_all[...])

    @pl.when(step >= steps + slabs)
    def _():
        start = pl.multiple_of(
            (step - steps - slabs) * (PAIR * side_tokens), PAIR * side_tokens
        )
        sides = []
        for half in range(PAIR):
            at = pl.ds(start + half * side_tokens, side_tokens)
            inside = mask[half][..., :1]
            later, scale = standardize(mixed[at, :])
            g = grad_n[at, :]
            sums[1:2, :] += jnp.sum(g * later, axis=0, keepdims=True)
            sums[2:3, :] += jnp.sum(g, axis=0, keepdims=True)
            g = low_out[at, :].astype(f32) + standardize_back(g * later_gain[...], later, scale)
            sides.append(inside * g.reshape(square))
            later_grad[half] = sides[-1]
            result[half] = (inside * branch[at, :].reshape(square)).astype(bf16)
        pack(sides, back, width, step - steps - slabs)

    @pl.when(step == pl.num_programs(0) - 1)
    def _():
        copies = [
            pltpu.make_async_copy(near, far, copy_sem.at[n])
            for n, (far, near) in enumerate(parts_of(grads_hbm))
        ]
        for c in copies:
            c.start()
        for c in copies:
            c.wait()


def last_kernel(width, arrays, *refs):
    spat, (states, later_grad, mask, gain) = refs[:arrays], refs[arrays : arrays + 4]
    out, sums = refs[-2:]
    chans = states.shape[3]

    @pl.when(pl.program_id(0) == 0)
    def _():
        sums[...] = jnp.zeros_like(sums)

    for half in range(PAIR):
        inside = mask[half][..., :1]
        normal, scale = standardize(inside * states[half].astype(f32))
        grad_mixed = later_grad[half]
        grad = inside * (grad_mixed + unpack(spat, half, width, pl.program_id(0)))
        flat = (-1, chans)
        sums[0:1, :] += jnp.sum((grad * normal).reshape(flat), axis=0, keepdims=True)
        sums[1:2, :] += jnp.sum(grad.reshape(flat), axis=0, keepdims=True)
        grad = grad_mixed + standardize_back(grad * gain[...], normal, scale)
        out[half] = (inside * grad).astype(bf16)


def sum_kernel(ranks, groups, own, out, got, send_sem, recv_sem):
    devices = ranks * groups
    me = lax.axis_index("rows") * groups + lax.axis_index("cols")

    def place(i):
        other = lax.rem(me + i, devices)
        return lax.div(other, groups), lax.rem(other, groups)

    def copy(i):
        return pltpu.make_async_remote_copy(
            src_ref=own,
            dst_ref=got.at[i],
            send_sem=send_sem.at[i],
            recv_sem=recv_sem.at[i],
            device_id=place(i),
            device_id_type=pl.DeviceIdType.MESH,
        )

    barrier = pltpu.get_barrier_semaphore()

    def greet(i, carry):
        pl.semaphore_signal(
            barrier, inc=1, device_id=place(i), device_id_type=pl.DeviceIdType.MESH
        )
        return carry

    def start(i, carry):
        copy(i).start()
        return carry

    def finish(i, carry):
        copy(i).wait()
        return carry

    lax.fori_loop(1, devices, greet, 0)
    pl.semaphore_wait(barrier, devices - 1)
    lax.fori_loop(1, devices, start, 0)
    lax.fori_loop(1, devices, finish, 0)
    out[...] = lax.fori_loop(1, devices, lambda i, total: total + got[i], own[...])


def rows_sum_kernel(ranks, own, out, got, done, pick_send, pick_recv, give_send, give_recv):
    me = lax.axis_index("rows")
    piece = own.shape[0] // ranks

    def at(ref, r):
        return ref.at[pl.ds(pl.multiple_of(r * piece, piece), piece)]

    def copy(src, dst, i, send, recv):
        return pltpu.make_async_remote_copy(
            src_ref=src,
            dst_ref=dst,
            send_sem=send.at[i],
            recv_sem=recv.at[i],
            device_id={"rows": lax.rem(me + i, ranks)},
            device_id_type=pl.DeviceIdType.MESH,
        )

    barrier = pltpu.get_barrier_semaphore()
    for i in range(1, ranks):
        pl.semaphore_signal(
            barrier,
            inc=1,
            device_id={"rows": lax.rem(me + i, ranks)},
            device_id_type=pl.DeviceIdType.MESH,
        )
    pl.semaphore_wait(barrier, ranks - 1)
    picks = [
        copy(at(own, lax.rem(me + i, ranks)), got.at[i], i, pick_send, pick_recv)
        for i in range(1, ranks)
    ]
    for c in picks:
        c.start()
    for c in picks:
        c.wait()
    start = pl.ds(pl.multiple_of(me * piece, piece), piece)
    total = own[start, :]
    for i in range(1, ranks):
        total = total + got[i]
    done[0] = total
    gives = [copy(done.at[0], done.at[i], i, give_send, give_recv) for i in range(1, ranks)]
    for c in gives:
        c.start()
    for c in gives:
        c.wait()
    out[start, :] = total
    for i in range(1, ranks):
        source = lax.rem(me - i + ranks, ranks)
        out[pl.ds(pl.multiple_of(source * piece, piece), piece), :] = done[i]


def split_kernel(expand_in, reduce_in, expand_out, reduce_out):
    expand_out[...] = expand_in[...]
    reduce_out[...] = reduce_in[...]


def wide_tables(width):
    freq = np.arange(BINS)
    place = np.arange(width)
    angle = (freq[:, None] * place[None, :] % width) * (2.0 * math.pi / width)
    live = (2 * freq <= width).astype(np.float64)[:, None]
    edge = (freq == 0) | (2 * freq == width)
    weight = np.where(edge, 1.0, 2.0)[:, None] * live
    cosine, sine = np.cos(angle), np.sin(angle)
    plain = np.concatenate([live * cosine, -live * sine], axis=0)
    doubled = np.concatenate([weight * cosine, -weight * sine], axis=0)
    return plain, doubled


def tall_tables(height, rows_here):
    pairs = rows_here // PAIR
    rows = pairs // PARTS
    order = np.array(
        [
            r * rows_here + h * pairs + q * rows + j
            for h in range(PAIR)
            for q in range(PARTS)
            for r in range(height // rows_here)
            for j in range(rows)
        ]
    )
    freq = np.arange(height)
    angle = (freq[:, None] * order[None, :] % height) * (2.0 * math.pi / height)
    cosine, sine = np.cos(angle), np.sin(angle)
    down = np.block([[cosine, sine], [-sine, cosine]])
    up = np.block([[cosine.T, -sine.T], [sine.T, cosine.T]])
    return down, up


def spread(weight):
    count = weight.shape[1]
    eye = jnp.eye(count, dtype=weight.dtype)
    full = jnp.einsum("rbio,bd->rbido", weight, eye)
    return full.reshape(2, count * BS, count * BS)


def gather_blocks(full):
    count = full.shape[1] // BS
    return jnp.stack(
        [full[:, b * BS : (b + 1) * BS, b * BS : (b + 1) * BS] for b in range(count)], axis=1
    )


def bias_rows(bias):
    return bias.reshape(2, -1)


def whole(shape):
    return pl.BlockSpec(shape, lambda *_: (0,) * len(shape))


def call(kernel, grid, in_specs, out_specs, out_shape, name, flops=0, nbytes=0, scratch=(), **kw):
    return pl.pallas_call(
        kernel,
        grid=(grid,),
        in_specs=in_specs,
        out_specs=out_specs,
        out_shape=out_shape,
        scratch_shapes=scratch,
        compiler_params=pltpu.CompilerParams(
            dimension_semantics=("arbitrary",), vmem_limit_bytes=VMEM
        ),
        cost_estimate=pl.CostEstimate(flops=flops, bytes_accessed=nbytes, transcendentals=0),
        name=name,
        **kw,
    )


def body(
    states,
    heights,
    widths,
    first_gain,
    first_shift,
    filter_inner,
    inner_bias,
    filter_outer,
    outer_bias,
    later_gain,
    later_shift,
    expand_weight,
    expand_bias,
    reduce_weight,
    reduce_bias,
    cotangent,
):
    frames, rows_here, cols_here, chans = states.shape
    ranks, groups = lax.axis_size("rows"), lax.axis_size("cols")
    assert frames == ranks and rows_here % (PAIR * PARTS) == 0
    height, breadth = rows_here * ranks, cols_here * groups
    devices = ranks * groups
    pairs = rows_here // PAIR
    rows = pairs // PARTS
    pixels = rows * cols_here
    width = chans // groups
    lanes = width * PAIR
    hidden = expand_weight.shape[1]
    factor = 1.0 / math.sqrt(height * breadth)
    short = ranks * rows
    step_pixels = 8 if pixels % 8 == 0 else pixels
    steps = pixels // step_pixels
    tokens = PAIR * pixels * frames
    message = devices * pixels * lanes * 4
    row = lambda v: v.reshape(1, -1)
    shape = jax.ShapeDtypeStruct

    order = lambda v: jnp.transpose(v, (1, 2, 0, 3)).reshape(PAIR, pairs * cols_here, frames, chans)
    restore = lambda v: jnp.transpose(v.reshape(rows_here, cols_here, frames, chans), (2, 0, 1, 3))
    states_in, cot_in = order(states), order(cotangent)
    row_ids = lax.axis_index("rows") * rows_here + jnp.arange(rows_here, dtype=jnp.int32)
    col_ids = lax.axis_index("cols") * cols_here + jnp.arange(cols_here, dtype=jnp.int32)
    inside = (row_ids[:, None, None] < heights) & (col_ids[None, :, None] < widths)
    mask = jnp.broadcast_to(
        inside.astype(f32).reshape(PAIR, pairs * cols_here, frames, 1),
        (PAIR, pairs * cols_here, frames, 128),
    )

    buffers = {} if steps > 1 else {"pipeline_mode": pl.Buffered(1)}

    def token_spec(q, where, last=chans):
        return pl.BlockSpec(
            (PAIR, step_pixels, frames, last), lambda i: (0, q * steps + where(i), 0, 0), **buffers
        )

    def packed_spec(where):
        return pl.BlockSpec(
            (ranks, groups, step_pixels, lanes), lambda i: (0, 0, where(i), 0), **buffers
        )

    blocks_here = width // BS
    split = blocks_here > 1 and steps > 1 and (2 * PAIR * BS) % 128 == 0
    parties = blocks_here if split else 1
    cut = width // parties
    split_rows = 8 * (-(-steps // 2))

    def arrays_of(q):
        return parties if q == 0 else 1

    def message_specs(q, where):
        if arrays_of(q) == 1:
            return [packed_spec(where)]
        return [
            pl.BlockSpec(
                (ranks, groups, step_pixels, 2 * PAIR * cut), lambda i: (0, 0, where(i) // 2, 0)
            )
        ] * parties

    def message_shapes(q):
        if arrays_of(q) == 1:
            return [packed_shape]
        return [shape((ranks, groups, split_rows, 2 * PAIR * cut), f32)] * parties

    same = lambda i: i
    token_shape = shape((PAIR, pairs * cols_here, frames, chans), bf16)
    packed_shape = shape((ranks, groups, pixels, lanes), f32)
    chan_row = whole((1, chans))
    anywhere = pl.BlockSpec(memory_space=pl.ANY)

    def scatter(v, axis):
        return lax.psum_scatter(v, axis, scatter_dimension=0, tiled=True)

    def gather(v, axis):
        return lax.all_gather(v, axis, axis=0, tiled=True)

    def sum_small(v):
        flat = v.reshape(-1, 128)
        flat = jnp.pad(flat, ((0, -flat.shape[0] % 8), (0, 0)))
        vmem = pl.BlockSpec(memory_space=pltpu.VMEM)
        return pl.pallas_call(
            functools.partial(sum_kernel, ranks, groups),
            in_specs=[vmem],
            out_specs=vmem,
            out_shape=shape(flat.shape, f32),
            scratch_shapes=[
                pltpu.VMEM((devices,) + flat.shape, f32),
                pltpu.SemaphoreType.DMA((devices,)),
                pltpu.SemaphoreType.DMA((devices,)),
            ],
            compiler_params=pltpu.CompilerParams(collective_id=0, has_side_effects=True),
            name="small_sums",
        )(flat).reshape(-1)[: v.size].reshape(v.shape)

    def sum_rows(v):
        flat = v.reshape(-1)
        flat = jnp.pad(flat, (0, -flat.shape[0] % (ranks * 1024))).reshape(-1, 128)
        slots = (ranks, flat.shape[0] // ranks, 128)
        vmem = pl.BlockSpec(memory_space=pltpu.VMEM)
        return pl.pallas_call(
            functools.partial(rows_sum_kernel, ranks),
            in_specs=[vmem],
            out_specs=vmem,
            out_shape=shape(flat.shape, f32),
            scratch_shapes=[pltpu.VMEM(slots, f32)] * 2 + [pltpu.SemaphoreType.DMA((ranks,))] * 4,
            compiler_params=pltpu.CompilerParams(collective_id=1, has_side_effects=True),
            name="filter_sums",
        )(flat).reshape(-1)[: v.size]

    def split_grads(v):
        cuts = 4
        piece = (chans // cuts, chans)
        return call(
            split_kernel,
            slabs * cuts,
            [
                pl.BlockSpec(piece, lambda i: (i, 0)),
                pl.BlockSpec(piece, lambda i: (slabs * cuts + i, 0)),
            ],
            [
                pl.BlockSpec(piece, lambda i: (lax.rem(i, cuts), lax.div(i, cuts))),
                pl.BlockSpec(piece, lambda i: (i, 0)),
            ],
            [shape((chans, hidden), f32), shape((hidden, chans), f32)],
            "split_gradients",
            nbytes=16 * chans * hidden,
        )(v, v)

    def behind(v, *after):
        return lax.optimization_barrier((v,) + after)[0] if after else v

    def exchange(v):
        sent = v.reshape((devices,) + v.shape[2:])
        return lax.all_to_all(sent, ("rows", "cols"), 0, 0, tiled=True).reshape(v.shape)

    def tie(*values):
        return lax.optimization_barrier(values)

    def first_norm(q):
        return call(
            functools.partial(first_kernel, width),
            steps,
            [token_spec(q, same), token_spec(q, same, 128), chan_row, chan_row],
            message_specs(q, same),
            message_shapes(q),
            "first_norm",
            nbytes=2 * message,
        )(states_in, mask, row(first_gain), row(first_shift))

    plain, doubled = wide_tables(breadth)
    down, up = tall_tables(height, rows_here)
    as_table = lambda t: jnp.asarray(t, dtype=bf16)

    def fine_table(t):
        high = t.astype(jnp.bfloat16)
        return jnp.asarray(np.concatenate([high, (t - high.astype(np.float64)).astype(jnp.bfloat16)]))

    def mixes(weight):
        return [weight[:, g] for g in range(parties)] if split else [spread(weight)]

    inner_full, outer_full = mixes(filter_inner), mixes(filter_outer)
    turn = lambda t: jnp.swapaxes(t, 1, 2)
    bin_steps = BINS // GROUP
    group_rows = GROUP * 2 * height
    held_shape = shape((short, 2, BINS, lanes), f32)
    at_once = 2
    held_row = pl.BlockSpec((at_once * rows, 2, BINS, lanes), lambda i: (i, 0, 0, 0))
    held_bins = pl.BlockSpec((short, 2, GROUP, lanes), lambda i: (0, 0, i, 0))
    field = pl.BlockSpec((at_once, groups, pixels, lanes), lambda i: (i, 0, 0, 0))
    kept = pl.BlockSpec((group_rows, cut), lambda i: (i, 0))
    kept_shape = shape((bin_steps * group_rows, cut), bf16)
    mix_spec = whole((2, cut, cut))
    bias_spec = whole((2, cut))

    def held_of(last, by_row):
        if by_row:
            return pl.BlockSpec((at_once * rows, 2, BINS, last), lambda i: (i, 0, 0, 0))
        return pl.BlockSpec((short, 2, GROUP, last), lambda i: (0, 0, i, 0))

    cut_shape = shape((short, 2, BINS, PAIR * cut), f32)
    split_field = pl.BlockSpec(
        (at_once, groups, split_rows, 2 * PAIR * cut), lambda i: (i, 0, 0, 0)
    )
    natural = pltpu.VMEM((at_once, groups, pixels, PAIR * cut), f32)
    cut_in = [held_of(PAIR * cut if split else lanes, False)] + [held_bins] * (PARTS - 1)
    cut_out = [held_of(PAIR * cut, False)] * PARTS
    up_spec = whole((2 * height, 2 * height))

    def wide_in(v, table, fine):
        divided = v.shape != packed_shape.shape
        return call(
            functools.partial(wide_in_split_kernel if divided else wide_in_kernel, cols_here, fine),
            ranks // at_once,
            [split_field if divided else field, whole(table.shape)],
            held_of(PAIR * cut, True) if divided else held_row,
            cut_shape if divided else held_shape,
            "wide_in",
            nbytes=2 * message,
            scratch=[pltpu.VMEM((at_once * rows, breadth, PAIR * cut), f32), natural]
            if divided
            else [pltpu.VMEM((at_once * rows, breadth, lanes), f32)],
        )(v, table)

    def wide_out(parts, table):
        return call(
            functools.partial(wide_out_kernel, cols_here, factor),
            ranks // at_once,
            [held_of(PAIR * cut, True)] * len(parts) + [whole(table.shape)],
            field,
            packed_shape,
            "wide_out",
            nbytes=2 * message,
        )(*parts, table)

    def wide_out_split(part, table):
        return call(
            functools.partial(wide_out_split_kernel, cols_here, factor),
            ranks // at_once,
            [held_of(PAIR * cut, True), whole(table.shape)],
            split_field,
            message_shapes(0)[0],
            "wide_out",
            nbytes=2 * message,
            scratch=[natural],
        )(part, table)

    def first_message(given, table):
        return wide_out_split(given[0], table) if split else wide_out([given[0]], table)

    def messages_out(given, table, first):
        first = first + [first_message(v, table) for v in given[len(first) :]]
        return first + [wide_out([v[q] for v in given], table) for q in range(1, PARTS)]

    def of_group(v, g):
        return bias_rows(v)[:, g * cut : (g + 1) * cut]

    forward_mix = [
        (inner_full[g], of_group(inner_bias, g), outer_full[g], of_group(outer_bias, g))
        for g in range(parties)
    ]
    forward_specs = [mix_spec, bias_spec, mix_spec, bias_spec]

    def spectral_forward(g, held):
        table = fine_table(down)
        outs = call(
            functools.partial(spectral_forward_kernel, factor, g),
            bin_steps,
            cut_in + [whole(table.shape), up_spec] + forward_specs,
            cut_out + [kept],
            [cut_shape] * PARTS + [kept_shape],
            "spectral_forward",
            flops=20 * 10**9,
            nbytes=8 * PARTS * message // parties,
        )(*held, table, as_table(up), *forward_mix[g])
        return outs[:PARTS], outs[PARTS]

    def spectral_keep(g, entries):
        return call(
            functools.partial(spectral_keep_kernel, height),
            bin_steps,
            [kept] + forward_specs,
            [kept] * 3,
            [kept_shape] * 3,
            "spectral_keep",
            flops=10 * 10**9,
            nbytes=2 * PARTS * message // parties,
        )(entries, *forward_mix[g])

    def spectral_backward(g, held, slope, damp):
        outs = call(
            functools.partial(spectral_backward_kernel, factor, g),
            bin_steps,
            cut_in + [up_spec, up_spec, mix_spec, mix_spec] + [kept] * 2,
            cut_out + [kept, bias_spec] * 2,
            [cut_shape] * PARTS + [kept_shape, shape((2, cut), f32)] * 2,
            "spectral_backward",
            flops=20 * 10**9,
            nbytes=8 * PARTS * message // parties,
        )(*held, as_table(down), as_table(up), turn(inner_full[g]), turn(outer_full[g]), slope, damp)
        return outs[:PARTS], outs[PARTS:]

    def filter_grad(*operands):
        return call(
            functools.partial(filter_grad_kernel, height),
            bin_steps,
            [kept] * 4,
            [mix_spec] * 2,
            [shape((2, cut, cut), f32)] * 2,
            "filter_grad",
            flops=10 * 10**9,
            nbytes=2 * PARTS * message,
        )(*operands)

    slab = chans
    slabs = hidden // slab
    dense_steps = 2 * steps + slabs
    enter = lambda i: jnp.minimum(i, steps - 1)
    leave = lambda i: jnp.maximum(i - steps - slabs, 0)
    either = lambda i: jnp.where(i < steps + slabs, enter(i), leave(i))

    def dense(q, spatial, before):
        grads_before = () if q == 0 else before
        return call(
            functools.partial(dense_kernel, steps, slabs, width, q == 0, arrays_of(q)),
            dense_steps,
            message_specs(q, enter)
            + [token_spec(q, enter), token_spec(q, enter), token_spec(q, either, 128)]
            + [chan_row] * 4
            + [pl.BlockSpec((1, slab), lambda i: (0, jnp.clip(i - steps, 0, slabs - 1)))]
            + [chan_row]
            + [anywhere] * (2 + len(grads_before)),
            message_specs(q, leave)
            + [
                token_spec(q, leave),
                token_spec(0, leave),
                whole((8, chans)),
                whole((slabs, slab)),
                anywhere,
            ],
            message_shapes(q)
            + [
                token_shape,
                shape((PAIR, pixels, frames, chans), f32),
                shape((8, chans), f32),
                shape((slabs, slab), f32),
                shape((2 * hidden, chans), f32),
            ],
            "dense_both_ways",
            flops=12 * tokens * chans * hidden,
            nbytes=4 * message,
            scratch=[
                pltpu.VMEM((slabs, chans, slab), bf16),
                pltpu.VMEM((hidden, chans), bf16),
                pltpu.VMEM((slabs, chans, slab), f32),
                pltpu.VMEM((hidden, chans), f32),
                pltpu.VMEM((tokens, chans), f32),
                pltpu.VMEM((tokens, chans), bf16),
                pltpu.VMEM((tokens, chans), bf16),
                pltpu.VMEM((tokens, chans), f32),
                pltpu.VMEM((tokens, chans), f32),
                pltpu.VMEM((tokens, slab), bf16),
                pltpu.VMEM((tokens, slab), bf16),
                pltpu.SemaphoreType.DMA((2 * slabs + 2,)),
            ],
            input_output_aliases={} if q == 0 else {13: 1},
        )(
            *spatial,
            states_in,
            cot_in,
            mask,
            row(first_gain),
            row(first_shift),
            row(later_gain),
            row(later_shift),
            row(expand_bias),
            row(reduce_bias),
            expand_weight,
            reduce_weight,
            *grads_before,
        )

    def last_norm(q, later_grad, spatial, before):
        given = () if q == 0 else (before,)
        return call(
            functools.partial(last_kernel, width, arrays_of(q)),
            steps,
            message_specs(q, same)
            + [token_spec(q, same), token_spec(0, same), token_spec(q, same, 128)]
            + [chan_row]
            + [anywhere] * len(given),
            [token_spec(q, same), whole((8, chans))],
            [token_shape, shape((8, chans), f32)],
            "first_norm_backward",
            nbytes=4 * message,
            input_output_aliases={} if q == 0 else {5: 0},
        )(*spatial, states_in, later_grad, mask, row(first_gain), *given)

    every = range(PARTS)

    def send(made, got):
        if got:
            made, got[-1] = tie(made, got[-1])
        got.append(exchange(made))

    made = [v for q in (*every[1:], 0) for v in first_norm(q)]
    got, held = [], []
    for n, v in enumerate(made):
        if n > 1:
            v, held[-1] = tie(v, held[-1])
        send(v, got)
        if n > 0:
            held.append(wide_in(got[-2], fine_table(plain), True))
    held.append(wide_in(got[-1], fine_table(plain), True))
    rest, first = held[: PARTS - 1], held[PARTS - 1 :]
    done = [spectral_forward(g, [first[g]] + rest) for g in range(parties)]
    entries = [v[1] for v in done]
    made = messages_out([v[0] for v in done], as_table(doubled.T), [])
    keeps = [list(spectral_keep(g, entries[g])) for g in range(parties)]

    spatial = got[-1:]
    for n in range(parties):
        send(made[n], spatial)
    for keep in keeps:
        keep[0], made[parties] = tie(keep[0], made[parties])
    spatial = spatial[1:]
    backs, later_grads, sums, expand_bias_grad, before = [], [], 0.0, 0.0, ()
    for q in every:
        if q + 1 < PARTS:
            if backs:
                made[parties + q], backs[-1][-1] = tie(made[parties + q], backs[-1][-1])
            send(made[parties + q], spatial)
        received = spatial[:parties] if q == 0 else spatial[parties + q - 1 : parties + q]
        if q + 1 == PARTS:
            backs[-1][-1], spatial[-1] = tie(backs[-1][-1], spatial[-1])
            got = [exchange(backs[1][0])]
            received = spatial[-1:]
        outs = dense(q, received, before)
        backs.append(list(outs[: arrays_of(q)]))
        result, kept_grad, part, bias_part, grads = outs[arrays_of(q) :]
        before = (grads, result)
        later_grads.append(kept_grad)
        sums, expand_bias_grad = sums + part, expand_bias_grad + bias_part
    grads, got[0] = tie(grads, got[0])
    grads = scatter(grads, "cols")
    held = []
    for v in [w for q in (*every[2:], 0) for w in backs[q]]:
        held.append(wide_in(got[-1], as_table(doubled), False))
        if len(held) > 1:
            v, held[-2] = tie(v, held[-2])
        send(v, got)
    rest, first, done, ready = held[: PARTS - 1], held[PARTS - 1 :], [], []
    for g in range(parties):
        if g + 1 == parties:
            if done:
                ready = [first_message(done[0][0], as_table(plain.T))]
                ready[0], got[-1] = tie(ready[0], got[-1])
            first.append(wide_in(got[-1], as_table(doubled), False))
            grads, first[-1] = tie(grads, first[-1])
            grads = scatter(grads, "rows")
        given, extras = spectral_backward(g, [first[g]] + rest, keeps[g][1], keeps[g][2])
        done.append((list(given), extras))
    made = messages_out([v[0] for v in done], as_table(plain.T), ready)
    filter_grads = []
    for g in range(parties):
        inner_low, _, outer_low, _ = done[g][1]
        filter_grads.append(filter_grad(entries[g], inner_low, keeps[g][0], outer_low))

    def blocks(n):
        each = [v[n] for v in filter_grads]
        return jnp.stack(each, axis=1) if split else gather_blocks(each[0])

    filter_parts = (
        blocks(0),
        jnp.concatenate([v[1][1] for v in done], axis=1),
        blocks(1),
        jnp.concatenate([v[1][3] for v in done], axis=1),
    )
    flat = jnp.concatenate([v.reshape(-1) for v in filter_parts])

    got = got[-1:]
    for n in range(parties):
        if n > 0:
            made[n], made[parties] = tie(made[n], made[parties])
        send(made[n], got)
    grads = gather(tie(grads, got[-1])[0], ("cols", "rows"))
    expand_sum, reduce_sum = split_grads(grads)
    got = got[1:]
    first_sums, states_grad = [], None
    for q in every:
        if q + 1 < PARTS:
            if q + 2 == PARTS:
                made[parties + q], flat = tie(made[parties + q], flat)
            if first_sums:
                made[parties + q], first_sums[-1] = tie(made[parties + q], first_sums[-1])
            send(made[parties + q], got)
        else:
            states_grad, expand_sum = tie(states_grad, expand_sum)
        received = got[:parties] if q == 0 else got[parties + q - 1 : parties + q]
        states_grad, part = last_norm(q, later_grads[q], received, states_grad)
        first_sums.append(part)
        if q == 0:
            flat, first_sums[-1] = tie(flat, first_sums[-1])
            flat = sum_rows(flat)
    small = sum_small(
        jnp.concatenate([sum(first_sums)[:2], sums[:3], expand_bias_grad.reshape(-1, chans)])
    )
    sizes = [v.size for v in filter_parts]
    ends = np.cumsum(sizes)
    filter_sums = [
        flat[e - n : e].reshape(v.shape) for e, n, v in zip(ends, sizes, filter_parts)
    ]
    inner_sum, inner_bias_sum, outer_sum, outer_bias_sum = filter_sums
    return (
        restore(result),
        restore(states_grad),
        small[0],
        small[1],
        inner_sum,
        inner_bias_sum.reshape(2, -1, BS),
        outer_sum,
        outer_bias_sum.reshape(2, -1, BS),
        small[3],
        small[4],
        expand_sum,
        small[5:].reshape(-1),
        reduce_sum,
        small[2],
    )


def solution(mesh):
    tile = P(None, "rows", "cols", None)
    mix = P(None, "cols", None, None)
    bias = P(None, "cols", None)
    in_specs = (
        tile, P(), P(), P(), P(), mix, bias, mix, bias, P(), P(), P(), P(), P(), P(), tile,
    )
    out_specs = (
        tile, tile, P(), P(), mix, bias, mix, bias, P(), P(), P(), P(), P(), P(),
    )
    return jax.shard_map(body, mesh=mesh, in_specs=in_specs, out_specs=out_specs, check_vma=False)
```

```python
import functools
import math

import jax
import jax.numpy as jnp
import numpy as np
from jax import lax
from jax.experimental import pallas as pl
from jax.experimental.pallas import tpu as pltpu
from jax.sharding import PartitionSpec as P

BS = 96
BINS = 96
PAIR = 2
GROUP = 8
PARTS = 3
norm_eps = 1e-06
shrink_width = 0.01
VMEM = 60 * 1024 * 1024
f32 = jnp.float32
bf16 = jnp.bfloat16


def phi_parts(v):
    cdf = 0.5 * (1.0 + lax.erf(v * math.sqrt(0.5)))
    slope = cdf + v * (jnp.exp(v * v * -0.5) * (1.0 / math.sqrt(2.0 * math.pi)))
    return cdf, slope


def dot(a, b):
    return lax.dot_general(a, b, (((1,), (0,)), ((), ())), preferred_element_type=f32)


def dot_tn(a, b):
    return lax.dot_general(a, b, (((0,), (0,)), ((), ())), preferred_element_type=f32)


def dot_nt(a, b):
    return lax.dot_general(a, b, (((1,), (1,)), ((), ())), preferred_element_type=f32)


def standardize(v):
    centre = jnp.mean(v, axis=-1, keepdims=True)
    centred = v - centre
    spread = jnp.mean(centred * centred, axis=-1, keepdims=True)
    scale = lax.rsqrt(spread + norm_eps)
    return centred * scale, scale


def standardize_back(grad, normal, scale):
    first = jnp.mean(grad, axis=-1, keepdims=True)
    second = jnp.mean(grad * normal, axis=-1, keepdims=True)
    return scale * (grad - first - normal * second)


def pack(sides, outs, width, step):
    turned = [jnp.swapaxes(s, 0, 1) for s in sides]
    cut = width // len(outs)

    def lanes_of(c, g):
        start = c * width + g * cut
        return jnp.concatenate([t[:, :, start : start + cut] for t in turned], axis=2)

    for g, out in enumerate(outs):
        values = [lanes_of(c, g) for c in range(out.shape[1])]
        if len(outs) == 1:
            for c, v in enumerate(values):
                out[:, c] = v
            continue

        @pl.when(lax.rem(step, 2) == 0)
        def _():
            for c, v in enumerate(values):
                out[:, c] = jnp.concatenate([v, v], axis=2)

        @pl.when(lax.rem(step, 2) == 1)
        def _():
            for c, v in enumerate(values):
                out[:, c] = jnp.concatenate([out[:, c, :, : PAIR * cut], v], axis=2)


def unpack(refs, half, width, step):
    cut = width // len(refs)
    parts = []
    for c in range(refs[0].shape[1]):
        for ref in refs:
            part = ref[:, c, :, half * cut : (half + 1) * cut]
            if len(refs) > 1:
                later = (PAIR + half) * cut
                part = jnp.where(lax.rem(step, 2) == 1, ref[:, c, :, later : later + cut], part)
            parts.append(part)
    return jnp.swapaxes(jnp.concatenate(parts, axis=2) if len(parts) > 1 else parts[0], 0, 1)


def first_kernel(width, states, mask, gain, shift, *outs):
    sides = []
    for half in range(PAIR):
        inside = mask[half][..., :1]
        normal, _ = standardize(states[half].astype(f32) * inside)
        sides.append(inside * (normal * gain[...] + shift[...]))
    pack(sides, outs, width, pl.program_id(0))


def table_dot(table, x):
    rows = table.shape[0] // 2
    high = x.astype(bf16)
    both = dot(table[...], high)
    rest = dot(table[:rows, :], (x - high.astype(f32)).astype(bf16))
    return both[:rows] + both[rows:] + rest


def wide_in_kernel(cols_here, fine, block, table, held, wide):
    groups, rows = block.shape[1], block.shape[2] // cols_here
    for n in range(block.shape[0] * rows):
        r, j = divmod(n, rows)
        for c in range(groups):
            wide[n, c * cols_here : (c + 1) * cols_here, :] = block[
                r, c, j * cols_here : (j + 1) * cols_here, :
            ]
        x = wide[n]
        y = table_dot(table, x) if fine else dot(table[...], x.astype(bf16))
        held[n, 0] = y[:BINS]
        held[n, 1] = y[BINS:]


def wide_out_kernel(cols_here, factor, *refs):
    held, (table, block) = refs[:-2], refs[-2:]
    groups, rows = block.shape[1], block.shape[2] // cols_here
    cut = held[0].shape[3] // PAIR
    for n in range(block.shape[0] * rows):
        r, j = divmod(n, rows)
        x = [jnp.concatenate([part[n, 0], part[n, 1]], axis=0) for part in held]
        if len(x) > 1:
            x = [part[:, h * cut : (h + 1) * cut] for h in range(PAIR) for part in x]
            x = jnp.concatenate(x, axis=1)
        else:
            x = x[0]
        plane = dot(table[...], x.astype(bf16)) * factor
        for c in range(groups):
            block[r, c, j * cols_here : (j + 1) * cols_here, :] = plane[
                c * cols_here : (c + 1) * cols_here, :
            ]


def wide_in_split_kernel(cols_here, fine, block, table, held, wide, natural):
    groups, half = block.shape[1], block.shape[3] // 2
    rows = natural.shape[2] // cols_here
    for r in range(block.shape[0]):
        for c in range(groups):
            for s in range(natural.shape[2] // 8):
                natural[r, c, s * 8 : s * 8 + 8, :] = block[
                    r, c, (s // 2) * 8 : (s // 2) * 8 + 8, (s % 2) * half : (s % 2 + 1) * half
                ]
        for j in range(rows):
            n = r * rows + j
            for c in range(groups):
                wide[n, c * cols_here : (c + 1) * cols_here, :] = natural[
                    r, c, j * cols_here : (j + 1) * cols_here, :
                ]
            x = wide[n]
            y = table_dot(table, x) if fine else dot(table[...], x.astype(bf16))
            held[n, 0] = y[:BINS]
            held[n, 1] = y[BINS:]


def wide_out_split_kernel(cols_here, factor, held, table, block, natural):
    groups = block.shape[1]
    rows = natural.shape[2] // cols_here
    last = natural.shape[2] // 8 - 1
    for r in range(block.shape[0]):
        for j in range(rows):
            n = r * rows + j
            x = jnp.concatenate([held[n, 0], held[n, 1]], axis=0).astype(bf16)
            plane = dot(table[...], x) * factor
            for c in range(groups):
                natural[r, c, j * cols_here : (j + 1) * cols_here, :] = plane[
                    c * cols_here : (c + 1) * cols_here, :
                ]
        for c in range(groups):
            for m in range(block.shape[2] // 8):
                sides = [natural[r, c, at * 8 : at * 8 + 8, :] for at in (2 * m, min(2 * m + 1, last))]
                block[r, c, m * 8 : m * 8 + 8, :] = jnp.concatenate(sides, axis=1)


def bins_in(held, table, width, group, fine):
    kind = f32 if fine else bf16

    def lane(part, h):
        whole_width = part.shape[-1] // PAIR
        return h * whole_width + (group * width if whole_width > width else 0)

    turned = [
        [jnp.swapaxes(part[:, side], 0, 1).astype(kind) for part in held] for side in range(2)
    ]
    outs = []
    for k in range(GROUP):
        x = jnp.concatenate(
            [
                part[k][:, lane(part, h) : lane(part, h) + width]
                for side in turned
                for h in range(PAIR)
                for part in side
            ],
            axis=0,
        )
        outs.append(table_dot(table, x) if fine else dot(table[...], x))
    return outs


def bins_out(held, table, width, values):
    short = held[0].shape[0]
    count = len(held)
    products = [dot(table[...], value) for value in values]
    for side in range(2):
        for q in range(count):
            rows = []
            for z in products:
                at = [((side * PAIR + h) * count + q) * short for h in range(PAIR)]
                rows.append(jnp.concatenate([z[a : a + short] for a in at], axis=1))
            held[q][:, side] = jnp.swapaxes(jnp.stack(rows, axis=0), 0, 1)


def halves(v, count, tall):
    return [
        (v[k * 2 * tall : k * 2 * tall + tall], v[k * 2 * tall + tall : (k + 1) * 2 * tall])
        for k in range(count)
    ]


def complex_product(x, first, second, count, tall, conj):
    a = dot(x, first)
    b = dot(x, second)
    parts = []
    for (a_re, a_im), (b_re, b_im) in zip(halves(a, count, tall), halves(b, count, tall)):
        if conj:
            parts += [a_re + b_im, a_im - b_re]
        else:
            parts += [a_re - b_im, a_im + b_re]
    return parts


def activate(low, mix, bias, tall):
    parts = complex_product(low, mix[0], mix[1], low.shape[0] // (2 * tall), tall, False)
    return [part + bias[n % 2 : n % 2 + 1, :] for n, part in enumerate(parts)]


def gelu_low(v):
    return (v * (0.5 * (1.0 + lax.erf(v * math.sqrt(0.5))))).astype(bf16)


def spectral_forward_kernel(factor, group, *refs):
    held, refs = refs[:PARTS], refs[PARTS:]
    table_down, table_up, inner, inner_bias, outer, outer_bias = refs[:6]
    given, entries = refs[6 : 6 + PARTS], refs[6 + PARTS]
    width = inner.shape[2]
    tall = table_up.shape[0] // 2
    spec = bins_in(held, table_down, width, group, True)
    low = jnp.concatenate([(s * factor).astype(bf16) for s in spec], axis=0)
    entries[...] = low
    act = jnp.concatenate([gelu_low(v) for v in activate(low, inner, inner_bias, tall)], axis=0)
    shrunk = [
        (v - shrink_width * jnp.tanh(v * (1.0 / shrink_width))).astype(bf16)
        for v in activate(act, outer, outer_bias, tall)
    ]
    values = [jnp.concatenate(shrunk[2 * k : 2 * k + 2], axis=0) for k in range(GROUP)]
    bins_out(given, table_up, width, values)


def spectral_keep_kernel(tall, entries, inner, inner_bias, outer, outer_bias, active, slope, damp):
    acts = []
    for n, v in enumerate(activate(entries[...], inner, inner_bias, tall)):
        cdf, der = phi_parts(v)
        acts.append((v * cdf).astype(bf16))
        slope[n * tall : (n + 1) * tall, :] = der.astype(bf16)
    act = jnp.concatenate(acts, axis=0)
    active[...] = act
    for n, v in enumerate(activate(act, outer, outer_bias, tall)):
        t = jnp.tanh(v * (1.0 / shrink_width))
        damp[n * tall : (n + 1) * tall, :] = (t * t).astype(bf16)


def joined(refs):
    return jnp.concatenate([r[...] for r in refs], axis=1) if len(refs) > 1 else refs[0][...]


def spectral_backward_kernel(factor, parties, *refs):
    held, refs = refs[:PARTS], refs[PARTS:]
    table_down, table_up, inner_t, outer_t = refs[:4]
    slope, damp = joined(refs[4 : 4 + parties]), joined(refs[4 + parties : 4 + 2 * parties])
    refs = refs[4 + 2 * parties :]
    given, refs = refs[:PARTS], refs[PARTS:]
    inner_low, inner_bias_grad, outer_low, outer_bias_grad = refs
    width = inner_t.shape[2]
    tall = table_up.shape[0] // 2

    @pl.when(pl.program_id(0) == 0)
    def _():
        for ref in (inner_bias_grad, outer_bias_grad):
            ref[...] = jnp.zeros_like(ref)

    spec = bins_in(held, table_down, width, 0, False)
    grads = []
    sums = [0.0, 0.0]
    for k in range(GROUP):
        for side in range(2):
            at = (2 * k + side) * tall
            g = spec[k][side * tall : (side + 1) * tall] * factor
            g = g * damp[at : at + tall].astype(f32)
            sums[side] = sums[side] + jnp.sum(g, axis=0, keepdims=True)
            grads.append(g.astype(bf16))
    outer_bias_grad[...] += jnp.concatenate(sums, axis=0)
    low = jnp.concatenate(grads, axis=0)
    outer_low[...] = low
    parts = complex_product(low, outer_t[0], outer_t[1], GROUP, tall, True)
    grads = []
    sums = [0.0, 0.0]
    for n, part in enumerate(parts):
        g = part * slope[n * tall : (n + 1) * tall].astype(f32)
        sums[n % 2] = sums[n % 2] + jnp.sum(g, axis=0, keepdims=True)
        grads.append(g.astype(bf16))
    inner_bias_grad[...] += jnp.concatenate(sums, axis=0)
    low = jnp.concatenate(grads, axis=0)
    inner_low[...] = low
    parts = complex_product(low, inner_t[0], inner_t[1], GROUP, tall, True)
    values = [
        jnp.concatenate([parts[2 * k], parts[2 * k + 1]], axis=0).astype(bf16)
        for k in range(GROUP)
    ]
    bins_out(given, table_up, width, values)


def filter_grad_kernel(tall, parties, *refs):
    entries, active = refs[:parties], refs[parties : 2 * parties]
    inner_low, outer_low, inner_grad, outer_grad = refs[2 * parties :]

    @pl.when(pl.program_id(0) == 0)
    def _():
        inner_grad[...] = jnp.zeros_like(inner_grad)
        outer_grad[...] = jnp.zeros_like(outer_grad)

    for before, low, grad in ((entries, inner_low, inner_grad), (active, outer_low, outer_grad)):
        turned = []
        for k in range(GROUP):
            top, bottom = low[2 * k * tall : (2 * k + 1) * tall], low[(2 * k + 1) * tall : (2 * k + 2) * tall]
            turned += [bottom, -top]
        known = joined(before)
        grad[0] += dot_tn(known, low[...])
        grad[1] += dot_tn(known, jnp.concatenate(turned, axis=0))


def dense_kernel(steps, slabs, width, first_part, arrays, *refs):
    spat, refs = refs[:arrays], refs[arrays:]
    (
        states, cot, mask, first_gain, first_shift, later_gain, later_shift,
        expand_bias, reduce_bias, expand_hbm, reduce_hbm,
    ) = refs[:11]
    refs = refs[11:]
    if not first_part:
        grads_before = refs[0]
        refs = refs[2:]
    back, refs = refs[:1], refs[1:]
    result, later_grad, sums, expand_bias_grad, grads_hbm = refs[:5]
    (
        expand, reduce, expand_grad, reduce_grad, mixed, normed, low_out, branch, grad_n,
        hidden_all, grad_all, copy_sem,
    ) = refs[5:]
    step = pl.program_id(0)
    chans = states.shape[3]
    side_tokens = states.shape[1] * states.shape[2]
    slab = expand.shape[2]
    tokens = mixed.shape[0]
    square = states.shape[1:]

    def parts_of(grads):
        pairs = [(grads.at[pl.ds(s * chans, chans)], expand_grad.at[s]) for s in range(slabs)]
        return pairs + [(grads.at[pl.ds(slabs * chans, slabs * slab)], reduce_grad)]

    def fetches():
        copies = [
            pltpu.make_async_copy(
                expand_hbm.at[:, pl.ds(s * slab, slab)], expand.at[s], copy_sem.at[s]
            )
            for s in range(slabs)
        ]
        copies.append(pltpu.make_async_copy(reduce_hbm, reduce, copy_sem.at[slabs]))
        if not first_part:
            copies += [
                pltpu.make_async_copy(far, near, copy_sem.at[slabs + 1 + n])
                for n, (far, near) in enumerate(parts_of(grads_before))
            ]
        return copies

    @pl.when(step == 0)
    def _():
        for c in fetches():
            c.start()
        if first_part:
            expand_grad[...] = jnp.zeros_like(expand_grad)
            reduce_grad[...] = jnp.zeros_like(reduce_grad)
        sums[...] = jnp.zeros_like(sums)
        expand_bias_grad[...] = jnp.zeros_like(expand_bias_grad)

    @pl.when(step < steps)
    def _():
        start = pl.multiple_of(step * (PAIR * side_tokens), PAIR * side_tokens)
        for half in range(PAIR):
            at = pl.ds(start + half * side_tokens, side_tokens)
            inside = mask[half][..., :1]
            lower = inside * states[half].astype(f32)
            first, _ = standardize(lower)
            filter_in = first * first_gain[...] + first_shift[...]
            full = lower + inside * (unpack(spat, half, width, step) + filter_in)
            later, _ = standardize(full)
            full = full.reshape(side_tokens, chans)
            mixed[at, :] = full
            branch[at, :] = full + reduce_bias[...]
            normal = (later * later_gain[...] + later_shift[...]).reshape(side_tokens, chans)
            normed[at, :] = normal.astype(bf16)
            go = (inside * cot[half].astype(f32)).reshape(side_tokens, chans)
            low_out[at, :] = go.astype(bf16)
            grad_n[at, :] = jnp.zeros_like(full)
            sums[0:1, :] += jnp.sum(go, axis=0, keepdims=True)

    @pl.when(step == steps)
    def _():
        for c in fetches():
            c.wait()

    @pl.when((step >= steps) & (step < steps + slabs))
    def _():
        hc = step - steps
        at = pl.ds(pl.multiple_of(hc * slab, slab), slab)
        piece = tokens // 4 if tokens % 64 == 0 else tokens

        def some(n, carry):
            here = pl.ds(pl.multiple_of(n * piece, piece), piece)
            weight_up = expand[hc]
            weight_down = reduce[at, :]
            go = low_out[here, :]
            pre = dot(normed[here, :], weight_up) + expand_bias[...]
            cdf, der = phi_parts(pre)
            hidden = (pre * cdf).astype(bf16)
            hidden_all[here, :] = hidden
            branch[here, :] += dot(hidden, weight_down)
            grad_pre = dot_nt(go, weight_down) * der
            expand_bias_grad[pl.ds(hc, 1), :] += jnp.sum(grad_pre, axis=0, keepdims=True)
            grad_low = grad_pre.astype(bf16)
            grad_all[here, :] = grad_low
            grad_n[here, :] += dot_nt(grad_low, weight_up)
            return carry

        lax.fori_loop(0, tokens // piece, some, 0)
        reduce_grad[at, :] += dot_tn(hidden_all[...], low_out[...])
        expand_grad[hc] += dot_tn(normed[...], grad_all[...])

    @pl.when(step >= steps + slabs)
    def _():
        start = pl.multiple_of(
            (step - steps - slabs) * (PAIR * side_tokens), PAIR * side_tokens
        )
        sides = []
        for half in range(PAIR):
            at = pl.ds(start + half * side_tokens, side_tokens)
            inside = mask[half][..., :1]
            later, scale = standardize(mixed[at, :])
            g = grad_n[at, :]
            sums[1:2, :] += jnp.sum(g * later, axis=0, keepdims=True)
            sums[2:3, :] += jnp.sum(g, axis=0, keepdims=True)
            g = low_out[at, :].astype(f32) + standardize_back(g * later_gain[...], later, scale)
            sides.append(inside * g.reshape(square))
            later_grad[half] = sides[-1]
            result[half] = (inside * branch[at, :].reshape(square)).astype(bf16)
        pack(sides, back, width, step - steps - slabs)

    @pl.when(step == pl.num_programs(0) - 1)
    def _():
        copies = [
            pltpu.make_async_copy(near, far, copy_sem.at[n])
            for n, (far, near) in enumerate(parts_of(grads_hbm))
        ]
        for c in copies:
            c.start()
        for c in copies:
            c.wait()


def last_kernel(width, arrays, *refs):
    spat, (states, later_grad, mask, gain) = refs[:arrays], refs[arrays : arrays + 4]
    out, sums = refs[-2:]
    chans = states.shape[3]

    @pl.when(pl.program_id(0) == 0)
    def _():
        sums[...] = jnp.zeros_like(sums)

    for half in range(PAIR):
        inside = mask[half][..., :1]
        normal, scale = standardize(inside * states[half].astype(f32))
        grad_mixed = later_grad[half]
        grad = inside * (grad_mixed + unpack(spat, half, width, pl.program_id(0)))
        flat = (-1, chans)
        sums[0:1, :] += jnp.sum((grad * normal).reshape(flat), axis=0, keepdims=True)
        sums[1:2, :] += jnp.sum(grad.reshape(flat), axis=0, keepdims=True)
        grad = grad_mixed + standardize_back(grad * gain[...], normal, scale)
        out[half] = (inside * grad).astype(bf16)


def sum_kernel(
    ranks, groups, own, flat, out, flat_out,
    got, picked, done, send_sem, recv_sem, pick_send, pick_recv, give_send, give_recv,
):
    devices = ranks * groups
    my_row = lax.axis_index("rows")
    me = my_row * groups + lax.axis_index("cols")
    piece = flat.shape[0] // ranks

    def place(i):
        other = lax.rem(me + i, devices)
        return lax.div(other, groups), lax.rem(other, groups)

    def copy(i):
        return pltpu.make_async_remote_copy(
            src_ref=own,
            dst_ref=got.at[i],
            send_sem=send_sem.at[i],
            recv_sem=recv_sem.at[i],
            device_id=place(i),
            device_id_type=pl.DeviceIdType.MESH,
        )

    def along(src, dst, i, send, recv):
        return pltpu.make_async_remote_copy(
            src_ref=src,
            dst_ref=dst,
            send_sem=send.at[i],
            recv_sem=recv.at[i],
            device_id=(lax.rem(my_row + i, ranks), lax.axis_index("cols")),
            device_id_type=pl.DeviceIdType.MESH,
        )

    def rows_of(r):
        return pl.ds(pl.multiple_of(r * piece, piece), piece)

    barrier = pltpu.get_barrier_semaphore()

    def greet(i, carry):
        pl.semaphore_signal(
            barrier, inc=1, device_id=place(i), device_id_type=pl.DeviceIdType.MESH
        )
        return carry

    def start(i, carry):
        copy(i).start()
        return carry

    def finish(i, carry):
        copy(i).wait()
        return carry

    lax.fori_loop(1, devices, greet, 0)
    pl.semaphore_wait(barrier, devices - 1)
    picks = [
        along(flat.at[rows_of(lax.rem(my_row + i, ranks))], picked.at[i], i, pick_send, pick_recv)
        for i in range(1, ranks)
    ]
    for c in picks:
        c.start()
    lax.fori_loop(1, devices, start, 0)
    for c in picks:
        c.wait()
    total = flat[rows_of(my_row), :]
    for i in range(1, ranks):
        total = total + picked[i]
    done[0] = total
    gives = [along(done.at[0], done.at[i], i, give_send, give_recv) for i in range(1, ranks)]
    for c in gives:
        c.start()
    lax.fori_loop(1, devices, finish, 0)
    out[...] = lax.fori_loop(1, devices, lambda i, total: total + got[i], own[...])
    for c in gives:
        c.wait()
    flat_out[rows_of(my_row), :] = total
    for i in range(1, ranks):
        flat_out[rows_of(lax.rem(my_row - i + ranks, ranks)), :] = done[i]


def split_kernel(expand_in, reduce_in, expand_out, reduce_out):
    expand_out[...] = expand_in[...]
    reduce_out[...] = reduce_in[...]


def wide_tables(width):
    freq = np.arange(BINS)
    place = np.arange(width)
    angle = (freq[:, None] * place[None, :] % width) * (2.0 * math.pi / width)
    live = (2 * freq <= width).astype(np.float64)[:, None]
    edge = (freq == 0) | (2 * freq == width)
    weight = np.where(edge, 1.0, 2.0)[:, None] * live
    cosine, sine = np.cos(angle), np.sin(angle)
    plain = np.concatenate([live * cosine, -live * sine], axis=0)
    doubled = np.concatenate([weight * cosine, -weight * sine], axis=0)
    return plain, doubled


def tall_tables(height, rows_here):
    pairs = rows_here // PAIR
    rows = pairs // PARTS
    order = np.array(
        [
            r * rows_here + h * pairs + q * rows + j
            for h in range(PAIR)
            for q in range(PARTS)
            for r in range(height // rows_here)
            for j in range(rows)
        ]
    )
    freq = np.arange(height)
    angle = (freq[:, None] * order[None, :] % height) * (2.0 * math.pi / height)
    cosine, sine = np.cos(angle), np.sin(angle)
    down = np.block([[cosine, sine], [-sine, cosine]])
    up = np.block([[cosine.T, -sine.T], [sine.T, cosine.T]])
    return down, up


def spread(weight):
    count = weight.shape[1]
    eye = jnp.eye(count, dtype=weight.dtype)
    full = jnp.einsum("rbio,bd->rbido", weight, eye)
    return full.reshape(2, count * BS, count * BS)


def gather_blocks(full):
    count = full.shape[1] // BS
    return jnp.stack(
        [full[:, b * BS : (b + 1) * BS, b * BS : (b + 1) * BS] for b in range(count)], axis=1
    )


def bias_rows(bias):
    return bias.reshape(2, -1)


def whole(shape):
    return pl.BlockSpec(shape, lambda *_: (0,) * len(shape))


def call(kernel, grid, in_specs, out_specs, out_shape, name, flops=0, nbytes=0, scratch=(), **kw):
    return pl.pallas_call(
        kernel,
        grid=(grid,),
        in_specs=in_specs,
        out_specs=out_specs,
        out_shape=out_shape,
        scratch_shapes=scratch,
        compiler_params=pltpu.CompilerParams(
            dimension_semantics=("arbitrary",), vmem_limit_bytes=VMEM
        ),
        cost_estimate=pl.CostEstimate(flops=flops, bytes_accessed=nbytes, transcendentals=0),
        name=name,
        **kw,
    )


def body(
    states,
    heights,
    widths,
    first_gain,
    first_shift,
    filter_inner,
    inner_bias,
    filter_outer,
    outer_bias,
    later_gain,
    later_shift,
    expand_weight,
    expand_bias,
    reduce_weight,
    reduce_bias,
    cotangent,
):
    frames, rows_here, cols_here, chans = states.shape
    ranks, groups = lax.axis_size("rows"), lax.axis_size("cols")
    assert frames == ranks and rows_here % (PAIR * PARTS) == 0
    height, breadth = rows_here * ranks, cols_here * groups
    devices = ranks * groups
    pairs = rows_here // PAIR
    rows = pairs // PARTS
    pixels = rows * cols_here
    width = chans // groups
    lanes = width * PAIR
    hidden = expand_weight.shape[1]
    factor = 1.0 / math.sqrt(height * breadth)
    short = ranks * rows
    step_pixels = 8 if pixels % 8 == 0 else pixels
    steps = pixels // step_pixels
    tokens = PAIR * pixels * frames
    message = devices * pixels * lanes * 4
    row = lambda v: v.reshape(1, -1)
    shape = jax.ShapeDtypeStruct

    order = lambda v: jnp.transpose(v, (1, 2, 0, 3)).reshape(PAIR, pairs * cols_here, frames, chans)
    restore = lambda v: jnp.transpose(v.reshape(rows_here, cols_here, frames, chans), (2, 0, 1, 3))
    states_in, cot_in = order(states), order(cotangent)
    row_ids = lax.axis_index("rows") * rows_here + jnp.arange(rows_here, dtype=jnp.int32)
    col_ids = lax.axis_index("cols") * cols_here + jnp.arange(cols_here, dtype=jnp.int32)
    inside = (row_ids[:, None, None] < heights) & (col_ids[None, :, None] < widths)
    mask = jnp.broadcast_to(
        inside.astype(f32).reshape(PAIR, pairs * cols_here, frames, 1),
        (PAIR, pairs * cols_here, frames, 128),
    )

    buffers = {} if steps > 1 else {"pipeline_mode": pl.Buffered(1)}

    def token_spec(q, where, last=chans):
        return pl.BlockSpec(
            (PAIR, step_pixels, frames, last), lambda i: (0, q * steps + where(i), 0, 0), **buffers
        )

    def packed_spec(where):
        return pl.BlockSpec(
            (ranks, groups, step_pixels, lanes), lambda i: (0, 0, where(i), 0), **buffers
        )

    blocks_here = width // BS
    split = blocks_here > 1 and steps > 1 and (2 * PAIR * BS) % 128 == 0
    parties = blocks_here if split else 1
    cut = width // parties
    split_rows = 8 * (-(-steps // 2))

    def arrays_of(q):
        return parties if q == 0 else 1

    def message_specs(q, where):
        if arrays_of(q) == 1:
            return [packed_spec(where)]
        return [
            pl.BlockSpec(
                (ranks, groups, step_pixels, 2 * PAIR * cut), lambda i: (0, 0, where(i) // 2, 0)
            )
        ] * parties

    def message_shapes(q):
        if arrays_of(q) == 1:
            return [packed_shape]
        return [shape((ranks, groups, split_rows, 2 * PAIR * cut), f32)] * parties

    same = lambda i: i
    token_shape = shape((PAIR, pairs * cols_here, frames, chans), bf16)
    packed_shape = shape((ranks, groups, pixels, lanes), f32)
    chan_row = whole((1, chans))
    anywhere = pl.BlockSpec(memory_space=pl.ANY)

    def scatter(v, axis):
        return lax.psum_scatter(v, axis, scatter_dimension=0, tiled=True)

    def gather(v, axis):
        return lax.all_gather(v, axis, axis=0, tiled=True)

    def sum_small(v, by_rows):
        def as_rows(v, unit):
            v = v.reshape(-1)
            return jnp.pad(v, (0, -v.shape[0] % (unit * 128))).reshape(-1, 128)

        own, flat = as_rows(v, 8), as_rows(by_rows, 8 * ranks)
        slots = pltpu.VMEM((ranks, flat.shape[0] // ranks, 128), f32)
        vmem = pl.BlockSpec(memory_space=pltpu.VMEM)
        out, flat_out = pl.pallas_call(
            functools.partial(sum_kernel, ranks, groups),
            in_specs=[vmem, vmem],
            out_specs=[vmem, vmem],
            out_shape=[shape(own.shape, f32), shape(flat.shape, f32)],
            scratch_shapes=[pltpu.VMEM((devices,) + own.shape, f32), slots, slots]
            + [pltpu.SemaphoreType.DMA((devices,))] * 2
            + [pltpu.SemaphoreType.DMA((ranks,))] * 4,
            compiler_params=pltpu.CompilerParams(collective_id=0, has_side_effects=True),
            name="small_sums",
        )(own, flat)
        return out.reshape(-1)[: v.size].reshape(v.shape), flat_out.reshape(-1)

    def split_grads(v):
        cuts = 4
        piece = (chans // cuts, chans)
        return call(
            split_kernel,
            slabs * cuts,
            [
                pl.BlockSpec(piece, lambda i: (i, 0)),
                pl.BlockSpec(piece, lambda i: (slabs * cuts + i, 0)),
            ],
            [
                pl.BlockSpec(piece, lambda i: (lax.rem(i, cuts), lax.div(i, cuts))),
                pl.BlockSpec(piece, lambda i: (i, 0)),
            ],
            [shape((chans, hidden), f32), shape((hidden, chans), f32)],
            "split_gradients",
            nbytes=16 * chans * hidden,
        )(v, v)

    def behind(v, *after):
        return lax.optimization_barrier((v,) + after)[0] if after else v

    def exchange(v):
        sent = v.reshape((devices,) + v.shape[2:])
        return lax.all_to_all(sent, ("rows", "cols"), 0, 0, tiled=True).reshape(v.shape)

    def tie(*values):
        return lax.optimization_barrier(values)

    def first_norm(q):
        return call(
            functools.partial(first_kernel, width),
            steps,
            [token_spec(q, same), token_spec(q, same, 128), chan_row, chan_row],
            message_specs(q, same),
            message_shapes(q),
            "first_norm",
            nbytes=2 * message,
        )(states_in, mask, row(first_gain), row(first_shift))

    plain, doubled = wide_tables(breadth)
    down, up = tall_tables(height, rows_here)
    as_table = lambda t: jnp.asarray(t, dtype=bf16)

    def fine_table(t):
        high = t.astype(jnp.bfloat16)
        return jnp.asarray(np.concatenate([high, (t - high.astype(np.float64)).astype(jnp.bfloat16)]))

    def mixes(weight):
        return [weight[:, g] for g in range(parties)] if split else [spread(weight)]

    inner_full, outer_full = mixes(filter_inner), mixes(filter_outer)
    turn = lambda t: jnp.swapaxes(t, 1, 2)
    bin_steps = BINS // GROUP
    group_rows = GROUP * 2 * height
    held_shape = shape((short, 2, BINS, lanes), f32)
    at_once = 2
    held_row = pl.BlockSpec((at_once * rows, 2, BINS, lanes), lambda i: (i, 0, 0, 0))
    held_bins = pl.BlockSpec((short, 2, GROUP, lanes), lambda i: (0, 0, i, 0))
    field = pl.BlockSpec((at_once, groups, pixels, lanes), lambda i: (i, 0, 0, 0))
    kept = pl.BlockSpec((group_rows, cut), lambda i: (i, 0))
    kept_shape = shape((bin_steps * group_rows, cut), bf16)
    mix_spec = whole((2, cut, cut))
    bias_spec = whole((2, cut))

    def held_of(last, by_row):
        if by_row:
            return pl.BlockSpec((at_once * rows, 2, BINS, last), lambda i: (i, 0, 0, 0))
        return pl.BlockSpec((short, 2, GROUP, last), lambda i: (0, 0, i, 0))

    cut_shape = shape((short, 2, BINS, PAIR * cut), f32)
    split_field = pl.BlockSpec(
        (at_once, groups, split_rows, 2 * PAIR * cut), lambda i: (i, 0, 0, 0)
    )
    natural = pltpu.VMEM((at_once, groups, pixels, PAIR * cut), f32)
    cut_in = [held_of(PAIR * cut if split else lanes, False)] + [held_bins] * (PARTS - 1)
    cut_out = [held_of(PAIR * cut, False)] * PARTS
    up_spec = whole((2 * height, 2 * height))

    def wide_in(v, table, fine):
        divided = v.shape != packed_shape.shape
        return call(
            functools.partial(wide_in_split_kernel if divided else wide_in_kernel, cols_here, fine),
            ranks // at_once,
            [split_field if divided else field, whole(table.shape)],
            held_of(PAIR * cut, True) if divided else held_row,
            cut_shape if divided else held_shape,
            "wide_in",
            nbytes=2 * message,
            scratch=[pltpu.VMEM((at_once * rows, breadth, PAIR * cut), f32), natural]
            if divided
            else [pltpu.VMEM((at_once * rows, breadth, lanes), f32)],
        )(v, table)

    def wide_out(parts, table):
        return call(
            functools.partial(wide_out_kernel, cols_here, factor),
            ranks // at_once,
            [held_of(v.shape[3], True) for v in parts] + [whole(table.shape)],
            field,
            packed_shape,
            "wide_out",
            nbytes=2 * message,
        )(*parts, table)

    def wide_out_split(part, table):
        return call(
            functools.partial(wide_out_split_kernel, cols_here, factor),
            ranks // at_once,
            [held_of(PAIR * cut, True), whole(table.shape)],
            split_field,
            message_shapes(0)[0],
            "wide_out",
            nbytes=2 * message,
            scratch=[natural],
        )(part, table)

    def messages_out(given, table):
        first = [wide_out_split(v[0], table) for v in given] if split else [wide_out([given[0][0]], table)]
        return first + [wide_out([v[q] for v in given], table) for q in range(1, PARTS)]

    def of_group(v, g):
        return bias_rows(v)[:, g * cut : (g + 1) * cut]

    forward_mix = [
        (inner_full[g], of_group(inner_bias, g), outer_full[g], of_group(outer_bias, g))
        for g in range(parties)
    ]
    forward_specs = [mix_spec, bias_spec, mix_spec, bias_spec]

    def spectral_forward(g, held):
        table = fine_table(down)
        outs = call(
            functools.partial(spectral_forward_kernel, factor, g),
            bin_steps,
            cut_in + [whole(table.shape), up_spec] + forward_specs,
            cut_out + [kept],
            [cut_shape] * PARTS + [kept_shape],
            "spectral_forward",
            flops=20 * 10**9,
            nbytes=8 * PARTS * message // parties,
        )(*held, table, as_table(up), *forward_mix[g])
        return outs[:PARTS], outs[PARTS]

    def spectral_keep(g, entries):
        return call(
            functools.partial(spectral_keep_kernel, height),
            bin_steps,
            [kept] + forward_specs,
            [kept] * 3,
            [kept_shape] * 3,
            "spectral_keep",
            flops=10 * 10**9,
            nbytes=2 * PARTS * message // parties,
        )(entries, *forward_mix[g])

    full = pl.BlockSpec((group_rows, width), lambda i: (i, 0))
    full_shape = shape((bin_steps * group_rows, width), bf16)
    full_mix, full_bias = whole((2, width, width)), whole((2, width))
    inner_t, outer_t = turn(spread(filter_inner)), turn(spread(filter_outer))

    def spectral_backward(held, slope, damp):
        outs = call(
            functools.partial(spectral_backward_kernel, factor, parties),
            bin_steps,
            [held_bins] * PARTS + [up_spec, up_spec, full_mix, full_mix] + [kept] * (2 * parties),
            [held_bins] * PARTS + [full, full_bias] * 2,
            [held_shape] * PARTS + [full_shape, shape((2, width), f32)] * 2,
            "spectral_backward",
            flops=20 * 10**9,
            nbytes=8 * PARTS * message,
        )(*held, as_table(down), as_table(up), inner_t, outer_t, *slope, *damp)
        return outs[:PARTS], outs[PARTS:]

    def filter_grad(entries, active, inner_low, outer_low):
        return call(
            functools.partial(filter_grad_kernel, height, parties),
            bin_steps,
            [kept] * (2 * parties) + [full] * 2,
            [full_mix] * 2,
            [shape((2, width, width), f32)] * 2,
            "filter_grad",
            flops=10 * 10**9,
            nbytes=2 * PARTS * message,
        )(*entries, *active, inner_low, outer_low)

    slab = chans
    slabs = hidden // slab
    dense_steps = 2 * steps + slabs
    enter = lambda i: jnp.minimum(i, steps - 1)
    leave = lambda i: jnp.maximum(i - steps - slabs, 0)
    either = lambda i: jnp.where(i < steps + slabs, enter(i), leave(i))

    def dense(q, spatial, before):
        grads_before = () if q == 0 else before
        return call(
            functools.partial(dense_kernel, steps, slabs, width, q == 0, arrays_of(q)),
            dense_steps,
            message_specs(q, enter)
            + [token_spec(q, enter), token_spec(q, enter), token_spec(q, either, 128)]
            + [chan_row] * 4
            + [pl.BlockSpec((1, slab), lambda i: (0, jnp.clip(i - steps, 0, slabs - 1)))]
            + [chan_row]
            + [anywhere] * (2 + len(grads_before)),
            [packed_spec(leave)]
            + [
                token_spec(q, leave),
                token_spec(0, leave),
                whole((8, chans)),
                whole((slabs, slab)),
                anywhere,
            ],
            [packed_shape]
            + [
                token_shape,
                shape((PAIR, pixels, frames, chans), f32),
                shape((8, chans), f32),
                shape((slabs, slab), f32),
                shape((2 * hidden, chans), f32),
            ],
            "dense_both_ways",
            flops=12 * tokens * chans * hidden,
            nbytes=4 * message,
            scratch=[
                pltpu.VMEM((slabs, chans, slab), bf16),
                pltpu.VMEM((hidden, chans), bf16),
                pltpu.VMEM((slabs, chans, slab), f32),
                pltpu.VMEM((hidden, chans), f32),
                pltpu.VMEM((tokens, chans), f32),
                pltpu.VMEM((tokens, chans), bf16),
                pltpu.VMEM((tokens, chans), bf16),
                pltpu.VMEM((tokens, chans), f32),
                pltpu.VMEM((tokens, chans), f32),
                pltpu.VMEM((tokens, slab), bf16),
                pltpu.VMEM((tokens, slab), bf16),
                pltpu.SemaphoreType.DMA((2 * slabs + 2,)),
            ],
            input_output_aliases={} if q == 0 else {13: 1},
        )(
            *spatial,
            states_in,
            cot_in,
            mask,
            row(first_gain),
            row(first_shift),
            row(later_gain),
            row(later_shift),
            row(expand_bias),
            row(reduce_bias),
            expand_weight,
            reduce_weight,
            *grads_before,
        )

    def last_norm(q, later_grad, spatial, before):
        given = () if q == 0 else (before,)
        return call(
            functools.partial(last_kernel, width, 1),
            steps,
            [packed_spec(same)]
            + [token_spec(q, same), token_spec(0, same), token_spec(q, same, 128)]
            + [chan_row]
            + [anywhere] * len(given),
            [token_spec(q, same), whole((8, chans))],
            [token_shape, shape((8, chans), f32)],
            "first_norm_backward",
            nbytes=4 * message,
            input_output_aliases={} if q == 0 else {5: 0},
        )(spatial, states_in, later_grad, mask, row(first_gain), *given)

    every = range(PARTS)

    def send(made, got):
        if got:
            made, got[-1] = tie(made, got[-1])
        got.append(exchange(made))

    made = [v for q in (*every[1:], 0) for v in first_norm(q)]
    got, held = [], []
    for n, v in enumerate(made):
        if n > 1:
            v, held[-1] = tie(v, held[-1])
        send(v, got)
        if n > 0:
            held.append(wide_in(got[-2], fine_table(plain), True))
    held.append(wide_in(got[-1], fine_table(plain), True))
    rest, first = held[: PARTS - 1], held[PARTS - 1 :]
    done = [spectral_forward(g, [first[g]] + rest) for g in range(parties)]
    entries = [v[1] for v in done]
    made = messages_out([v[0] for v in done], as_table(doubled.T))
    keeps = [list(spectral_keep(g, entries[g])) for g in range(parties)]

    spatial = got[-1:]
    for n in range(parties):
        send(made[n], spatial)
    for keep in keeps:
        keep[0], made[parties] = tie(keep[0], made[parties])
    spatial = spatial[1:]
    backs, later_grads, sums, expand_bias_grad, before = [], [], 0.0, 0.0, ()
    for q in every:
        if q + 1 < PARTS:
            if backs:
                made[parties + q], backs[-1] = tie(made[parties + q], backs[-1])
            send(made[parties + q], spatial)
        received = spatial[:parties] if q == 0 else spatial[parties + q - 1 : parties + q]
        if q + 1 == PARTS:
            backs[-1], spatial[-1] = tie(backs[-1], spatial[-1])
            got = [exchange(backs[1])]
            received = spatial[-1:]
        outs = dense(q, received, before)
        back, result, kept_grad, part, bias_part, grads = outs
        backs.append(back)
        before = (grads, result)
        later_grads.append(kept_grad)
        sums, expand_bias_grad = sums + part, expand_bias_grad + bias_part
    grads, got[0] = tie(grads, got[0])
    grads = scatter(grads, "cols")
    held = []
    for v in [backs[q] for q in (*every[2:], 0)]:
        held.append(wide_in(got[-1], as_table(doubled), False))
        if len(held) > 1:
            v, held[-2] = tie(v, held[-2])
        send(v, got)
    got[-1], held[-1] = tie(got[-1], held[-1])
    held.append(wide_in(got[-1], as_table(doubled), False))
    grads, held[-1] = tie(grads, held[-1])
    grads = scatter(grads, "rows")
    given, (inner_low, inner_bias_grad, outer_low, outer_bias_grad) = spectral_backward(
        [held[-1]] + held[:-1], [k[1] for k in keeps], [k[2] for k in keeps]
    )
    made = [wide_out([v], as_table(plain.T)) for v in given]
    inner_grad, outer_grad = filter_grad(entries, [k[0] for k in keeps], inner_low, outer_low)
    filter_parts = (
        gather_blocks(inner_grad), inner_bias_grad, gather_blocks(outer_grad), outer_bias_grad
    )
    flat = jnp.concatenate([v.reshape(-1) for v in filter_parts])

    got = [exchange(made[0])]
    send(made[1], got)
    grads, got[0] = tie(grads, got[0])
    grads = gather(grads, ("cols", "rows"))
    expand_sum, reduce_sum = split_grads(grads)
    first_sums, states_grad = [], None
    for q in every:
        if q + 1 < PARTS:
            if q > 0:
                made[q + 1], first_sums[-1] = tie(made[q + 1], first_sums[-1])
                send(made[q + 1], got)
        else:
            flat, states_grad = tie(flat, states_grad)
            states_grad, expand_sum = tie(states_grad, expand_sum)
        states_grad, part = last_norm(q, later_grads[q], got[q], states_grad)
        first_sums.append(part)
    small, flat = sum_small(
        jnp.concatenate([sum(first_sums)[:2], sums[:3], expand_bias_grad.reshape(-1, chans)]), flat
    )
    sizes = [v.size for v in filter_parts]
    ends = np.cumsum(sizes)
    filter_sums = [
        flat[e - n : e].reshape(v.shape) for e, n, v in zip(ends, sizes, filter_parts)
    ]
    inner_sum, inner_bias_sum, outer_sum, outer_bias_sum = filter_sums
    return (
        restore(result),
        restore(states_grad),
        small[0],
        small[1],
        inner_sum,
        inner_bias_sum.reshape(2, -1, BS),
        outer_sum,
        outer_bias_sum.reshape(2, -1, BS),
        small[3],
        small[4],
        expand_sum,
        small[5:].reshape(-1),
        reduce_sum,
        small[2],
    )


def solution(mesh):
    tile = P(None, "rows", "cols", None)
    mix = P(None, "cols", None, None)
    bias = P(None, "cols", None)
    in_specs = (
        tile, P(), P(), P(), P(), mix, bias, mix, bias, P(), P(), P(), P(), P(), P(), tile,
    )
    out_specs = (
        tile, tile, P(), P(), mix, bias, mix, bias, P(), P(), P(), P(), P(), P(),
    )
    return jax.shard_map(body, mesh=mesh, in_specs=in_specs, out_specs=out_specs, check_vma=False)
```

```python
import functools
import math

import jax
import jax.numpy as jnp
import numpy as np
from jax import lax
from jax.experimental import pallas as pl
from jax.experimental.pallas import tpu as pltpu
from jax.sharding import PartitionSpec as P

BS = 96
BINS = 96
PAIR = 2
GROUP = 8
PARTS = 3
norm_eps = 1e-06
shrink_width = 0.01
VMEM = 60 * 1024 * 1024
f32 = jnp.float32
bf16 = jnp.bfloat16


def phi_parts(v):
    cdf = 0.5 * (1.0 + lax.erf(v * math.sqrt(0.5)))
    slope = cdf + v * (jnp.exp(v * v * -0.5) * (1.0 / math.sqrt(2.0 * math.pi)))
    return cdf, slope


def dot(a, b):
    return lax.dot_general(a, b, (((1,), (0,)), ((), ())), preferred_element_type=f32)


def dot_tn(a, b):
    return lax.dot_general(a, b, (((0,), (0,)), ((), ())), preferred_element_type=f32)


def dot_nt(a, b):
    return lax.dot_general(a, b, (((1,), (1,)), ((), ())), preferred_element_type=f32)


def standardize(v):
    centre = jnp.mean(v, axis=-1, keepdims=True)
    centred = v - centre
    spread = jnp.mean(centred * centred, axis=-1, keepdims=True)
    scale = lax.rsqrt(spread + norm_eps)
    return centred * scale, scale


def standardize_back(grad, normal, scale):
    first = jnp.mean(grad, axis=-1, keepdims=True)
    second = jnp.mean(grad * normal, axis=-1, keepdims=True)
    return scale * (grad - first - normal * second)


def pack(sides, outs, width, step):
    turned = [jnp.swapaxes(s, 0, 1) for s in sides]
    cut = width // len(outs)

    def lanes_of(c, g):
        start = c * width + g * cut
        return jnp.concatenate([t[:, :, start : start + cut] for t in turned], axis=2)

    for g, out in enumerate(outs):
        values = [lanes_of(c, g) for c in range(out.shape[1])]
        if len(outs) == 1:
            for c, v in enumerate(values):
                out[:, c] = v
            continue

        @pl.when(lax.rem(step, 2) == 0)
        def _():
            for c, v in enumerate(values):
                out[:, c] = jnp.concatenate([v, v], axis=2)

        @pl.when(lax.rem(step, 2) == 1)
        def _():
            for c, v in enumerate(values):
                out[:, c] = jnp.concatenate([out[:, c, :, : PAIR * cut], v], axis=2)


def unpack(refs, half, width, step):
    cut = width // len(refs)
    parts = []
    for c in range(refs[0].shape[1]):
        for ref in refs:
            part = ref[:, c, :, half * cut : (half + 1) * cut]
            if len(refs) > 1:
                later = (PAIR + half) * cut
                part = jnp.where(lax.rem(step, 2) == 1, ref[:, c, :, later : later + cut], part)
            parts.append(part)
    return jnp.swapaxes(jnp.concatenate(parts, axis=2) if len(parts) > 1 else parts[0], 0, 1)


def first_kernel(width, states, mask, gain, shift, *outs):
    sides = []
    for half in range(PAIR):
        inside = mask[half][..., :1]
        normal, _ = standardize(states[half].astype(f32) * inside)
        sides.append(inside * (normal * gain[...] + shift[...]))
    pack(sides, outs, width, pl.program_id(0))


def table_dot(table, x):
    rows = table.shape[0] // 2
    high = x.astype(bf16)
    both = dot(table[...], high)
    rest = dot(table[:rows, :], (x - high.astype(f32)).astype(bf16))
    return both[:rows] + both[rows:] + rest


def wide_in_kernel(cols_here, fine, block, table, held, wide):
    groups, rows = block.shape[1], block.shape[2] // cols_here
    for n in range(block.shape[0] * rows):
        r, j = divmod(n, rows)
        for c in range(groups):
            wide[n, c * cols_here : (c + 1) * cols_here, :] = block[
                r, c, j * cols_here : (j + 1) * cols_here, :
            ]
        x = wide[n]
        y = table_dot(table, x) if fine else dot(table[...], x.astype(bf16))
        held[n, 0] = y[:BINS]
        held[n, 1] = y[BINS:]


def wide_out_kernel(cols_here, factor, *refs):
    held, (table, block) = refs[:-2], refs[-2:]
    groups, rows = block.shape[1], block.shape[2] // cols_here
    cut = held[0].shape[3] // PAIR
    for n in range(block.shape[0] * rows):
        r, j = divmod(n, rows)
        x = [jnp.concatenate([part[n, 0], part[n, 1]], axis=0) for part in held]
        if len(x) > 1:
            x = [part[:, h * cut : (h + 1) * cut] for h in range(PAIR) for part in x]
            x = jnp.concatenate(x, axis=1)
        else:
            x = x[0]
        plane = dot(table[...], x.astype(bf16)) * factor
        for c in range(groups):
            block[r, c, j * cols_here : (j + 1) * cols_here, :] = plane[
                c * cols_here : (c + 1) * cols_here, :
            ]


def wide_in_split_kernel(cols_here, fine, block, table, held, wide, natural):
    groups, half = block.shape[1], block.shape[3] // 2
    rows = natural.shape[2] // cols_here
    for r in range(block.shape[0]):
        for c in range(groups):
            for s in range(natural.shape[2] // 8):
                natural[r, c, s * 8 : s * 8 + 8, :] = block[
                    r, c, (s // 2) * 8 : (s // 2) * 8 + 8, (s % 2) * half : (s % 2 + 1) * half
                ]
        for j in range(rows):
            n = r * rows + j
            for c in range(groups):
                wide[n, c * cols_here : (c + 1) * cols_here, :] = natural[
                    r, c, j * cols_here : (j + 1) * cols_here, :
                ]
            x = wide[n]
            y = table_dot(table, x) if fine else dot(table[...], x.astype(bf16))
            held[n, 0] = y[:BINS]
            held[n, 1] = y[BINS:]


def wide_out_split_kernel(cols_here, factor, held, table, block, natural):
    groups = block.shape[1]
    rows = natural.shape[2] // cols_here
    last = natural.shape[2] // 8 - 1
    for r in range(block.shape[0]):
        for j in range(rows):
            n = r * rows + j
            x = jnp.concatenate([held[n, 0], held[n, 1]], axis=0).astype(bf16)
            plane = dot(table[...], x) * factor
            for c in range(groups):
                natural[r, c, j * cols_here : (j + 1) * cols_here, :] = plane[
                    c * cols_here : (c + 1) * cols_here, :
                ]
        for c in range(groups):
            for m in range(block.shape[2] // 8):
                sides = [natural[r, c, at * 8 : at * 8 + 8, :] for at in (2 * m, min(2 * m + 1, last))]
                block[r, c, m * 8 : m * 8 + 8, :] = jnp.concatenate(sides, axis=1)


def bins_in(held, table, width, group, fine):
    kind = f32 if fine else bf16

    def lane(part, h):
        whole_width = part.shape[-1] // PAIR
        return h * whole_width + (group * width if whole_width > width else 0)

    turned = [
        [jnp.swapaxes(part[:, side], 0, 1).astype(kind) for part in held] for side in range(2)
    ]
    outs = []
    for k in range(GROUP):
        x = jnp.concatenate(
            [
                part[k][:, lane(part, h) : lane(part, h) + width]
                for side in turned
                for h in range(PAIR)
                for part in side
            ],
            axis=0,
        )
        outs.append(table_dot(table, x) if fine else dot(table[...], x))
    return outs


def bins_out(held, table, width, values):
    short = held[0].shape[0]
    count = len(held)
    products = [dot(table[...], value) for value in values]
    for side in range(2):
        for q in range(count):
            rows = []
            for z in products:
                at = [((side * PAIR + h) * count + q) * short for h in range(PAIR)]
                rows.append(jnp.concatenate([z[a : a + short] for a in at], axis=1))
            held[q][:, side] = jnp.swapaxes(jnp.stack(rows, axis=0), 0, 1)


def halves(v, count, tall):
    return [
        (v[k * 2 * tall : k * 2 * tall + tall], v[k * 2 * tall + tall : (k + 1) * 2 * tall])
        for k in range(count)
    ]


def complex_product(x, first, second, count, tall, conj):
    a = dot(x, first)
    b = dot(x, second)
    parts = []
    for (a_re, a_im), (b_re, b_im) in zip(halves(a, count, tall), halves(b, count, tall)):
        if conj:
            parts += [a_re + b_im, a_im - b_re]
        else:
            parts += [a_re - b_im, a_im + b_re]
    return parts


def activate(low, mix, bias, tall):
    parts = complex_product(low, mix[0], mix[1], low.shape[0] // (2 * tall), tall, False)
    return [part + bias[n % 2 : n % 2 + 1, :] for n, part in enumerate(parts)]


def gelu_low(v):
    return (v * (0.5 * (1.0 + lax.erf(v * math.sqrt(0.5))))).astype(bf16)


def spectral_forward_kernel(factor, group, *refs):
    held, refs = refs[:PARTS], refs[PARTS:]
    table_down, table_up, inner, inner_bias, outer, outer_bias = refs[:6]
    given, entries = refs[6 : 6 + PARTS], refs[6 + PARTS]
    width = inner.shape[2]
    tall = table_up.shape[0] // 2
    spec = bins_in(held, table_down, width, group, True)
    low = jnp.concatenate([(s * factor).astype(bf16) for s in spec], axis=0)
    entries[...] = low
    act = jnp.concatenate([gelu_low(v) for v in activate(low, inner, inner_bias, tall)], axis=0)
    shrunk = [
        (v - shrink_width * jnp.tanh(v * (1.0 / shrink_width))).astype(bf16)
        for v in activate(act, outer, outer_bias, tall)
    ]
    values = [jnp.concatenate(shrunk[2 * k : 2 * k + 2], axis=0) for k in range(GROUP)]
    bins_out(given, table_up, width, values)


def spectral_keep_kernel(tall, entries, inner, inner_bias, outer, outer_bias, active, slope, damp):
    acts = []
    for n, v in enumerate(activate(entries[...], inner, inner_bias, tall)):
        cdf, der = phi_parts(v)
        acts.append((v * cdf).astype(bf16))
        slope[n * tall : (n + 1) * tall, :] = der.astype(bf16)
    act = jnp.concatenate(acts, axis=0)
    active[...] = act
    for n, v in enumerate(activate(act, outer, outer_bias, tall)):
        t = jnp.tanh(v * (1.0 / shrink_width))
        damp[n * tall : (n + 1) * tall, :] = (t * t).astype(bf16)


def joined(refs):
    return jnp.concatenate([r[...] for r in refs], axis=1) if len(refs) > 1 else refs[0][...]


def spectral_backward_kernel(factor, parties, *refs):
    held, refs = refs[:PARTS], refs[PARTS:]
    table_down, table_up, inner_t, outer_t = refs[:4]
    slope, damp = joined(refs[4 : 4 + parties]), joined(refs[4 + parties : 4 + 2 * parties])
    refs = refs[4 + 2 * parties :]
    given, refs = refs[:PARTS], refs[PARTS:]
    inner_low, inner_bias_grad, outer_low, outer_bias_grad = refs
    width = inner_t.shape[2]
    tall = table_up.shape[0] // 2

    @pl.when(pl.program_id(0) == 0)
    def _():
        for ref in (inner_bias_grad, outer_bias_grad):
            ref[...] = jnp.zeros_like(ref)

    spec = bins_in(held, table_down, width, 0, False)
    grads = []
    sums = [0.0, 0.0]
    for k in range(GROUP):
        for side in range(2):
            at = (2 * k + side) * tall
            g = spec[k][side * tall : (side + 1) * tall] * factor
            g = g * damp[at : at + tall].astype(f32)
            sums[side] = sums[side] + jnp.sum(g, axis=0, keepdims=True)
            grads.append(g.astype(bf16))
    outer_bias_grad[...] += jnp.concatenate(sums, axis=0)
    low = jnp.concatenate(grads, axis=0)
    outer_low[...] = low
    parts = complex_product(low, outer_t[0], outer_t[1], GROUP, tall, True)
    grads = []
    sums = [0.0, 0.0]
    for n, part in enumerate(parts):
        g = part * slope[n * tall : (n + 1) * tall].astype(f32)
        sums[n % 2] = sums[n % 2] + jnp.sum(g, axis=0, keepdims=True)
        grads.append(g.astype(bf16))
    inner_bias_grad[...] += jnp.concatenate(sums, axis=0)
    low = jnp.concatenate(grads, axis=0)
    inner_low[...] = low
    parts = complex_product(low, inner_t[0], inner_t[1], GROUP, tall, True)
    values = [
        jnp.concatenate([parts[2 * k], parts[2 * k + 1]], axis=0).astype(bf16)
        for k in range(GROUP)
    ]
    bins_out(given, table_up, width, values)


def filter_grad_kernel(tall, parties, *refs):
    entries, active = refs[:parties], refs[parties : 2 * parties]
    inner_low, outer_low, inner_grad, outer_grad = refs[2 * parties :]

    @pl.when(pl.program_id(0) == 0)
    def _():
        inner_grad[...] = jnp.zeros_like(inner_grad)
        outer_grad[...] = jnp.zeros_like(outer_grad)

    for before, low, grad in ((entries, inner_low, inner_grad), (active, outer_low, outer_grad)):
        turned = []
        for k in range(GROUP):
            top, bottom = low[2 * k * tall : (2 * k + 1) * tall], low[(2 * k + 1) * tall : (2 * k + 2) * tall]
            turned += [bottom, -top]
        known = joined(before)
        grad[0] += dot_tn(known, low[...])
        grad[1] += dot_tn(known, jnp.concatenate(turned, axis=0))


def dense_kernel(steps, slabs, width, first_part, arrays, *refs):
    spat, refs = refs[:arrays], refs[arrays:]
    (
        states, cot, mask, first_gain, first_shift, later_gain, later_shift,
        expand_bias, reduce_bias, expand_hbm, reduce_hbm,
    ) = refs[:11]
    refs = refs[11:]
    if not first_part:
        grads_before = refs[0]
        refs = refs[2:]
    back, refs = refs[:1], refs[1:]
    result, later_grad, sums, expand_bias_grad, grads_hbm = refs[:5]
    (
        expand, reduce, expand_grad, reduce_grad, mixed, normed, low_out, branch, grad_n,
        hidden_all, grad_all, copy_sem,
    ) = refs[5:]
    step = pl.program_id(0)
    chans = states.shape[3]
    side_tokens = states.shape[1] * states.shape[2]
    slab = expand.shape[2]
    tokens = mixed.shape[0]
    square = states.shape[1:]

    def parts_of(grads):
        pairs = [(grads.at[pl.ds(s * chans, chans)], expand_grad.at[s]) for s in range(slabs)]
        return pairs + [(grads.at[pl.ds(slabs * chans, slabs * slab)], reduce_grad)]

    def fetches():
        copies = [
            pltpu.make_async_copy(
                expand_hbm.at[:, pl.ds(s * slab, slab)], expand.at[s], copy_sem.at[s]
            )
            for s in range(slabs)
        ]
        copies.append(pltpu.make_async_copy(reduce_hbm, reduce, copy_sem.at[slabs]))
        if not first_part:
            copies += [
                pltpu.make_async_copy(far, near, copy_sem.at[slabs + 1 + n])
                for n, (far, near) in enumerate(parts_of(grads_before))
            ]
        return copies

    @pl.when(step == 0)
    def _():
        for c in fetches():
            c.start()
        if first_part:
            expand_grad[...] = jnp.zeros_like(expand_grad)
            reduce_grad[...] = jnp.zeros_like(reduce_grad)
        sums[...] = jnp.zeros_like(sums)
        expand_bias_grad[...] = jnp.zeros_like(expand_bias_grad)

    @pl.when(step < steps)
    def _():
        start = pl.multiple_of(step * (PAIR * side_tokens), PAIR * side_tokens)
        for half in range(PAIR):
            at = pl.ds(start + half * side_tokens, side_tokens)
            inside = mask[half][..., :1]
            lower = inside * states[half].astype(f32)
            first, _ = standardize(lower)
            filter_in = first * first_gain[...] + first_shift[...]
            full = lower + inside * (unpack(spat, half, width, step) + filter_in)
            later, _ = standardize(full)
            full = full.reshape(side_tokens, chans)
            mixed[at, :] = full
            branch[at, :] = full + reduce_bias[...]
            normal = (later * later_gain[...] + later_shift[...]).reshape(side_tokens, chans)
            normed[at, :] = normal.astype(bf16)
            go = (inside * cot[half].astype(f32)).reshape(side_tokens, chans)
            low_out[at, :] = go.astype(bf16)
            grad_n[at, :] = jnp.zeros_like(full)
            sums[0:1, :] += jnp.sum(go, axis=0, keepdims=True)

    @pl.when(step == steps)
    def _():
        for c in fetches():
            c.wait()

    @pl.when((step >= steps) & (step < steps + slabs))
    def _():
        hc = step - steps
        at = pl.ds(pl.multiple_of(hc * slab, slab), slab)
        piece = tokens // 4 if tokens % 64 == 0 else tokens

        def some(n, carry):
            here = pl.ds(pl.multiple_of(n * piece, piece), piece)
            weight_up = expand[hc]
            weight_down = reduce[at, :]
            go = low_out[here, :]
            pre = dot(normed[here, :], weight_up) + expand_bias[...]
            cdf, der = phi_parts(pre)
            hidden = (pre * cdf).astype(bf16)
            hidden_all[here, :] = hidden
            branch[here, :] += dot(hidden, weight_down)
            grad_pre = dot_nt(go, weight_down) * der
            expand_bias_grad[pl.ds(hc, 1), :] += jnp.sum(grad_pre, axis=0, keepdims=True)
            grad_low = grad_pre.astype(bf16)
            grad_all[here, :] = grad_low
            grad_n[here, :] += dot_nt(grad_low, weight_up)
            return carry

        lax.fori_loop(0, tokens // piece, some, 0)
        reduce_grad[at, :] += dot_tn(hidden_all[...], low_out[...])
        expand_grad[hc] += dot_tn(normed[...], grad_all[...])

    @pl.when(step >= steps + slabs)
    def _():
        start = pl.multiple_of(
            (step - steps - slabs) * (PAIR * side_tokens), PAIR * side_tokens
        )
        sides = []
        for half in range(PAIR):
            at = pl.ds(start + half * side_tokens, side_tokens)
            inside = mask[half][..., :1]
            later, scale = standardize(mixed[at, :])
            g = grad_n[at, :]
            sums[1:2, :] += jnp.sum(g * later, axis=0, keepdims=True)
            sums[2:3, :] += jnp.sum(g, axis=0, keepdims=True)
            g = low_out[at, :].astype(f32) + standardize_back(g * later_gain[...], later, scale)
            sides.append(inside * g.reshape(square))
            later_grad[half] = sides[-1]
            result[half] = (inside * branch[at, :].reshape(square)).astype(bf16)
        pack(sides, back, width, step - steps - slabs)

    @pl.when(step == pl.num_programs(0) - 1)
    def _():
        copies = [
            pltpu.make_async_copy(near, far, copy_sem.at[n])
            for n, (far, near) in enumerate(parts_of(grads_hbm))
        ]
        for c in copies:
            c.start()
        for c in copies:
            c.wait()


def last_kernel(width, arrays, *refs):
    spat, (states, later_grad, mask, gain) = refs[:arrays], refs[arrays : arrays + 4]
    out, sums = refs[-2:]
    chans = states.shape[3]

    @pl.when(pl.program_id(0) == 0)
    def _():
        sums[...] = jnp.zeros_like(sums)

    for half in range(PAIR):
        inside = mask[half][..., :1]
        normal, scale = standardize(inside * states[half].astype(f32))
        grad_mixed = later_grad[half]
        grad = inside * (grad_mixed + unpack(spat, half, width, pl.program_id(0)))
        flat = (-1, chans)
        sums[0:1, :] += jnp.sum((grad * normal).reshape(flat), axis=0, keepdims=True)
        sums[1:2, :] += jnp.sum(grad.reshape(flat), axis=0, keepdims=True)
        grad = grad_mixed + standardize_back(grad * gain[...], normal, scale)
        out[half] = (inside * grad).astype(bf16)


def row_copies(ranks, sources, slots, send, recv):
    my_row = lax.axis_index("rows")
    return [
        pltpu.make_async_remote_copy(
            src_ref=sources(i),
            dst_ref=slots.at[i],
            send_sem=send.at[i],
            recv_sem=recv.at[i],
            device_id=(lax.rem(my_row + i, ranks), lax.axis_index("cols")),
            device_id_type=pl.DeviceIdType.MESH,
        )
        for i in range(1, ranks)
    ]


def row_piece(r, piece):
    return pl.ds(pl.multiple_of(r * piece, piece), piece)


def pick_kernel(ranks, flat, out, picked, send, recv):
    my_row = lax.axis_index("rows")
    piece = out.shape[0]
    barrier = pltpu.get_barrier_semaphore()
    for i in range(1, ranks):
        pl.semaphore_signal(
            barrier,
            inc=1,
            device_id=(lax.rem(my_row + i, ranks), lax.axis_index("cols")),
            device_id_type=pl.DeviceIdType.MESH,
        )
    pl.semaphore_wait(barrier, ranks - 1)
    copies = row_copies(
        ranks, lambda i: flat.at[row_piece(lax.rem(my_row + i, ranks), piece)], picked, send, recv
    )
    for c in copies:
        c.start()
    for c in copies:
        c.wait()
    total = flat[row_piece(my_row, piece), :]
    for i in range(1, ranks):
        total = total + picked[i]
    out[...] = total


def sum_kernel(
    ranks, groups, own, mine, out, flat_out, got, done, send_sem, recv_sem, give_send, give_recv
):
    devices = ranks * groups
    my_row = lax.axis_index("rows")
    me = my_row * groups + lax.axis_index("cols")
    piece = mine.shape[0]

    def place(i):
        other = lax.rem(me + i, devices)
        return lax.div(other, groups), lax.rem(other, groups)

    def copy(i):
        return pltpu.make_async_remote_copy(
            src_ref=own,
            dst_ref=got.at[i],
            send_sem=send_sem.at[i],
            recv_sem=recv_sem.at[i],
            device_id=place(i),
            device_id_type=pl.DeviceIdType.MESH,
        )

    barrier = pltpu.get_barrier_semaphore()

    def greet(i, carry):
        pl.semaphore_signal(
            barrier, inc=1, device_id=place(i), device_id_type=pl.DeviceIdType.MESH
        )
        return carry

    def start(i, carry):
        copy(i).start()
        return carry

    def finish(i, carry):
        copy(i).wait()
        return carry

    lax.fori_loop(1, devices, greet, 0)
    pl.semaphore_wait(barrier, devices - 1)
    gives = row_copies(ranks, lambda i: mine, done, give_send, give_recv)
    for c in gives:
        c.start()
    lax.fori_loop(1, devices, start, 0)
    flat_out[row_piece(my_row, piece), :] = mine[...]
    lax.fori_loop(1, devices, finish, 0)
    out[...] = lax.fori_loop(1, devices, lambda i, total: total + got[i], own[...])
    for c in gives:
        c.wait()
    for i in range(1, ranks):
        flat_out[row_piece(lax.rem(my_row - i + ranks, ranks), piece), :] = done[i]


def split_kernel(expand_in, reduce_in, expand_out, reduce_out):
    expand_out[...] = expand_in[...]
    reduce_out[...] = reduce_in[...]


def wide_tables(width):
    freq = np.arange(BINS)
    place = np.arange(width)
    angle = (freq[:, None] * place[None, :] % width) * (2.0 * math.pi / width)
    live = (2 * freq <= width).astype(np.float64)[:, None]
    edge = (freq == 0) | (2 * freq == width)
    weight = np.where(edge, 1.0, 2.0)[:, None] * live
    cosine, sine = np.cos(angle), np.sin(angle)
    plain = np.concatenate([live * cosine, -live * sine], axis=0)
    doubled = np.concatenate([weight * cosine, -weight * sine], axis=0)
    return plain, doubled


def tall_tables(height, rows_here):
    pairs = rows_here // PAIR
    rows = pairs // PARTS
    order = np.array(
        [
            r * rows_here + h * pairs + q * rows + j
            for h in range(PAIR)
            for q in range(PARTS)
            for r in range(height // rows_here)
            for j in range(rows)
        ]
    )
    freq = np.arange(height)
    angle = (freq[:, None] * order[None, :] % height) * (2.0 * math.pi / height)
    cosine, sine = np.cos(angle), np.sin(angle)
    down = np.block([[cosine, sine], [-sine, cosine]])
    up = np.block([[cosine.T, -sine.T], [sine.T, cosine.T]])
    return down, up


def spread(weight):
    count = weight.shape[1]
    eye = jnp.eye(count, dtype=weight.dtype)
    full = jnp.einsum("rbio,bd->rbido", weight, eye)
    return full.reshape(2, count * BS, count * BS)


def gather_blocks(full):
    count = full.shape[1] // BS
    return jnp.stack(
        [full[:, b * BS : (b + 1) * BS, b * BS : (b + 1) * BS] for b in range(count)], axis=1
    )


def bias_rows(bias):
    return bias.reshape(2, -1)


def whole(shape):
    return pl.BlockSpec(shape, lambda *_: (0,) * len(shape))


def call(kernel, grid, in_specs, out_specs, out_shape, name, flops=0, nbytes=0, scratch=(), **kw):
    return pl.pallas_call(
        kernel,
        grid=(grid,),
        in_specs=in_specs,
        out_specs=out_specs,
        out_shape=out_shape,
        scratch_shapes=scratch,
        compiler_params=pltpu.CompilerParams(
            dimension_semantics=("arbitrary",), vmem_limit_bytes=VMEM
        ),
        cost_estimate=pl.CostEstimate(flops=flops, bytes_accessed=nbytes, transcendentals=0),
        name=name,
        **kw,
    )


def body(
    states,
    heights,
    widths,
    first_gain,
    first_shift,
    filter_inner,
    inner_bias,
    filter_outer,
    outer_bias,
    later_gain,
    later_shift,
    expand_weight,
    expand_bias,
    reduce_weight,
    reduce_bias,
    cotangent,
):
    frames, rows_here, cols_here, chans = states.shape
    ranks, groups = lax.axis_size("rows"), lax.axis_size("cols")
    assert frames == ranks and rows_here % (PAIR * PARTS) == 0
    height, breadth = rows_here * ranks, cols_here * groups
    devices = ranks * groups
    pairs = rows_here // PAIR
    rows = pairs // PARTS
    pixels = rows * cols_here
    width = chans // groups
    lanes = width * PAIR
    hidden = expand_weight.shape[1]
    factor = 1.0 / math.sqrt(height * breadth)
    short = ranks * rows
    step_pixels = 8 if pixels % 8 == 0 else pixels
    steps = pixels // step_pixels
    tokens = PAIR * pixels * frames
    message = devices * pixels * lanes * 4
    row = lambda v: v.reshape(1, -1)
    shape = jax.ShapeDtypeStruct

    order = lambda v: jnp.transpose(v, (1, 2, 0, 3)).reshape(PAIR, pairs * cols_here, frames, chans)
    restore = lambda v: jnp.transpose(v.reshape(rows_here, cols_here, frames, chans), (2, 0, 1, 3))
    states_in, cot_in = order(states), order(cotangent)
    row_ids = lax.axis_index("rows") * rows_here + jnp.arange(rows_here, dtype=jnp.int32)
    col_ids = lax.axis_index("cols") * cols_here + jnp.arange(cols_here, dtype=jnp.int32)
    inside = (row_ids[:, None, None] < heights) & (col_ids[None, :, None] < widths)
    mask = jnp.broadcast_to(
        inside.astype(f32).reshape(PAIR, pairs * cols_here, frames, 1),
        (PAIR, pairs * cols_here, frames, 128),
    )

    buffers = {} if steps > 1 else {"pipeline_mode": pl.Buffered(1)}

    def token_spec(q, where, last=chans):
        return pl.BlockSpec(
            (PAIR, step_pixels, frames, last), lambda i: (0, q * steps + where(i), 0, 0), **buffers
        )

    def packed_spec(where):
        return pl.BlockSpec(
            (ranks, groups, step_pixels, lanes), lambda i: (0, 0, where(i), 0), **buffers
        )

    blocks_here = width // BS
    split = blocks_here > 1 and steps > 1 and (2 * PAIR * BS) % 128 == 0
    parties = blocks_here if split else 1
    cut = width // parties
    split_rows = 8 * (-(-steps // 2))

    def arrays_of(q):
        return parties if q == 0 else 1

    def message_specs(q, where):
        if arrays_of(q) == 1:
            return [packed_spec(where)]
        return [
            pl.BlockSpec(
                (ranks, groups, step_pixels, 2 * PAIR * cut), lambda i: (0, 0, where(i) // 2, 0)
            )
        ] * parties

    def message_shapes(q):
        if arrays_of(q) == 1:
            return [packed_shape]
        return [shape((ranks, groups, split_rows, 2 * PAIR * cut), f32)] * parties

    same = lambda i: i
    token_shape = shape((PAIR, pairs * cols_here, frames, chans), bf16)
    packed_shape = shape((ranks, groups, pixels, lanes), f32)
    chan_row = whole((1, chans))
    anywhere = pl.BlockSpec(memory_space=pl.ANY)

    def scatter(v, axis):
        return lax.psum_scatter(v, axis, scatter_dimension=0, tiled=True)

    def gather(v, axis):
        return lax.all_gather(v, axis, axis=0, tiled=True)

    vmem = pl.BlockSpec(memory_space=pltpu.VMEM)

    def as_rows(v, unit):
        v = v.reshape(-1)
        return jnp.pad(v, (0, -v.shape[0] % (unit * 128))).reshape(-1, 128)

    def pick_sums(v):
        flat = as_rows(v, 8 * ranks)
        piece = (flat.shape[0] // ranks, 128)
        return pl.pallas_call(
            functools.partial(pick_kernel, ranks),
            in_specs=[vmem],
            out_specs=vmem,
            out_shape=shape(piece, f32),
            scratch_shapes=[pltpu.VMEM((ranks,) + piece, f32)]
            + [pltpu.SemaphoreType.DMA((ranks,))] * 2,
            compiler_params=pltpu.CompilerParams(collective_id=1, has_side_effects=True),
            name="filter_sums",
        )(flat)

    def sum_small(v, mine):
        own = as_rows(v, 8)
        out, flat_out = pl.pallas_call(
            functools.partial(sum_kernel, ranks, groups),
            in_specs=[vmem, vmem],
            out_specs=[vmem, vmem],
            out_shape=[shape(own.shape, f32), shape((ranks * mine.shape[0], 128), f32)],
            scratch_shapes=[
                pltpu.VMEM((devices,) + own.shape, f32),
                pltpu.VMEM((ranks,) + mine.shape, f32),
            ]
            + [pltpu.SemaphoreType.DMA((devices,))] * 2
            + [pltpu.SemaphoreType.DMA((ranks,))] * 2,
            compiler_params=pltpu.CompilerParams(collective_id=0, has_side_effects=True),
            name="small_sums",
        )(own, mine)
        return out.reshape(-1)[: v.size].reshape(v.shape), flat_out.reshape(-1)

    def split_grads(v):
        cuts = 4
        piece = (chans // cuts, chans)
        return call(
            split_kernel,
            slabs * cuts,
            [
                pl.BlockSpec(piece, lambda i: (i, 0)),
                pl.BlockSpec(piece, lambda i: (slabs * cuts + i, 0)),
            ],
            [
                pl.BlockSpec(piece, lambda i: (lax.rem(i, cuts), lax.div(i, cuts))),
                pl.BlockSpec(piece, lambda i: (i, 0)),
            ],
            [shape((chans, hidden), f32), shape((hidden, chans), f32)],
            "split_gradients",
            nbytes=16 * chans * hidden,
        )(v, v)

    def behind(v, *after):
        return lax.optimization_barrier((v,) + after)[0] if after else v

    def exchange(v):
        sent = v.reshape((devices,) + v.shape[2:])
        return lax.all_to_all(sent, ("rows", "cols"), 0, 0, tiled=True).reshape(v.shape)

    def tie(*values):
        return lax.optimization_barrier(values)

    def first_norm(q):
        return call(
            functools.partial(first_kernel, width),
            steps,
            [token_spec(q, same), token_spec(q, same, 128), chan_row, chan_row],
            message_specs(q, same),
            message_shapes(q),
            "first_norm",
            nbytes=2 * message,
        )(states_in, mask, row(first_gain), row(first_shift))

    plain, doubled = wide_tables(breadth)
    down, up = tall_tables(height, rows_here)
    as_table = lambda t: jnp.asarray(t, dtype=bf16)

    def fine_table(t):
        high = t.astype(jnp.bfloat16)
        return jnp.asarray(np.concatenate([high, (t - high.astype(np.float64)).astype(jnp.bfloat16)]))

    def mixes(weight):
        return [weight[:, g] for g in range(parties)] if split else [spread(weight)]

    inner_full, outer_full = mixes(filter_inner), mixes(filter_outer)
    turn = lambda t: jnp.swapaxes(t, 1, 2)
    bin_steps = BINS // GROUP
    group_rows = GROUP * 2 * height
    held_shape = shape((short, 2, BINS, lanes), f32)
    at_once = 2
    held_row = pl.BlockSpec((at_once * rows, 2, BINS, lanes), lambda i: (i, 0, 0, 0))
    held_bins = pl.BlockSpec((short, 2, GROUP, lanes), lambda i: (0, 0, i, 0))
    field = pl.BlockSpec((at_once, groups, pixels, lanes), lambda i: (i, 0, 0, 0))
    kept = pl.BlockSpec((group_rows, cut), lambda i: (i, 0))
    kept_shape = shape((bin_steps * group_rows, cut), bf16)
    mix_spec = whole((2, cut, cut))
    bias_spec = whole((2, cut))

    def held_of(last, by_row):
        if by_row:
            return pl.BlockSpec((at_once * rows, 2, BINS, last), lambda i: (i, 0, 0, 0))
        return pl.BlockSpec((short, 2, GROUP, last), lambda i: (0, 0, i, 0))

    cut_shape = shape((short, 2, BINS, PAIR * cut), f32)
    split_field = pl.BlockSpec(
        (at_once, groups, split_rows, 2 * PAIR * cut), lambda i: (i, 0, 0, 0)
    )
    natural = pltpu.VMEM((at_once, groups, pixels, PAIR * cut), f32)
    cut_in = [held_of(PAIR * cut if split else lanes, False)] + [held_bins] * (PARTS - 1)
    cut_out = [held_of(PAIR * cut, False)] * PARTS
    up_spec = whole((2 * height, 2 * height))

    def wide_in(v, table, fine):
        divided = v.shape != packed_shape.shape
        return call(
            functools.partial(wide_in_split_kernel if divided else wide_in_kernel, cols_here, fine),
            ranks // at_once,
            [split_field if divided else field, whole(table.shape)],
            held_of(PAIR * cut, True) if divided else held_row,
            cut_shape if divided else held_shape,
            "wide_in",
            nbytes=2 * message,
            scratch=[pltpu.VMEM((at_once * rows, breadth, PAIR * cut), f32), natural]
            if divided
            else [pltpu.VMEM((at_once * rows, breadth, lanes), f32)],
        )(v, table)

    def wide_out(parts, table):
        return call(
            functools.partial(wide_out_kernel, cols_here, factor),
            ranks // at_once,
            [held_of(v.shape[3], True) for v in parts] + [whole(table.shape)],
            field,
            packed_shape,
            "wide_out",
            nbytes=2 * message,
        )(*parts, table)

    def wide_out_split(part, table):
        return call(
            functools.partial(wide_out_split_kernel, cols_here, factor),
            ranks // at_once,
            [held_of(PAIR * cut, True), whole(table.shape)],
            split_field,
            message_shapes(0)[0],
            "wide_out",
            nbytes=2 * message,
            scratch=[natural],
        )(part, table)

    def messages_out(given, table):
        first = [wide_out_split(v[0], table) for v in given] if split else [wide_out([given[0][0]], table)]
        return first + [wide_out([v[q] for v in given], table) for q in range(1, PARTS)]

    def of_group(v, g):
        return bias_rows(v)[:, g * cut : (g + 1) * cut]

    forward_mix = [
        (inner_full[g], of_group(inner_bias, g), outer_full[g], of_group(outer_bias, g))
        for g in range(parties)
    ]
    forward_specs = [mix_spec, bias_spec, mix_spec, bias_spec]

    def spectral_forward(g, held):
        table = fine_table(down)
        outs = call(
            functools.partial(spectral_forward_kernel, factor, g),
            bin_steps,
            cut_in + [whole(table.shape), up_spec] + forward_specs,
            cut_out + [kept],
            [cut_shape] * PARTS + [kept_shape],
            "spectral_forward",
            flops=20 * 10**9,
            nbytes=8 * PARTS * message // parties,
        )(*held, table, as_table(up), *forward_mix[g])
        return outs[:PARTS], outs[PARTS]

    def spectral_keep(g, entries):
        return call(
            functools.partial(spectral_keep_kernel, height),
            bin_steps,
            [kept] + forward_specs,
            [kept] * 3,
            [kept_shape] * 3,
            "spectral_keep",
            flops=10 * 10**9,
            nbytes=2 * PARTS * message // parties,
        )(entries, *forward_mix[g])

    full = pl.BlockSpec((group_rows, width), lambda i: (i, 0))
    full_shape = shape((bin_steps * group_rows, width), bf16)
    full_mix, full_bias = whole((2, width, width)), whole((2, width))
    inner_t, outer_t = turn(spread(filter_inner)), turn(spread(filter_outer))

    def spectral_backward(held, slope, damp):
        outs = call(
            functools.partial(spectral_backward_kernel, factor, parties),
            bin_steps,
            [held_bins] * PARTS + [up_spec, up_spec, full_mix, full_mix] + [kept] * (2 * parties),
            [held_bins] * PARTS + [full, full_bias] * 2,
            [held_shape] * PARTS + [full_shape, shape((2, width), f32)] * 2,
            "spectral_backward",
            flops=20 * 10**9,
            nbytes=8 * PARTS * message,
        )(*held, as_table(down), as_table(up), inner_t, outer_t, *slope, *damp)
        return outs[:PARTS], outs[PARTS:]

    def filter_grad(entries, active, inner_low, outer_low):
        return call(
            functools.partial(filter_grad_kernel, height, parties),
            bin_steps,
            [kept] * (2 * parties) + [full] * 2,
            [full_mix] * 2,
            [shape((2, width, width), f32)] * 2,
            "filter_grad",
            flops=10 * 10**9,
            nbytes=2 * PARTS * message,
        )(*entries, *active, inner_low, outer_low)

    slab = chans
    slabs = hidden // slab
    dense_steps = 2 * steps + slabs
    enter = lambda i: jnp.minimum(i, steps - 1)
    leave = lambda i: jnp.maximum(i - steps - slabs, 0)
    either = lambda i: jnp.where(i < steps + slabs, enter(i), leave(i))

    def dense(q, spatial, before):
        grads_before = () if q == 0 else before
        return call(
            functools.partial(dense_kernel, steps, slabs, width, q == 0, arrays_of(q)),
            dense_steps,
            message_specs(q, enter)
            + [token_spec(q, enter), token_spec(q, enter), token_spec(q, either, 128)]
            + [chan_row] * 4
            + [pl.BlockSpec((1, slab), lambda i: (0, jnp.clip(i - steps, 0, slabs - 1)))]
            + [chan_row]
            + [anywhere] * (2 + len(grads_before)),
            [packed_spec(leave)]
            + [
                token_spec(q, leave),
                token_spec(0, leave),
                whole((8, chans)),
                whole((slabs, slab)),
                anywhere,
            ],
            [packed_shape]
            + [
                token_shape,
                shape((PAIR, pixels, frames, chans), f32),
                shape((8, chans), f32),
                shape((slabs, slab), f32),
                shape((2 * hidden, chans), f32),
            ],
            "dense_both_ways",
            flops=12 * tokens * chans * hidden,
            nbytes=4 * message,
            scratch=[
                pltpu.VMEM((slabs, chans, slab), bf16),
                pltpu.VMEM((hidden, chans), bf16),
                pltpu.VMEM((slabs, chans, slab), f32),
                pltpu.VMEM((hidden, chans), f32),
                pltpu.VMEM((tokens, chans), f32),
                pltpu.VMEM((tokens, chans), bf16),
                pltpu.VMEM((tokens, chans), bf16),
                pltpu.VMEM((tokens, chans), f32),
                pltpu.VMEM((tokens, chans), f32),
                pltpu.VMEM((tokens, slab), bf16),
                pltpu.VMEM((tokens, slab), bf16),
                pltpu.SemaphoreType.DMA((2 * slabs + 2,)),
            ],
            input_output_aliases={} if q == 0 else {13: 1},
        )(
            *spatial,
            states_in,
            cot_in,
            mask,
            row(first_gain),
            row(first_shift),
            row(later_gain),
            row(later_shift),
            row(expand_bias),
            row(reduce_bias),
            expand_weight,
            reduce_weight,
            *grads_before,
        )

    def last_norm(q, later_grad, spatial, before):
        given = () if q == 0 else (before,)
        return call(
            functools.partial(last_kernel, width, 1),
            steps,
            [packed_spec(same)]
            + [token_spec(q, same), token_spec(0, same), token_spec(q, same, 128)]
            + [chan_row]
            + [anywhere] * len(given),
            [token_spec(q, same), whole((8, chans))],
            [token_shape, shape((8, chans), f32)],
            "first_norm_backward",
            nbytes=4 * message,
            input_output_aliases={} if q == 0 else {5: 0},
        )(spatial, states_in, later_grad, mask, row(first_gain), *given)

    every = range(PARTS)

    def send(made, got):
        if got:
            made, got[-1] = tie(made, got[-1])
        got.append(exchange(made))

    made = [v for q in (*every[1:], 0) for v in first_norm(q)]
    got, held = [], []
    for n, v in enumerate(made):
        if n > 1:
            v, held[-1] = tie(v, held[-1])
        send(v, got)
        if n > 0:
            held.append(wide_in(got[-2], fine_table(plain), True))
    held.append(wide_in(got[-1], fine_table(plain), True))
    rest, first = held[: PARTS - 1], held[PARTS - 1 :]
    done = [spectral_forward(g, [first[g]] + rest) for g in range(parties)]
    entries = [v[1] for v in done]
    made = messages_out([v[0] for v in done], as_table(doubled.T))
    keeps = [list(spectral_keep(g, entries[g])) for g in range(parties)]

    spatial = got[-1:]
    for n in range(parties):
        send(made[n], spatial)
    for keep in keeps:
        keep[0], made[parties] = tie(keep[0], made[parties])
    spatial = spatial[1:]
    backs, later_grads, sums, expand_bias_grad, before = [], [], 0.0, 0.0, ()
    for q in every:
        if q + 1 < PARTS:
            if backs:
                made[parties + q], backs[-1] = tie(made[parties + q], backs[-1])
            send(made[parties + q], spatial)
        received = spatial[:parties] if q == 0 else spatial[parties + q - 1 : parties + q]
        if q + 1 == PARTS:
            backs[-1], spatial[-1] = tie(backs[-1], spatial[-1])
            got = [exchange(backs[1])]
            received = spatial[-1:]
        outs = dense(q, received, before)
        back, result, kept_grad, part, bias_part, grads = outs
        backs.append(back)
        before = (grads, result)
        later_grads.append(kept_grad)
        sums, expand_bias_grad = sums + part, expand_bias_grad + bias_part
    grads, got[0] = tie(grads, got[0])
    grads = scatter(grads, "cols")
    held = []
    for v in [backs[q] for q in (*every[2:], 0)]:
        held.append(wide_in(got[-1], as_table(doubled), False))
        if len(held) > 1:
            v, held[-2] = tie(v, held[-2])
        send(v, got)
    got[-1], held[-1] = tie(got[-1], held[-1])
    held.append(wide_in(got[-1], as_table(doubled), False))
    grads, held[-1] = tie(grads, held[-1])
    grads = scatter(grads, "rows")
    given, (inner_low, inner_bias_grad, outer_low, outer_bias_grad) = spectral_backward(
        [held[-1]] + held[:-1], [k[1] for k in keeps], [k[2] for k in keeps]
    )
    made = [wide_out([v], as_table(plain.T)) for v in given]
    inner_grad, outer_grad = filter_grad(entries, [k[0] for k in keeps], inner_low, outer_low)
    filter_parts = (
        gather_blocks(inner_grad), inner_bias_grad, gather_blocks(outer_grad), outer_bias_grad
    )
    flat = jnp.concatenate([v.reshape(-1) for v in filter_parts])

    got = [exchange(made[0])]
    send(made[1], got)
    grads, got[0] = tie(grads, got[0])
    grads = gather(grads, ("cols", "rows"))
    expand_sum, reduce_sum = split_grads(grads)
    first_sums, states_grad = [], None
    for q in every:
        if q + 1 < PARTS:
            if q > 0:
                made[q + 1], first_sums[-1] = tie(made[q + 1], first_sums[-1])
                send(made[q + 1], got)
        else:
            states_grad, expand_sum = tie(states_grad, expand_sum)
        states_grad, part = last_norm(q, later_grads[q], got[q], states_grad)
        first_sums.append(part)
        if q == 0:
            flat, first_sums[0] = tie(flat, first_sums[0])
            flat = pick_sums(flat)
            made[2], flat = tie(made[2], flat)
    small, flat = sum_small(
        jnp.concatenate([sum(first_sums)[:2], sums[:3], expand_bias_grad.reshape(-1, chans)]), flat
    )
    sizes = [v.size for v in filter_parts]
    ends = np.cumsum(sizes)
    filter_sums = [
        flat[e - n : e].reshape(v.shape) for e, n, v in zip(ends, sizes, filter_parts)
    ]
    inner_sum, inner_bias_sum, outer_sum, outer_bias_sum = filter_sums
    return (
        restore(result),
        restore(states_grad),
        small[0],
        small[1],
        inner_sum,
        inner_bias_sum.reshape(2, -1, BS),
        outer_sum,
        outer_bias_sum.reshape(2, -1, BS),
        small[3],
        small[4],
        expand_sum,
        small[5:].reshape(-1),
        reduce_sum,
        small[2],
    )


def solution(mesh):
    tile = P(None, "rows", "cols", None)
    mix = P(None, "cols", None, None)
    bias = P(None, "cols", None)
    in_specs = (
        tile, P(), P(), P(), P(), mix, bias, mix, bias, P(), P(), P(), P(), P(), P(), tile,
    )
    out_specs = (
        tile, tile, P(), P(), mix, bias, mix, bias, P(), P(), P(), P(), P(), P(),
    )
    return jax.shard_map(body, mesh=mesh, in_specs=in_specs, out_specs=out_specs, check_vma=False)
```

```python
import functools
import math

import jax
import jax.numpy as jnp
import numpy as np
from jax import lax
from jax.experimental import pallas as pl
from jax.experimental.pallas import tpu as pltpu
from jax.sharding import PartitionSpec as P

BS = 96
BINS = 96
PAIR = 2
GROUP = 8
PARTS = 3
norm_eps = 1e-06
shrink_width = 0.01
VMEM = 60 * 1024 * 1024
f32 = jnp.float32
bf16 = jnp.bfloat16


def phi_parts(v):
    cdf = 0.5 * (1.0 + lax.erf(v * math.sqrt(0.5)))
    slope = cdf + v * (jnp.exp(v * v * -0.5) * (1.0 / math.sqrt(2.0 * math.pi)))
    return cdf, slope


def dot(a, b):
    return lax.dot_general(a, b, (((1,), (0,)), ((), ())), preferred_element_type=f32)


def dot_tn(a, b):
    return lax.dot_general(a, b, (((0,), (0,)), ((), ())), preferred_element_type=f32)


def dot_nt(a, b):
    return lax.dot_general(a, b, (((1,), (1,)), ((), ())), preferred_element_type=f32)


def standardize(v):
    centre = jnp.mean(v, axis=-1, keepdims=True)
    centred = v - centre
    spread = jnp.mean(centred * centred, axis=-1, keepdims=True)
    scale = lax.rsqrt(spread + norm_eps)
    return centred * scale, scale


def standardize_back(grad, normal, scale):
    first = jnp.mean(grad, axis=-1, keepdims=True)
    second = jnp.mean(grad * normal, axis=-1, keepdims=True)
    return scale * (grad - first - normal * second)


def pack(sides, outs, width, step):
    turned = [jnp.swapaxes(s, 0, 1) for s in sides]
    cut = width // len(outs)

    def lanes_of(c, g):
        start = c * width + g * cut
        return jnp.concatenate([t[:, :, start : start + cut] for t in turned], axis=2)

    for g, out in enumerate(outs):
        values = [lanes_of(c, g) for c in range(out.shape[1])]
        if len(outs) == 1:
            for c, v in enumerate(values):
                out[:, c] = v
            continue

        @pl.when(lax.rem(step, 2) == 0)
        def _():
            for c, v in enumerate(values):
                out[:, c] = jnp.concatenate([v, v], axis=2)

        @pl.when(lax.rem(step, 2) == 1)
        def _():
            for c, v in enumerate(values):
                out[:, c] = jnp.concatenate([out[:, c, :, : PAIR * cut], v], axis=2)


def unpack(refs, half, width, step):
    cut = width // len(refs)
    parts = []
    for c in range(refs[0].shape[1]):
        for ref in refs:
            part = ref[:, c, :, half * cut : (half + 1) * cut]
            if len(refs) > 1:
                later = (PAIR + half) * cut
                part = jnp.where(lax.rem(step, 2) == 1, ref[:, c, :, later : later + cut], part)
            parts.append(part)
    return jnp.swapaxes(jnp.concatenate(parts, axis=2) if len(parts) > 1 else parts[0], 0, 1)


def first_kernel(width, states, mask, gain, shift, *outs):
    sides = []
    for half in range(PAIR):
        inside = mask[half][..., :1]
        normal, _ = standardize(states[half].astype(f32) * inside)
        sides.append(inside * (normal * gain[...] + shift[...]))
    pack(sides, outs, width, pl.program_id(0))


def table_dot(table, x):
    rows = table.shape[0] // 2
    high = x.astype(bf16)
    both = dot(table[...], high)
    rest = dot(table[:rows, :], (x - high.astype(f32)).astype(bf16))
    return both[:rows] + both[rows:] + rest


def wide_in_kernel(cols_here, fine, block, table, held, wide):
    groups, rows = block.shape[1], block.shape[2] // cols_here
    for n in range(block.shape[0] * rows):
        r, j = divmod(n, rows)
        for c in range(groups):
            wide[n, c * cols_here : (c + 1) * cols_here, :] = block[
                r, c, j * cols_here : (j + 1) * cols_here, :
            ]
        x = wide[n]
        y = table_dot(table, x) if fine else dot(table[...], x.astype(bf16))
        held[n, 0] = y[:BINS]
        held[n, 1] = y[BINS:]


def wide_out_kernel(cols_here, factor, *refs):
    held, (table, block) = refs[:-2], refs[-2:]
    groups, rows = block.shape[1], block.shape[2] // cols_here
    cut = held[0].shape[3] // PAIR
    for n in range(block.shape[0] * rows):
        r, j = divmod(n, rows)
        x = [jnp.concatenate([part[n, 0], part[n, 1]], axis=0) for part in held]
        if len(x) > 1:
            x = [part[:, h * cut : (h + 1) * cut] for h in range(PAIR) for part in x]
            x = jnp.concatenate(x, axis=1)
        else:
            x = x[0]
        plane = dot(table[...], x.astype(bf16)) * factor
        for c in range(groups):
            block[r, c, j * cols_here : (j + 1) * cols_here, :] = plane[
                c * cols_here : (c + 1) * cols_here, :
            ]


def wide_in_split_kernel(cols_here, fine, block, table, held, wide, natural):
    groups, half = block.shape[1], block.shape[3] // 2
    rows = natural.shape[2] // cols_here
    for r in range(block.shape[0]):
        for c in range(groups):
            for s in range(natural.shape[2] // 8):
                natural[r, c, s * 8 : s * 8 + 8, :] = block[
                    r, c, (s // 2) * 8 : (s // 2) * 8 + 8, (s % 2) * half : (s % 2 + 1) * half
                ]
        for j in range(rows):
            n = r * rows + j
            for c in range(groups):
                wide[n, c * cols_here : (c + 1) * cols_here, :] = natural[
                    r, c, j * cols_here : (j + 1) * cols_here, :
                ]
            x = wide[n]
            y = table_dot(table, x) if fine else dot(table[...], x.astype(bf16))
            held[n, 0] = y[:BINS]
            held[n, 1] = y[BINS:]


def wide_out_split_kernel(cols_here, factor, held, table, block, natural):
    groups = block.shape[1]
    rows = natural.shape[2] // cols_here
    last = natural.shape[2] // 8 - 1
    for r in range(block.shape[0]):
        for j in range(rows):
            n = r * rows + j
            x = jnp.concatenate([held[n, 0], held[n, 1]], axis=0).astype(bf16)
            plane = dot(table[...], x) * factor
            for c in range(groups):
                natural[r, c, j * cols_here : (j + 1) * cols_here, :] = plane[
                    c * cols_here : (c + 1) * cols_here, :
                ]
        for c in range(groups):
            for m in range(block.shape[2] // 8):
                sides = [natural[r, c, at * 8 : at * 8 + 8, :] for at in (2 * m, min(2 * m + 1, last))]
                block[r, c, m * 8 : m * 8 + 8, :] = jnp.concatenate(sides, axis=1)


def bins_in(held, table, width, group, fine):
    kind = f32 if fine else bf16

    def lane(part, h):
        whole_width = part.shape[-1] // PAIR
        return h * whole_width + (group * width if whole_width > width else 0)

    turned = [
        [jnp.swapaxes(part[:, side], 0, 1).astype(kind) for part in held] for side in range(2)
    ]
    outs = []
    for k in range(GROUP):
        x = jnp.concatenate(
            [
                part[k][:, lane(part, h) : lane(part, h) + width]
                for side in turned
                for h in range(PAIR)
                for part in side
            ],
            axis=0,
        )
        outs.append(table_dot(table, x) if fine else dot(table[...], x))
    return outs


def bins_out(held, table, width, values):
    short = held[0].shape[0]
    count = len(held)
    products = [dot(table[...], value) for value in values]
    for side in range(2):
        for q in range(count):
            rows = []
            for z in products:
                at = [((side * PAIR + h) * count + q) * short for h in range(PAIR)]
                rows.append(jnp.concatenate([z[a : a + short] for a in at], axis=1))
            held[q][:, side] = jnp.swapaxes(jnp.stack(rows, axis=0), 0, 1)


def halves(v, count, tall):
    return [
        (v[k * 2 * tall : k * 2 * tall + tall], v[k * 2 * tall + tall : (k + 1) * 2 * tall])
        for k in range(count)
    ]


def complex_product(x, first, second, count, tall, conj):
    a = dot(x, first)
    b = dot(x, second)
    parts = []
    for (a_re, a_im), (b_re, b_im) in zip(halves(a, count, tall), halves(b, count, tall)):
        if conj:
            parts += [a_re + b_im, a_im - b_re]
        else:
            parts += [a_re - b_im, a_im + b_re]
    return parts


def activate(low, mix, bias, tall):
    parts = complex_product(low, mix[0], mix[1], low.shape[0] // (2 * tall), tall, False)
    return [part + bias[n % 2 : n % 2 + 1, :] for n, part in enumerate(parts)]


def gelu_low(v):
    return (v * (0.5 * (1.0 + lax.erf(v * math.sqrt(0.5))))).astype(bf16)


def spectral_forward_kernel(factor, group, *refs):
    held, refs = refs[:PARTS], refs[PARTS:]
    table_down, table_up, inner, inner_bias, outer, outer_bias = refs[:6]
    given, entries = refs[6 : 6 + PARTS], refs[6 + PARTS]
    width = inner.shape[2]
    tall = table_up.shape[0] // 2
    spec = bins_in(held, table_down, width, group, True)
    low = jnp.concatenate([(s * factor).astype(bf16) for s in spec], axis=0)
    entries[...] = low
    act = jnp.concatenate([gelu_low(v) for v in activate(low, inner, inner_bias, tall)], axis=0)
    shrunk = [
        (v - shrink_width * jnp.tanh(v * (1.0 / shrink_width))).astype(bf16)
        for v in activate(act, outer, outer_bias, tall)
    ]
    values = [jnp.concatenate(shrunk[2 * k : 2 * k + 2], axis=0) for k in range(GROUP)]
    bins_out(given, table_up, width, values)


def spectral_keep_kernel(tall, parties, *refs):
    entries, refs = refs[:parties], refs[parties:]
    mixes, (active, slope, damp) = refs[: 4 * parties], refs[4 * parties :]

    def joined_parts(each):
        return [jnp.concatenate(v, axis=1) if parties > 1 else v[0] for v in zip(*each)]

    acts, slopes, damps = [], [], []
    for g in range(parties):
        inner, inner_bias, outer, outer_bias = mixes[4 * g : 4 * g + 4]
        acts.append([])
        slopes.append([])
        damps.append([])
        for v in activate(entries[g][...], inner, inner_bias, tall):
            cdf, der = phi_parts(v)
            acts[g].append((v * cdf).astype(bf16))
            slopes[g].append(der.astype(bf16))
        for v in activate(jnp.concatenate(acts[g], axis=0), outer, outer_bias, tall):
            t = jnp.tanh(v * (1.0 / shrink_width))
            damps[g].append((t * t).astype(bf16))
    for ref, each in ((active, acts), (slope, slopes), (damp, damps)):
        for n, v in enumerate(joined_parts(each)):
            ref[n * tall : (n + 1) * tall, :] = v


def joined(refs):
    return jnp.concatenate([r[...] for r in refs], axis=1) if len(refs) > 1 else refs[0][...]


def spectral_backward_kernel(factor, parties, *refs):
    held, refs = refs[:PARTS], refs[PARTS:]
    table_down, table_up, inner_t, outer_t = refs[:4]
    slope, damp = joined(refs[4 : 4 + parties]), joined(refs[4 + parties : 4 + 2 * parties])
    refs = refs[4 + 2 * parties :]
    given, refs = refs[:PARTS], refs[PARTS:]
    inner_low, inner_bias_grad, outer_low, outer_bias_grad = refs
    width = inner_t.shape[2]
    tall = table_up.shape[0] // 2

    @pl.when(pl.program_id(0) == 0)
    def _():
        for ref in (inner_bias_grad, outer_bias_grad):
            ref[...] = jnp.zeros_like(ref)

    spec = bins_in(held, table_down, width, 0, False)
    grads = []
    sums = [0.0, 0.0]
    for k in range(GROUP):
        for side in range(2):
            at = (2 * k + side) * tall
            g = spec[k][side * tall : (side + 1) * tall] * factor
            g = g * damp[at : at + tall].astype(f32)
            sums[side] = sums[side] + jnp.sum(g, axis=0, keepdims=True)
            grads.append(g.astype(bf16))
    outer_bias_grad[...] += jnp.concatenate(sums, axis=0)
    low = jnp.concatenate(grads, axis=0)
    outer_low[...] = low
    parts = complex_product(low, outer_t[0], outer_t[1], GROUP, tall, True)
    grads = []
    sums = [0.0, 0.0]
    for n, part in enumerate(parts):
        g = part * slope[n * tall : (n + 1) * tall].astype(f32)
        sums[n % 2] = sums[n % 2] + jnp.sum(g, axis=0, keepdims=True)
        grads.append(g.astype(bf16))
    inner_bias_grad[...] += jnp.concatenate(sums, axis=0)
    low = jnp.concatenate(grads, axis=0)
    inner_low[...] = low
    parts = complex_product(low, inner_t[0], inner_t[1], GROUP, tall, True)
    values = [
        jnp.concatenate([parts[2 * k], parts[2 * k + 1]], axis=0).astype(bf16)
        for k in range(GROUP)
    ]
    bins_out(given, table_up, width, values)


def filter_grad_kernel(tall, parties, *refs):
    entries, active = refs[:parties], refs[parties : parties + 1]
    inner_low, outer_low, inner_grad, outer_grad = refs[parties + 1 :]

    @pl.when(pl.program_id(0) == 0)
    def _():
        inner_grad[...] = jnp.zeros_like(inner_grad)
        outer_grad[...] = jnp.zeros_like(outer_grad)

    for before, low, grad in ((entries, inner_low, inner_grad), (active, outer_low, outer_grad)):
        turned = []
        for k in range(GROUP):
            top, bottom = low[2 * k * tall : (2 * k + 1) * tall], low[(2 * k + 1) * tall : (2 * k + 2) * tall]
            turned += [bottom, -top]
        known = joined(before)
        grad[0] += dot_tn(known, low[...])
        grad[1] += dot_tn(known, jnp.concatenate(turned, axis=0))


def dense_kernel(steps, slabs, width, first_part, arrays, *refs):
    spat, refs = refs[:arrays], refs[arrays:]
    (
        states, cot, mask, first_gain, first_shift, later_gain, later_shift,
        expand_bias, reduce_bias, expand_hbm, reduce_hbm,
    ) = refs[:11]
    refs = refs[11:]
    if not first_part:
        grads_before = refs[0]
        refs = refs[2:]
    back, refs = refs[:1], refs[1:]
    result, later_grad, sums, expand_bias_grad, grads_hbm = refs[:5]
    (
        expand, reduce, expand_grad, reduce_grad, mixed, normed, low_out, branch, grad_n,
        hidden_all, grad_all, copy_sem,
    ) = refs[5:]
    step = pl.program_id(0)
    chans = states.shape[3]
    side_tokens = states.shape[1] * states.shape[2]
    slab = expand.shape[2]
    tokens = mixed.shape[0]
    square = states.shape[1:]

    def parts_of(grads):
        pairs = [(grads.at[pl.ds(s * chans, chans)], expand_grad.at[s]) for s in range(slabs)]
        return pairs + [(grads.at[pl.ds(slabs * chans, slabs * slab)], reduce_grad)]

    def fetches():
        copies = [
            pltpu.make_async_copy(
                expand_hbm.at[:, pl.ds(s * slab, slab)], expand.at[s], copy_sem.at[s]
            )
            for s in range(slabs)
        ]
        copies.append(pltpu.make_async_copy(reduce_hbm, reduce, copy_sem.at[slabs]))
        if not first_part:
            copies += [
                pltpu.make_async_copy(far, near, copy_sem.at[slabs + 1 + n])
                for n, (far, near) in enumerate(parts_of(grads_before))
            ]
        return copies

    @pl.when(step == 0)
    def _():
        for c in fetches():
            c.start()
        if first_part:
            expand_grad[...] = jnp.zeros_like(expand_grad)
            reduce_grad[...] = jnp.zeros_like(reduce_grad)
        sums[...] = jnp.zeros_like(sums)
        expand_bias_grad[...] = jnp.zeros_like(expand_bias_grad)

    @pl.when(step < steps)
    def _():
        start = pl.multiple_of(step * (PAIR * side_tokens), PAIR * side_tokens)
        for half in range(PAIR):
            at = pl.ds(start + half * side_tokens, side_tokens)
            inside = mask[half][..., :1]
            lower = inside * states[half].astype(f32)
            first, _ = standardize(lower)
            filter_in = first * first_gain[...] + first_shift[...]
            full = lower + inside * (unpack(spat, half, width, step) + filter_in)
            later, _ = standardize(full)
            full = full.reshape(side_tokens, chans)
            mixed[at, :] = full
            branch[at, :] = full + reduce_bias[...]
            normal = (later * later_gain[...] + later_shift[...]).reshape(side_tokens, chans)
            normed[at, :] = normal.astype(bf16)
            go = (inside * cot[half].astype(f32)).reshape(side_tokens, chans)
            low_out[at, :] = go.astype(bf16)
            grad_n[at, :] = jnp.zeros_like(full)
            sums[0:1, :] += jnp.sum(go, axis=0, keepdims=True)

    @pl.when(step == steps)
    def _():
        for c in fetches():
            c.wait()

    @pl.when((step >= steps) & (step < steps + slabs))
    def _():
        hc = step - steps
        at = pl.ds(pl.multiple_of(hc * slab, slab), slab)
        piece = tokens // 4 if tokens % 64 == 0 else tokens

        def some(n, carry):
            here = pl.ds(pl.multiple_of(n * piece, piece), piece)
            weight_up = expand[hc]
            weight_down = reduce[at, :]
            go = low_out[here, :]
            pre = dot(normed[here, :], weight_up) + expand_bias[...]
            cdf, der = phi_parts(pre)
            hidden = (pre * cdf).astype(bf16)
            hidden_all[here, :] = hidden
            branch[here, :] += dot(hidden, weight_down)
            grad_pre = dot_nt(go, weight_down) * der
            expand_bias_grad[pl.ds(hc, 1), :] += jnp.sum(grad_pre, axis=0, keepdims=True)
            grad_low = grad_pre.astype(bf16)
            grad_all[here, :] = grad_low
            grad_n[here, :] += dot_nt(grad_low, weight_up)
            return carry

        lax.fori_loop(0, tokens // piece, some, 0)
        reduce_grad[at, :] += dot_tn(hidden_all[...], low_out[...])
        expand_grad[hc] += dot_tn(normed[...], grad_all[...])

    @pl.when(step >= steps + slabs)
    def _():
        start = pl.multiple_of(
            (step - steps - slabs) * (PAIR * side_tokens), PAIR * side_tokens
        )
        sides = []
        for half in range(PAIR):
            at = pl.ds(start + half * side_tokens, side_tokens)
            inside = mask[half][..., :1]
            later, scale = standardize(mixed[at, :])
            g = grad_n[at, :]
            sums[1:2, :] += jnp.sum(g * later, axis=0, keepdims=True)
            sums[2:3, :] += jnp.sum(g, axis=0, keepdims=True)
            g = low_out[at, :].astype(f32) + standardize_back(g * later_gain[...], later, scale)
            sides.append(inside * g.reshape(square))
            later_grad[half] = sides[-1]
            result[half] = (inside * branch[at, :].reshape(square)).astype(bf16)
        pack(sides, back, width, step - steps - slabs)

    @pl.when(step == pl.num_programs(0) - 1)
    def _():
        copies = [
            pltpu.make_async_copy(near, far, copy_sem.at[n])
            for n, (far, near) in enumerate(parts_of(grads_hbm))
        ]
        for c in copies:
            c.start()
        for c in copies:
            c.wait()


def last_kernel(width, arrays, *refs):
    spat, (states, later_grad, mask, gain) = refs[:arrays], refs[arrays : arrays + 4]
    out, sums = refs[-2:]
    chans = states.shape[3]

    @pl.when(pl.program_id(0) == 0)
    def _():
        sums[...] = jnp.zeros_like(sums)

    for half in range(PAIR):
        inside = mask[half][..., :1]
        normal, scale = standardize(inside * states[half].astype(f32))
        grad_mixed = later_grad[half]
        grad = inside * (grad_mixed + unpack(spat, half, width, pl.program_id(0)))
        flat = (-1, chans)
        sums[0:1, :] += jnp.sum((grad * normal).reshape(flat), axis=0, keepdims=True)
        sums[1:2, :] += jnp.sum(grad.reshape(flat), axis=0, keepdims=True)
        grad = grad_mixed + standardize_back(grad * gain[...], normal, scale)
        out[half] = (inside * grad).astype(bf16)


def row_copies(ranks, sources, slots, send, recv):
    my_row = lax.axis_index("rows")
    return [
        pltpu.make_async_remote_copy(
            src_ref=sources(i),
            dst_ref=slots.at[i],
            send_sem=send.at[i],
            recv_sem=recv.at[i],
            device_id=(lax.rem(my_row + i, ranks), lax.axis_index("cols")),
            device_id_type=pl.DeviceIdType.MESH,
        )
        for i in range(1, ranks)
    ]


def row_piece(r, piece):
    return pl.ds(pl.multiple_of(r * piece, piece), piece)


def pick_kernel(ranks, flat, out, picked, send, recv):
    my_row = lax.axis_index("rows")
    piece = out.shape[0]
    barrier = pltpu.get_barrier_semaphore()
    for i in range(1, ranks):
        pl.semaphore_signal(
            barrier,
            inc=1,
            device_id=(lax.rem(my_row + i, ranks), lax.axis_index("cols")),
            device_id_type=pl.DeviceIdType.MESH,
        )
    pl.semaphore_wait(barrier, ranks - 1)
    copies = row_copies(
        ranks, lambda i: flat.at[row_piece(lax.rem(my_row + i, ranks), piece)], picked, send, recv
    )
    for c in copies:
        c.start()
    for c in copies:
        c.wait()
    total = flat[row_piece(my_row, piece), :]
    for i in range(1, ranks):
        total = total + picked[i]
    out[...] = total


def sum_kernel(
    ranks, groups, own, mine, out, flat_out, got, done, send_sem, recv_sem, give_send, give_recv
):
    devices = ranks * groups
    my_row = lax.axis_index("rows")
    me = my_row * groups + lax.axis_index("cols")
    piece = mine.shape[0]

    def place(i):
        other = lax.rem(me + i, devices)
        return lax.div(other, groups), lax.rem(other, groups)

    def copy(i):
        return pltpu.make_async_remote_copy(
            src_ref=own,
            dst_ref=got.at[i],
            send_sem=send_sem.at[i],
            recv_sem=recv_sem.at[i],
            device_id=place(i),
            device_id_type=pl.DeviceIdType.MESH,
        )

    barrier = pltpu.get_barrier_semaphore()

    def greet(i, carry):
        pl.semaphore_signal(
            barrier, inc=1, device_id=place(i), device_id_type=pl.DeviceIdType.MESH
        )
        return carry

    def start(i, carry):
        copy(i).start()
        return carry

    def finish(i, carry):
        copy(i).wait()
        return carry

    lax.fori_loop(1, devices, greet, 0)
    pl.semaphore_wait(barrier, devices - 1)
    gives = row_copies(ranks, lambda i: mine, done, give_send, give_recv)
    for c in gives:
        c.start()
    lax.fori_loop(1, devices, start, 0)
    flat_out[row_piece(my_row, piece), :] = mine[...]
    lax.fori_loop(1, devices, finish, 0)
    out[...] = lax.fori_loop(1, devices, lambda i, total: total + got[i], own[...])
    for c in gives:
        c.wait()
    for i in range(1, ranks):
        flat_out[row_piece(lax.rem(my_row - i + ranks, ranks), piece), :] = done[i]


def split_kernel(expand_in, reduce_in, expand_out, reduce_out):
    expand_out[...] = expand_in[...]
    reduce_out[...] = reduce_in[...]


def wide_tables(width):
    freq = np.arange(BINS)
    place = np.arange(width)
    angle = (freq[:, None] * place[None, :] % width) * (2.0 * math.pi / width)
    live = (2 * freq <= width).astype(np.float64)[:, None]
    edge = (freq == 0) | (2 * freq == width)
    weight = np.where(edge, 1.0, 2.0)[:, None] * live
    cosine, sine = np.cos(angle), np.sin(angle)
    plain = np.concatenate([live * cosine, -live * sine], axis=0)
    doubled = np.concatenate([weight * cosine, -weight * sine], axis=0)
    return plain, doubled


def tall_tables(height, rows_here):
    pairs = rows_here // PAIR
    rows = pairs // PARTS
    order = np.array(
        [
            r * rows_here + h * pairs + q * rows + j
            for h in range(PAIR)
            for q in range(PARTS)
            for r in range(height // rows_here)
            for j in range(rows)
        ]
    )
    freq = np.arange(height)
    angle = (freq[:, None] * order[None, :] % height) * (2.0 * math.pi / height)
    cosine, sine = np.cos(angle), np.sin(angle)
    down = np.block([[cosine, sine], [-sine, cosine]])
    up = np.block([[cosine.T, -sine.T], [sine.T, cosine.T]])
    return down, up


def spread(weight):
    count = weight.shape[1]
    eye = jnp.eye(count, dtype=weight.dtype)
    full = jnp.einsum("rbio,bd->rbido", weight, eye)
    return full.reshape(2, count * BS, count * BS)


def gather_blocks(full):
    count = full.shape[1] // BS
    return jnp.stack(
        [full[:, b * BS : (b + 1) * BS, b * BS : (b + 1) * BS] for b in range(count)], axis=1
    )


def bias_rows(bias):
    return bias.reshape(2, -1)


def whole(shape):
    return pl.BlockSpec(shape, lambda *_: (0,) * len(shape))


def call(kernel, grid, in_specs, out_specs, out_shape, name, flops=0, nbytes=0, scratch=(), **kw):
    return pl.pallas_call(
        kernel,
        grid=(grid,),
        in_specs=in_specs,
        out_specs=out_specs,
        out_shape=out_shape,
        scratch_shapes=scratch,
        compiler_params=pltpu.CompilerParams(
            dimension_semantics=("arbitrary",), vmem_limit_bytes=VMEM
        ),
        cost_estimate=pl.CostEstimate(flops=flops, bytes_accessed=nbytes, transcendentals=0),
        name=name,
        **kw,
    )


def body(
    states,
    heights,
    widths,
    first_gain,
    first_shift,
    filter_inner,
    inner_bias,
    filter_outer,
    outer_bias,
    later_gain,
    later_shift,
    expand_weight,
    expand_bias,
    reduce_weight,
    reduce_bias,
    cotangent,
):
    frames, rows_here, cols_here, chans = states.shape
    ranks, groups = lax.axis_size("rows"), lax.axis_size("cols")
    assert frames == ranks and rows_here % (PAIR * PARTS) == 0
    height, breadth = rows_here * ranks, cols_here * groups
    devices = ranks * groups
    pairs = rows_here // PAIR
    rows = pairs // PARTS
    pixels = rows * cols_here
    width = chans // groups
    lanes = width * PAIR
    hidden = expand_weight.shape[1]
    factor = 1.0 / math.sqrt(height * breadth)
    short = ranks * rows
    step_pixels = 8 if pixels % 8 == 0 else pixels
    steps = pixels // step_pixels
    tokens = PAIR * pixels * frames
    message = devices * pixels * lanes * 4
    row = lambda v: v.reshape(1, -1)
    shape = jax.ShapeDtypeStruct

    order = lambda v: jnp.transpose(v, (1, 2, 0, 3)).reshape(PAIR, pairs * cols_here, frames, chans)
    restore = lambda v: jnp.transpose(v.reshape(rows_here, cols_here, frames, chans), (2, 0, 1, 3))
    states_in, cot_in = order(states), order(cotangent)
    row_ids = lax.axis_index("rows") * rows_here + jnp.arange(rows_here, dtype=jnp.int32)
    col_ids = lax.axis_index("cols") * cols_here + jnp.arange(cols_here, dtype=jnp.int32)
    inside = (row_ids[:, None, None] < heights) & (col_ids[None, :, None] < widths)
    mask = jnp.broadcast_to(
        inside.astype(f32).reshape(PAIR, pairs * cols_here, frames, 1),
        (PAIR, pairs * cols_here, frames, 128),
    )

    buffers = {} if steps > 1 else {"pipeline_mode": pl.Buffered(1)}

    def token_spec(q, where, last=chans):
        return pl.BlockSpec(
            (PAIR, step_pixels, frames, last), lambda i: (0, q * steps + where(i), 0, 0), **buffers
        )

    def packed_spec(where):
        return pl.BlockSpec(
            (ranks, groups, step_pixels, lanes), lambda i: (0, 0, where(i), 0), **buffers
        )

    blocks_here = width // BS
    split = blocks_here > 1 and steps > 1 and (2 * PAIR * BS) % 128 == 0
    parties = blocks_here if split else 1
    cut = width // parties
    split_rows = 8 * (-(-steps // 2))

    def arrays_of(q):
        return parties if q == 0 else 1

    def message_specs(q, where):
        if arrays_of(q) == 1:
            return [packed_spec(where)]
        return [
            pl.BlockSpec(
                (ranks, groups, step_pixels, 2 * PAIR * cut), lambda i: (0, 0, where(i) // 2, 0)
            )
        ] * parties

    def message_shapes(q):
        if arrays_of(q) == 1:
            return [packed_shape]
        return [shape((ranks, groups, split_rows, 2 * PAIR * cut), f32)] * parties

    same = lambda i: i
    token_shape = shape((PAIR, pairs * cols_here, frames, chans), bf16)
    packed_shape = shape((ranks, groups, pixels, lanes), f32)
    chan_row = whole((1, chans))
    anywhere = pl.BlockSpec(memory_space=pl.ANY)

    def scatter(v, axis):
        return lax.psum_scatter(v, axis, scatter_dimension=0, tiled=True)

    def gather(v, axis):
        return lax.all_gather(v, axis, axis=0, tiled=True)

    vmem = pl.BlockSpec(memory_space=pltpu.VMEM)

    def as_rows(v, unit):
        v = v.reshape(-1)
        return jnp.pad(v, (0, -v.shape[0] % (unit * 128))).reshape(-1, 128)

    def pick_sums(v):
        flat = as_rows(v, 8 * ranks)
        piece = (flat.shape[0] // ranks, 128)
        return pl.pallas_call(
            functools.partial(pick_kernel, ranks),
            in_specs=[vmem],
            out_specs=vmem,
            out_shape=shape(piece, f32),
            scratch_shapes=[pltpu.VMEM((ranks,) + piece, f32)]
            + [pltpu.SemaphoreType.DMA((ranks,))] * 2,
            compiler_params=pltpu.CompilerParams(collective_id=1, has_side_effects=True),
            name="filter_sums",
        )(flat)

    def sum_small(v, mine):
        own = as_rows(v, 8)
        out, flat_out = pl.pallas_call(
            functools.partial(sum_kernel, ranks, groups),
            in_specs=[vmem, vmem],
            out_specs=[vmem, vmem],
            out_shape=[shape(own.shape, f32), shape((ranks * mine.shape[0], 128), f32)],
            scratch_shapes=[
                pltpu.VMEM((devices,) + own.shape, f32),
                pltpu.VMEM((ranks,) + mine.shape, f32),
            ]
            + [pltpu.SemaphoreType.DMA((devices,))] * 2
            + [pltpu.SemaphoreType.DMA((ranks,))] * 2,
            compiler_params=pltpu.CompilerParams(collective_id=0, has_side_effects=True),
            name="small_sums",
        )(own, mine)
        return out.reshape(-1)[: v.size].reshape(v.shape), flat_out.reshape(-1)

    def split_grads(v):
        cuts = 4
        piece = (chans // cuts, chans)
        return call(
            split_kernel,
            slabs * cuts,
            [
                pl.BlockSpec(piece, lambda i: (i, 0)),
                pl.BlockSpec(piece, lambda i: (slabs * cuts + i, 0)),
            ],
            [
                pl.BlockSpec(piece, lambda i: (lax.rem(i, cuts), lax.div(i, cuts))),
                pl.BlockSpec(piece, lambda i: (i, 0)),
            ],
            [shape((chans, hidden), f32), shape((hidden, chans), f32)],
            "split_gradients",
            nbytes=16 * chans * hidden,
        )(v, v)

    def behind(v, *after):
        return lax.optimization_barrier((v,) + after)[0] if after else v

    def exchange(v):
        sent = v.reshape((devices,) + v.shape[2:])
        return lax.all_to_all(sent, ("rows", "cols"), 0, 0, tiled=True).reshape(v.shape)

    def tie(*values):
        return lax.optimization_barrier(values)

    def first_norm(q):
        return call(
            functools.partial(first_kernel, width),
            steps,
            [token_spec(q, same), token_spec(q, same, 128), chan_row, chan_row],
            message_specs(q, same),
            message_shapes(q),
            "first_norm",
            nbytes=2 * message,
        )(states_in, mask, row(first_gain), row(first_shift))

    plain, doubled = wide_tables(breadth)
    down, up = tall_tables(height, rows_here)
    as_table = lambda t: jnp.asarray(t, dtype=bf16)

    def fine_table(t):
        high = t.astype(jnp.bfloat16)
        return jnp.asarray(np.concatenate([high, (t - high.astype(np.float64)).astype(jnp.bfloat16)]))

    def mixes(weight):
        return [weight[:, g] for g in range(parties)] if split else [spread(weight)]

    inner_full, outer_full = mixes(filter_inner), mixes(filter_outer)
    turn = lambda t: jnp.swapaxes(t, 1, 2)
    bin_steps = BINS // GROUP
    group_rows = GROUP * 2 * height
    held_shape = shape((short, 2, BINS, lanes), f32)
    at_once = 2
    held_row = pl.BlockSpec((at_once * rows, 2, BINS, lanes), lambda i: (i, 0, 0, 0))
    held_bins = pl.BlockSpec((short, 2, GROUP, lanes), lambda i: (0, 0, i, 0))
    field = pl.BlockSpec((at_once, groups, pixels, lanes), lambda i: (i, 0, 0, 0))
    kept = pl.BlockSpec((group_rows, cut), lambda i: (i, 0))
    kept_shape = shape((bin_steps * group_rows, cut), bf16)
    mix_spec = whole((2, cut, cut))
    bias_spec = whole((2, cut))

    def held_of(last, by_row):
        if by_row:
            return pl.BlockSpec((at_once * rows, 2, BINS, last), lambda i: (i, 0, 0, 0))
        return pl.BlockSpec((short, 2, GROUP, last), lambda i: (0, 0, i, 0))

    cut_shape = shape((short, 2, BINS, PAIR * cut), f32)
    split_field = pl.BlockSpec(
        (at_once, groups, split_rows, 2 * PAIR * cut), lambda i: (i, 0, 0, 0)
    )
    natural = pltpu.VMEM((at_once, groups, pixels, PAIR * cut), f32)
    cut_in = [held_of(PAIR * cut if split else lanes, False)] + [held_bins] * (PARTS - 1)
    cut_out = [held_of(PAIR * cut, False)] * PARTS
    up_spec = whole((2 * height, 2 * height))

    def wide_in(v, table, fine):
        divided = v.shape != packed_shape.shape
        return call(
            functools.partial(wide_in_split_kernel if divided else wide_in_kernel, cols_here, fine),
            ranks // at_once,
            [split_field if divided else field, whole(table.shape)],
            held_of(PAIR * cut, True) if divided else held_row,
            cut_shape if divided else held_shape,
            "wide_in",
            nbytes=2 * message,
            scratch=[pltpu.VMEM((at_once * rows, breadth, PAIR * cut), f32), natural]
            if divided
            else [pltpu.VMEM((at_once * rows, breadth, lanes), f32)],
        )(v, table)

    def wide_out(parts, table):
        return call(
            functools.partial(wide_out_kernel, cols_here, factor),
            ranks // at_once,
            [held_of(v.shape[3], True) for v in parts] + [whole(table.shape)],
            field,
            packed_shape,
            "wide_out",
            nbytes=2 * message,
        )(*parts, table)

    def wide_out_split(part, table):
        return call(
            functools.partial(wide_out_split_kernel, cols_here, factor),
            ranks // at_once,
            [held_of(PAIR * cut, True), whole(table.shape)],
            split_field,
            message_shapes(0)[0],
            "wide_out",
            nbytes=2 * message,
            scratch=[natural],
        )(part, table)

    def messages_out(given, table):
        first = [wide_out_split(v[0], table) for v in given] if split else [wide_out([given[0][0]], table)]
        return first + [wide_out([v[q] for v in given], table) for q in range(1, PARTS)]

    def of_group(v, g):
        return bias_rows(v)[:, g * cut : (g + 1) * cut]

    forward_mix = [
        (inner_full[g], of_group(inner_bias, g), outer_full[g], of_group(outer_bias, g))
        for g in range(parties)
    ]
    forward_specs = [mix_spec, bias_spec, mix_spec, bias_spec]

    def spectral_forward(g, held):
        table = fine_table(down)
        outs = call(
            functools.partial(spectral_forward_kernel, factor, g),
            bin_steps,
            cut_in + [whole(table.shape), up_spec] + forward_specs,
            cut_out + [kept],
            [cut_shape] * PARTS + [kept_shape],
            "spectral_forward",
            flops=20 * 10**9,
            nbytes=8 * PARTS * message // parties,
        )(*held, table, as_table(up), *forward_mix[g])
        return outs[:PARTS], outs[PARTS]

    full = pl.BlockSpec((group_rows, width), lambda i: (i, 0))
    full_shape = shape((bin_steps * group_rows, width), bf16)
    full_mix, full_bias = whole((2, width, width)), whole((2, width))
    inner_t, outer_t = turn(spread(filter_inner)), turn(spread(filter_outer))

    def spectral_keep(entries):
        return call(
            functools.partial(spectral_keep_kernel, height, parties),
            bin_steps,
            [kept] * parties + forward_specs * parties,
            [full] * 3,
            [full_shape] * 3,
            "spectral_keep",
            flops=10 * 10**9,
            nbytes=2 * PARTS * message,
        )(*entries, *[v for mix in forward_mix for v in mix])

    def spectral_backward(held, slope, damp):
        outs = call(
            functools.partial(spectral_backward_kernel, factor, 1),
            bin_steps,
            [held_bins] * PARTS + [up_spec, up_spec, full_mix, full_mix] + [full] * 2,
            [held_bins] * PARTS + [full, full_bias] * 2,
            [held_shape] * PARTS + [full_shape, shape((2, width), f32)] * 2,
            "spectral_backward",
            flops=20 * 10**9,
            nbytes=8 * PARTS * message,
        )(*held, as_table(down), as_table(up), inner_t, outer_t, slope, damp)
        return outs[:PARTS], outs[PARTS:]

    def filter_grad(entries, active, inner_low, outer_low):
        return call(
            functools.partial(filter_grad_kernel, height, parties),
            bin_steps,
            [kept] * parties + [full] * 3,
            [full_mix] * 2,
            [shape((2, width, width), f32)] * 2,
            "filter_grad",
            flops=10 * 10**9,
            nbytes=2 * PARTS * message,
        )(*entries, active, inner_low, outer_low)

    slab = chans
    slabs = hidden // slab
    dense_steps = 2 * steps + slabs
    enter = lambda i: jnp.minimum(i, steps - 1)
    leave = lambda i: jnp.maximum(i - steps - slabs, 0)
    either = lambda i: jnp.where(i < steps + slabs, enter(i), leave(i))

    def dense(q, spatial, before):
        grads_before = () if q == 0 else before
        return call(
            functools.partial(dense_kernel, steps, slabs, width, q == 0, arrays_of(q)),
            dense_steps,
            message_specs(q, enter)
            + [token_spec(q, enter), token_spec(q, enter), token_spec(q, either, 128)]
            + [chan_row] * 4
            + [pl.BlockSpec((1, slab), lambda i: (0, jnp.clip(i - steps, 0, slabs - 1)))]
            + [chan_row]
            + [anywhere] * (2 + len(grads_before)),
            [packed_spec(leave)]
            + [
                token_spec(q, leave),
                token_spec(0, leave),
                whole((8, chans)),
                whole((slabs, slab)),
                anywhere,
            ],
            [packed_shape]
            + [
                token_shape,
                shape((PAIR, pixels, frames, chans), f32),
                shape((8, chans), f32),
                shape((slabs, slab), f32),
                shape((2 * hidden, chans), f32),
            ],
            "dense_both_ways",
            flops=12 * tokens * chans * hidden,
            nbytes=4 * message,
            scratch=[
                pltpu.VMEM((slabs, chans, slab), bf16),
                pltpu.VMEM((hidden, chans), bf16),
                pltpu.VMEM((slabs, chans, slab), f32),
                pltpu.VMEM((hidden, chans), f32),
                pltpu.VMEM((tokens, chans), f32),
                pltpu.VMEM((tokens, chans), bf16),
                pltpu.VMEM((tokens, chans), bf16),
                pltpu.VMEM((tokens, chans), f32),
                pltpu.VMEM((tokens, chans), f32),
                pltpu.VMEM((tokens, slab), bf16),
                pltpu.VMEM((tokens, slab), bf16),
                pltpu.SemaphoreType.DMA((2 * slabs + 2,)),
            ],
            input_output_aliases={} if q == 0 else {13: 1},
        )(
            *spatial,
            states_in,
            cot_in,
            mask,
            row(first_gain),
            row(first_shift),
            row(later_gain),
            row(later_shift),
            row(expand_bias),
            row(reduce_bias),
            expand_weight,
            reduce_weight,
            *grads_before,
        )

    def last_norm(q, later_grad, spatial, before):
        given = () if q == 0 else (before,)
        return call(
            functools.partial(last_kernel, width, 1),
            steps,
            [packed_spec(same)]
            + [token_spec(q, same), token_spec(0, same), token_spec(q, same, 128)]
            + [chan_row]
            + [anywhere] * len(given),
            [token_spec(q, same), whole((8, chans))],
            [token_shape, shape((8, chans), f32)],
            "first_norm_backward",
            nbytes=4 * message,
            input_output_aliases={} if q == 0 else {5: 0},
        )(spatial, states_in, later_grad, mask, row(first_gain), *given)

    every = range(PARTS)

    def send(made, got):
        if got:
            made, got[-1] = tie(made, got[-1])
        got.append(exchange(made))

    made = [v for q in (*every[1:], 0) for v in first_norm(q)]
    got, held = [], []
    for n, v in enumerate(made):
        if n > 1:
            v, held[-1] = tie(v, held[-1])
        send(v, got)
        if n > 0:
            held.append(wide_in(got[-2], fine_table(plain), True))
    held.append(wide_in(got[-1], fine_table(plain), True))
    rest, first = held[: PARTS - 1], held[PARTS - 1 :]
    done = [spectral_forward(g, [first[g]] + rest) for g in range(parties)]
    entries = [v[1] for v in done]
    made = messages_out([v[0] for v in done], as_table(doubled.T))
    active, slope, damp = spectral_keep(entries)

    spatial = got[-1:]
    for n in range(parties):
        send(made[n], spatial)
    active, made[parties] = tie(active, made[parties])
    spatial = spatial[1:]
    backs, later_grads, sums, expand_bias_grad, before = [], [], 0.0, 0.0, ()
    for q in every:
        if q + 1 < PARTS:
            if backs:
                made[parties + q], backs[-1] = tie(made[parties + q], backs[-1])
            send(made[parties + q], spatial)
        received = spatial[:parties] if q == 0 else spatial[parties + q - 1 : parties + q]
        if q + 1 == PARTS:
            backs[-1], spatial[-1] = tie(backs[-1], spatial[-1])
            got = [exchange(backs[1])]
            received = spatial[-1:]
        outs = dense(q, received, before)
        back, result, kept_grad, part, bias_part, grads = outs
        backs.append(back)
        before = (grads, result)
        later_grads.append(kept_grad)
        sums, expand_bias_grad = sums + part, expand_bias_grad + bias_part
    grads, got[0] = tie(grads, got[0])
    grads = scatter(grads, "cols")
    held = []
    for v in [backs[q] for q in (*every[2:], 0)]:
        held.append(wide_in(got[-1], as_table(doubled), False))
        if len(held) > 1:
            v, held[-2] = tie(v, held[-2])
        send(v, got)
    got[-1], held[-1] = tie(got[-1], held[-1])
    held.append(wide_in(got[-1], as_table(doubled), False))
    grads, held[-1] = tie(grads, held[-1])
    grads = scatter(grads, "rows")
    given, (inner_low, inner_bias_grad, outer_low, outer_bias_grad) = spectral_backward(
        [held[-1]] + held[:-1], slope, damp
    )
    made = [wide_out([v], as_table(plain.T)) for v in given]
    inner_grad, outer_grad = filter_grad(entries, active, inner_low, outer_low)
    filter_parts = (
        gather_blocks(inner_grad), inner_bias_grad, gather_blocks(outer_grad), outer_bias_grad
    )
    flat = jnp.concatenate([v.reshape(-1) for v in filter_parts])

    got = [exchange(made[0])]
    send(made[1], got)
    grads, got[0] = tie(grads, got[0])
    grads = gather(grads, ("cols", "rows"))
    expand_sum, reduce_sum = split_grads(grads)
    first_sums, states_grad = [], None
    for q in every:
        if q + 1 < PARTS:
            if q > 0:
                made[q + 1], first_sums[-1] = tie(made[q + 1], first_sums[-1])
                send(made[q + 1], got)
        else:
            flat, expand_sum = tie(flat, expand_sum)
            flat = pick_sums(flat)
            states_grad, flat = tie(states_grad, flat)
            states_grad, expand_sum = tie(states_grad, expand_sum)
        states_grad, part = last_norm(q, later_grads[q], got[q], states_grad)
        first_sums.append(part)
        if q == 0:
            flat, first_sums[0] = tie(flat, first_sums[0])
    small, flat = sum_small(
        jnp.concatenate([sum(first_sums)[:2], sums[:3], expand_bias_grad.reshape(-1, chans)]), flat
    )
    sizes = [v.size for v in filter_parts]
    ends = np.cumsum(sizes)
    filter_sums = [
        flat[e - n : e].reshape(v.shape) for e, n, v in zip(ends, sizes, filter_parts)
    ]
    inner_sum, inner_bias_sum, outer_sum, outer_bias_sum = filter_sums
    return (
        restore(result),
        restore(states_grad),
        small[0],
        small[1],
        inner_sum,
        inner_bias_sum.reshape(2, -1, BS),
        outer_sum,
        outer_bias_sum.reshape(2, -1, BS),
        small[3],
        small[4],
        expand_sum,
        small[5:].reshape(-1),
        reduce_sum,
        small[2],
    )


def solution(mesh):
    tile = P(None, "rows", "cols", None)
    mix = P(None, "cols", None, None)
    bias = P(None, "cols", None)
    in_specs = (
        tile, P(), P(), P(), P(), mix, bias, mix, bias, P(), P(), P(), P(), P(), P(), tile,
    )
    out_specs = (
        tile, tile, P(), P(), mix, bias, mix, bias, P(), P(), P(), P(), P(), P(),
    )
    return jax.shard_map(body, mesh=mesh, in_specs=in_specs, out_specs=out_specs, check_vma=False)
```

```python
import functools
import math

import jax
import jax.numpy as jnp
import numpy as np
from jax import lax
from jax.experimental import pallas as pl
from jax.experimental.pallas import tpu as pltpu
from jax.sharding import PartitionSpec as P

BS = 96
BINS = 96
PAIR = 2
GROUP = 8
PARTS = 3
norm_eps = 1e-06
shrink_width = 0.01
VMEM = 60 * 1024 * 1024
f32 = jnp.float32
bf16 = jnp.bfloat16


def phi_parts(v):
    cdf = 0.5 * (1.0 + lax.erf(v * math.sqrt(0.5)))
    slope = cdf + v * (jnp.exp(v * v * -0.5) * (1.0 / math.sqrt(2.0 * math.pi)))
    return cdf, slope


def dot(a, b):
    return lax.dot_general(a, b, (((1,), (0,)), ((), ())), preferred_element_type=f32)


def dot_tn(a, b):
    return lax.dot_general(a, b, (((0,), (0,)), ((), ())), preferred_element_type=f32)


def dot_nt(a, b):
    return lax.dot_general(a, b, (((1,), (1,)), ((), ())), preferred_element_type=f32)


def standardize(v):
    centre = jnp.mean(v, axis=-1, keepdims=True)
    centred = v - centre
    spread = jnp.mean(centred * centred, axis=-1, keepdims=True)
    scale = lax.rsqrt(spread + norm_eps)
    return centred * scale, scale


def standardize_back(grad, normal, scale):
    first = jnp.mean(grad, axis=-1, keepdims=True)
    second = jnp.mean(grad * normal, axis=-1, keepdims=True)
    return scale * (grad - first - normal * second)


def pack(sides, outs, width, step):
    turned = [jnp.swapaxes(s, 0, 1) for s in sides]
    cut = width // len(outs)

    def lanes_of(c, g):
        start = c * width + g * cut
        return jnp.concatenate([t[:, :, start : start + cut] for t in turned], axis=2)

    for g, out in enumerate(outs):
        values = [lanes_of(c, g) for c in range(out.shape[1])]
        if len(outs) == 1:
            for c, v in enumerate(values):
                out[:, c] = v
            continue

        @pl.when(lax.rem(step, 2) == 0)
        def _():
            for c, v in enumerate(values):
                out[:, c] = jnp.concatenate([v, v], axis=2)

        @pl.when(lax.rem(step, 2) == 1)
        def _():
            for c, v in enumerate(values):
                out[:, c] = jnp.concatenate([out[:, c, :, : PAIR * cut], v], axis=2)


def unpack(refs, half, width, step):
    cut = width // len(refs)
    parts = []
    for c in range(refs[0].shape[1]):
        for ref in refs:
            part = ref[:, c, :, half * cut : (half + 1) * cut]
            if len(refs) > 1:
                later = (PAIR + half) * cut
                part = jnp.where(lax.rem(step, 2) == 1, ref[:, c, :, later : later + cut], part)
            parts.append(part)
    return jnp.swapaxes(jnp.concatenate(parts, axis=2) if len(parts) > 1 else parts[0], 0, 1)


def first_kernel(width, states, mask, gain, shift, *outs):
    sides = []
    for half in range(PAIR):
        inside = mask[half][..., :1]
        normal, _ = standardize(states[half].astype(f32) * inside)
        sides.append(inside * (normal * gain[...] + shift[...]))
    pack(sides, outs, width, pl.program_id(0))


def table_dot(table, x):
    rows = table.shape[0] // 2
    high = x.astype(bf16)
    both = dot(table[...], high)
    rest = dot(table[:rows, :], (x - high.astype(f32)).astype(bf16))
    return both[:rows] + both[rows:] + rest


def wide_in_kernel(cols_here, fine, block, table, held, wide):
    groups, rows = block.shape[1], block.shape[2] // cols_here
    for n in range(block.shape[0] * rows):
        r, j = divmod(n, rows)
        for c in range(groups):
            wide[n, c * cols_here : (c + 1) * cols_here, :] = block[
                r, c, j * cols_here : (j + 1) * cols_here, :
            ]
        x = wide[n]
        y = table_dot(table, x) if fine else dot(table[...], x.astype(bf16))
        held[n, 0] = y[:BINS]
        held[n, 1] = y[BINS:]


def wide_out_kernel(cols_here, factor, *refs):
    held, (table, block) = refs[:-2], refs[-2:]
    groups, rows = block.shape[1], block.shape[2] // cols_here
    cut = held[0].shape[3] // PAIR
    for n in range(block.shape[0] * rows):
        r, j = divmod(n, rows)
        x = [jnp.concatenate([part[n, 0], part[n, 1]], axis=0) for part in held]
        if len(x) > 1:
            x = [part[:, h * cut : (h + 1) * cut] for h in range(PAIR) for part in x]
            x = jnp.concatenate(x, axis=1)
        else:
            x = x[0]
        plane = dot(table[...], x.astype(bf16)) * factor
        for c in range(groups):
            block[r, c, j * cols_here : (j + 1) * cols_here, :] = plane[
                c * cols_here : (c + 1) * cols_here, :
            ]


def wide_in_split_kernel(cols_here, fine, block, table, held, wide, natural):
    groups, half = block.shape[1], block.shape[3] // 2
    rows = natural.shape[2] // cols_here
    for r in range(block.shape[0]):
        for c in range(groups):
            for s in range(natural.shape[2] // 8):
                natural[r, c, s * 8 : s * 8 + 8, :] = block[
                    r, c, (s // 2) * 8 : (s // 2) * 8 + 8, (s % 2) * half : (s % 2 + 1) * half
                ]
        for j in range(rows):
            n = r * rows + j
            for c in range(groups):
                wide[n, c * cols_here : (c + 1) * cols_here, :] = natural[
                    r, c, j * cols_here : (j + 1) * cols_here, :
                ]
            x = wide[n]
            y = table_dot(table, x) if fine else dot(table[...], x.astype(bf16))
            held[n, 0] = y[:BINS]
            held[n, 1] = y[BINS:]


def wide_out_split_kernel(cols_here, factor, held, table, block, natural):
    groups = block.shape[1]
    rows = natural.shape[2] // cols_here
    last = natural.shape[2] // 8 - 1
    for r in range(block.shape[0]):
        for j in range(rows):
            n = r * rows + j
            x = jnp.concatenate([held[n, 0], held[n, 1]], axis=0).astype(bf16)
            plane = dot(table[...], x) * factor
            for c in range(groups):
                natural[r, c, j * cols_here : (j + 1) * cols_here, :] = plane[
                    c * cols_here : (c + 1) * cols_here, :
                ]
        for c in range(groups):
            for m in range(block.shape[2] // 8):
                sides = [natural[r, c, at * 8 : at * 8 + 8, :] for at in (2 * m, min(2 * m + 1, last))]
                block[r, c, m * 8 : m * 8 + 8, :] = jnp.concatenate(sides, axis=1)


def bins_in(held, table, width, group, fine):
    kind = f32 if fine else bf16

    def lane(part, h):
        whole_width = part.shape[-1] // PAIR
        return h * whole_width + (group * width if whole_width > width else 0)

    turned = [
        [jnp.swapaxes(part[:, side], 0, 1).astype(kind) for part in held] for side in range(2)
    ]
    outs = []
    for k in range(GROUP):
        x = jnp.concatenate(
            [
                part[k][:, lane(part, h) : lane(part, h) + width]
                for side in turned
                for h in range(PAIR)
                for part in side
            ],
            axis=0,
        )
        outs.append(table_dot(table, x) if fine else dot(table[...], x))
    return outs


def bins_out(held, table, width, values):
    short = held[0].shape[0]
    count = len(held)
    products = [dot(table[...], value) for value in values]
    for side in range(2):
        for q in range(count):
            rows = []
            for z in products:
                at = [((side * PAIR + h) * count + q) * short for h in range(PAIR)]
                rows.append(jnp.concatenate([z[a : a + short] for a in at], axis=1))
            held[q][:, side] = jnp.swapaxes(jnp.stack(rows, axis=0), 0, 1)


def halves(v, count, tall):
    return [
        (v[k * 2 * tall : k * 2 * tall + tall], v[k * 2 * tall + tall : (k + 1) * 2 * tall])
        for k in range(count)
    ]


def complex_product(x, first, second, count, tall, conj):
    a = dot(x, first)
    b = dot(x, second)
    parts = []
    for (a_re, a_im), (b_re, b_im) in zip(halves(a, count, tall), halves(b, count, tall)):
        if conj:
            parts += [a_re + b_im, a_im - b_re]
        else:
            parts += [a_re - b_im, a_im + b_re]
    return parts


def activate(low, mix, bias, tall):
    parts = complex_product(low, mix[0], mix[1], low.shape[0] // (2 * tall), tall, False)
    return [part + bias[n % 2 : n % 2 + 1, :] for n, part in enumerate(parts)]


def gelu_low(v):
    return (v * (0.5 * (1.0 + lax.erf(v * math.sqrt(0.5))))).astype(bf16)


def spectral_forward_kernel(factor, group, *refs):
    held, refs = refs[:PARTS], refs[PARTS:]
    table_down, table_up, inner, inner_bias, outer, outer_bias = refs[:6]
    given, entries = refs[6 : 6 + PARTS], refs[6 + PARTS]
    width = inner.shape[2]
    tall = table_up.shape[0] // 2
    spec = bins_in(held, table_down, width, group, True)
    low = jnp.concatenate([(s * factor).astype(bf16) for s in spec], axis=0)
    entries[...] = low
    act = jnp.concatenate([gelu_low(v) for v in activate(low, inner, inner_bias, tall)], axis=0)
    shrunk = [
        (v - shrink_width * jnp.tanh(v * (1.0 / shrink_width))).astype(bf16)
        for v in activate(act, outer, outer_bias, tall)
    ]
    values = [jnp.concatenate(shrunk[2 * k : 2 * k + 2], axis=0) for k in range(GROUP)]
    bins_out(given, table_up, width, values)


def spectral_keep_kernel(tall, parties, *refs):
    entries, refs = refs[:parties], refs[parties:]
    mixes, (active, slope, damp) = refs[: 4 * parties], refs[4 * parties :]

    def joined_parts(each):
        return [jnp.concatenate(v, axis=1) if parties > 1 else v[0] for v in zip(*each)]

    acts, slopes, damps = [], [], []
    for g in range(parties):
        inner, inner_bias, outer, outer_bias = mixes[4 * g : 4 * g + 4]
        acts.append([])
        slopes.append([])
        damps.append([])
        for v in activate(entries[g][...], inner, inner_bias, tall):
            cdf, der = phi_parts(v)
            acts[g].append((v * cdf).astype(bf16))
            slopes[g].append(der.astype(bf16))
        for v in activate(jnp.concatenate(acts[g], axis=0), outer, outer_bias, tall):
            t = jnp.tanh(v * (1.0 / shrink_width))
            damps[g].append((t * t).astype(bf16))
    for ref, each in ((active, acts), (slope, slopes), (damp, damps)):
        for n, v in enumerate(joined_parts(each)):
            ref[n * tall : (n + 1) * tall, :] = v


def joined(refs):
    return jnp.concatenate([r[...] for r in refs], axis=1) if len(refs) > 1 else refs[0][...]


def spectral_backward_kernel(factor, parties, *refs):
    held, refs = refs[:PARTS], refs[PARTS:]
    table_down, table_up, inner_t, outer_t = refs[:4]
    slope, damp = joined(refs[4 : 4 + parties]), joined(refs[4 + parties : 4 + 2 * parties])
    refs = refs[4 + 2 * parties :]
    given, refs = refs[:PARTS], refs[PARTS:]
    inner_low, inner_bias_grad, outer_low, outer_bias_grad = refs
    width = inner_t.shape[2]
    tall = table_up.shape[0] // 2

    @pl.when(pl.program_id(0) == 0)
    def _():
        for ref in (inner_bias_grad, outer_bias_grad):
            ref[...] = jnp.zeros_like(ref)

    spec = bins_in(held, table_down, width, 0, False)
    grads = []
    sums = [0.0, 0.0]
    for k in range(GROUP):
        for side in range(2):
            at = (2 * k + side) * tall
            g = spec[k][side * tall : (side + 1) * tall] * factor
            g = g * damp[at : at + tall].astype(f32)
            sums[side] = sums[side] + jnp.sum(g, axis=0, keepdims=True)
            grads.append(g.astype(bf16))
    outer_bias_grad[...] += jnp.concatenate(sums, axis=0)
    low = jnp.concatenate(grads, axis=0)
    outer_low[...] = low
    parts = complex_product(low, outer_t[0], outer_t[1], GROUP, tall, True)
    grads = []
    sums = [0.0, 0.0]
    for n, part in enumerate(parts):
        g = part * slope[n * tall : (n + 1) * tall].astype(f32)
        sums[n % 2] = sums[n % 2] + jnp.sum(g, axis=0, keepdims=True)
        grads.append(g.astype(bf16))
    inner_bias_grad[...] += jnp.concatenate(sums, axis=0)
    low = jnp.concatenate(grads, axis=0)
    inner_low[...] = low
    parts = complex_product(low, inner_t[0], inner_t[1], GROUP, tall, True)
    values = [
        jnp.concatenate([parts[2 * k], parts[2 * k + 1]], axis=0).astype(bf16)
        for k in range(GROUP)
    ]
    bins_out(given, table_up, width, values)


def filter_grad_kernel(tall, parties, *refs):
    entries, active = refs[:parties], refs[parties : parties + 1]
    inner_low, outer_low, inner_grad, outer_grad = refs[parties + 1 :]

    @pl.when(pl.program_id(0) == 0)
    def _():
        inner_grad[...] = jnp.zeros_like(inner_grad)
        outer_grad[...] = jnp.zeros_like(outer_grad)

    for before, low, grad in ((entries, inner_low, inner_grad), (active, outer_low, outer_grad)):
        turned = []
        for k in range(GROUP):
            top, bottom = low[2 * k * tall : (2 * k + 1) * tall], low[(2 * k + 1) * tall : (2 * k + 2) * tall]
            turned += [bottom, -top]
        known = joined(before)
        grad[0] += dot_tn(known, low[...])
        grad[1] += dot_tn(known, jnp.concatenate(turned, axis=0))


def dense_kernel(steps, slabs, width, first_part, arrays, *refs):
    spat, refs = refs[:arrays], refs[arrays:]
    (
        states, cot, mask, first_gain, first_shift, later_gain, later_shift,
        expand_bias, reduce_bias, expand_hbm, reduce_hbm,
    ) = refs[:11]
    refs = refs[11:]
    if not first_part:
        grads_before = refs[0]
        refs = refs[2:]
    back, refs = refs[:1], refs[1:]
    result, later_grad, sums, expand_bias_grad, grads_hbm = refs[:5]
    (
        expand, reduce, expand_grad, reduce_grad, mixed, normed, low_out, branch, grad_n,
        hidden_all, grad_all, copy_sem,
    ) = refs[5:]
    step = pl.program_id(0)
    chans = states.shape[3]
    side_tokens = states.shape[1] * states.shape[2]
    slab = expand.shape[2]
    tokens = mixed.shape[0]
    square = states.shape[1:]

    def parts_of(grads):
        pairs = [(grads.at[pl.ds(s * chans, chans)], expand_grad.at[s]) for s in range(slabs)]
        return pairs + [(grads.at[pl.ds(slabs * chans, slabs * slab)], reduce_grad)]

    def fetches():
        copies = [
            pltpu.make_async_copy(
                expand_hbm.at[:, pl.ds(s * slab, slab)], expand.at[s], copy_sem.at[s]
            )
            for s in range(slabs)
        ]
        copies.append(pltpu.make_async_copy(reduce_hbm, reduce, copy_sem.at[slabs]))
        if not first_part:
            copies += [
                pltpu.make_async_copy(far, near, copy_sem.at[slabs + 1 + n])
                for n, (far, near) in enumerate(parts_of(grads_before))
            ]
        return copies

    @pl.when(step == 0)
    def _():
        for c in fetches():
            c.start()
        if first_part:
            expand_grad[...] = jnp.zeros_like(expand_grad)
            reduce_grad[...] = jnp.zeros_like(reduce_grad)
        sums[...] = jnp.zeros_like(sums)
        expand_bias_grad[...] = jnp.zeros_like(expand_bias_grad)

    @pl.when(step < steps)
    def _():
        start = pl.multiple_of(step * (PAIR * side_tokens), PAIR * side_tokens)
        for half in range(PAIR):
            at = pl.ds(start + half * side_tokens, side_tokens)
            inside = mask[half][..., :1]
            lower = inside * states[half].astype(f32)
            first, _ = standardize(lower)
            filter_in = first * first_gain[...] + first_shift[...]
            full = lower + inside * (unpack(spat, half, width, step) + filter_in)
            later, _ = standardize(full)
            full = full.reshape(side_tokens, chans)
            mixed[at, :] = full
            branch[at, :] = full + reduce_bias[...]
            normal = (later * later_gain[...] + later_shift[...]).reshape(side_tokens, chans)
            normed[at, :] = normal.astype(bf16)
            go = (inside * cot[half].astype(f32)).reshape(side_tokens, chans)
            low_out[at, :] = go.astype(bf16)
            grad_n[at, :] = jnp.zeros_like(full)
            sums[0:1, :] += jnp.sum(go, axis=0, keepdims=True)

    @pl.when(step == steps)
    def _():
        for c in fetches():
            c.wait()

    @pl.when((step >= steps) & (step < steps + slabs))
    def _():
        hc = step - steps
        at = pl.ds(pl.multiple_of(hc * slab, slab), slab)
        piece = tokens // 4 if tokens % 64 == 0 else tokens

        def some(n, carry):
            here = pl.ds(pl.multiple_of(n * piece, piece), piece)
            weight_up = expand[hc]
            weight_down = reduce[at, :]
            go = low_out[here, :]
            pre = dot(normed[here, :], weight_up) + expand_bias[...]
            cdf, der = phi_parts(pre)
            hidden = (pre * cdf).astype(bf16)
            hidden_all[here, :] = hidden
            branch[here, :] += dot(hidden, weight_down)
            grad_pre = dot_nt(go, weight_down) * der
            expand_bias_grad[pl.ds(hc, 1), :] += jnp.sum(grad_pre, axis=0, keepdims=True)
            grad_low = grad_pre.astype(bf16)
            grad_all[here, :] = grad_low
            grad_n[here, :] += dot_nt(grad_low, weight_up)
            return carry

        lax.fori_loop(0, tokens // piece, some, 0)
        reduce_grad[at, :] += dot_tn(hidden_all[...], low_out[...])
        expand_grad[hc] += dot_tn(normed[...], grad_all[...])

    @pl.when(step >= steps + slabs)
    def _():
        start = pl.multiple_of(
            (step - steps - slabs) * (PAIR * side_tokens), PAIR * side_tokens
        )
        sides = []
        for half in range(PAIR):
            at = pl.ds(start + half * side_tokens, side_tokens)
            inside = mask[half][..., :1]
            later, scale = standardize(mixed[at, :])
            g = grad_n[at, :]
            sums[1:2, :] += jnp.sum(g * later, axis=0, keepdims=True)
            sums[2:3, :] += jnp.sum(g, axis=0, keepdims=True)
            g = low_out[at, :].astype(f32) + standardize_back(g * later_gain[...], later, scale)
            sides.append(inside * g.reshape(square))
            later_grad[half] = sides[-1]
            result[half] = (inside * branch[at, :].reshape(square)).astype(bf16)
        pack(sides, back, width, step - steps - slabs)

    @pl.when(step == pl.num_programs(0) - 1)
    def _():
        copies = [
            pltpu.make_async_copy(near, far, copy_sem.at[n])
            for n, (far, near) in enumerate(parts_of(grads_hbm))
        ]
        for c in copies:
            c.start()
        for c in copies:
            c.wait()


def last_kernel(width, arrays, *refs):
    spat, (states, later_grad, mask, gain) = refs[:arrays], refs[arrays : arrays + 4]
    out, sums = refs[-2:]
    chans = states.shape[3]

    @pl.when(pl.program_id(0) == 0)
    def _():
        sums[...] = jnp.zeros_like(sums)

    for half in range(PAIR):
        inside = mask[half][..., :1]
        normal, scale = standardize(inside * states[half].astype(f32))
        grad_mixed = later_grad[half]
        grad = inside * (grad_mixed + unpack(spat, half, width, pl.program_id(0)))
        flat = (-1, chans)
        sums[0:1, :] += jnp.sum((grad * normal).reshape(flat), axis=0, keepdims=True)
        sums[1:2, :] += jnp.sum(grad.reshape(flat), axis=0, keepdims=True)
        grad = grad_mixed + standardize_back(grad * gain[...], normal, scale)
        out[half] = (inside * grad).astype(bf16)


def row_copies(ranks, sources, slots, send, recv):
    my_row = lax.axis_index("rows")
    return [
        pltpu.make_async_remote_copy(
            src_ref=sources(i),
            dst_ref=slots.at[i],
            send_sem=send.at[i],
            recv_sem=recv.at[i],
            device_id=(lax.rem(my_row + i, ranks), lax.axis_index("cols")),
            device_id_type=pl.DeviceIdType.MESH,
        )
        for i in range(1, ranks)
    ]


def row_piece(r, piece):
    return pl.ds(pl.multiple_of(r * piece, piece), piece)


def pick_kernel(ranks, flat, out, picked, send, recv):
    my_row = lax.axis_index("rows")
    piece = out.shape[0]
    barrier = pltpu.get_barrier_semaphore()
    for i in range(1, ranks):
        pl.semaphore_signal(
            barrier,
            inc=1,
            device_id=(lax.rem(my_row + i, ranks), lax.axis_index("cols")),
            device_id_type=pl.DeviceIdType.MESH,
        )
    pl.semaphore_wait(barrier, ranks - 1)
    copies = row_copies(
        ranks, lambda i: flat.at[row_piece(lax.rem(my_row + i, ranks), piece)], picked, send, recv
    )
    for c in copies:
        c.start()
    for c in copies:
        c.wait()
    total = flat[row_piece(my_row, piece), :]
    for i in range(1, ranks):
        total = total + picked[i]
    out[...] = total


def sum_kernel(
    ranks, groups, own, mine, out, flat_out, got, done, send_sem, recv_sem, give_send, give_recv
):
    devices = ranks * groups
    my_row = lax.axis_index("rows")
    me = my_row * groups + lax.axis_index("cols")
    piece = mine.shape[0]

    def place(i):
        other = lax.rem(me + i, devices)
        return lax.div(other, groups), lax.rem(other, groups)

    def copy(i):
        return pltpu.make_async_remote_copy(
            src_ref=own,
            dst_ref=got.at[i],
            send_sem=send_sem.at[i],
            recv_sem=recv_sem.at[i],
            device_id=place(i),
            device_id_type=pl.DeviceIdType.MESH,
        )

    barrier = pltpu.get_barrier_semaphore()

    def greet(i, carry):
        pl.semaphore_signal(
            barrier, inc=1, device_id=place(i), device_id_type=pl.DeviceIdType.MESH
        )
        return carry

    def start(i, carry):
        copy(i).start()
        return carry

    def finish(i, carry):
        copy(i).wait()
        return carry

    lax.fori_loop(1, devices, greet, 0)
    pl.semaphore_wait(barrier, devices - 1)
    gives = row_copies(ranks, lambda i: mine, done, give_send, give_recv)
    for c in gives:
        c.start()
    lax.fori_loop(1, devices, start, 0)
    flat_out[row_piece(my_row, piece), :] = mine[...]
    lax.fori_loop(1, devices, finish, 0)
    out[...] = lax.fori_loop(1, devices, lambda i, total: total + got[i], own[...])
    for c in gives:
        c.wait()
    for i in range(1, ranks):
        flat_out[row_piece(lax.rem(my_row - i + ranks, ranks), piece), :] = done[i]


def split_kernel(expand_in, reduce_in, expand_out, reduce_out):
    expand_out[...] = expand_in[...]
    reduce_out[...] = reduce_in[...]


def wide_tables(width):
    freq = np.arange(BINS)
    place = np.arange(width)
    angle = (freq[:, None] * place[None, :] % width) * (2.0 * math.pi / width)
    live = (2 * freq <= width).astype(np.float64)[:, None]
    edge = (freq == 0) | (2 * freq == width)
    weight = np.where(edge, 1.0, 2.0)[:, None] * live
    cosine, sine = np.cos(angle), np.sin(angle)
    plain = np.concatenate([live * cosine, -live * sine], axis=0)
    doubled = np.concatenate([weight * cosine, -weight * sine], axis=0)
    return plain, doubled


def tall_tables(height, rows_here):
    pairs = rows_here // PAIR
    rows = pairs // PARTS
    order = np.array(
        [
            r * rows_here + h * pairs + q * rows + j
            for h in range(PAIR)
            for q in range(PARTS)
            for r in range(height // rows_here)
            for j in range(rows)
        ]
    )
    freq = np.arange(height)
    angle = (freq[:, None] * order[None, :] % height) * (2.0 * math.pi / height)
    cosine, sine = np.cos(angle), np.sin(angle)
    down = np.block([[cosine, sine], [-sine, cosine]])
    up = np.block([[cosine.T, -sine.T], [sine.T, cosine.T]])
    return down, up


def spread(weight):
    count = weight.shape[1]
    eye = jnp.eye(count, dtype=weight.dtype)
    full = jnp.einsum("rbio,bd->rbido", weight, eye)
    return full.reshape(2, count * BS, count * BS)


def gather_blocks(full):
    count = full.shape[1] // BS
    return jnp.stack(
        [full[:, b * BS : (b + 1) * BS, b * BS : (b + 1) * BS] for b in range(count)], axis=1
    )


def bias_rows(bias):
    return bias.reshape(2, -1)


def whole(shape):
    return pl.BlockSpec(shape, lambda *_: (0,) * len(shape))


def call(kernel, grid, in_specs, out_specs, out_shape, name, flops=0, nbytes=0, scratch=(), **kw):
    return pl.pallas_call(
        kernel,
        grid=(grid,),
        in_specs=in_specs,
        out_specs=out_specs,
        out_shape=out_shape,
        scratch_shapes=scratch,
        compiler_params=pltpu.CompilerParams(
            dimension_semantics=("arbitrary",), vmem_limit_bytes=VMEM
        ),
        cost_estimate=pl.CostEstimate(flops=flops, bytes_accessed=nbytes, transcendentals=0),
        name=name,
        **kw,
    )


def body(
    states,
    heights,
    widths,
    first_gain,
    first_shift,
    filter_inner,
    inner_bias,
    filter_outer,
    outer_bias,
    later_gain,
    later_shift,
    expand_weight,
    expand_bias,
    reduce_weight,
    reduce_bias,
    cotangent,
):
    frames, rows_here, cols_here, chans = states.shape
    ranks, groups = lax.axis_size("rows"), lax.axis_size("cols")
    assert frames == ranks and rows_here % (PAIR * PARTS) == 0
    height, breadth = rows_here * ranks, cols_here * groups
    devices = ranks * groups
    pairs = rows_here // PAIR
    rows = pairs // PARTS
    pixels = rows * cols_here
    width = chans // groups
    lanes = width * PAIR
    hidden = expand_weight.shape[1]
    factor = 1.0 / math.sqrt(height * breadth)
    short = ranks * rows
    step_pixels = 8 if pixels % 8 == 0 else pixels
    steps = pixels // step_pixels
    tokens = PAIR * pixels * frames
    message = devices * pixels * lanes * 4
    row = lambda v: v.reshape(1, -1)
    shape = jax.ShapeDtypeStruct

    order = lambda v: jnp.transpose(v, (1, 2, 0, 3)).reshape(PAIR, pairs * cols_here, frames, chans)
    restore = lambda v: jnp.transpose(v.reshape(rows_here, cols_here, frames, chans), (2, 0, 1, 3))
    states_in, cot_in = order(states), order(cotangent)
    row_ids = lax.axis_index("rows") * rows_here + jnp.arange(rows_here, dtype=jnp.int32)
    col_ids = lax.axis_index("cols") * cols_here + jnp.arange(cols_here, dtype=jnp.int32)
    inside = (row_ids[:, None, None] < heights) & (col_ids[None, :, None] < widths)
    mask = jnp.broadcast_to(
        inside.astype(f32).reshape(PAIR, pairs * cols_here, frames, 1),
        (PAIR, pairs * cols_here, frames, 128),
    )

    buffers = {} if steps > 1 else {"pipeline_mode": pl.Buffered(1)}

    def token_spec(q, where, last=chans):
        return pl.BlockSpec(
            (PAIR, step_pixels, frames, last), lambda i: (0, q * steps + where(i), 0, 0), **buffers
        )

    def packed_spec(where):
        return pl.BlockSpec(
            (ranks, groups, step_pixels, lanes), lambda i: (0, 0, where(i), 0), **buffers
        )

    blocks_here = width // BS
    split = blocks_here > 1 and steps > 1 and (2 * PAIR * BS) % 128 == 0
    parties = blocks_here if split else 1
    cut = width // parties
    split_rows = 8 * (-(-steps // 2))

    def arrays_of(q):
        return parties if q == 0 else 1

    def message_specs(q, where):
        if arrays_of(q) == 1:
            return [packed_spec(where)]
        return [
            pl.BlockSpec(
                (ranks, groups, step_pixels, 2 * PAIR * cut), lambda i: (0, 0, where(i) // 2, 0)
            )
        ] * parties

    def message_shapes(q):
        if arrays_of(q) == 1:
            return [packed_shape]
        return [shape((ranks, groups, split_rows, 2 * PAIR * cut), f32)] * parties

    same = lambda i: i
    token_shape = shape((PAIR, pairs * cols_here, frames, chans), bf16)
    packed_shape = shape((ranks, groups, pixels, lanes), f32)
    chan_row = whole((1, chans))
    anywhere = pl.BlockSpec(memory_space=pl.ANY)

    def scatter(v, axis):
        return lax.psum_scatter(v, axis, scatter_dimension=0, tiled=True)

    def gather(v, axis):
        return lax.all_gather(v, axis, axis=0, tiled=True)

    vmem = pl.BlockSpec(memory_space=pltpu.VMEM)

    def as_rows(v, unit):
        v = v.reshape(-1)
        return jnp.pad(v, (0, -v.shape[0] % (unit * 128))).reshape(-1, 128)

    def pick_sums(v):
        flat = as_rows(v, 8 * ranks)
        piece = (flat.shape[0] // ranks, 128)
        return pl.pallas_call(
            functools.partial(pick_kernel, ranks),
            in_specs=[vmem],
            out_specs=vmem,
            out_shape=shape(piece, f32),
            scratch_shapes=[pltpu.VMEM((ranks,) + piece, f32)]
            + [pltpu.SemaphoreType.DMA((ranks,))] * 2,
            compiler_params=pltpu.CompilerParams(collective_id=1, has_side_effects=True),
            name="filter_sums",
        )(flat)

    def sum_small(v, mine):
        own = as_rows(v, 8)
        out, flat_out = pl.pallas_call(
            functools.partial(sum_kernel, ranks, groups),
            in_specs=[vmem, vmem],
            out_specs=[vmem, vmem],
            out_shape=[shape(own.shape, f32), shape((ranks * mine.shape[0], 128), f32)],
            scratch_shapes=[
                pltpu.VMEM((devices,) + own.shape, f32),
                pltpu.VMEM((ranks,) + mine.shape, f32),
            ]
            + [pltpu.SemaphoreType.DMA((devices,))] * 2
            + [pltpu.SemaphoreType.DMA((ranks,))] * 2,
            compiler_params=pltpu.CompilerParams(collective_id=0, has_side_effects=True),
            name="small_sums",
        )(own, mine)
        return out.reshape(-1)[: v.size].reshape(v.shape), flat_out.reshape(-1)

    def split_grads(v):
        cuts = 4
        piece = (chans // cuts, chans)
        return call(
            split_kernel,
            slabs * cuts,
            [
                pl.BlockSpec(piece, lambda i: (i, 0)),
                pl.BlockSpec(piece, lambda i: (slabs * cuts + i, 0)),
            ],
            [
                pl.BlockSpec(piece, lambda i: (lax.rem(i, cuts), lax.div(i, cuts))),
                pl.BlockSpec(piece, lambda i: (i, 0)),
            ],
            [shape((chans, hidden), f32), shape((hidden, chans), f32)],
            "split_gradients",
            nbytes=16 * chans * hidden,
        )(v, v)

    def behind(v, *after):
        return lax.optimization_barrier((v,) + after)[0] if after else v

    def exchange(v):
        sent = v.reshape((devices,) + v.shape[2:])
        return lax.all_to_all(sent, ("rows", "cols"), 0, 0, tiled=True).reshape(v.shape)

    def tie(*values):
        return lax.optimization_barrier(values)

    def first_norm(q):
        return call(
            functools.partial(first_kernel, width),
            steps,
            [token_spec(q, same), token_spec(q, same, 128), chan_row, chan_row],
            message_specs(q, same),
            message_shapes(q),
            "first_norm",
            nbytes=2 * message,
        )(states_in, mask, row(first_gain), row(first_shift))

    plain, doubled = wide_tables(breadth)
    down, up = tall_tables(height, rows_here)
    as_table = lambda t: jnp.asarray(t, dtype=bf16)

    def fine_table(t):
        high = t.astype(jnp.bfloat16)
        return jnp.asarray(np.concatenate([high, (t - high.astype(np.float64)).astype(jnp.bfloat16)]))

    def mixes(weight):
        return [weight[:, g] for g in range(parties)] if split else [spread(weight)]

    inner_full, outer_full = mixes(filter_inner), mixes(filter_outer)
    turn = lambda t: jnp.swapaxes(t, 1, 2)
    bin_steps = BINS // GROUP
    group_rows = GROUP * 2 * height
    held_shape = shape((short, 2, BINS, lanes), f32)
    at_once = 2
    held_row = pl.BlockSpec((at_once * rows, 2, BINS, lanes), lambda i: (i, 0, 0, 0))
    held_bins = pl.BlockSpec((short, 2, GROUP, lanes), lambda i: (0, 0, i, 0))
    field = pl.BlockSpec((at_once, groups, pixels, lanes), lambda i: (i, 0, 0, 0))
    kept = pl.BlockSpec((group_rows, cut), lambda i: (i, 0))
    kept_shape = shape((bin_steps * group_rows, cut), bf16)
    mix_spec = whole((2, cut, cut))
    bias_spec = whole((2, cut))

    def held_of(last, by_row):
        if by_row:
            return pl.BlockSpec((at_once * rows, 2, BINS, last), lambda i: (i, 0, 0, 0))
        return pl.BlockSpec((short, 2, GROUP, last), lambda i: (0, 0, i, 0))

    cut_shape = shape((short, 2, BINS, PAIR * cut), f32)
    split_field = pl.BlockSpec(
        (at_once, groups, split_rows, 2 * PAIR * cut), lambda i: (i, 0, 0, 0)
    )
    natural = pltpu.VMEM((at_once, groups, pixels, PAIR * cut), f32)
    cut_in = [held_of(PAIR * cut if split else lanes, False)] + [held_bins] * (PARTS - 1)
    cut_out = [held_of(PAIR * cut, False)] * PARTS
    up_spec = whole((2 * height, 2 * height))

    def wide_in(v, table, fine):
        divided = v.shape != packed_shape.shape
        return call(
            functools.partial(wide_in_split_kernel if divided else wide_in_kernel, cols_here, fine),
            ranks // at_once,
            [split_field if divided else field, whole(table.shape)],
            held_of(PAIR * cut, True) if divided else held_row,
            cut_shape if divided else held_shape,
            "wide_in",
            nbytes=2 * message,
            scratch=[pltpu.VMEM((at_once * rows, breadth, PAIR * cut), f32), natural]
            if divided
            else [pltpu.VMEM((at_once * rows, breadth, lanes), f32)],
        )(v, table)

    def wide_out(parts, table):
        return call(
            functools.partial(wide_out_kernel, cols_here, factor),
            ranks // at_once,
            [held_of(v.shape[3], True) for v in parts] + [whole(table.shape)],
            field,
            packed_shape,
            "wide_out",
            nbytes=2 * message,
        )(*parts, table)

    def wide_out_split(part, table):
        return call(
            functools.partial(wide_out_split_kernel, cols_here, factor),
            ranks // at_once,
            [held_of(PAIR * cut, True), whole(table.shape)],
            split_field,
            message_shapes(0)[0],
            "wide_out",
            nbytes=2 * message,
            scratch=[natural],
        )(part, table)

    def messages_out(given, table):
        first = [wide_out_split(v[0], table) for v in given] if split else [wide_out([given[0][0]], table)]
        return first + [wide_out([v[q] for v in given], table) for q in range(1, PARTS)]

    def of_group(v, g):
        return bias_rows(v)[:, g * cut : (g + 1) * cut]

    forward_mix = [
        (inner_full[g], of_group(inner_bias, g), outer_full[g], of_group(outer_bias, g))
        for g in range(parties)
    ]
    forward_specs = [mix_spec, bias_spec, mix_spec, bias_spec]

    def spectral_forward(g, held):
        table = fine_table(down)
        outs = call(
            functools.partial(spectral_forward_kernel, factor, g),
            bin_steps,
            cut_in + [whole(table.shape), up_spec] + forward_specs,
            cut_out + [kept],
            [cut_shape] * PARTS + [kept_shape],
            "spectral_forward",
            flops=20 * 10**9,
            nbytes=8 * PARTS * message // parties,
        )(*held, table, as_table(up), *forward_mix[g])
        return outs[:PARTS], outs[PARTS]

    full = pl.BlockSpec((group_rows, width), lambda i: (i, 0))
    full_shape = shape((bin_steps * group_rows, width), bf16)
    full_mix, full_bias = whole((2, width, width)), whole((2, width))
    inner_t, outer_t = turn(spread(filter_inner)), turn(spread(filter_outer))

    def spectral_keep(entries):
        return call(
            functools.partial(spectral_keep_kernel, height, parties),
            bin_steps,
            [kept] * parties + forward_specs * parties,
            [full] * 3,
            [full_shape] * 3,
            "spectral_keep",
            flops=10 * 10**9,
            nbytes=2 * PARTS * message,
        )(*entries, *[v for mix in forward_mix for v in mix])

    def spectral_backward(held, slope, damp):
        outs = call(
            functools.partial(spectral_backward_kernel, factor, 1),
            bin_steps,
            [held_bins] * PARTS + [up_spec, up_spec, full_mix, full_mix] + [full] * 2,
            [held_bins] * PARTS + [full, full_bias] * 2,
            [held_shape] * PARTS + [full_shape, shape((2, width), f32)] * 2,
            "spectral_backward",
            flops=20 * 10**9,
            nbytes=8 * PARTS * message,
        )(*held, as_table(down), as_table(up), inner_t, outer_t, slope, damp)
        return outs[:PARTS], outs[PARTS:]

    def filter_grad(entries, active, inner_low, outer_low):
        return call(
            functools.partial(filter_grad_kernel, height, parties),
            bin_steps,
            [kept] * parties + [full] * 3,
            [full_mix] * 2,
            [shape((2, width, width), f32)] * 2,
            "filter_grad",
            flops=10 * 10**9,
            nbytes=2 * PARTS * message,
        )(*entries, active, inner_low, outer_low)

    slab = chans
    slabs = hidden // slab
    dense_steps = 2 * steps + slabs
    enter = lambda i: jnp.minimum(i, steps - 1)
    leave = lambda i: jnp.maximum(i - steps - slabs, 0)
    either = lambda i: jnp.where(i < steps + slabs, enter(i), leave(i))

    def dense(q, spatial, before):
        grads_before = () if q == 0 else before
        return call(
            functools.partial(dense_kernel, steps, slabs, width, q == 0, arrays_of(q)),
            dense_steps,
            message_specs(q, enter)
            + [token_spec(q, enter), token_spec(q, enter), token_spec(q, either, 128)]
            + [chan_row] * 4
            + [pl.BlockSpec((1, slab), lambda i: (0, jnp.clip(i - steps, 0, slabs - 1)))]
            + [chan_row]
            + [anywhere] * (2 + len(grads_before)),
            [packed_spec(leave)]
            + [
                token_spec(q, leave),
                token_spec(0, leave),
                whole((8, chans)),
                whole((slabs, slab)),
                anywhere,
            ],
            [packed_shape]
            + [
                token_shape,
                shape((PAIR, pixels, frames, chans), f32),
                shape((8, chans), f32),
                shape((slabs, slab), f32),
                shape((2 * hidden, chans), f32),
            ],
            "dense_both_ways",
            flops=12 * tokens * chans * hidden,
            nbytes=4 * message,
            scratch=[
                pltpu.VMEM((slabs, chans, slab), bf16),
                pltpu.VMEM((hidden, chans), bf16),
                pltpu.VMEM((slabs, chans, slab), f32),
                pltpu.VMEM((hidden, chans), f32),
                pltpu.VMEM((tokens, chans), f32),
                pltpu.VMEM((tokens, chans), bf16),
                pltpu.VMEM((tokens, chans), bf16),
                pltpu.VMEM((tokens, chans), f32),
                pltpu.VMEM((tokens, chans), f32),
                pltpu.VMEM((tokens, slab), bf16),
                pltpu.VMEM((tokens, slab), bf16),
                pltpu.SemaphoreType.DMA((2 * slabs + 2,)),
            ],
            input_output_aliases={} if q == 0 else {13: 1},
        )(
            *spatial,
            states_in,
            cot_in,
            mask,
            row(first_gain),
            row(first_shift),
            row(later_gain),
            row(later_shift),
            row(expand_bias),
            row(reduce_bias),
            expand_weight,
            reduce_weight,
            *grads_before,
        )

    def last_norm(q, later_grad, spatial, before):
        given = () if q == 0 else (before,)
        return call(
            functools.partial(last_kernel, width, 1),
            steps,
            [packed_spec(same)]
            + [token_spec(q, same), token_spec(0, same), token_spec(q, same, 128)]
            + [chan_row]
            + [anywhere] * len(given),
            [token_spec(q, same), whole((8, chans))],
            [token_shape, shape((8, chans), f32)],
            "first_norm_backward",
            nbytes=4 * message,
            input_output_aliases={} if q == 0 else {5: 0},
        )(spatial, states_in, later_grad, mask, row(first_gain), *given)

    every = range(PARTS)

    def send(made, got):
        if got:
            made, got[-1] = tie(made, got[-1])
        got.append(exchange(made))

    made = [v for q in (*every[1:], 0) for v in first_norm(q)]
    got, held = [], []
    for n, v in enumerate(made):
        if n > 1:
            v, held[-1] = tie(v, held[-1])
        send(v, got)
        if n > 0:
            held.append(wide_in(got[-2], fine_table(plain), True))
    held.append(wide_in(got[-1], fine_table(plain), True))
    rest, first = held[: PARTS - 1], held[PARTS - 1 :]
    done = [spectral_forward(g, [first[g]] + rest) for g in range(parties)]
    entries = [v[1] for v in done]
    made = messages_out([v[0] for v in done], as_table(doubled.T))
    active, slope, damp = spectral_keep(entries)

    spatial = got[-1:]
    for n in range(parties):
        send(made[n], spatial)
    active, made[parties] = tie(active, made[parties])
    spatial = spatial[1:]
    backs, later_grads, sums, expand_bias_grad, before = [], [], 0.0, 0.0, ()
    for q in every:
        if q + 1 < PARTS:
            if backs:
                made[parties + q], backs[-1] = tie(made[parties + q], backs[-1])
            send(made[parties + q], spatial)
        received = spatial[:parties] if q == 0 else spatial[parties + q - 1 : parties + q]
        if q + 1 == PARTS:
            backs[-1], spatial[-1] = tie(backs[-1], spatial[-1])
            got = [exchange(backs[1])]
            received = spatial[-1:]
        outs = dense(q, received, before)
        back, result, kept_grad, part, bias_part, grads = outs
        backs.append(back)
        before = (grads, result)
        later_grads.append(kept_grad)
        sums, expand_bias_grad = sums + part, expand_bias_grad + bias_part
    grads, got[0] = tie(grads, got[0])
    grads = scatter(grads, "cols")
    held = []
    for v in [backs[q] for q in (*every[2:], 0)]:
        held.append(wide_in(got[-1], as_table(doubled), False))
        if len(held) > 1:
            v, held[-2] = tie(v, held[-2])
        send(v, got)
    got[-1], held[-1] = tie(got[-1], held[-1])
    held.append(wide_in(got[-1], as_table(doubled), False))
    grads, held[-1] = tie(grads, held[-1])
    grads = scatter(grads, "rows")
    given, (inner_low, inner_bias_grad, outer_low, outer_bias_grad) = spectral_backward(
        [held[-1]] + held[:-1], slope, damp
    )
    made = [wide_out([v], as_table(plain.T)) for v in given]
    inner_grad, outer_grad = filter_grad(entries, active, inner_low, outer_low)
    filter_parts = (
        gather_blocks(inner_grad), inner_bias_grad, gather_blocks(outer_grad), outer_bias_grad
    )
    flat = jnp.concatenate([v.reshape(-1) for v in filter_parts])

    got = [exchange(made[0])]
    send(made[1], got)
    grads, got[0] = tie(grads, got[0])
    grads = gather(grads, ("cols", "rows"))
    first_sums, states_grad = [], None
    for q in every:
        if q + 1 < PARTS:
            if q > 0:
                made[q + 1], first_sums[-1] = tie(made[q + 1], first_sums[-1])
                send(made[q + 1], got)
        else:
            flat, first_sums[-1] = tie(flat, first_sums[-1])
            flat = pick_sums(flat)
            grads, flat = tie(grads, flat)
            expand_sum, reduce_sum = split_grads(grads)
            states_grad, expand_sum = tie(states_grad, expand_sum)
        states_grad, part = last_norm(q, later_grads[q], got[q], states_grad)
        first_sums.append(part)
        if q == 0:
            flat, first_sums[0] = tie(flat, first_sums[0])
    small, flat = sum_small(
        jnp.concatenate([sum(first_sums)[:2], sums[:3], expand_bias_grad.reshape(-1, chans)]), flat
    )
    sizes = [v.size for v in filter_parts]
    ends = np.cumsum(sizes)
    filter_sums = [
        flat[e - n : e].reshape(v.shape) for e, n, v in zip(ends, sizes, filter_parts)
    ]
    inner_sum, inner_bias_sum, outer_sum, outer_bias_sum = filter_sums
    return (
        restore(result),
        restore(states_grad),
        small[0],
        small[1],
        inner_sum,
        inner_bias_sum.reshape(2, -1, BS),
        outer_sum,
        outer_bias_sum.reshape(2, -1, BS),
        small[3],
        small[4],
        expand_sum,
        small[5:].reshape(-1),
        reduce_sum,
        small[2],
    )


def solution(mesh):
    tile = P(None, "rows", "cols", None)
    mix = P(None, "cols", None, None)
    bias = P(None, "cols", None)
    in_specs = (
        tile, P(), P(), P(), P(), mix, bias, mix, bias, P(), P(), P(), P(), P(), P(), tile,
    )
    out_specs = (
        tile, tile, P(), P(), mix, bias, mix, bias, P(), P(), P(), P(), P(), P(),
    )
    return jax.shard_map(body, mesh=mesh, in_specs=in_specs, out_specs=out_specs, check_vma=False)
```

```python
import functools
import math

import jax
import jax.numpy as jnp
import numpy as np
from jax import lax
from jax.experimental import pallas as pl
from jax.experimental.pallas import tpu as pltpu
from jax.sharding import PartitionSpec as P

BS = 96
BINS = 96
PAIR = 2
GROUP = 8
PARTS = 3
norm_eps = 1e-06
shrink_width = 0.01
VMEM = 60 * 1024 * 1024
f32 = jnp.float32
bf16 = jnp.bfloat16


def phi_parts(v):
    cdf = 0.5 * (1.0 + lax.erf(v * math.sqrt(0.5)))
    slope = cdf + v * (jnp.exp(v * v * -0.5) * (1.0 / math.sqrt(2.0 * math.pi)))
    return cdf, slope


def dot(a, b):
    return lax.dot_general(a, b, (((1,), (0,)), ((), ())), preferred_element_type=f32)


def dot_tn(a, b):
    return lax.dot_general(a, b, (((0,), (0,)), ((), ())), preferred_element_type=f32)


def dot_nt(a, b):
    return lax.dot_general(a, b, (((1,), (1,)), ((), ())), preferred_element_type=f32)


def standardize(v):
    centre = jnp.mean(v, axis=-1, keepdims=True)
    centred = v - centre
    spread = jnp.mean(centred * centred, axis=-1, keepdims=True)
    scale = lax.rsqrt(spread + norm_eps)
    return centred * scale, scale


def standardize_back(grad, normal, scale):
    first = jnp.mean(grad, axis=-1, keepdims=True)
    second = jnp.mean(grad * normal, axis=-1, keepdims=True)
    return scale * (grad - first - normal * second)


def pack(sides, outs, width, step):
    turned = [jnp.swapaxes(s, 0, 1) for s in sides]
    cut = width // len(outs)

    def lanes_of(c, g):
        start = c * width + g * cut
        return jnp.concatenate([t[:, :, start : start + cut] for t in turned], axis=2)

    for g, out in enumerate(outs):
        values = [lanes_of(c, g) for c in range(out.shape[1])]
        if len(outs) == 1:
            for c, v in enumerate(values):
                out[:, c] = v
            continue

        @pl.when(lax.rem(step, 2) == 0)
        def _():
            for c, v in enumerate(values):
                out[:, c] = jnp.concatenate([v, v], axis=2)

        @pl.when(lax.rem(step, 2) == 1)
        def _():
            for c, v in enumerate(values):
                out[:, c] = jnp.concatenate([out[:, c, :, : PAIR * cut], v], axis=2)


def unpack(refs, half, width, step):
    cut = width // len(refs)
    parts = []
    for c in range(refs[0].shape[1]):
        for ref in refs:
            part = ref[:, c, :, half * cut : (half + 1) * cut]
            if len(refs) > 1:
                later = (PAIR + half) * cut
                part = jnp.where(lax.rem(step, 2) == 1, ref[:, c, :, later : later + cut], part)
            parts.append(part)
    return jnp.swapaxes(jnp.concatenate(parts, axis=2) if len(parts) > 1 else parts[0], 0, 1)


def first_kernel(width, states, mask, gain, shift, *outs):
    sides = []
    for half in range(PAIR):
        inside = mask[half][..., :1]
        normal, _ = standardize(states[half].astype(f32) * inside)
        sides.append(inside * (normal * gain[...] + shift[...]))
    pack(sides, outs, width, pl.program_id(0))


def table_dot(table, x):
    rows = table.shape[0] // 2
    high = x.astype(bf16)
    both = dot(table[...], high)
    rest = dot(table[:rows, :], (x - high.astype(f32)).astype(bf16))
    return both[:rows] + both[rows:] + rest


def wide_in_kernel(cols_here, fine, block, table, held, wide):
    groups, rows = block.shape[1], block.shape[2] // cols_here
    for n in range(block.shape[0] * rows):
        r, j = divmod(n, rows)
        for c in range(groups):
            wide[n, c * cols_here : (c + 1) * cols_here, :] = block[
                r, c, j * cols_here : (j + 1) * cols_here, :
            ]
        x = wide[n]
        y = table_dot(table, x) if fine else dot(table[...], x.astype(bf16))
        held[n, 0] = y[:BINS]
        held[n, 1] = y[BINS:]


def wide_out_kernel(cols_here, factor, *refs):
    held, (table, block) = refs[:-2], refs[-2:]
    groups, rows = block.shape[1], block.shape[2] // cols_here
    cut = held[0].shape[3] // PAIR
    for n in range(block.shape[0] * rows):
        r, j = divmod(n, rows)
        x = [jnp.concatenate([part[n, 0], part[n, 1]], axis=0) for part in held]
        if len(x) > 1:
            x = [part[:, h * cut : (h + 1) * cut] for h in range(PAIR) for part in x]
            x = jnp.concatenate(x, axis=1)
        else:
            x = x[0]
        plane = dot(table[...], x.astype(bf16)) * factor
        for c in range(groups):
            block[r, c, j * cols_here : (j + 1) * cols_here, :] = plane[
                c * cols_here : (c + 1) * cols_here, :
            ]


def wide_in_split_kernel(cols_here, fine, block, table, held, wide, natural):
    groups, half = block.shape[1], block.shape[3] // 2
    rows = natural.shape[2] // cols_here
    for r in range(block.shape[0]):
        for c in range(groups):
            for s in range(natural.shape[2] // 8):
                natural[r, c, s * 8 : s * 8 + 8, :] = block[
                    r, c, (s // 2) * 8 : (s // 2) * 8 + 8, (s % 2) * half : (s % 2 + 1) * half
                ]
        for j in range(rows):
            n = r * rows + j
            for c in range(groups):
                wide[n, c * cols_here : (c + 1) * cols_here, :] = natural[
                    r, c, j * cols_here : (j + 1) * cols_here, :
                ]
            x = wide[n]
            y = table_dot(table, x) if fine else dot(table[...], x.astype(bf16))
            held[n, 0] = y[:BINS]
            held[n, 1] = y[BINS:]


def wide_out_split_kernel(cols_here, factor, held, table, block, natural):
    groups = block.shape[1]
    rows = natural.shape[2] // cols_here
    last = natural.shape[2] // 8 - 1
    for r in range(block.shape[0]):
        for j in range(rows):
            n = r * rows + j
            x = jnp.concatenate([held[n, 0], held[n, 1]], axis=0).astype(bf16)
            plane = dot(table[...], x) * factor
            for c in range(groups):
                natural[r, c, j * cols_here : (j + 1) * cols_here, :] = plane[
                    c * cols_here : (c + 1) * cols_here, :
                ]
        for c in range(groups):
            for m in range(block.shape[2] // 8):
                sides = [natural[r, c, at * 8 : at * 8 + 8, :] for at in (2 * m, min(2 * m + 1, last))]
                block[r, c, m * 8 : m * 8 + 8, :] = jnp.concatenate(sides, axis=1)


def bins_in(held, table, width, group, fine):
    kind = f32 if fine else bf16

    def lane(part, h):
        whole_width = part.shape[-1] // PAIR
        return h * whole_width + (group * width if whole_width > width else 0)

    turned = [
        [jnp.swapaxes(part[:, side], 0, 1).astype(kind) for part in held] for side in range(2)
    ]
    outs = []
    for k in range(GROUP):
        x = jnp.concatenate(
            [
                part[k][:, lane(part, h) : lane(part, h) + width]
                for side in turned
                for h in range(PAIR)
                for part in side
            ],
            axis=0,
        )
        outs.append(table_dot(table, x) if fine else dot(table[...], x))
    return outs


def bins_out(held, table, width, values):
    short = held[0].shape[0]
    count = len(held)
    products = [dot(table[...], value) for value in values]
    for side in range(2):
        for q in range(count):
            rows = []
            for z in products:
                at = [((side * PAIR + h) * count + q) * short for h in range(PAIR)]
                rows.append(jnp.concatenate([z[a : a + short] for a in at], axis=1))
            held[q][:, side] = jnp.swapaxes(jnp.stack(rows, axis=0), 0, 1)


def halves(v, count, tall):
    return [
        (v[k * 2 * tall : k * 2 * tall + tall], v[k * 2 * tall + tall : (k + 1) * 2 * tall])
        for k in range(count)
    ]


def complex_product(x, first, second, count, tall, conj):
    a = dot(x, first)
    b = dot(x, second)
    parts = []
    for (a_re, a_im), (b_re, b_im) in zip(halves(a, count, tall), halves(b, count, tall)):
        if conj:
            parts += [a_re + b_im, a_im - b_re]
        else:
            parts += [a_re - b_im, a_im + b_re]
    return parts


def activate(low, mix, bias, tall):
    parts = complex_product(low, mix[0], mix[1], low.shape[0] // (2 * tall), tall, False)
    return [part + bias[n % 2 : n % 2 + 1, :] for n, part in enumerate(parts)]


def gelu_low(v):
    return (v * (0.5 * (1.0 + lax.erf(v * math.sqrt(0.5))))).astype(bf16)


def spectral_forward_kernel(factor, group, *refs):
    held, refs = refs[:PARTS], refs[PARTS:]
    table_down, table_up, inner, inner_bias, outer, outer_bias = refs[:6]
    given, entries = refs[6 : 6 + PARTS], refs[6 + PARTS]
    width = inner.shape[2]
    tall = table_up.shape[0] // 2
    spec = bins_in(held, table_down, width, group, True)
    low = jnp.concatenate([(s * factor).astype(bf16) for s in spec], axis=0)
    entries[...] = low
    act = jnp.concatenate([gelu_low(v) for v in activate(low, inner, inner_bias, tall)], axis=0)
    shrunk = [
        (v - shrink_width * jnp.tanh(v * (1.0 / shrink_width))).astype(bf16)
        for v in activate(act, outer, outer_bias, tall)
    ]
    values = [jnp.concatenate(shrunk[2 * k : 2 * k + 2], axis=0) for k in range(GROUP)]
    bins_out(given, table_up, width, values)


def spectral_keep_kernel(tall, parties, *refs):
    entries, refs = refs[:parties], refs[parties:]
    mixes, (active, slope, damp) = refs[: 4 * parties], refs[4 * parties :]

    def joined_parts(each):
        return [jnp.concatenate(v, axis=1) if parties > 1 else v[0] for v in zip(*each)]

    acts, slopes, damps = [], [], []
    for g in range(parties):
        inner, inner_bias, outer, outer_bias = mixes[4 * g : 4 * g + 4]
        acts.append([])
        slopes.append([])
        damps.append([])
        for v in activate(entries[g][...], inner, inner_bias, tall):
            cdf, der = phi_parts(v)
            acts[g].append((v * cdf).astype(bf16))
            slopes[g].append(der.astype(bf16))
        for v in activate(jnp.concatenate(acts[g], axis=0), outer, outer_bias, tall):
            t = jnp.tanh(v * (1.0 / shrink_width))
            damps[g].append((t * t).astype(bf16))
    for ref, each in ((active, acts), (slope, slopes), (damp, damps)):
        for n, v in enumerate(joined_parts(each)):
            ref[n * tall : (n + 1) * tall, :] = v


def joined(refs):
    return jnp.concatenate([r[...] for r in refs], axis=1) if len(refs) > 1 else refs[0][...]


def spectral_backward_kernel(factor, parties, *refs):
    held, refs = refs[:PARTS], refs[PARTS:]
    table_down, table_up, inner_t, outer_t = refs[:4]
    slope, damp = joined(refs[4 : 4 + parties]), joined(refs[4 + parties : 4 + 2 * parties])
    refs = refs[4 + 2 * parties :]
    given, refs = refs[:PARTS], refs[PARTS:]
    inner_low, inner_bias_grad, outer_low, outer_bias_grad = refs
    width = inner_t.shape[2]
    tall = table_up.shape[0] // 2

    @pl.when(pl.program_id(0) == 0)
    def _():
        for ref in (inner_bias_grad, outer_bias_grad):
            ref[...] = jnp.zeros_like(ref)

    spec = bins_in(held, table_down, width, 0, False)
    grads = []
    sums = [0.0, 0.0]
    for k in range(GROUP):
        for side in range(2):
            at = (2 * k + side) * tall
            g = spec[k][side * tall : (side + 1) * tall] * factor
            g = g * damp[at : at + tall].astype(f32)
            sums[side] = sums[side] + jnp.sum(g, axis=0, keepdims=True)
            grads.append(g.astype(bf16))
    outer_bias_grad[...] += jnp.concatenate(sums, axis=0)
    low = jnp.concatenate(grads, axis=0)
    outer_low[...] = low
    parts = complex_product(low, outer_t[0], outer_t[1], GROUP, tall, True)
    grads = []
    sums = [0.0, 0.0]
    for n, part in enumerate(parts):
        g = part * slope[n * tall : (n + 1) * tall].astype(f32)
        sums[n % 2] = sums[n % 2] + jnp.sum(g, axis=0, keepdims=True)
        grads.append(g.astype(bf16))
    inner_bias_grad[...] += jnp.concatenate(sums, axis=0)
    low = jnp.concatenate(grads, axis=0)
    inner_low[...] = low
    parts = complex_product(low, inner_t[0], inner_t[1], GROUP, tall, True)
    values = [
        jnp.concatenate([parts[2 * k], parts[2 * k + 1]], axis=0).astype(bf16)
        for k in range(GROUP)
    ]
    bins_out(given, table_up, width, values)


def filter_grad_kernel(tall, parties, *refs):
    entries, active = refs[:parties], refs[parties : parties + 1]
    inner_low, outer_low, inner_grad, outer_grad = refs[parties + 1 :]

    @pl.when(pl.program_id(0) == 0)
    def _():
        inner_grad[...] = jnp.zeros_like(inner_grad)
        outer_grad[...] = jnp.zeros_like(outer_grad)

    for before, low, grad in ((entries, inner_low, inner_grad), (active, outer_low, outer_grad)):
        turned = []
        for k in range(GROUP):
            top, bottom = low[2 * k * tall : (2 * k + 1) * tall], low[(2 * k + 1) * tall : (2 * k + 2) * tall]
            turned += [bottom, -top]
        known = joined(before)
        grad[0] += dot_tn(known, low[...])
        grad[1] += dot_tn(known, jnp.concatenate(turned, axis=0))


def dense_kernel(steps, slabs, width, first_part, arrays, *refs):
    spat, refs = refs[:arrays], refs[arrays:]
    (
        states, cot, mask, first_gain, first_shift, later_gain, later_shift,
        expand_bias, reduce_bias, expand_hbm, reduce_hbm,
    ) = refs[:11]
    refs = refs[11:]
    if not first_part:
        grads_before = refs[0]
        refs = refs[2:]
    back, refs = refs[:1], refs[1:]
    result, later_grad, sums, expand_bias_grad, grads_hbm = refs[:5]
    (
        expand, reduce, expand_grad, reduce_grad, mixed, normed, low_out, branch, grad_n,
        hidden_all, grad_all, copy_sem,
    ) = refs[5:]
    step = pl.program_id(0)
    chans = states.shape[3]
    side_tokens = states.shape[1] * states.shape[2]
    slab = expand.shape[2]
    tokens = mixed.shape[0]
    square = states.shape[1:]

    def parts_of(grads):
        pairs = [(grads.at[pl.ds(s * chans, chans)], expand_grad.at[s]) for s in range(slabs)]
        return pairs + [(grads.at[pl.ds(slabs * chans, slabs * slab)], reduce_grad)]

    def fetches():
        copies = [
            pltpu.make_async_copy(
                expand_hbm.at[:, pl.ds(s * slab, slab)], expand.at[s], copy_sem.at[s]
            )
            for s in range(slabs)
        ]
        copies.append(pltpu.make_async_copy(reduce_hbm, reduce, copy_sem.at[slabs]))
        if not first_part:
            copies += [
                pltpu.make_async_copy(far, near, copy_sem.at[slabs + 1 + n])
                for n, (far, near) in enumerate(parts_of(grads_before))
            ]
        return copies

    @pl.when(step == 0)
    def _():
        for c in fetches():
            c.start()
        if first_part:
            expand_grad[...] = jnp.zeros_like(expand_grad)
            reduce_grad[...] = jnp.zeros_like(reduce_grad)
        sums[...] = jnp.zeros_like(sums)
        expand_bias_grad[...] = jnp.zeros_like(expand_bias_grad)

    @pl.when(step < steps)
    def _():
        start = pl.multiple_of(step * (PAIR * side_tokens), PAIR * side_tokens)
        for half in range(PAIR):
            at = pl.ds(start + half * side_tokens, side_tokens)
            inside = mask[half][..., :1]
            lower = inside * states[half].astype(f32)
            first, _ = standardize(lower)
            filter_in = first * first_gain[...] + first_shift[...]
            full = lower + inside * (unpack(spat, half, width, step) + filter_in)
            later, _ = standardize(full)
            full = full.reshape(side_tokens, chans)
            mixed[at, :] = full
            branch[at, :] = full + reduce_bias[...]
            normal = (later * later_gain[...] + later_shift[...]).reshape(side_tokens, chans)
            normed[at, :] = normal.astype(bf16)
            go = (inside * cot[half].astype(f32)).reshape(side_tokens, chans)
            low_out[at, :] = go.astype(bf16)
            grad_n[at, :] = jnp.zeros_like(full)
            sums[0:1, :] += jnp.sum(go, axis=0, keepdims=True)

    @pl.when(step == steps)
    def _():
        for c in fetches():
            c.wait()

    @pl.when((step >= steps) & (step < steps + slabs))
    def _():
        hc = step - steps
        at = pl.ds(pl.multiple_of(hc * slab, slab), slab)
        piece = tokens // 4 if tokens % 64 == 0 else tokens

        def some(n, carry):
            here = pl.ds(pl.multiple_of(n * piece, piece), piece)
            weight_up = expand[hc]
            weight_down = reduce[at, :]
            go = low_out[here, :]
            pre = dot(normed[here, :], weight_up) + expand_bias[...]
            cdf, der = phi_parts(pre)
            hidden = (pre * cdf).astype(bf16)
            hidden_all[here, :] = hidden
            branch[here, :] += dot(hidden, weight_down)
            grad_pre = dot_nt(go, weight_down) * der
            expand_bias_grad[pl.ds(hc, 1), :] += jnp.sum(grad_pre, axis=0, keepdims=True)
            grad_low = grad_pre.astype(bf16)
            grad_all[here, :] = grad_low
            grad_n[here, :] += dot_nt(grad_low, weight_up)
            return carry

        lax.fori_loop(0, tokens // piece, some, 0)
        reduce_grad[at, :] += dot_tn(hidden_all[...], low_out[...])
        expand_grad[hc] += dot_tn(normed[...], grad_all[...])

    @pl.when(step >= steps + slabs)
    def _():
        start = pl.multiple_of(
            (step - steps - slabs) * (PAIR * side_tokens), PAIR * side_tokens
        )
        sides = []
        for half in range(PAIR):
            at = pl.ds(start + half * side_tokens, side_tokens)
            inside = mask[half][..., :1]
            later, scale = standardize(mixed[at, :])
            g = grad_n[at, :]
            sums[1:2, :] += jnp.sum(g * later, axis=0, keepdims=True)
            sums[2:3, :] += jnp.sum(g, axis=0, keepdims=True)
            g = low_out[at, :].astype(f32) + standardize_back(g * later_gain[...], later, scale)
            sides.append(inside * g.reshape(square))
            later_grad[half] = sides[-1]
            result[half] = (inside * branch[at, :].reshape(square)).astype(bf16)
        pack(sides, back, width, step - steps - slabs)

    @pl.when(step == pl.num_programs(0) - 1)
    def _():
        copies = [
            pltpu.make_async_copy(near, far, copy_sem.at[n])
            for n, (far, near) in enumerate(parts_of(grads_hbm))
        ]
        for c in copies:
            c.start()
        for c in copies:
            c.wait()


def last_kernel(width, arrays, *refs):
    spat, (states, later_grad, mask, gain) = refs[:arrays], refs[arrays : arrays + 4]
    out, sums = refs[-2:]
    chans = states.shape[3]

    @pl.when(pl.program_id(0) == 0)
    def _():
        sums[...] = jnp.zeros_like(sums)

    for half in range(PAIR):
        inside = mask[half][..., :1]
        normal, scale = standardize(inside * states[half].astype(f32))
        grad_mixed = later_grad[half]
        grad = inside * (grad_mixed + unpack(spat, half, width, pl.program_id(0)))
        flat = (-1, chans)
        sums[0:1, :] += jnp.sum((grad * normal).reshape(flat), axis=0, keepdims=True)
        sums[1:2, :] += jnp.sum(grad.reshape(flat), axis=0, keepdims=True)
        grad = grad_mixed + standardize_back(grad * gain[...], normal, scale)
        out[half] = (inside * grad).astype(bf16)


def row_copies(ranks, sources, slots, send, recv):
    my_row = lax.axis_index("rows")
    return [
        pltpu.make_async_remote_copy(
            src_ref=sources(i),
            dst_ref=slots.at[i],
            send_sem=send.at[i],
            recv_sem=recv.at[i],
            device_id=(lax.rem(my_row + i, ranks), lax.axis_index("cols")),
            device_id_type=pl.DeviceIdType.MESH,
        )
        for i in range(1, ranks)
    ]


def row_piece(r, piece):
    return pl.ds(pl.multiple_of(r * piece, piece), piece)


def pick_kernel(ranks, flat, out, picked, send, recv):
    my_row = lax.axis_index("rows")
    piece = out.shape[0]
    barrier = pltpu.get_barrier_semaphore()
    for i in range(1, ranks):
        pl.semaphore_signal(
            barrier,
            inc=1,
            device_id=(lax.rem(my_row + i, ranks), lax.axis_index("cols")),
            device_id_type=pl.DeviceIdType.MESH,
        )
    pl.semaphore_wait(barrier, ranks - 1)
    copies = row_copies(
        ranks, lambda i: flat.at[row_piece(lax.rem(my_row + i, ranks), piece)], picked, send, recv
    )
    for c in copies:
        c.start()
    for c in copies:
        c.wait()
    total = flat[row_piece(my_row, piece), :]
    for i in range(1, ranks):
        total = total + picked[i]
    out[...] = total


def sum_kernel(
    ranks, groups, own, mine, out, flat_out, got, done, send_sem, recv_sem, give_send, give_recv
):
    devices = ranks * groups
    my_row = lax.axis_index("rows")
    me = my_row * groups + lax.axis_index("cols")
    piece = mine.shape[0]

    def place(i):
        other = lax.rem(me + i, devices)
        return lax.div(other, groups), lax.rem(other, groups)

    def copy(i):
        return pltpu.make_async_remote_copy(
            src_ref=own,
            dst_ref=got.at[i],
            send_sem=send_sem.at[i],
            recv_sem=recv_sem.at[i],
            device_id=place(i),
            device_id_type=pl.DeviceIdType.MESH,
        )

    barrier = pltpu.get_barrier_semaphore()

    def greet(i, carry):
        pl.semaphore_signal(
            barrier, inc=1, device_id=place(i), device_id_type=pl.DeviceIdType.MESH
        )
        return carry

    def start(i, carry):
        copy(i).start()
        return carry

    def finish(i, carry):
        copy(i).wait()
        return carry

    lax.fori_loop(1, devices, greet, 0)
    pl.semaphore_wait(barrier, devices - 1)
    gives = row_copies(ranks, lambda i: mine, done, give_send, give_recv)
    for c in gives:
        c.start()
    lax.fori_loop(1, devices, start, 0)
    flat_out[row_piece(my_row, piece), :] = mine[...]
    lax.fori_loop(1, devices, finish, 0)
    out[...] = lax.fori_loop(1, devices, lambda i, total: total + got[i], own[...])
    for c in gives:
        c.wait()
    for i in range(1, ranks):
        flat_out[row_piece(lax.rem(my_row - i + ranks, ranks), piece), :] = done[i]


def split_kernel(expand_in, reduce_in, expand_out, reduce_out):
    expand_out[...] = expand_in[...]
    reduce_out[...] = reduce_in[...]


def wide_tables(width):
    freq = np.arange(BINS)
    place = np.arange(width)
    angle = (freq[:, None] * place[None, :] % width) * (2.0 * math.pi / width)
    live = (2 * freq <= width).astype(np.float64)[:, None]
    edge = (freq == 0) | (2 * freq == width)
    weight = np.where(edge, 1.0, 2.0)[:, None] * live
    cosine, sine = np.cos(angle), np.sin(angle)
    plain = np.concatenate([live * cosine, -live * sine], axis=0)
    doubled = np.concatenate([weight * cosine, -weight * sine], axis=0)
    return plain, doubled


def tall_tables(height, rows_here):
    pairs = rows_here // PAIR
    rows = pairs // PARTS
    order = np.array(
        [
            r * rows_here + h * pairs + q * rows + j
            for h in range(PAIR)
            for q in range(PARTS)
            for r in range(height // rows_here)
            for j in range(rows)
        ]
    )
    freq = np.arange(height)
    angle = (freq[:, None] * order[None, :] % height) * (2.0 * math.pi / height)
    cosine, sine = np.cos(angle), np.sin(angle)
    down = np.block([[cosine, sine], [-sine, cosine]])
    up = np.block([[cosine.T, -sine.T], [sine.T, cosine.T]])
    return down, up


def spread(weight):
    count = weight.shape[1]
    eye = jnp.eye(count, dtype=weight.dtype)
    full = jnp.einsum("rbio,bd->rbido", weight, eye)
    return full.reshape(2, count * BS, count * BS)


def gather_blocks(full):
    count = full.shape[1] // BS
    return jnp.stack(
        [full[:, b * BS : (b + 1) * BS, b * BS : (b + 1) * BS] for b in range(count)], axis=1
    )


def bias_rows(bias):
    return bias.reshape(2, -1)


def whole(shape):
    return pl.BlockSpec(shape, lambda *_: (0,) * len(shape))


def call(kernel, grid, in_specs, out_specs, out_shape, name, flops=0, nbytes=0, scratch=(), **kw):
    return pl.pallas_call(
        kernel,
        grid=(grid,),
        in_specs=in_specs,
        out_specs=out_specs,
        out_shape=out_shape,
        scratch_shapes=scratch,
        compiler_params=pltpu.CompilerParams(
            dimension_semantics=("arbitrary",), vmem_limit_bytes=VMEM
        ),
        cost_estimate=pl.CostEstimate(flops=flops, bytes_accessed=nbytes, transcendentals=0),
        name=name,
        **kw,
    )


def body(
    states,
    heights,
    widths,
    first_gain,
    first_shift,
    filter_inner,
    inner_bias,
    filter_outer,
    outer_bias,
    later_gain,
    later_shift,
    expand_weight,
    expand_bias,
    reduce_weight,
    reduce_bias,
    cotangent,
):
    frames, rows_here, cols_here, chans = states.shape
    ranks, groups = lax.axis_size("rows"), lax.axis_size("cols")
    assert frames == ranks and rows_here % (PAIR * PARTS) == 0
    height, breadth = rows_here * ranks, cols_here * groups
    devices = ranks * groups
    pairs = rows_here // PAIR
    rows = pairs // PARTS
    pixels = rows * cols_here
    width = chans // groups
    lanes = width * PAIR
    hidden = expand_weight.shape[1]
    factor = 1.0 / math.sqrt(height * breadth)
    short = ranks * rows
    step_pixels = 8 if pixels % 8 == 0 else pixels
    steps = pixels // step_pixels
    tokens = PAIR * pixels * frames
    message = devices * pixels * lanes * 4
    row = lambda v: v.reshape(1, -1)
    shape = jax.ShapeDtypeStruct

    order = lambda v: jnp.transpose(v, (1, 2, 0, 3)).reshape(PAIR, pairs * cols_here, frames, chans)
    restore = lambda v: jnp.transpose(v.reshape(rows_here, cols_here, frames, chans), (2, 0, 1, 3))
    states_in, cot_in = order(states), order(cotangent)
    row_ids = lax.axis_index("rows") * rows_here + jnp.arange(rows_here, dtype=jnp.int32)
    col_ids = lax.axis_index("cols") * cols_here + jnp.arange(cols_here, dtype=jnp.int32)
    inside = (row_ids[:, None, None] < heights) & (col_ids[None, :, None] < widths)
    mask = jnp.broadcast_to(
        inside.astype(f32).reshape(PAIR, pairs * cols_here, frames, 1),
        (PAIR, pairs * cols_here, frames, 128),
    )

    buffers = {} if steps > 1 else {"pipeline_mode": pl.Buffered(1)}

    def token_spec(q, where, last=chans):
        return pl.BlockSpec(
            (PAIR, step_pixels, frames, last), lambda i: (0, q * steps + where(i), 0, 0), **buffers
        )

    def packed_spec(where):
        return pl.BlockSpec(
            (ranks, groups, step_pixels, lanes), lambda i: (0, 0, where(i), 0), **buffers
        )

    blocks_here = width // BS
    split = blocks_here > 1 and steps > 1 and (2 * PAIR * BS) % 128 == 0
    parties = blocks_here if split else 1
    cut = width // parties
    split_rows = 8 * (-(-steps // 2))

    def arrays_of(q):
        return parties if q == 0 else 1

    def message_specs(q, where):
        if arrays_of(q) == 1:
            return [packed_spec(where)]
        return [
            pl.BlockSpec(
                (ranks, groups, step_pixels, 2 * PAIR * cut), lambda i: (0, 0, where(i) // 2, 0)
            )
        ] * parties

    def message_shapes(q):
        if arrays_of(q) == 1:
            return [packed_shape]
        return [shape((ranks, groups, split_rows, 2 * PAIR * cut), f32)] * parties

    same = lambda i: i
    token_shape = shape((PAIR, pairs * cols_here, frames, chans), bf16)
    packed_shape = shape((ranks, groups, pixels, lanes), f32)
    chan_row = whole((1, chans))
    anywhere = pl.BlockSpec(memory_space=pl.ANY)

    def scatter(v, axis):
        return lax.psum_scatter(v, axis, scatter_dimension=0, tiled=True)

    def gather(v, axis):
        return lax.all_gather(v, axis, axis=0, tiled=True)

    vmem = pl.BlockSpec(memory_space=pltpu.VMEM)

    def as_rows(v, unit):
        v = v.reshape(-1)
        return jnp.pad(v, (0, -v.shape[0] % (unit * 128))).reshape(-1, 128)

    def pick_sums(v):
        flat = as_rows(v, 8 * ranks)
        piece = (flat.shape[0] // ranks, 128)
        return pl.pallas_call(
            functools.partial(pick_kernel, ranks),
            in_specs=[vmem],
            out_specs=vmem,
            out_shape=shape(piece, f32),
            scratch_shapes=[pltpu.VMEM((ranks,) + piece, f32)]
            + [pltpu.SemaphoreType.DMA((ranks,))] * 2,
            compiler_params=pltpu.CompilerParams(collective_id=1, has_side_effects=True),
            name="filter_sums",
        )(flat)

    def sum_small(v, mine):
        own = as_rows(v, 8)
        out, flat_out = pl.pallas_call(
            functools.partial(sum_kernel, ranks, groups),
            in_specs=[vmem, vmem],
            out_specs=[vmem, vmem],
            out_shape=[shape(own.shape, f32), shape((ranks * mine.shape[0], 128), f32)],
            scratch_shapes=[
                pltpu.VMEM((devices,) + own.shape, f32),
                pltpu.VMEM((ranks,) + mine.shape, f32),
            ]
            + [pltpu.SemaphoreType.DMA((devices,))] * 2
            + [pltpu.SemaphoreType.DMA((ranks,))] * 2,
            compiler_params=pltpu.CompilerParams(collective_id=0, has_side_effects=True),
            name="small_sums",
        )(own, mine)
        return out.reshape(-1)[: v.size].reshape(v.shape), flat_out.reshape(-1)

    def split_grads(v):
        cuts = 4
        piece = (chans // cuts, chans)
        return call(
            split_kernel,
            slabs * cuts,
            [
                pl.BlockSpec(piece, lambda i: (i, 0)),
                pl.BlockSpec(piece, lambda i: (slabs * cuts + i, 0)),
            ],
            [
                pl.BlockSpec(piece, lambda i: (lax.rem(i, cuts), lax.div(i, cuts))),
                pl.BlockSpec(piece, lambda i: (i, 0)),
            ],
            [shape((chans, hidden), f32), shape((hidden, chans), f32)],
            "split_gradients",
            nbytes=16 * chans * hidden,
        )(v, v)

    def behind(v, *after):
        return lax.optimization_barrier((v,) + after)[0] if after else v

    def exchange(v):
        sent = v.reshape((devices,) + v.shape[2:])
        return lax.all_to_all(sent, ("rows", "cols"), 0, 0, tiled=True).reshape(v.shape)

    def tie(*values):
        return lax.optimization_barrier(values)

    def first_norm(q):
        return call(
            functools.partial(first_kernel, width),
            steps,
            [token_spec(q, same), token_spec(q, same, 128), chan_row, chan_row],
            message_specs(q, same),
            message_shapes(q),
            "first_norm",
            nbytes=2 * message,
        )(states_in, mask, row(first_gain), row(first_shift))

    plain, doubled = wide_tables(breadth)
    down, up = tall_tables(height, rows_here)
    as_table = lambda t: jnp.asarray(t, dtype=bf16)

    def fine_table(t):
        high = t.astype(jnp.bfloat16)
        return jnp.asarray(np.concatenate([high, (t - high.astype(np.float64)).astype(jnp.bfloat16)]))

    def mixes(weight):
        return [weight[:, g] for g in range(parties)] if split else [spread(weight)]

    inner_full, outer_full = mixes(filter_inner), mixes(filter_outer)
    turn = lambda t: jnp.swapaxes(t, 1, 2)
    bin_steps = BINS // GROUP
    group_rows = GROUP * 2 * height
    held_shape = shape((short, 2, BINS, lanes), f32)
    at_once = 4
    held_row = pl.BlockSpec((at_once * rows, 2, BINS, lanes), lambda i: (i, 0, 0, 0))
    held_bins = pl.BlockSpec((short, 2, GROUP, lanes), lambda i: (0, 0, i, 0))
    field = pl.BlockSpec((at_once, groups, pixels, lanes), lambda i: (i, 0, 0, 0))
    kept = pl.BlockSpec((group_rows, cut), lambda i: (i, 0))
    kept_shape = shape((bin_steps * group_rows, cut), bf16)
    mix_spec = whole((2, cut, cut))
    bias_spec = whole((2, cut))

    def held_of(last, by_row):
        if by_row:
            return pl.BlockSpec((at_once * rows, 2, BINS, last), lambda i: (i, 0, 0, 0))
        return pl.BlockSpec((short, 2, GROUP, last), lambda i: (0, 0, i, 0))

    cut_shape = shape((short, 2, BINS, PAIR * cut), f32)
    split_field = pl.BlockSpec(
        (at_once, groups, split_rows, 2 * PAIR * cut), lambda i: (i, 0, 0, 0)
    )
    natural = pltpu.VMEM((at_once, groups, pixels, PAIR * cut), f32)
    cut_in = [held_of(PAIR * cut if split else lanes, False)] + [held_bins] * (PARTS - 1)
    cut_out = [held_of(PAIR * cut, False)] * PARTS
    up_spec = whole((2 * height, 2 * height))

    def wide_in(v, table, fine):
        divided = v.shape != packed_shape.shape
        return call(
            functools.partial(wide_in_split_kernel if divided else wide_in_kernel, cols_here, fine),
            ranks // at_once,
            [split_field if divided else field, whole(table.shape)],
            held_of(PAIR * cut, True) if divided else held_row,
            cut_shape if divided else held_shape,
            "wide_in",
            nbytes=2 * message,
            scratch=[pltpu.VMEM((at_once * rows, breadth, PAIR * cut), f32), natural]
            if divided
            else [pltpu.VMEM((at_once * rows, breadth, lanes), f32)],
        )(v, table)

    def wide_out(parts, table):
        return call(
            functools.partial(wide_out_kernel, cols_here, factor),
            ranks // at_once,
            [held_of(v.shape[3], True) for v in parts] + [whole(table.shape)],
            field,
            packed_shape,
            "wide_out",
            nbytes=2 * message,
        )(*parts, table)

    def wide_out_split(part, table):
        return call(
            functools.partial(wide_out_split_kernel, cols_here, factor),
            ranks // at_once,
            [held_of(PAIR * cut, True), whole(table.shape)],
            split_field,
            message_shapes(0)[0],
            "wide_out",
            nbytes=2 * message,
            scratch=[natural],
        )(part, table)

    def messages_out(given, table):
        first = [wide_out_split(v[0], table) for v in given] if split else [wide_out([given[0][0]], table)]
        return first + [wide_out([v[q] for v in given], table) for q in range(1, PARTS)]

    def of_group(v, g):
        return bias_rows(v)[:, g * cut : (g + 1) * cut]

    forward_mix = [
        (inner_full[g], of_group(inner_bias, g), outer_full[g], of_group(outer_bias, g))
        for g in range(parties)
    ]
    forward_specs = [mix_spec, bias_spec, mix_spec, bias_spec]

    def spectral_forward(g, held):
        table = fine_table(down)
        outs = call(
            functools.partial(spectral_forward_kernel, factor, g),
            bin_steps,
            cut_in + [whole(table.shape), up_spec] + forward_specs,
            cut_out + [kept],
            [cut_shape] * PARTS + [kept_shape],
            "spectral_forward",
            flops=20 * 10**9,
            nbytes=8 * PARTS * message // parties,
        )(*held, table, as_table(up), *forward_mix[g])
        return outs[:PARTS], outs[PARTS]

    full = pl.BlockSpec((group_rows, width), lambda i: (i, 0))
    full_shape = shape((bin_steps * group_rows, width), bf16)
    full_mix, full_bias = whole((2, width, width)), whole((2, width))
    inner_t, outer_t = turn(spread(filter_inner)), turn(spread(filter_outer))

    def spectral_keep(entries):
        return call(
            functools.partial(spectral_keep_kernel, height, parties),
            bin_steps,
            [kept] * parties + forward_specs * parties,
            [full] * 3,
            [full_shape] * 3,
            "spectral_keep",
            flops=10 * 10**9,
            nbytes=2 * PARTS * message,
        )(*entries, *[v for mix in forward_mix for v in mix])

    def spectral_backward(held, slope, damp):
        outs = call(
            functools.partial(spectral_backward_kernel, factor, 1),
            bin_steps,
            [held_bins] * PARTS + [up_spec, up_spec, full_mix, full_mix] + [full] * 2,
            [held_bins] * PARTS + [full, full_bias] * 2,
            [held_shape] * PARTS + [full_shape, shape((2, width), f32)] * 2,
            "spectral_backward",
            flops=20 * 10**9,
            nbytes=8 * PARTS * message,
        )(*held, as_table(down), as_table(up), inner_t, outer_t, slope, damp)
        return outs[:PARTS], outs[PARTS:]

    def filter_grad(entries, active, inner_low, outer_low):
        return call(
            functools.partial(filter_grad_kernel, height, parties),
            bin_steps,
            [kept] * parties + [full] * 3,
            [full_mix] * 2,
            [shape((2, width, width), f32)] * 2,
            "filter_grad",
            flops=10 * 10**9,
            nbytes=2 * PARTS * message,
        )(*entries, active, inner_low, outer_low)

    slab = chans
    slabs = hidden // slab
    dense_steps = 2 * steps + slabs
    enter = lambda i: jnp.minimum(i, steps - 1)
    leave = lambda i: jnp.maximum(i - steps - slabs, 0)
    either = lambda i: jnp.where(i < steps + slabs, enter(i), leave(i))

    def dense(q, spatial, before):
        grads_before = () if q == 0 else before
        return call(
            functools.partial(dense_kernel, steps, slabs, width, q == 0, arrays_of(q)),
            dense_steps,
            message_specs(q, enter)
            + [token_spec(q, enter), token_spec(q, enter), token_spec(q, either, 128)]
            + [chan_row] * 4
            + [pl.BlockSpec((1, slab), lambda i: (0, jnp.clip(i - steps, 0, slabs - 1)))]
            + [chan_row]
            + [anywhere] * (2 + len(grads_before)),
            [packed_spec(leave)]
            + [
                token_spec(q, leave),
                token_spec(0, leave),
                whole((8, chans)),
                whole((slabs, slab)),
                anywhere,
            ],
            [packed_shape]
            + [
                token_shape,
                shape((PAIR, pixels, frames, chans), f32),
                shape((8, chans), f32),
                shape((slabs, slab), f32),
                shape((2 * hidden, chans), f32),
            ],
            "dense_both_ways",
            flops=12 * tokens * chans * hidden,
            nbytes=4 * message,
            scratch=[
                pltpu.VMEM((slabs, chans, slab), bf16),
                pltpu.VMEM((hidden, chans), bf16),
                pltpu.VMEM((slabs, chans, slab), f32),
                pltpu.VMEM((hidden, chans), f32),
                pltpu.VMEM((tokens, chans), f32),
                pltpu.VMEM((tokens, chans), bf16),
                pltpu.VMEM((tokens, chans), bf16),
                pltpu.VMEM((tokens, chans), f32),
                pltpu.VMEM((tokens, chans), f32),
                pltpu.VMEM((tokens, slab), bf16),
                pltpu.VMEM((tokens, slab), bf16),
                pltpu.SemaphoreType.DMA((2 * slabs + 2,)),
            ],
            input_output_aliases={} if q == 0 else {13: 1},
        )(
            *spatial,
            states_in,
            cot_in,
            mask,
            row(first_gain),
            row(first_shift),
            row(later_gain),
            row(later_shift),
            row(expand_bias),
            row(reduce_bias),
            expand_weight,
            reduce_weight,
            *grads_before,
        )

    def last_norm(q, later_grad, spatial, before):
        given = () if q == 0 else (before,)
        return call(
            functools.partial(last_kernel, width, 1),
            steps,
            [packed_spec(same)]
            + [token_spec(q, same), token_spec(0, same), token_spec(q, same, 128)]
            + [chan_row]
            + [anywhere] * len(given),
            [token_spec(q, same), whole((8, chans))],
            [token_shape, shape((8, chans), f32)],
            "first_norm_backward",
            nbytes=4 * message,
            input_output_aliases={} if q == 0 else {5: 0},
        )(spatial, states_in, later_grad, mask, row(first_gain), *given)

    every = range(PARTS)

    def send(made, got):
        if got:
            made, got[-1] = tie(made, got[-1])
        got.append(exchange(made))

    made = [v for q in (*every[1:], 0) for v in first_norm(q)]
    got, held = [], []
    for n, v in enumerate(made):
        if n > 1:
            v, held[-1] = tie(v, held[-1])
        send(v, got)
        if n > 0:
            held.append(wide_in(got[-2], fine_table(plain), True))
    held.append(wide_in(got[-1], fine_table(plain), True))
    rest, first = held[: PARTS - 1], held[PARTS - 1 :]
    done = [spectral_forward(g, [first[g]] + rest) for g in range(parties)]
    entries = [v[1] for v in done]
    made = messages_out([v[0] for v in done], as_table(doubled.T))
    active, slope, damp = spectral_keep(entries)

    spatial = got[-1:]
    for n in range(parties):
        send(made[n], spatial)
    active, made[parties] = tie(active, made[parties])
    spatial = spatial[1:]
    backs, later_grads, sums, expand_bias_grad, before = [], [], 0.0, 0.0, ()
    for q in every:
        if q + 1 < PARTS:
            if backs:
                made[parties + q], backs[-1] = tie(made[parties + q], backs[-1])
            send(made[parties + q], spatial)
        received = spatial[:parties] if q == 0 else spatial[parties + q - 1 : parties + q]
        if q + 1 == PARTS:
            backs[-1], spatial[-1] = tie(backs[-1], spatial[-1])
            got = [exchange(backs[1])]
            received = spatial[-1:]
        outs = dense(q, received, before)
        back, result, kept_grad, part, bias_part, grads = outs
        backs.append(back)
        before = (grads, result)
        later_grads.append(kept_grad)
        sums, expand_bias_grad = sums + part, expand_bias_grad + bias_part
    grads, got[0] = tie(grads, got[0])
    grads = scatter(grads, "cols")
    held = []
    for v in [backs[q] for q in (*every[2:], 0)]:
        held.append(wide_in(got[-1], as_table(doubled), False))
        if len(held) > 1:
            v, held[-2] = tie(v, held[-2])
        send(v, got)
    got[-1], held[-1] = tie(got[-1], held[-1])
    held.append(wide_in(got[-1], as_table(doubled), False))
    grads, held[-1] = tie(grads, held[-1])
    grads = scatter(grads, "rows")
    given, (inner_low, inner_bias_grad, outer_low, outer_bias_grad) = spectral_backward(
        [held[-1]] + held[:-1], slope, damp
    )
    made = [wide_out([v], as_table(plain.T)) for v in given]
    inner_grad, outer_grad = filter_grad(entries, active, inner_low, outer_low)
    filter_parts = (
        gather_blocks(inner_grad), inner_bias_grad, gather_blocks(outer_grad), outer_bias_grad
    )
    flat = jnp.concatenate([v.reshape(-1) for v in filter_parts])

    got = [exchange(made[0])]
    send(made[1], got)
    grads, got[0] = tie(grads, got[0])
    grads = gather(grads, ("cols", "rows"))
    expand_sum, reduce_sum = split_grads(grads)
    first_sums, states_grad = [], None
    for q in every:
        if q + 1 < PARTS:
            if q > 0:
                made[q + 1], first_sums[-1] = tie(made[q + 1], first_sums[-1])
                send(made[q + 1], got)
        else:
            flat, expand_sum = tie(flat, expand_sum)
            flat = pick_sums(flat)
            states_grad, flat = tie(states_grad, flat)
            states_grad, expand_sum = tie(states_grad, expand_sum)
        states_grad, part = last_norm(q, later_grads[q], got[q], states_grad)
        first_sums.append(part)
        if q == 0:
            flat, first_sums[0] = tie(flat, first_sums[0])
    small, flat = sum_small(
        jnp.concatenate([sum(first_sums)[:2], sums[:3], expand_bias_grad.reshape(-1, chans)]), flat
    )
    sizes = [v.size for v in filter_parts]
    ends = np.cumsum(sizes)
    filter_sums = [
        flat[e - n : e].reshape(v.shape) for e, n, v in zip(ends, sizes, filter_parts)
    ]
    inner_sum, inner_bias_sum, outer_sum, outer_bias_sum = filter_sums
    return (
        restore(result),
        restore(states_grad),
        small[0],
        small[1],
        inner_sum,
        inner_bias_sum.reshape(2, -1, BS),
        outer_sum,
        outer_bias_sum.reshape(2, -1, BS),
        small[3],
        small[4],
        expand_sum,
        small[5:].reshape(-1),
        reduce_sum,
        small[2],
    )


def solution(mesh):
    tile = P(None, "rows", "cols", None)
    mix = P(None, "cols", None, None)
    bias = P(None, "cols", None)
    in_specs = (
        tile, P(), P(), P(), P(), mix, bias, mix, bias, P(), P(), P(), P(), P(), P(), tile,
    )
    out_specs = (
        tile, tile, P(), P(), mix, bias, mix, bias, P(), P(), P(), P(), P(), P(),
    )
    return jax.shard_map(body, mesh=mesh, in_specs=in_specs, out_specs=out_specs, check_vma=False)
```
